256 devices in a mesh: grp: 4 (over z_hi), seq: 16 (over z_lo, y, core), dp: 4 (over x).
Axes of the slice: x: 4, y: 4, z: 8 (z_hi: 4, z_lo: 2; z = z_hi * 2 + z_lo), core: 2. Of those that a mesh axis runs over, the one named last changes fastest.
Arguments:
- image_hidden: bfloat16 [8, 4, 512, 3072], P('grp', 'dp', 'seq'), may hold values from -6 to 6
- control_hidden: bfloat16 [8, 4, 512, 3072], P(None, 'dp', 'seq', 'grp'), may hold values from -6 to 6
- text_qkv: bfloat16 [3, 8, 4, 512, 2048], P(None, 'grp', 'dp', 'seq')
- text_lengths: int32 [8, 4], P('grp', 'dp'), may hold values from 64 to 512, as said below
- timesteps: int32 [8, 4], P('grp', 'dp'), may hold values from 0 to 999
- mod_weight: bfloat16 [256, 6144], replicated, may hold values from -0.375 to 0.375
- qkv_weight: bfloat16 [3072, 3, 2048], P('dp', None, 'seq'), may hold values from -0.078125 to 0.078125
- zero_weight: bfloat16 [3072, 3072], P('grp'), may hold values from -0.109375 to 0.109375
- image_cotangent: bfloat16 [8, 4, 512, 2048], P('grp', 'dp', 'seq'), may hold values from -6 to 6
- text_cotangent: bfloat16 [8, 4, 512, 2048], P('grp', 'dp', 'seq'), may hold values from -6 to 6
Outputs:
- image_attn: bfloat16 [8, 4, 512, 2048], P('grp', 'dp', 'seq')
- text_attn: bfloat16 [8, 4, 512, 2048], P('grp', 'dp', 'seq')
- control_grad: bfloat16 [8, 4, 512, 3072], P(None, 'dp', 'seq', 'grp')
- zero_grad: float32 [3072, 3072], P('grp', 'seq')
The draws below stay inside these ranges and needn't reach their ends.
Inputs may be any that keep to these rules, and one draw needn't show every extreme that they name: `text_lengths`: text positions at or beyond a sample's length are padding.
All inputs are finite; a program needn't handle non-finite values.
Results may differ from the reference program's by a relative error of at most 0.029.
Values may be sent and summed in bfloat16 or wider, within the bound.
A program may use at most 128 MiB of HBM per device.

```python
import math
import jax
import jax.numpy as jnp
from jax import lax

D = 3072
HEADS = 16
HD = 128
Q = 2048
IMG = 512
TXT = 512
FREQ = 256
TSTEPS = 1000
BG = 8
BD = 4
N_SEQ = 16


def draw_text_qkv(key, part):
    key = jax.random.fold_in(key, 11)
    shape = (3, BG, BD, TXT, HEADS * HD)
    field = jax.random.truncated_normal(key, -4.0, 4.0, shape, jnp.float32)
    return jnp.stack([field[0] * math.sqrt(3.0), field[1] * math.sqrt(3.0), field[2] * 0.5]).astype(jnp.bfloat16)


def draw_text_lengths(key, part):
    key = jax.random.fold_in(key, 23)
    sample_total = BG * BD
    lengths = jax.random.randint(jax.random.fold_in(key, 1), (sample_total,), TXT // 8, TXT + 1)
    first_slot = jax.random.randint(jax.random.fold_in(key, 2), (), 0, sample_total)
    second_slot = (first_slot + 1 + jax.random.randint(jax.random.fold_in(key, 3), (), 0, sample_total - 1)) % sample_total
    slots = jnp.arange(sample_total)
    lengths = jnp.where(slots == first_slot, TXT, jnp.where(slots == second_slot, TXT // 8, lengths))
    return lengths.reshape(BG, BD).astype(jnp.int32)


def set_ends(values, stream_key, low, high):
    longest = values.shape.index(max(values.shape))
    spots = []
    for shift in (0, 1):
        where = [jax.random.randint(jax.random.fold_in(stream_key, axis), (), 0, length) for axis, length in enumerate(values.shape)]
        where[longest] = (where[longest] + shift) % values.shape[longest]
        spots.append(tuple(where))
    return values.at[spots[0]].set(low).at[spots[1]].set(high)


def levels(key, shape, split, least, high):
    def one(axis_at, parts):
        steps = jax.random.uniform(jax.random.fold_in(jax.random.fold_in(key, 6), axis_at), (parts,), jnp.float32, least / len(split), high / len(split))
        return jnp.repeat(jnp.exp(steps), shape[axis_at] // parts).reshape((-1,) + (1,) * (len(shape) - axis_at - 1))

    factor_of = one(*split[0])
    for cut in split[1:]:
        factor_of = factor_of * one(*cut)
    return factor_of


def gaussian(stream_key, shape, scale, limit, shards=(), kind=jnp.bfloat16):
    loudness = levels(stream_key, shape, shards, -0.22, 0.18) if shards else 1.0
    values = jax.random.normal(stream_key, shape, jnp.float32) * scale * loudness
    return jnp.minimum(jnp.maximum(values, -limit), limit).astype(kind)


def setup_inputs(seed: int = 0) -> dict:
    key_list = jax.random.split(jax.random.key(seed), 11)
    return {
        "image_hidden": gaussian(key_list[0], (BG, BD, IMG, D), 1.0, 6.0, ((0, 4), (1, 4), (2, 16))),
        "control_hidden": gaussian(key_list[1], (BG, BD, IMG, D), 1.0, 6.0, ((1, 4), (2, 16), (3, 4))),
        "text_qkv": draw_text_qkv(jax.random.fold_in(key_list[10], 71), 0),
        "text_lengths": draw_text_lengths(jax.random.fold_in(key_list[10], 71), 0),
        "timesteps": set_ends(jax.random.randint(key_list[4], (BG, BD), 0, TSTEPS), jax.random.fold_in(key_list[4], 1), 0, TSTEPS - 1).astype(jnp.int32),
        "mod_weight": gaussian(key_list[5], (FREQ, 2 * D), FREQ ** -0.5, 0.375),
        "qkv_weight": gaussian(key_list[6], (D, 3, Q), (2 * D) ** -0.5, 0.078125, ((0, 4), (2, 16))),
        "zero_weight": gaussian(key_list[7], (D, D), D ** -0.5, 0.109375, ((0, 4),)),
        "image_cotangent": gaussian(key_list[8], (BG, BD, IMG, Q), 1.0, 6.0, ((0, 4), (1, 4), (2, 16))),
        "text_cotangent": gaussian(key_list[9], (BG, BD, TXT, Q), 1.0, 6.0, ((0, 4), (1, 4), (2, 16))),
    }


def timestep_modulation(timesteps, mod_weight):
    half_freq = FREQ // 2
    frequency = jnp.exp(-math.log(10000.0) * jnp.arange(half_freq, dtype=jnp.float32) / half_freq)
    angles = timesteps.astype(jnp.float32)[..., None] * frequency
    embedding = jnp.concatenate([jnp.cos(angles), jnp.sin(angles)], axis=-1)
    activated = jax.nn.silu(embedding).astype(jnp.bfloat16)
    return jnp.dot(activated.reshape(-1, FREQ), mod_weight, preferred_element_type=jnp.float32)

def normalize(rows):
    values = rows.astype(jnp.float32)
    average = lax.optimization_barrier(jnp.mean(values, axis=-1, keepdims=True))
    centred = values - average
    reciprocal = lax.rsqrt(lax.optimization_barrier(jnp.mean(centred * centred, axis=-1, keepdims=True)) + 1e-06)
    return (centred * reciprocal, reciprocal)

def head_pass(query, key_rows, value_rows, cotangent, live_keys, first_row):
    scaling = query.shape[-1] ** (-0.5)
    dims = (((0,), (0,)), ((), ()))
    scores = jnp.dot(query, key_rows.T, preferred_element_type=jnp.float32) * scaling
    scores = jnp.where(live_keys[None, :], scores, -jnp.inf)
    row_max = lax.optimization_barrier(jnp.max(scores, axis=1, keepdims=True))
    exp_terms = jnp.exp(scores - row_max)
    prob_rows = exp_terms / lax.optimization_barrier(jnp.sum(exp_terms, axis=1, keepdims=True))
    prob_low = prob_rows.astype(jnp.bfloat16)
    attended = jnp.dot(prob_low, value_rows, preferred_element_type=jnp.float32).astype(jnp.bfloat16)
    row_dots = lax.optimization_barrier(jnp.sum(cotangent.astype(jnp.float32) * attended.astype(jnp.float32), axis=1, keepdims=True))
    prob_grad = jnp.dot(cotangent, value_rows.T, preferred_element_type=jnp.float32)
    score_grad = (prob_rows * (prob_grad - row_dots)).astype(jnp.bfloat16)
    query_grad = (jnp.dot(score_grad[first_row:], key_rows, preferred_element_type=jnp.float32) * scaling).astype(jnp.bfloat16)
    key_grad = (lax.dot_general(score_grad[:, first_row:], query, dims, preferred_element_type=jnp.float32) * scaling).astype(jnp.bfloat16)
    value_grad = lax.dot_general(prob_low[:, first_row:], cotangent, dims, preferred_element_type=jnp.float32).astype(jnp.bfloat16)
    return (attended, query_grad, key_grad, value_grad)

def reference(image_hidden, control_hidden, text_qkv, text_lengths, timesteps, mod_weight, qkv_weight, zero_weight, image_cotangent, text_cotangent):
    sample_total = BG * BD
    joint_len = TXT + IMG
    modulation = timestep_modulation(timesteps, mod_weight).reshape(BG, BD, 1, 2 * D)
    offset = modulation[..., :D]
    stretch = 1.0 + modulation[..., D:]
    residual = jnp.dot(control_hidden.reshape(-1, D), zero_weight, preferred_element_type=jnp.float32).reshape(BG, BD, IMG, D)
    hidden = (image_hidden.astype(jnp.float32) + residual).astype(jnp.bfloat16)
    standard, reciprocal = normalize(hidden)
    normed = (standard * stretch + offset).astype(jnp.bfloat16)
    image_qkv = jnp.dot(normed.reshape(-1, D), qkv_weight.reshape(D, 3 * Q), preferred_element_type=jnp.float32).astype(jnp.bfloat16)
    image_heads = jnp.transpose(image_qkv.reshape(sample_total, IMG, 3, HEADS, HD), (2, 0, 3, 1, 4))
    text_heads = jnp.transpose(text_qkv.reshape(3, sample_total, TXT, HEADS, HD), (0, 1, 3, 2, 4))
    joint = jnp.concatenate([text_heads, image_heads], axis=3).reshape(3, sample_total * HEADS, joint_len, HD)
    cotangent = jnp.concatenate([text_cotangent.reshape(sample_total, TXT, HEADS, HD), image_cotangent.reshape(sample_total, IMG, HEADS, HD)], axis=1)
    cotangent = jnp.transpose(cotangent, (0, 2, 1, 3)).reshape(sample_total * HEADS, joint_len, HD)
    position = jnp.arange(joint_len)
    live_keys = (position[None, :] >= TXT) | (position[None, :] < text_lengths.reshape(sample_total, 1))
    live_keys = jnp.repeat(live_keys, HEADS, axis=0)
    attended, query_grad, key_grad, value_grad = lax.map(lambda item_args: head_pass(*item_args, TXT), (joint[0], joint[1], joint[2], cotangent, live_keys))
    attended = jnp.transpose(attended.reshape(sample_total, HEADS, joint_len, HD), (0, 2, 1, 3))
    text_attn = attended[:, :TXT].reshape(BG, BD, TXT, Q)
    image_attn = attended[:, TXT:].reshape(BG, BD, IMG, Q)
    image_grads = jnp.stack([query_grad, key_grad, value_grad]).reshape(3, sample_total, HEADS, IMG, HD)
    image_grads = jnp.transpose(image_grads, (1, 3, 0, 2, 4)).reshape(sample_total * IMG, 3, N_SEQ, HEADS // N_SEQ * HD)
    weight_groups = qkv_weight.reshape(D, 3, N_SEQ, HEADS // N_SEQ * HD)

    def add_group(running, pieces):
        grad_group, weight_group = pieces
        group_part = jnp.dot(grad_group.reshape(sample_total * IMG, -1), weight_group.reshape(D, -1).T, preferred_element_type=jnp.float32)
        group_part = lax.optimization_barrier(group_part.astype(jnp.bfloat16))
        return (running + group_part.astype(jnp.float32), None)
    normed_grad, _ = lax.scan(add_group, jnp.zeros((sample_total * IMG, D), jnp.float32), (jnp.moveaxis(image_grads, 2, 0), jnp.moveaxis(weight_groups, 2, 0)))
    normed_grad = normed_grad.reshape(BG, BD, IMG, D)
    scaled_grad = normed_grad * stretch
    residual_grad = (reciprocal * (scaled_grad - lax.optimization_barrier(jnp.mean(scaled_grad, axis=-1, keepdims=True)) - standard * lax.optimization_barrier(jnp.mean(scaled_grad * standard, axis=-1, keepdims=True)))).astype(jnp.bfloat16)
    control_grad = jnp.dot(residual_grad.reshape(-1, D), zero_weight.T, preferred_element_type=jnp.float32).astype(jnp.bfloat16).reshape(BG, BD, IMG, D)
    zero_grad = jnp.dot(control_hidden.reshape(-1, D).T, residual_grad.reshape(-1, D), preferred_element_type=jnp.float32) * (BG * BD * IMG) ** (-0.5)
    return (image_attn, text_attn, control_grad, zero_grad)
```

```python
import math

import jax
import jax.numpy as jnp
from jax import lax
from jax.experimental import pallas as pl
from jax.experimental.pallas import tpu as pltpu
from jax.sharding import PartitionSpec as P

D = 3072
HEADS = 16
HD = 128
IMG = 512
TXT = 512
FREQ = 256
ROWS = 32
HALF = D // 2
MESH = pl.DeviceIdType.MESH
BF = jnp.bfloat16
F32 = jnp.float32
VMEM_LIMIT = 56 * 1024 * 1024
ANY = pl.BlockSpec(memory_space=pl.ANY)
VMEM = pl.BlockSpec(memory_space=pltpu.VMEM)


class Sends:
    def __init__(self, sems):
        self.sems = sems
        self.copies = []

    def __call__(self, src, dst, recv, **to):
        copy = pltpu.make_async_remote_copy(
            src_ref=src,
            dst_ref=dst,
            send_sem=self.sems.at[len(self.copies)],
            recv_sem=recv,
            device_id=to,
            device_id_type=MESH,
        )
        copy.start()
        self.copies.append(copy)

    def drain(self):
        for copy in self.copies:
            copy.wait_send()


def arrived(dst, recv):
    pltpu.make_async_copy(dst, dst, recv).wait()


def greet(groups):
    barrier = pltpu.get_barrier_semaphore()
    for to in groups:
        pl.semaphore_signal(barrier, inc=1, device_id=to, device_id_type=MESH)
    pl.semaphore_wait(barrier, len(groups))


class Place:
    def __init__(self):
        self.s = lax.axis_index("seq")
        self.g = lax.axis_index("grp")
        self.d = lax.axis_index("dp")
        self.z = self.s // 8
        self.y = (self.s // 2) % 4
        self.c = self.s % 2
        self.zo = 1 - self.z
        self.co = 1 - self.c
        self.yl = (self.y + 3) % 4
        self.yr = (self.y + 1) % 4
        self.yo = (self.y + 2) % 4
        self.gl = (self.g + 3) % 4
        self.gr = (self.g + 1) % 4
        self.go = (self.g + 2) % 4
        self.dl = (self.d + 3) % 4
        self.dr = (self.d + 1) % 4
        self.do = (self.d + 2) % 4

    def seq(self, z, y, c):
        return z * 8 + y * 2 + c


def add_into(dst, *others):
    total = dst[...].astype(F32)
    for other in others:
        total = total + other[...].astype(F32)
    dst[...] = total.astype(dst.dtype)


class Scatter4:
    def __init__(self, send, src, relay, from_left, from_right, sems, me, left, right, far, to):
        self.send, self.src, self.relay = send, src, relay
        self.from_left, self.from_right, self.sems = from_left, from_right, sems
        self.me, self.left, self.right, self.far, self.to = me, left, right, far, to

    def start(self):
        self.send(self.src(self.far, 0), self.relay(0), self.sems.at[0], **self.to(self.left))
        self.send(self.src(self.far, 1), self.relay(1), self.sems.at[1], **self.to(self.right))

    def direct(self):
        self.send(
            self.src(self.left, 1), self.from_right(1), self.sems.at[2], **self.to(self.left)
        )
        self.send(
            self.src(self.right, 0), self.from_left(0), self.sems.at[3], **self.to(self.right)
        )

    def pass_on(self):
        arrived(self.relay(0), self.sems.at[0])
        add_into(self.src(self.left, 0), self.relay(0))
        self.send(
            self.src(self.left, 0), self.from_right(0), self.sems.at[4], **self.to(self.left)
        )
        arrived(self.relay(1), self.sems.at[1])
        add_into(self.src(self.right, 1), self.relay(1))
        self.send(
            self.src(self.right, 1), self.from_left(1), self.sems.at[5], **self.to(self.right)
        )

    def finish(self):
        arrived(self.from_right(1), self.sems.at[2])
        arrived(self.from_left(0), self.sems.at[3])
        arrived(self.from_right(0), self.sems.at[4])
        arrived(self.from_left(1), self.sems.at[5])


class Gather4:
    def __init__(self, send, slot, half, sems, me, left, right, far, to):
        self.send, self.slot, self.half, self.sems = send, slot, half, sems
        self.me, self.left, self.right, self.far, self.to = me, left, right, far, to

    def start(self, own=None):
        own = self.slot(self.me) if own is None else own
        self.send(own, self.slot(self.me), self.sems.at[0], **self.to(self.right))
        self.send(own, self.slot(self.me), self.sems.at[1], **self.to(self.left))

    def pass_left(self):
        arrived(self.slot(self.left), self.sems.at[0])
        part = self.half(self.left, 0)
        self.send(part, part, self.sems.at[2], **self.to(self.right))

    def pass_right(self):
        arrived(self.slot(self.right), self.sems.at[1])
        part = self.half(self.right, 1)
        self.send(part, part, self.sems.at[3], **self.to(self.left))

    def finish(self):
        arrived(self.half(self.far, 0), self.sems.at[2])
        arrived(self.half(self.far, 1), self.sems.at[3])


def seq_peers(p):
    return [{"seq": (p.s + k) % 16} for k in range(1, 16)]


def front_kernel(
    control,
    zero_weight,
    image_hidden,
    stretch,
    offset,
    weight,
    text,
    text_cot,
    image_cot,
    normed_all,
    hidden_out,
    weight_all,
    text_all,
    text_cot_all,
    image_cot_all,
    partial,
    relay,
    from_left,
    from_right,
    own,
    send_sem,
    rs_sem,
    ag_sem,
    w_sem,
    text_send,
    text_recv,
    local_sem,
):
    p = Place()
    greet(
        seq_peers(p) + [{"grp": p.gl}, {"grp": p.gr}, {"dp": p.dl}, {"dp": p.dr}]
    )
    send = Sends(send_sem)

    weights = Gather4(
        send,
        lambda d: weight_all.at[d],
        lambda d, h: weight_all.at[d, pl.ds(h * 384, 384)],
        w_sem,
        p.d,
        p.dl,
        p.dr,
        p.do,
        lambda d: {"dp": d},
    )
    weights.start(weight)
    keep_weight = pltpu.make_async_copy(weight, weight_all.at[p.d], local_sem.at[0])
    keep_weight.start()

    for block in range(6):
        cols = pl.ds(block * 512, 512)
        product = jnp.dot(control[...], zero_weight[:, cols], preferred_element_type=F32)
        partial[:, :, :, cols] = product.astype(BF).reshape(4, 2, ROWS, 512)

    scatters = []
    for i in range(2):
        scatters.append(
            Scatter4(
                send,
                lambda g, h, i=i: partial.at[g, i, :, pl.ds(h * HALF, HALF)],
                lambda h, i=i: relay.at[i, h],
                lambda h, i=i: from_left.at[i, h],
                lambda h, i=i: from_right.at[i, h],
                rs_sem.at[i],
                p.g,
                p.gl,
                p.gr,
                p.go,
                lambda g: {"grp": g},
            )
        )
    for i in range(2):
        scatters[i].start()
        scatters[i].direct()

    col = pl.multiple_of(p.s * HD, HD)
    row = pl.multiple_of(p.s * ROWS, ROWS)
    locals_ = [
        pltpu.make_async_copy(
            text.at[:, :, :, pl.ds(col, HD)], text_all.at[:, :, pl.ds(row, ROWS)], text_recv.at[0]
        ),
        pltpu.make_async_copy(
            text_cot.at[:, :, pl.ds(col, HD)], text_cot_all.at[:, pl.ds(row, ROWS)], text_recv.at[1]
        ),
        pltpu.make_async_copy(
            image_cot.at[:, :, pl.ds(col, HD)],
            image_cot_all.at[:, pl.ds(row, ROWS)],
            text_recv.at[2],
        ),
    ]
    for copy in locals_:
        copy.start()

    def text_copies(k):
        to = (p.s + k) % 16
        far_col = pl.multiple_of(to * HD, HD)
        pairs = (
            (text.at[:, :, :, pl.ds(far_col, HD)], text_all.at[:, :, pl.ds(row, ROWS)]),
            (text_cot.at[:, :, pl.ds(far_col, HD)], text_cot_all.at[:, pl.ds(row, ROWS)]),
            (image_cot.at[:, :, pl.ds(far_col, HD)], image_cot_all.at[:, pl.ds(row, ROWS)]),
        )
        return [
            pltpu.make_async_remote_copy(
                src_ref=src,
                dst_ref=dst,
                send_sem=text_send.at[n, k],
                recv_sem=text_recv.at[n],
                device_id={"seq": to},
                device_id_type=MESH,
            )
            for n, (src, dst) in enumerate(pairs)
        ]

    @pl.loop(1, 16)
    def _(k):
        for copy in text_copies(k):
            copy.start()

    for i in range(2):
        scatters[i].pass_on()

    gathers = []
    for i in range(2):
        pair = []
        for which, z in enumerate((p.z, p.zo)):
            pair.append(
                Gather4(
                    send,
                    lambda y, i=i, z=z: normed_all.at[i, z, y, p.c],
                    lambda y, h, i=i, z=z: normed_all.at[i, z, y, p.c, pl.ds(h * 16, 16)],
                    ag_sem.at[i, pl.ds(which * 4, 4)],
                    p.y,
                    p.yl,
                    p.yr,
                    p.yo,
                    lambda y: {"seq": p.seq(p.z, y, p.c)},
                )
            )
        gathers.append(pair)

    partner = {"seq": p.seq(p.z, p.y, p.co)}
    across = {"seq": p.seq(p.zo, p.y, p.c)}

    def share(i, z, y, sem):
        slot = normed_all.at[i, z, y, p.c]
        send(slot, slot, ag_sem.at[i, sem], **partner)

    keeps = []

    def first(i):
        scatters[i].finish()
        halves = []
        for h in range(2):
            cols = pl.ds(h * HALF, HALF)
            residual = (
                partial[p.g, i, :, cols].astype(F32)
                + from_left[i, h].astype(F32)
                + from_right[i, h].astype(F32)
            )
            halves.append((image_hidden[i, :, cols].astype(F32) + residual).astype(BF))
        for h in range(2):
            hidden_out[i, :, pl.ds(h * HALF, HALF)] = halves[h]
        values = hidden_out[i].astype(F32)
        average = jnp.mean(values, axis=-1, keepdims=True)
        centred = values - average
        reciprocal = lax.rsqrt(jnp.mean(centred * centred, axis=-1, keepdims=True) + 1e-06)
        own[i] = (centred * reciprocal * stretch[i : i + 1] + offset[i : i + 1]).astype(BF)
        mine = normed_all.at[i, p.z, p.y, p.c]
        send(own.at[i], mine, ag_sem.at[i, 8], **across)
        gathers[i][0].start(own.at[i])
        send(own.at[i], mine, ag_sem.at[i, 9], **partner)
        keep = pltpu.make_async_copy(own.at[i], mine, local_sem.at[1 + i])
        keep.start()
        keeps.append(keep)

    def second(i):
        arrived(normed_all.at[i, p.zo, p.y, p.c], ag_sem.at[i, 8])
        gathers[i][1].start()
        share(i, p.zo, p.y, 10)

    def third(i, which):
        z = (p.z, p.zo)[which]
        gathers[i][which].pass_left()
        gathers[i][which].pass_right()
        share(i, z, p.yl, 11 + 3 * which)
        share(i, z, p.yr, 12 + 3 * which)

    def fourth(i, which):
        z = (p.z, p.zo)[which]
        gathers[i][which].finish()
        share(i, z, p.yo, 13 + 3 * which)

    first(0)
    second(0)
    third(0, 0)
    weights.pass_left()
    weights.pass_right()
    first(1)
    third(0, 1)
    second(1)
    fourth(0, 0)
    third(1, 0)
    fourth(0, 1)
    third(1, 1)
    fourth(1, 0)
    fourth(1, 1)
    for i in range(2):
        arrived(normed_all.at[i, p.z, p.y, p.co], ag_sem.at[i, 9])
        arrived(normed_all.at[i, p.zo, p.y, p.co], ag_sem.at[i, 10])
        for which, z in enumerate((p.z, p.zo)):
            for n, y in enumerate((p.yl, p.yr, p.yo)):
                arrived(normed_all.at[i, z, y, p.co], ag_sem.at[i, 11 + 3 * which + n])
    weights.finish()
    arrived(text_all, text_recv.at[0])
    arrived(text_cot_all, text_recv.at[1])
    arrived(image_cot_all, text_recv.at[2])
    keep_weight.wait()
    for keep in keeps:
        keep.wait()
    send.drain()

    @pl.loop(1, 16)
    def _(k):
        for copy in text_copies(k):
            copy.wait_send()


def front(control, zero_weight, image_hidden, stretch, offset, weight, text, text_cot, image_cot):
    return pl.pallas_call(
        front_kernel,
        out_shape=(
            jax.ShapeDtypeStruct((2, 2, 4, 2, ROWS, D), BF),
            jax.ShapeDtypeStruct((2, ROWS, D), BF),
            jax.ShapeDtypeStruct((4, 768, 384), BF),
            jax.ShapeDtypeStruct((3, 2, TXT, HD), BF),
            jax.ShapeDtypeStruct((2, TXT, HD), BF),
            jax.ShapeDtypeStruct((2, IMG, HD), BF),
        ),
        in_specs=[VMEM] * 5 + [ANY] * 4,
        out_specs=(ANY, VMEM, ANY, ANY, ANY, ANY),
        scratch_shapes=[
            pltpu.VMEM((4, 2, ROWS, D), BF),
            pltpu.VMEM((2, 2, ROWS, HALF), BF),
            pltpu.VMEM((2, 2, ROWS, HALF), BF),
            pltpu.VMEM((2, 2, ROWS, HALF), BF),
            pltpu.VMEM((2, ROWS, D), BF),
            pltpu.SemaphoreType.DMA((64,)),
            pltpu.SemaphoreType.DMA((2, 6)),
            pltpu.SemaphoreType.DMA((2, 17)),
            pltpu.SemaphoreType.DMA((4,)),
            pltpu.SemaphoreType.DMA((3, 16)),
            pltpu.SemaphoreType.DMA((3,)),
            pltpu.SemaphoreType.DMA((3,)),
        ],
        compiler_params=pltpu.CompilerParams(
            collective_id=1, has_side_effects=True, vmem_limit_bytes=VMEM_LIMIT
        ),
        name="front",
    )(control, zero_weight, image_hidden, stretch, offset, weight, text, text_cot, image_cot)


NT = (((1,), (1,)), ((), ()))
TN = (((0,), (0,)), ((), ()))
BLOCK = 256


def attention_kernel(
    lengths, normed, weight, text, text_cot, image_cot, attn, dnormed, q_s, k_s, v_s, cot_s, grads
):
    scaling = HD ** (-0.5)
    length = lengths[pl.program_id(0)]
    qkv = jnp.dot(normed[0], weight[...], preferred_element_type=F32).astype(BF)
    for n, ref in enumerate((q_s, k_s, v_s)):
        ref[:TXT] = text[n, 0]
        ref[TXT:] = qkv[:, n * HD : (n + 1) * HD]
    cot_s[:TXT] = text_cot[0]
    cot_s[TXT:] = image_cot[0]
    keys = k_s[...]
    values = v_s[...]
    position = lax.broadcasted_iota(jnp.int32, (1, TXT + IMG), 1)
    bias = jnp.where((position >= TXT) | (position < length), 0.0, -jnp.inf)
    key_grad = jnp.zeros((IMG, HD), F32)
    value_grad = jnp.zeros((IMG, HD), F32)
    for block in range((TXT + IMG) // BLOCK):
        rows = pl.ds(block * BLOCK, BLOCK)
        query = q_s[rows]
        cot = cot_s[rows]
        scores = lax.dot_general(query, keys, NT, preferred_element_type=F32) + bias
        row_max = jnp.max(scores, axis=1, keepdims=True)
        terms = jnp.exp2((scores - row_max) * (scaling * math.log2(math.e)))
        prob = terms * (1.0 / jnp.sum(terms, axis=1, keepdims=True))
        low = prob.astype(BF)
        attended = jnp.dot(low, values, preferred_element_type=F32).astype(BF)
        attn[block // 2, 0, pl.ds(block % 2 * BLOCK, BLOCK)] = attended
        dots = jnp.sum(cot.astype(F32) * attended.astype(F32), axis=1, keepdims=True)
        prob_grad = lax.dot_general(cot, values, NT, preferred_element_type=F32)
        score_grad = (prob * (prob_grad - dots)).astype(BF)
        if block >= 2:
            grads[pl.ds((block - 2) * BLOCK, BLOCK), :HD] = (
                jnp.dot(score_grad, keys, preferred_element_type=F32) * scaling
            ).astype(BF)
        key_grad += lax.dot_general(score_grad[:, TXT:], query, TN, preferred_element_type=F32)
        value_grad += lax.dot_general(low[:, TXT:], cot, TN, preferred_element_type=F32)
    grads[:, HD : 2 * HD] = (key_grad * scaling).astype(BF)
    grads[:, 2 * HD :] = value_grad.astype(BF)
    for block in range(6):
        cols = pl.ds(block * 512, 512)
        dnormed[0, :, cols] = lax.dot_general(
            grads[...], weight[cols], NT, preferred_element_type=F32
        ).astype(BF)


def attention(lengths, normed, weight, text, text_cot, image_cot):
    return pl.pallas_call(
        attention_kernel,
        grid=(2,),
        out_shape=(
            jax.ShapeDtypeStruct((2, 2, 512, HD), BF),
            jax.ShapeDtypeStruct((2, IMG, D), BF),
        ),
        in_specs=[
            pl.BlockSpec(memory_space=pltpu.SMEM),
            pl.BlockSpec((1, IMG, D), lambda i: (i, 0, 0)),
            pl.BlockSpec((D, 384), lambda i: (0, 0)),
            pl.BlockSpec((3, 1, TXT, HD), lambda i: (0, i, 0, 0)),
            pl.BlockSpec((1, TXT, HD), lambda i: (i, 0, 0)),
            pl.BlockSpec((1, IMG, HD), lambda i: (i, 0, 0)),
        ],
        out_specs=(
            pl.BlockSpec((2, 1, 512, HD), lambda i: (0, i, 0, 0)),
            pl.BlockSpec((1, IMG, D), lambda i: (i, 0, 0)),
        ),
        scratch_shapes=[pltpu.VMEM((TXT + IMG, HD), BF) for _ in range(4)]
        + [pltpu.VMEM((IMG, 384), BF)],
        compiler_params=pltpu.CompilerParams(vmem_limit_bytes=VMEM_LIMIT),
        name="attention",
    )(lengths, normed, weight, text, text_cot, image_cot)


def back_kernel(
    dnormed,
    attn,
    hidden,
    stretch,
    control,
    zero_weight,
    attn_out,
    control_grad,
    zero_out,
    rows_all,
    pair_in,
    pair_sum,
    relay,
    from_left,
    from_right,
    cross_out,
    cross_in,
    zpart,
    zpair_in,
    zsum,
    zx_relay,
    zx_left,
    zx_right,
    zy_relay,
    zy_left,
    zy_right,
    za_out,
    zb_out,
    za_in,
    zb_in,
    zown,
    zall,
    send_sem,
    pair_sem,
    rs_sem,
    cross_sem,
    ag_sem,
    attn_send,
    attn_recv,
    zpair_sem,
    zx_sem,
    zy_sem,
    za_sem,
    zb_sem,
    zg_sem,
):
    p = Place()
    greet(
        seq_peers(p)
        + [{"grp": p.gl}, {"grp": p.gr}]
        + [{"dp": (p.d + k) % 4} for k in range(1, 4)]
        + [{"dp": (p.d + k) % 4, "seq": p.seq(p.zo, p.y, p.c)} for k in range(1, 4)]
    )
    send = Sends(send_sem)
    partner = {"seq": p.seq(p.z, p.y, p.co)}
    across = {"seq": p.seq(p.zo, p.y, p.c)}
    to_y = lambda y: {"seq": p.seq(p.z, y, p.c)}

    for i in range(2):
        send(dnormed.at[i, :, :, p.co], pair_in.at[i], pair_sem.at[i], **partner)

    def attn_copies(k):
        to = (p.s + k) % 16
        row = pl.multiple_of(to * ROWS, ROWS)
        col = pl.multiple_of(p.s * HD, HD)
        return pltpu.make_async_remote_copy(
            src_ref=attn.at[:, :, pl.ds(row, ROWS)],
            dst_ref=attn_out.at[:, :, :, pl.ds(col, HD)],
            send_sem=attn_send.at[k],
            recv_sem=attn_recv,
            device_id={"seq": to},
            device_id_type=MESH,
        )

    scatters, gathers = [], []
    for i in range(2):
        scatters.append(
            Scatter4(
                send,
                lambda y, h, i=i: pair_sum.at[i, :, y, :, pl.ds(h * HALF, HALF)],
                lambda h, i=i: relay.at[i, h],
                lambda h, i=i: from_left.at[i, h],
                lambda h, i=i: from_right.at[i, h],
                rs_sem.at[i],
                p.y,
                p.yl,
                p.yr,
                p.yo,
                to_y,
            )
        )
        gathers.append(
            Gather4(
                send,
                lambda g, i=i: rows_all.at[g, i],
                lambda g, h, i=i: rows_all.at[g, i, pl.ds(h * 16, 16)],
                ag_sem.at[i],
                p.g,
                p.gl,
                p.gr,
                p.go,
                lambda g: {"grp": g},
            )
        )

    def join(i, y):
        for z in range(2):
            pair_sum[i, z, y] = (
                dnormed[i, z, y, p.c].astype(F32) + pair_in[i, z, y].astype(F32)
            ).astype(BF)

    def first(i):
        arrived(pair_in.at[i], pair_sem.at[i])
        join(i, p.yo)
        scatters[i].start()
        join(i, p.yl)
        join(i, p.yr)
        scatters[i].direct()
        join(i, p.y)

    def second(i):
        scatters[i].finish()
        for h in range(2):
            cols = pl.ds(h * HALF, HALF)
            cross_out[i, :, cols] = (
                pair_sum[i, p.zo, p.y, :, cols].astype(F32)
                + from_left[i, h, p.zo].astype(F32)
                + from_right[i, h, p.zo].astype(F32)
            ).astype(BF)
        send(cross_out.at[i], cross_in.at[i], cross_sem.at[i], **across)

    def third(i):
        parts = []
        for h in range(2):
            cols = pl.ds(h * HALF, HALF)
            parts.append(
                pair_sum[i, p.z, p.y, :, cols].astype(F32)
                + from_left[i, h, p.z].astype(F32)
                + from_right[i, h, p.z].astype(F32)
            )
        own = jnp.concatenate(parts, axis=1)
        values = hidden[i].astype(F32)
        average = jnp.mean(values, axis=-1, keepdims=True)
        centred = values - average
        reciprocal = lax.rsqrt(jnp.mean(centred * centred, axis=-1, keepdims=True) + 1e-06)
        standard = centred * reciprocal
        arrived(cross_in.at[i], cross_sem.at[i])
        scaled = (own + cross_in[i].astype(F32)) * stretch[i : i + 1]
        rows_all[p.g, i] = (
            reciprocal
            * (
                scaled
                - jnp.mean(scaled, axis=-1, keepdims=True)
                - standard * jnp.mean(scaled * standard, axis=-1, keepdims=True)
            )
        ).astype(BF)
        gathers[i].start()

    first(0)
    first(1)
    scatters[0].pass_on()
    second(0)

    @pl.loop(1, 16)
    def _(k):
        attn_copies(k).start()

    mine = pltpu.make_async_copy(
        attn.at[:, :, pl.ds(pl.multiple_of(p.s * ROWS, ROWS), ROWS)],
        attn_out.at[:, :, :, pl.ds(pl.multiple_of(p.s * HD, HD), HD)],
        attn_recv,
    )
    mine.start()
    scatters[1].pass_on()
    third(0)
    second(1)
    gathers[0].pass_left()
    gathers[0].pass_right()
    third(1)
    gathers[1].pass_left()
    gathers[1].pass_right()
    gathers[0].finish()
    gathers[1].finish()

    for z in range(2):
        for y in range(4):
            cols = pl.ds((z * 4 + y) * 384, 384)
            grad_cols = rows_all[:, :, :, cols].reshape(256, 384)
            product = lax.dot_general(grad_cols, control[...], TN, preferred_element_type=F32)
            zpart[z, y] = product.astype(BF).reshape(2, 192, 768)
            send(
                zpart.at[z, y, p.co], zpair_in.at[z, y], zpair_sem.at[z * 4 + y], **partner
            )

    colA, colB = pl.ds(0, 384), pl.ds(384, 384)
    xs = Scatter4(
        send,
        lambda d, h: zsum.at[h, :, pl.ds(pl.multiple_of(d * 48, 16), 48), colA],
        lambda h: zx_relay.at[h],
        lambda h: zx_left.at[h],
        lambda h: zx_right.at[h],
        zx_sem,
        p.d,
        p.dl,
        p.dr,
        p.do,
        lambda d: {"dp": d},
    )
    ys = Scatter4(
        send,
        lambda y, h: zsum.at[h, y, :, colB],
        lambda h: zy_relay.at[h],
        lambda h: zy_left.at[h],
        lambda h: zy_right.at[h],
        zy_sem,
        p.y,
        p.yl,
        p.yr,
        p.yo,
        to_y,
    )
    for z in range(2):
        for y in range(4):
            arrived(zpair_in.at[z, y], zpair_sem.at[z * 4 + y])
            zsum[z, y] = (
                zpart[z, y, p.c].astype(F32) + zpair_in[z, y].astype(F32)
            ).astype(BF)
    xs.start()
    ys.start()
    xs.direct()
    ys.direct()
    xs.pass_on()
    ys.pass_on()

    for block in range(3):
        out = pl.ds(block * 256, 256)
        control_grad[:, out] = lax.dot_general(
            rows_all[...].reshape(256, D), zero_weight[out], NT, preferred_element_type=F32
        ).astype(BF)

    xs.finish()
    for z in range(2):
        za_out[z] = (
            zsum[z, :, pl.ds(pl.multiple_of(p.d * 48, 16), 48), colA].astype(F32)
            + zx_left[z].astype(F32)
            + zx_right[z].astype(F32)
        ).astype(BF)
    n = 0
    for dz in range(2):
        for dy in range(4):
            if dz or dy:
                z, y = (p.z + dz) % 2, (p.y + dy) % 4
                send(
                    za_out.at[z, y], za_in.at[n], za_sem.at[n], seq=p.seq(z, y, p.c)
                )
                n += 1
    ys.finish()
    for z in range(2):
        zb_out[z] = (
            zsum[z, p.y, :, colB].astype(F32) + zy_left[z].astype(F32) + zy_right[z].astype(F32)
        ).astype(BF).reshape(4, 48, 384)
    n = 0
    for dz in range(2):
        for dd in range(4):
            if dz or dd:
                z, d = (p.z + dz) % 2, (p.d + dd) % 4
                send(
                    zb_out.at[z, d],
                    zb_in.at[n],
                    zb_sem.at[n],
                    seq=p.seq(z, p.y, p.c),
                    dp=d,
                )
                n += 1
    total = za_out[p.z, p.y].astype(F32)
    for n in range(7):
        arrived(za_in.at[n], za_sem.at[n])
        total = total + za_in[n].astype(F32)
    zown[:, colA] = total.astype(BF)
    total = zb_out[p.z, p.d].astype(F32)
    for n in range(7):
        arrived(zb_in.at[n], zb_sem.at[n])
        total = total + zb_in[n].astype(F32)
    zown[:, colB] = total.astype(BF)
    for k in range(1, 4):
        send(zown, zall.at[p.d], zg_sem.at[k - 1], dp=(p.d + k) % 4)
    zall[p.d] = zown[...]
    for k in range(1, 4):
        arrived(zall.at[(p.d + 4 - k) % 4], zg_sem.at[k - 1])
    zero_out[...] = zall[...].reshape(192, 768)

    arrived(attn_out, attn_recv)
    send.drain()

    @pl.loop(1, 16)
    def _(k):
        attn_copies(k).wait_send()


def back(dnormed, attn, hidden, stretch, control, zero_weight):
    dma = pltpu.SemaphoreType.DMA
    return pl.pallas_call(
        back_kernel,
        out_shape=(
            jax.ShapeDtypeStruct((2, 2, ROWS, HEADS * HD), BF),
            jax.ShapeDtypeStruct((256, 768), BF),
            jax.ShapeDtypeStruct((192, 768), BF),
        ),
        in_specs=[VMEM] * 6,
        out_specs=(VMEM, VMEM, VMEM),
        scratch_shapes=[
            pltpu.VMEM((4, 2, ROWS, D), BF),
            pltpu.VMEM((2, 2, 4, ROWS, D), BF),
            pltpu.VMEM((2, 2, 4, ROWS, D), BF),
            pltpu.VMEM((2, 2, 2, ROWS, HALF), BF),
            pltpu.VMEM((2, 2, 2, ROWS, HALF), BF),
            pltpu.VMEM((2, 2, 2, ROWS, HALF), BF),
            pltpu.VMEM((2, ROWS, D), BF),
            pltpu.VMEM((2, ROWS, D), BF),
            pltpu.VMEM((2, 4, 2, 192, 768), BF),
            pltpu.VMEM((2, 4, 192, 768), BF),
            pltpu.VMEM((2, 4, 192, 768), BF),
            pltpu.VMEM((2, 4, 48, 384), BF),
            pltpu.VMEM((2, 4, 48, 384), BF),
            pltpu.VMEM((2, 4, 48, 384), BF),
            pltpu.VMEM((2, 192, 384), BF),
            pltpu.VMEM((2, 192, 384), BF),
            pltpu.VMEM((2, 192, 384), BF),
            pltpu.VMEM((2, 4, 48, 384), BF),
            pltpu.VMEM((2, 4, 48, 384), BF),
            pltpu.VMEM((7, 48, 384), BF),
            pltpu.VMEM((7, 48, 384), BF),
            pltpu.VMEM((48, 768), BF),
            pltpu.VMEM((4, 48, 768), BF),
            dma((64,)),
            dma((2,)),
            dma((2, 6)),
            dma((2,)),
            dma((2, 4)),
            dma((16,)),
            dma,
            dma((8,)),
            dma((6,)),
            dma((6,)),
            dma((7,)),
            dma((7,)),
            dma((3,)),
        ],
        compiler_params=pltpu.CompilerParams(
            collective_id=2, has_side_effects=True, vmem_limit_bytes=VMEM_LIMIT
        ),
        name="back",
    )(dnormed, attn, hidden, stretch, control, zero_weight)


def timestep_modulation(timesteps, mod_weight):
    half_freq = FREQ // 2
    frequency = jnp.exp(-math.log(10000.0) * jnp.arange(half_freq, dtype=F32) / half_freq)
    angles = timesteps.astype(F32)[..., None] * frequency
    embedding = jnp.concatenate([jnp.cos(angles), jnp.sin(angles)], axis=-1)
    activated = jax.nn.silu(embedding).astype(BF)
    return jnp.dot(activated.reshape(-1, FREQ), mod_weight, preferred_element_type=F32)


def body(
    image_hidden,
    control_hidden,
    text_qkv,
    text_lengths,
    timesteps,
    mod_weight,
    qkv_weight,
    zero_weight,
    image_cotangent,
    text_cotangent,
):
    modulation = timestep_modulation(timesteps, mod_weight)
    offset = modulation[:, :D]
    stretch = 1.0 + modulation[:, D:]
    control = control_hidden.reshape(256, 768)
    normed, hidden, weight, text, text_cot, image_cot = front(
        control,
        zero_weight,
        image_hidden.reshape(2, ROWS, D),
        stretch,
        offset,
        qkv_weight.reshape(768, 384),
        text_qkv.reshape(3, 2, ROWS, HEADS * HD),
        text_cotangent.reshape(2, ROWS, HEADS * HD),
        image_cotangent.reshape(2, ROWS, HEADS * HD),
    )
    attn, dnormed = attention(
        text_lengths.reshape(2),
        normed.reshape(2, IMG, D),
        weight.reshape(D, 384),
        text,
        text_cot,
        image_cot,
    )
    attn_out, control_grad, zero_t = back(
        dnormed.reshape(2, 2, 4, 2, ROWS, D), attn, hidden, stretch, control, zero_weight
    )
    norm_factor = 16384 ** (-0.5)
    zero_grad = jnp.transpose(zero_t).astype(F32) * norm_factor
    return (
        attn_out[1].reshape(2, 1, ROWS, HEADS * HD),
        attn_out[0].reshape(2, 1, ROWS, HEADS * HD),
        control_grad.reshape(8, 1, ROWS, 768),
        zero_grad,
    )


def solution(mesh):
    placed = (
        P("grp", "dp", "seq", None),
        P(None, "dp", "seq", "grp"),
        P(None, "grp", "dp", "seq", None),
        P("grp", "dp"),
        P("grp", "dp"),
        P(),
        P("dp", None, "seq"),
        P("grp", None),
        P("grp", "dp", "seq", None),
        P("grp", "dp", "seq", None),
    )
    return jax.shard_map(
        body,
        mesh=mesh,
        in_specs=placed,
        out_specs=(
            P("grp", "dp", "seq", None),
            P("grp", "dp", "seq", None),
            P(None, "dp", "seq", "grp"),
            P("grp", "seq"),
        ),
        check_vma=False,
    )
```

```python
import math

import jax
import jax.numpy as jnp
from jax import lax
from jax.experimental import pallas as pl
from jax.experimental.pallas import tpu as pltpu
from jax.sharding import PartitionSpec as P

D = 3072
HEADS = 16
HD = 128
IMG = 512
TXT = 512
FREQ = 256
ROWS = 32
HALF = D // 2
MESH = pl.DeviceIdType.MESH
BF = jnp.bfloat16
F32 = jnp.float32
VMEM_LIMIT = 60 * 1024 * 1024
ANY = pl.BlockSpec(memory_space=pl.ANY)
VMEM = pl.BlockSpec(memory_space=pltpu.VMEM)


class Sends:
    def __init__(self, sems):
        self.sems = sems
        self.copies = []

    def __call__(self, src, dst, recv, **to):
        copy = pltpu.make_async_remote_copy(
            src_ref=src,
            dst_ref=dst,
            send_sem=self.sems.at[len(self.copies)],
            recv_sem=recv,
            device_id=to,
            device_id_type=MESH,
        )
        copy.start()
        self.copies.append(copy)

    def drain(self):
        for copy in self.copies:
            copy.wait_send()


def arrived(dst, recv):
    pltpu.make_async_copy(dst, dst, recv).wait()


def greet(groups):
    barrier = pltpu.get_barrier_semaphore()
    for to in groups:
        pl.semaphore_signal(barrier, inc=1, device_id=to, device_id_type=MESH)
    pl.semaphore_wait(barrier, len(groups))


class Place:
    def __init__(self):
        self.s = lax.axis_index("seq")
        self.g = lax.axis_index("grp")
        self.d = lax.axis_index("dp")
        self.z = self.s // 8
        self.y = (self.s // 2) % 4
        self.c = self.s % 2
        self.zo = 1 - self.z
        self.co = 1 - self.c
        self.yl = (self.y + 3) % 4
        self.yr = (self.y + 1) % 4
        self.yo = (self.y + 2) % 4
        self.gl = (self.g + 3) % 4
        self.gr = (self.g + 1) % 4
        self.go = (self.g + 2) % 4
        self.dl = (self.d + 3) % 4
        self.dr = (self.d + 1) % 4
        self.do = (self.d + 2) % 4

    def seq(self, z, y, c):
        return z * 8 + y * 2 + c


def add_into(dst, *others):
    total = dst[...].astype(F32)
    for other in others:
        total = total + other[...].astype(F32)
    dst[...] = total.astype(dst.dtype)


class Scatter4:
    def __init__(self, send, src, relay, from_left, from_right, sems, me, left, right, far, to):
        self.send, self.src, self.relay = send, src, relay
        self.from_left, self.from_right, self.sems = from_left, from_right, sems
        self.me, self.left, self.right, self.far, self.to = me, left, right, far, to

    def start(self):
        self.send(self.src(self.far, 0), self.relay(0), self.sems.at[0], **self.to(self.left))
        self.send(self.src(self.far, 1), self.relay(1), self.sems.at[1], **self.to(self.right))

    def direct(self):
        self.send(
            self.src(self.left, 1), self.from_right(1), self.sems.at[2], **self.to(self.left)
        )
        self.send(
            self.src(self.right, 0), self.from_left(0), self.sems.at[3], **self.to(self.right)
        )

    def pass_on(self):
        arrived(self.relay(0), self.sems.at[0])
        add_into(self.src(self.left, 0), self.relay(0))
        self.send(
            self.src(self.left, 0), self.from_right(0), self.sems.at[4], **self.to(self.left)
        )
        arrived(self.relay(1), self.sems.at[1])
        add_into(self.src(self.right, 1), self.relay(1))
        self.send(
            self.src(self.right, 1), self.from_left(1), self.sems.at[5], **self.to(self.right)
        )

    def finish(self):
        arrived(self.from_right(1), self.sems.at[2])
        arrived(self.from_left(0), self.sems.at[3])
        arrived(self.from_right(0), self.sems.at[4])
        arrived(self.from_left(1), self.sems.at[5])


class Gather4:
    def __init__(self, send, slot, half, sems, me, left, right, far, to):
        self.send, self.slot, self.half, self.sems = send, slot, half, sems
        self.me, self.left, self.right, self.far, self.to = me, left, right, far, to

    def start(self, own=None):
        own = self.slot(self.me) if own is None else own
        self.send(own, self.slot(self.me), self.sems.at[0], **self.to(self.right))
        self.send(own, self.slot(self.me), self.sems.at[1], **self.to(self.left))

    def pass_left(self):
        arrived(self.slot(self.left), self.sems.at[0])
        part = self.half(self.left, 0)
        self.send(part, part, self.sems.at[2], **self.to(self.right))

    def pass_right(self):
        arrived(self.slot(self.right), self.sems.at[1])
        part = self.half(self.right, 1)
        self.send(part, part, self.sems.at[3], **self.to(self.left))

    def finish(self):
        arrived(self.half(self.far, 0), self.sems.at[2])
        arrived(self.half(self.far, 1), self.sems.at[3])


NT = (((1,), (1,)), ((), ()))
TN = (((0,), (0,)), ((), ()))
BLOCK = 256


def block_kernel(
    lengths,
    activated,
    mod_weight,
    control,
    zero_weight,
    image_hidden,
    weight,
    text,
    text_cot,
    image_cot,
    attn_out,
    control_grad,
    zero_out,
    ctl,
    zw,
    base,
    wall,
    offset,
    stretch,
    partial,
    rg_relay,
    rg_left,
    rg_right,
    hidden,
    normed,
    joint,
    cots,
    tstage,
    cstage,
    attn,
    ostage,
    grads,
    key_acc,
    value_acc,
    dn,
    pair_in,
    pair_sum,
    ry_relay,
    ry_left,
    ry_right,
    cross_out,
    cross_in,
    rows_all,
    zpart,
    zpair_in,
    zsum,
    zx_relay,
    zx_left,
    zx_right,
    zy_relay,
    zy_left,
    zy_right,
    za_out,
    zb_out,
    za_in,
    zb_in,
    zown,
    zall,
    load_sem,
    send_sem,
    w_sem,
    rg_sem,
    ag_sem,
    text_send,
    text_recv,
    stage_recv,
    cross_recv,
    pair_sem,
    ry_sem,
    cross_sem,
    gg_sem,
    attn_send,
    attn_recv,
    zpair_sem,
    zx_sem,
    zy_sem,
    za_sem,
    zb_sem,
    zg_sem,
):
    p = Place()
    send = Sends(send_sem)
    q = p.y * 2 + p.c
    partner = {"seq": p.seq(p.z, p.y, p.co)}
    across = {"seq": p.seq(p.zo, p.y, p.c)}
    to_y = lambda y: {"seq": p.seq(p.z, y, p.c)}
    to_g = lambda g: {"grp": g}
    to_d = lambda d: {"dp": d}

    loads = []

    def load(src, dst):
        copy = pltpu.make_async_copy(src, dst, load_sem.at[len(loads)])
        copy.start()
        loads.append(copy)
        return copy

    load_weight = [
        load(weight.at[n], wall.at[p.d, :, pl.ds(n * HD, HD)]) for n in range(3)
    ]
    load_control = load(control, ctl)
    load_zero = [
        load(zero_weight.at[:, pl.ds(n * 512, 512)], zw.at[:, pl.ds(n * 512, 512)])
        for n in range(6)
    ]
    load_base = load(image_hidden, base)
    load_mod = [
        load(
            mod_weight.at[pl.ds(n % 8 * ROWS, ROWS), pl.ds(n // 8 * D, D)],
            dn.at[n],
        )
        for n in range(16)
    ]

    greet(
        [{"seq": (p.s + k) % 16} for k in range(1, 16)]
        + [{"grp": p.gl}, {"grp": p.gr}]
        + [{"dp": (p.d + k) % 4} for k in range(1, 4)]
        + [{"dp": (p.d + k) % 4, "seq": p.seq(p.zo, p.y, p.c)} for k in range(1, 4)]
    )

    row = pl.multiple_of(p.s * ROWS, ROWS)
    stage_row = pl.multiple_of(q * ROWS, ROWS)
    plane = pl.ds(pl.multiple_of(p.z * 256, 256), 256)
    other_plane = pl.ds(pl.multiple_of(p.zo * 256, 256), 256)

    def text_pairs(to):
        near = pl.ds(pl.multiple_of((p.z * 8 + to) * HD, HD), HD)
        far = pl.ds(pl.multiple_of((p.zo * 8 + to) * HD, HD), HD)
        rows = pl.ds(row, ROWS)
        image_rows = pl.ds(TXT + row, ROWS)
        staged = pl.ds(stage_row, ROWS)
        return (
            (text.at[:, :, :, near], joint.at[:, :, rows], text_recv.at[0]),
            (text_cot.at[:, :, near], cots.at[:, rows], text_recv.at[1]),
            (image_cot.at[:, :, near], cots.at[:, image_rows], text_recv.at[2]),
            (text.at[:, :, :, far], tstage.at[:, :, staged], stage_recv.at[0]),
            (text_cot.at[:, :, far], cstage.at[0, :, staged], stage_recv.at[1]),
            (image_cot.at[:, :, far], cstage.at[1, :, staged], stage_recv.at[2]),
        )

    def text_copies(k):
        to = (q + k) % 8
        return [
            pltpu.make_async_remote_copy(
                src_ref=src,
                dst_ref=dst,
                send_sem=text_send.at[n, k],
                recv_sem=recv,
                device_id={"seq": p.z * 8 + to},
                device_id_type=MESH,
            )
            for n, (src, dst, recv) in enumerate(text_pairs(to))
        ]

    @pl.loop(1, 8)
    def _(k):
        for copy in text_copies(k):
            copy.start()

    for src, dst, recv in text_pairs(q):
        pltpu.make_async_copy(src, dst, recv).start()

    def text_second_hop(i):
        send(tstage.at[:, i], joint.at[:, i, plane], cross_recv.at[i, 0], **across)
        send(cstage.at[0, i], cots.at[i, plane], cross_recv.at[i, 1], **across)
        image_rows = pl.ds(pl.multiple_of(TXT + p.z * 256, 256), 256)
        send(cstage.at[1, i], cots.at[i, image_rows], cross_recv.at[i, 2], **across)

    def text_wait(i):
        arrived(joint.at[:, i, other_plane], cross_recv.at[i, 0])
        arrived(cots.at[i, other_plane], cross_recv.at[i, 1])
        image_rows = pl.ds(pl.multiple_of(TXT + p.zo * 256, 256), 256)
        arrived(cots.at[i, image_rows], cross_recv.at[i, 2])

    for copy in load_weight:
        copy.wait()
    weights = Gather4(
        send,
        lambda d: wall.at[d],
        lambda d, h: wall.at[d, pl.ds(h * 384, 384)],
        w_sem,
        p.d,
        p.dl,
        p.dr,
        p.do,
        to_d,
    )
    weights.start()

    load_control.wait()
    for block in range(6):
        cols = pl.ds(block * 512, 512)
        load_zero[block].wait()
        product = jnp.dot(ctl[...], zw[:, cols], preferred_element_type=F32)
        partial[:, :, :, cols] = product.astype(BF).reshape(4, 2, ROWS, 512)
    to_group = [
        Scatter4(
            send,
            lambda g, h, i=i: partial.at[g, i, :, pl.ds(h * HALF, HALF)],
            lambda h, i=i: rg_relay.at[i, h],
            lambda h, i=i: rg_left.at[i, h],
            lambda h, i=i: rg_right.at[i, h],
            rg_sem.at[i],
            p.g,
            p.gl,
            p.gr,
            p.go,
            to_g,
        )
        for i in range(2)
    ]
    to_group[0].start()
    to_group[0].direct()

    for copy in load_mod:
        copy.wait()
    offset[...] = jnp.dot(
        activated[...], dn[:8].reshape(FREQ, D), preferred_element_type=F32
    )
    stretch[...] = 1.0 + jnp.dot(
        activated[...], dn[8:].reshape(FREQ, D), preferred_element_type=F32
    )
    load_base.wait()

    to_group[0].pass_on()
    to_group[1].start()
    weights.pass_left()
    weights.pass_right()

    gathers = [
        [
            Gather4(
                send,
                lambda y, i=i, z=z: normed.at[i, z, y, p.c],
                lambda y, h, i=i, z=z: normed.at[i, z, y, p.c, pl.ds(h * 16, 16)],
                ag_sem.at[i, pl.ds(which * 4, 4)],
                p.y,
                p.yl,
                p.yr,
                p.yo,
                to_y,
            )
            for which, z in enumerate((p.z, p.zo))
        ]
        for i in range(2)
    ]

    def share(i, z, y, sem):
        slot = normed.at[i, z, y, p.c]
        send(slot, slot, ag_sem.at[i, sem], **partner)

    def standardise(i):
        values = hidden[i].astype(F32)
        average = jnp.mean(values, axis=-1, keepdims=True)
        centred = values - average
        reciprocal = lax.rsqrt(jnp.mean(centred * centred, axis=-1, keepdims=True) + 1e-06)
        return centred * reciprocal, reciprocal

    def gather_first(i):
        for h in range(2):
            cols = pl.ds(h * HALF, HALF)
            residual = (
                partial[p.g, i, :, cols].astype(F32)
                + rg_left[i, h].astype(F32)
                + rg_right[i, h].astype(F32)
            )
            hidden[i, :, cols] = (base[i, :, cols].astype(F32) + residual).astype(BF)
        standard, _ = standardise(i)
        normed[i, p.z, p.y, p.c] = (
            standard * stretch[i : i + 1] + offset[i : i + 1]
        ).astype(BF)
        mine = normed.at[i, p.z, p.y, p.c]
        send(mine, mine, ag_sem.at[i, 8], **across)
        gathers[i][0].start()
        send(mine, mine, ag_sem.at[i, 9], **partner)

    def gather_second(i):
        arrived(normed.at[i, p.zo, p.y, p.c], ag_sem.at[i, 8])
        gathers[i][1].start()
        share(i, p.zo, p.y, 10)

    def gather_third(i, which):
        z = (p.z, p.zo)[which]
        gathers[i][which].pass_left()
        gathers[i][which].pass_right()
        share(i, z, p.yl, 11 + 3 * which)
        share(i, z, p.yr, 12 + 3 * which)

    def gather_fourth(i, which):
        z = (p.z, p.zo)[which]
        gathers[i][which].finish()
        share(i, z, p.yo, 13 + 3 * which)

    def gather_wait(i):
        arrived(normed.at[i, p.z, p.y, p.co], ag_sem.at[i, 9])
        arrived(normed.at[i, p.zo, p.y, p.co], ag_sem.at[i, 10])
        for which, z in enumerate((p.z, p.zo)):
            for n, y in enumerate((p.yl, p.yr, p.yo)):
                arrived(normed.at[i, z, y, p.co], ag_sem.at[i, 11 + 3 * which + n])

    scaling = HD ** (-0.5)
    position = lax.broadcasted_iota(jnp.int32, (1, TXT + IMG), 1)

    def project(i):
        product = jnp.dot(
            normed[i].reshape(IMG, D), wall[...].reshape(D, 384), preferred_element_type=F32
        ).astype(BF)
        for n in range(3):
            joint[n, i, TXT:] = product[:, n * HD : (n + 1) * HD]

    def attend(i, block):
        rows = pl.ds(block * BLOCK, BLOCK)
        bias = jnp.where((position >= TXT) | (position < lengths[i]), 0.0, -jnp.inf)
        query, cot = joint[0, i, rows], cots[i, rows]
        keys, values = joint[1, i], joint[2, i]
        scores = lax.dot_general(query, keys, NT, preferred_element_type=F32) + bias
        row_max = jnp.max(scores, axis=1, keepdims=True)
        terms = jnp.exp2((scores - row_max) * (scaling * math.log2(math.e)))
        prob = terms * (1.0 / jnp.sum(terms, axis=1, keepdims=True))
        low = prob.astype(BF)
        attended = jnp.dot(low, values, preferred_element_type=F32).astype(BF)
        attn[block // 2, i, pl.ds(block % 2 * BLOCK, BLOCK)] = attended
        dots = jnp.sum(cot.astype(F32) * attended.astype(F32), axis=1, keepdims=True)
        prob_grad = lax.dot_general(cot, values, NT, preferred_element_type=F32)
        score_grad = (prob * (prob_grad - dots)).astype(BF)
        if block >= 2:
            grads[pl.ds((block - 2) * BLOCK, BLOCK), :HD] = (
                jnp.dot(score_grad, keys, preferred_element_type=F32) * scaling
            ).astype(BF)
        key_part = lax.dot_general(score_grad[:, TXT:], query, TN, preferred_element_type=F32)
        value_part = lax.dot_general(low[:, TXT:], cot, TN, preferred_element_type=F32)
        if block == 0:
            key_acc[...] = key_part
            value_acc[...] = value_part
        elif block < 3:
            key_acc[...] += key_part
            value_acc[...] += value_part
        else:
            grads[:, HD : 2 * HD] = ((key_acc[...] + key_part) * scaling).astype(BF)
            grads[:, 2 * HD :] = (value_acc[...] + value_part).astype(BF)

    pair_sends = [Sends(send_sem.at[pl.ds(160 + 8 * i, 8)]) for i in range(2)]

    def back_project(i):
        if i:
            pair_sends[0].drain()
        for n in range(2):
            rows = pl.ds(n * 256, 256)
            for block in range(4):
                cols = pl.ds(block * 768, 768)
                product = lax.dot_general(
                    grads[rows], wall[block], NT, preferred_element_type=F32
                ).astype(BF)
                dn[pl.ds(n * 8, 8), :, cols] = product.reshape(8, ROWS, 768)
            for y in range(4):
                pair_sends[i](
                    dn.at[n * 8 + y * 2 + p.co], pair_in.at[i, n, y], pair_sem.at[i, n * 4 + y],
                    **partner
                )

    def join(i, y):
        for z in range(2):
            arrived(pair_in.at[i, z, y], pair_sem.at[i, z * 4 + y])
            pair_sum[i, z, y] = (
                dn[z * 8 + y * 2 + p.c].astype(F32) + pair_in[i, z, y].astype(F32)
            ).astype(BF)

    round_y = [
        Scatter4(
            send,
            lambda y, h, i=i: pair_sum.at[i, :, y, :, pl.ds(h * HALF, HALF)],
            lambda h, i=i: ry_relay.at[i, h],
            lambda h, i=i: ry_left.at[i, h],
            lambda h, i=i: ry_right.at[i, h],
            ry_sem.at[i],
            p.y,
            p.yl,
            p.yr,
            p.yo,
            to_y,
        )
        for i in range(2)
    ]
    rows_gather = [
        Gather4(
            send,
            lambda g, i=i: rows_all.at[g, i],
            lambda g, h, i=i: rows_all.at[g, i, pl.ds(h * 16, 16)],
            gg_sem.at[i],
            p.g,
            p.gl,
            p.gr,
            p.go,
            to_g,
        )
        for i in range(2)
    ]

    def back_first(i):
        join(i, p.yo)
        round_y[i].start()
        join(i, p.yl)
        join(i, p.yr)
        round_y[i].direct()
        join(i, p.y)

    def y_sum(i, z, h):
        cols = pl.ds(h * HALF, HALF)
        return (
            pair_sum[i, z, p.y, :, cols].astype(F32)
            + ry_left[i, h, z].astype(F32)
            + ry_right[i, h, z].astype(F32)
        )

    def back_second(i):
        round_y[i].finish()
        for h in range(2):
            cross_out[i, :, pl.ds(h * HALF, HALF)] = y_sum(i, p.zo, h).astype(BF)
        send(cross_out.at[i], cross_in.at[i], cross_sem.at[i], **across)

    def back_third(i):
        mine = jnp.concatenate([y_sum(i, p.z, h) for h in range(2)], axis=1)
        standard, reciprocal = standardise(i)
        arrived(cross_in.at[i], cross_sem.at[i])
        scaled = (mine + cross_in[i].astype(F32)) * stretch[i : i + 1]
        rows_all[p.g, i] = (
            reciprocal
            * (
                scaled
                - jnp.mean(scaled, axis=-1, keepdims=True)
                - standard * jnp.mean(scaled * standard, axis=-1, keepdims=True)
            )
        ).astype(BF)
        rows_gather[i].start()

    def attn_pairs(to):
        near = pl.ds(pl.multiple_of((p.z * 8 + to) * ROWS, ROWS), ROWS)
        far = pl.ds(pl.multiple_of((p.zo * 8 + to) * ROWS, ROWS), ROWS)
        cols = pl.ds(pl.multiple_of(p.s * HD, HD), HD)
        staged = pl.ds(pl.multiple_of(q * HD, HD), HD)
        return (
            (attn.at[:, :, near], attn_out.at[:, :, :, cols], attn_recv.at[0]),
            (attn.at[:, :, far], ostage.at[:, :, :, staged], attn_recv.at[1]),
        )

    def attn_copies(k):
        to = (q + k) % 8
        return [
            pltpu.make_async_remote_copy(
                src_ref=src,
                dst_ref=dst,
                send_sem=attn_send.at[n, k],
                recv_sem=recv,
                device_id={"seq": p.z * 8 + to},
                device_id_type=MESH,
            )
            for n, (src, dst, recv) in enumerate(attn_pairs(to))
        ]

    def attn_first_hop():
        @pl.loop(1, 8)
        def _(k):
            for copy in attn_copies(k):
                copy.start()

        for src, dst, recv in attn_pairs(q):
            pltpu.make_async_copy(src, dst, recv).start()

    half_cols = pl.ds(pl.multiple_of(p.z * 1024, 1024), 1024)
    other_cols = pl.ds(pl.multiple_of(p.zo * 1024, 1024), 1024)

    def attn_second_hop():
        arrived(ostage, attn_recv.at[1])
        send(ostage, attn_out.at[:, :, :, half_cols], attn_recv.at[2], **across)

    to_group[0].finish()
    to_group[1].direct()
    gather_first(0)
    to_group[1].pass_on()
    gather_third(0, 0)
    gather_second(0)
    to_group[1].finish()
    arrived(tstage, stage_recv.at[0])
    arrived(cstage.at[0], stage_recv.at[1])
    arrived(cstage.at[1], stage_recv.at[2])
    text_second_hop(0)
    gather_first(1)
    text_second_hop(1)
    gather_fourth(0, 0)
    gather_third(0, 1)
    gather_third(1, 0)
    gather_second(1)
    gather_fourth(0, 1)
    weights.finish()
    gather_wait(0)
    project(0)
    gather_fourth(1, 0)
    arrived(joint.at[:, :, plane], text_recv.at[0])
    arrived(cots.at[:, plane], text_recv.at[1])
    arrived(
        cots.at[:, pl.ds(pl.multiple_of(TXT + p.z * 256, 256), 256)], text_recv.at[2]
    )
    text_wait(0)
    attend(0, 0)
    gather_third(1, 1)
    attend(0, 1)
    attend(0, 2)
    gather_fourth(1, 1)
    attend(0, 3)
    back_project(0)
    gather_wait(1)
    project(1)
    back_first(0)
    text_wait(1)
    attend(1, 0)
    attend(1, 1)
    round_y[0].pass_on()
    attend(1, 2)
    attend(1, 3)
    back_second(0)
    back_project(1)
    back_third(0)
    back_first(1)
    rows_gather[0].pass_left()
    rows_gather[0].pass_right()
    round_y[1].pass_on()
    back_second(1)
    attn_first_hop()
    back_third(1)
    rows_gather[0].finish()

    def control_part(i):
        control_grad[:, i] = (
            lax.dot_general(
                rows_all[:, i].reshape(128, D), zw[...], NT, preferred_element_type=F32
            )
            .astype(BF)
            .reshape(4, ROWS, 768)
        )

    control_part(0)
    rows_gather[1].pass_left()
    rows_gather[1].pass_right()
    rows_gather[1].finish()

    for z in range(2):
        for y in range(4):
            cols = pl.ds((z * 4 + y) * 384, 384)
            grad_cols = rows_all[:, :, :, cols].reshape(256, 384)
            product = lax.dot_general(grad_cols, ctl[...], TN, preferred_element_type=F32)
            zpart[z, y] = product.astype(BF).reshape(2, 192, 768)
            send(
                zpart.at[z, y, p.co], zpair_in.at[z, y], zpair_sem.at[z * 4 + y], **partner
            )
    attn_second_hop()

    cols_a, cols_b = pl.ds(0, 384), pl.ds(384, 384)
    quarter = lambda d: pl.ds(pl.multiple_of(d * 48, 16), 48)
    round_x = Scatter4(
        send,
        lambda d, h: zsum.at[h, :, quarter(d), cols_a],
        lambda h: zx_relay.at[h],
        lambda h: zx_left.at[h],
        lambda h: zx_right.at[h],
        zx_sem,
        p.d,
        p.dl,
        p.dr,
        p.do,
        to_d,
    )
    zero_y = Scatter4(
        send,
        lambda y, h: zsum.at[h, y, :, cols_b],
        lambda h: zy_relay.at[h],
        lambda h: zy_left.at[h],
        lambda h: zy_right.at[h],
        zy_sem,
        p.y,
        p.yl,
        p.yr,
        p.yo,
        to_y,
    )
    for z in range(2):
        for y in range(4):
            arrived(zpair_in.at[z, y], zpair_sem.at[z * 4 + y])
            zsum[z, y] = (
                zpart[z, y, p.c].astype(F32) + zpair_in[z, y].astype(F32)
            ).astype(BF)
    round_x.start()
    zero_y.start()
    round_x.direct()
    zero_y.direct()
    control_part(1)
    round_x.pass_on()
    zero_y.pass_on()
    round_x.finish()
    for z in range(2):
        za_out[z] = (
            zsum[z, :, quarter(p.d), cols_a].astype(F32)
            + zx_left[z].astype(F32)
            + zx_right[z].astype(F32)
        ).astype(BF)
    others_a = [(dz, dy) for dz in range(2) for dy in range(4) if dz or dy]
    for n, (dz, dy) in enumerate(others_a):
        z, y = (p.z + dz) % 2, (p.y + dy) % 4
        send(za_out.at[z, y], za_in.at[n], za_sem.at[n], seq=p.seq(z, y, p.c))
    zero_y.finish()
    for z in range(2):
        zb_out[z] = (
            (
                zsum[z, p.y, :, cols_b].astype(F32)
                + zy_left[z].astype(F32)
                + zy_right[z].astype(F32)
            )
            .astype(BF)
            .reshape(4, 48, 384)
        )
    for n, (dz, dd) in enumerate(others_a):
        z, d = (p.z + dz) % 2, (p.d + dd) % 4
        send(zb_out.at[z, d], zb_in.at[n], zb_sem.at[n], seq=p.seq(z, p.y, p.c), dp=d)
    total = za_out[p.z, p.y].astype(F32)
    for n in range(7):
        arrived(za_in.at[n], za_sem.at[n])
        total = total + za_in[n].astype(F32)
    zown[:, cols_a] = total.astype(BF)
    total = zb_out[p.z, p.d].astype(F32)
    for n in range(7):
        arrived(zb_in.at[n], zb_sem.at[n])
        total = total + zb_in[n].astype(F32)
    zown[:, cols_b] = total.astype(BF)
    for k in range(1, 4):
        send(zown, zall.at[p.d], zg_sem.at[k - 1], dp=(p.d + k) % 4)
    zall[p.d] = zown[...]
    for k in range(1, 4):
        arrived(zall.at[(p.d + 4 - k) % 4], zg_sem.at[k - 1])
    zero_out[...] = zall[...].reshape(192, 768)

    arrived(attn_out.at[:, :, :, half_cols], attn_recv.at[0])
    arrived(attn_out.at[:, :, :, other_cols], attn_recv.at[2])
    send.drain()
    pair_sends[1].drain()

    @pl.loop(1, 8)
    def _(k):
        for copy in text_copies(k):
            copy.wait_send()
        for copy in attn_copies(k):
            copy.wait_send()


def whole_block(*operands):
    dma = pltpu.SemaphoreType.DMA
    bf = lambda *shape: pltpu.VMEM(shape, BF)
    return pl.pallas_call(
        block_kernel,
        out_shape=(
            jax.ShapeDtypeStruct((2, 2, ROWS, HEADS * HD), BF),
            jax.ShapeDtypeStruct((4, 2, ROWS, 768), BF),
            jax.ShapeDtypeStruct((192, 768), BF),
        ),
        in_specs=[pl.BlockSpec(memory_space=pltpu.SMEM), VMEM] + [ANY] * 8,
        out_specs=(ANY, VMEM, VMEM),
        scratch_shapes=[
            bf(256, 768),
            bf(768, D),
            bf(2, ROWS, D),
            bf(4, 768, 384),
            pltpu.VMEM((16, D), F32),
            pltpu.VMEM((16, D), F32),
            bf(4, 2, ROWS, D),
            bf(2, 2, ROWS, HALF),
            bf(2, 2, ROWS, HALF),
            bf(2, 2, ROWS, HALF),
            bf(2, ROWS, D),
            bf(2, 2, 4, 2, ROWS, D),
            bf(3, 2, TXT + IMG, HD),
            bf(2, TXT + IMG, HD),
            bf(3, 2, 256, HD),
            bf(2, 2, 256, HD),
            bf(2, 2, 512, HD),
            bf(2, 2, ROWS, 1024),
            bf(IMG, 384),
            pltpu.VMEM((IMG, HD), F32),
            pltpu.VMEM((IMG, HD), F32),
            bf(16, ROWS, D),
            bf(2, 2, 4, ROWS, D),
            bf(2, 2, 4, ROWS, D),
            bf(2, 2, 2, ROWS, HALF),
            bf(2, 2, 2, ROWS, HALF),
            bf(2, 2, 2, ROWS, HALF),
            bf(2, ROWS, D),
            bf(2, ROWS, D),
            bf(4, 2, ROWS, D),
            bf(2, 4, 2, 192, 768),
            bf(2, 4, 192, 768),
            bf(2, 4, 192, 768),
            bf(2, 4, 48, 384),
            bf(2, 4, 48, 384),
            bf(2, 4, 48, 384),
            bf(2, 192, 384),
            bf(2, 192, 384),
            bf(2, 192, 384),
            bf(2, 4, 48, 384),
            bf(2, 4, 48, 384),
            bf(7, 48, 384),
            bf(7, 48, 384),
            bf(48, 768),
            bf(4, 48, 768),
            dma((28,)),
            dma((176,)),
            dma((4,)),
            dma((2, 6)),
            dma((2, 17)),
            dma((6, 8)),
            dma((3,)),
            dma((3,)),
            dma((2, 3)),
            dma((2, 8)),
            dma((2, 6)),
            dma((2,)),
            dma((2, 4)),
            dma((2, 8)),
            dma((3,)),
            dma((8,)),
            dma((6,)),
            dma((6,)),
            dma((7,)),
            dma((7,)),
            dma((3,)),
        ],
        compiler_params=pltpu.CompilerParams(
            collective_id=1, has_side_effects=True, vmem_limit_bytes=VMEM_LIMIT
        ),
        name="whole_block",
    )(*operands)


def timestep_activation(timesteps):
    half_freq = FREQ // 2
    frequency = jnp.exp(-math.log(10000.0) * jnp.arange(half_freq, dtype=F32) / half_freq)
    angles = timesteps.astype(F32)[..., None] * frequency
    embedding = jnp.concatenate([jnp.cos(angles), jnp.sin(angles)], axis=-1)
    return jax.nn.silu(embedding).astype(BF)


def body(
    image_hidden,
    control_hidden,
    text_qkv,
    text_lengths,
    timesteps,
    mod_weight,
    qkv_weight,
    zero_weight,
    image_cotangent,
    text_cotangent,
):
    activated = timestep_activation(timesteps.reshape(2))
    activated = jnp.pad(activated, ((0, 14), (0, 0)))
    attn_out, control_grad, zero_t = whole_block(
        text_lengths.reshape(2),
        activated,
        mod_weight,
        control_hidden.reshape(256, 768),
        zero_weight,
        image_hidden.reshape(2, ROWS, D),
        jnp.transpose(qkv_weight, (1, 0, 2)),
        text_qkv.reshape(3, 2, ROWS, HEADS * HD),
        text_cotangent.reshape(2, ROWS, HEADS * HD),
        image_cotangent.reshape(2, ROWS, HEADS * HD),
    )
    norm_factor = 16384 ** (-0.5)
    zero_grad = jnp.transpose(zero_t).astype(F32) * norm_factor
    return (
        attn_out[1].reshape(2, 1, ROWS, HEADS * HD),
        attn_out[0].reshape(2, 1, ROWS, HEADS * HD),
        control_grad.reshape(8, 1, ROWS, 768),
        zero_grad,
    )


def solution(mesh):
    placed = (
        P("grp", "dp", "seq", None),
        P(None, "dp", "seq", "grp"),
        P(None, "grp", "dp", "seq", None),
        P("grp", "dp"),
        P("grp", "dp"),
        P(),
        P("dp", None, "seq"),
        P("grp", None),
        P("grp", "dp", "seq", None),
        P("grp", "dp", "seq", None),
    )
    return jax.shard_map(
        body,
        mesh=mesh,
        in_specs=placed,
        out_specs=(
            P("grp", "dp", "seq", None),
            P("grp", "dp", "seq", None),
            P(None, "dp", "seq", "grp"),
            P("grp", "seq"),
        ),
        check_vma=False,
    )
```

```python
import math

import jax
import jax.numpy as jnp
from jax import lax
from jax.experimental import pallas as pl
from jax.experimental.pallas import tpu as pltpu
from jax.sharding import PartitionSpec as P

D = 3072
HEADS = 16
HD = 128
IMG = 512
TXT = 512
FREQ = 256
ROWS = 32
HALF = D // 2
MESH = pl.DeviceIdType.MESH
BF = jnp.bfloat16
F32 = jnp.float32
VMEM_LIMIT = 60 * 1024 * 1024
ANY = pl.BlockSpec(memory_space=pl.ANY)
VMEM = pl.BlockSpec(memory_space=pltpu.VMEM)
HBM = pl.BlockSpec(memory_space=pltpu.HBM)


class Sends:
    def __init__(self, sems):
        self.sems = sems
        self.copies = []
        self.started = 0

    def __call__(self, src, dst, recv, **to):
        copy = pltpu.make_async_remote_copy(
            src_ref=src,
            dst_ref=dst,
            send_sem=self.sems.at[self.started],
            recv_sem=recv,
            device_id=to,
            device_id_type=MESH,
        )
        copy.start()
        self.started += 1
        self.copies.append(copy)

    def drain(self):
        for copy in self.copies:
            copy.wait_send()


def arrived(dst, recv):
    pltpu.make_async_copy(dst, dst, recv).wait()


def greet(groups):
    barrier = pltpu.get_barrier_semaphore()
    for to in groups:
        pl.semaphore_signal(barrier, inc=1, device_id=to, device_id_type=MESH)
    return lambda: pl.semaphore_wait(barrier, len(groups))


class Place:
    def __init__(self):
        self.s = lax.axis_index("seq")
        self.g = lax.axis_index("grp")
        self.d = lax.axis_index("dp")
        self.z = self.s // 8
        self.y = (self.s // 2) % 4
        self.c = self.s % 2
        self.zo = 1 - self.z
        self.co = 1 - self.c
        self.yl = (self.y + 3) % 4
        self.yr = (self.y + 1) % 4
        self.yo = (self.y + 2) % 4
        self.gl = (self.g + 3) % 4
        self.gr = (self.g + 1) % 4
        self.go = (self.g + 2) % 4
        self.dl = (self.d + 3) % 4
        self.dr = (self.d + 1) % 4
        self.do = (self.d + 2) % 4

    def seq(self, z, y, c):
        return z * 8 + y * 2 + c


def add_into(dst, *others):
    total = dst[...].astype(F32)
    for other in others:
        total = total + other[...].astype(F32)
    dst[...] = total.astype(dst.dtype)


class Scatter4:
    def __init__(self, send, src, relay, from_left, from_right, sems, me, left, right, far, to):
        self.send, self.src, self.relay = send, src, relay
        self.from_left, self.from_right, self.sems = from_left, from_right, sems
        self.me, self.left, self.right, self.far, self.to = me, left, right, far, to

    def start(self, *halves):
        for h in halves or (0, 1):
            to = (self.left, self.right)[h]
            self.send(self.src(self.far, h), self.relay(h), self.sems.at[h], **self.to(to))

    def direct(self):
        self.send(
            self.src(self.left, 1), self.from_right(1), self.sems.at[2], **self.to(self.left)
        )
        self.send(
            self.src(self.right, 0), self.from_left(0), self.sems.at[3], **self.to(self.right)
        )

    def pass_on(self):
        arrived(self.relay(0), self.sems.at[0])
        add_into(self.src(self.left, 0), self.relay(0))
        self.send(
            self.src(self.left, 0), self.from_right(0), self.sems.at[4], **self.to(self.left)
        )
        arrived(self.relay(1), self.sems.at[1])
        add_into(self.src(self.right, 1), self.relay(1))
        self.send(
            self.src(self.right, 1), self.from_left(1), self.sems.at[5], **self.to(self.right)
        )
        self.passed = self.send.copies[-2:]

    def sent(self):
        for copy in self.passed:
            copy.wait_send()
        waited = [id(copy) for copy in self.passed]
        self.send.copies = [copy for copy in self.send.copies if id(copy) not in waited]

    def finish(self):
        arrived(self.from_right(1), self.sems.at[2])
        arrived(self.from_left(0), self.sems.at[3])
        arrived(self.from_right(0), self.sems.at[4])
        arrived(self.from_left(1), self.sems.at[5])


class Gather4:
    def __init__(self, send, slot, half, sems, me, left, right, far, to):
        self.send, self.slot, self.half, self.sems = send, slot, half, sems
        self.me, self.left, self.right, self.far, self.to = me, left, right, far, to

    def start(self, own=None):
        own = self.slot(self.me) if own is None else own
        self.send(own, self.slot(self.me), self.sems.at[0], **self.to(self.right))
        self.send(own, self.slot(self.me), self.sems.at[1], **self.to(self.left))

    def pass_left(self):
        arrived(self.slot(self.left), self.sems.at[0])
        part = self.half(self.left, 0)
        self.send(part, part, self.sems.at[2], **self.to(self.right))

    def pass_right(self):
        arrived(self.slot(self.right), self.sems.at[1])
        part = self.half(self.right, 1)
        self.send(part, part, self.sems.at[3], **self.to(self.left))

    def finish(self):
        arrived(self.half(self.far, 0), self.sems.at[2])
        arrived(self.half(self.far, 1), self.sems.at[3])


NT = (((1,), (1,)), ((), ()))
TN = (((0,), (0,)), ((), ()))
BLOCK = 256


def block_kernel(
    lengths,
    activated,
    mod_weight,
    control,
    zero_weight,
    image_hidden,
    weight,
    text,
    text_cot,
    image_cot,
    attn_out,
    control_grad,
    zero_out,
    ctl,
    zw,
    base,
    wall,
    offset,
    stretch,
    partial,
    rg_relay,
    rg_left,
    rg_right,
    hidden,
    normed,
    joint,
    cots,
    tstage,
    cstage,
    attn,
    ostage,
    grads,
    key_acc,
    value_acc,
    dn,
    pair_in,
    pair_sum,
    ry_relay,
    ry_left,
    ry_right,
    cross_out,
    cross_in,
    rows_all,
    zpart,
    zpair_in,
    zsum,
    zx_relay,
    zx_left,
    zx_right,
    zy_relay,
    zy_left,
    zy_right,
    za_out,
    zb_out,
    za_in,
    zb_in,
    zown,
    zall,
    load_sem,
    send_sem,
    w_sem,
    rg_sem,
    ag_sem,
    text_send,
    text_recv,
    stage_recv,
    cross_recv,
    pair_sem,
    ry_sem,
    cross_sem,
    gg_sem,
    attn_send,
    attn_recv,
    zpair_sem,
    zx_sem,
    zy_sem,
    za_sem,
    zb_sem,
    zg_sem,
):
    p = Place()
    send = Sends(send_sem)
    q = p.y * 2 + p.c
    partner = {"seq": p.seq(p.z, p.y, p.co)}
    across = {"seq": p.seq(p.zo, p.y, p.c)}
    to_y = lambda y: {"seq": p.seq(p.z, y, p.c)}
    to_g = lambda g: {"grp": g}
    to_d = lambda d: {"dp": d}

    all_here = greet(
        [{"seq": (p.s + k) % 16} for k in range(1, 16)]
        + [{"grp": p.gl}, {"grp": p.gr}]
        + [{"dp": (p.d + k) % 4} for k in range(1, 4)]
        + [{"dp": (p.d + k) % 4, "seq": p.seq(p.zo, p.y, p.c)} for k in range(1, 4)]
    )

    loads = []

    def load(src, dst):
        copy = pltpu.make_async_copy(src, dst, load_sem.at[len(loads)])
        copy.start()
        loads.append(copy)
        return copy

    load_control = load(control, ctl)
    load_zero = [
        load(zero_weight.at[:, pl.ds(n * 512, 512)], zw.at[:, pl.ds(n * 512, 512)])
        for n in range(6)
    ]
    load_weight = [
        load(weight.at[n], wall.at[p.d, :, pl.ds(n * HD, HD)]) for n in range(3)
    ]
    load_base = load(image_hidden, base)
    load_mod = [
        load(
            mod_weight.at[pl.ds(n % 8 * ROWS, ROWS), pl.ds(n // 8 * D, D)],
            dn.at[n],
        )
        for n in range(16)
    ]

    load_control.wait()

    def residual_part(h):
        for block in range(3 * h, 3 * h + 3):
            cols = pl.ds(block * 512, 512)
            load_zero[block].wait()
            product = jnp.dot(ctl[...], zw[:, cols], preferred_element_type=F32)
            partial[:, :, :, cols] = product.astype(BF).reshape(4, 2, ROWS, 512)

    to_group = [
        Scatter4(
            send,
            lambda g, h, i=i: partial.at[g, i, :, pl.ds(h * HALF, HALF)],
            lambda h, i=i: rg_relay.at[i, h],
            lambda h, i=i: rg_left.at[i, h],
            lambda h, i=i: rg_right.at[i, h],
            rg_sem.at[i],
            p.g,
            p.gl,
            p.gr,
            p.go,
            to_g,
        )
        for i in range(2)
    ]
    residual_part(0)
    residual_part(1)
    all_here()
    to_group[0].start()
    to_group[0].direct()

    row = pl.multiple_of(p.s * ROWS, ROWS)
    stage_row = pl.multiple_of(q * ROWS, ROWS)
    plane = pl.ds(pl.multiple_of(p.z * 256, 256), 256)
    other_plane = pl.ds(pl.multiple_of(p.zo * 256, 256), 256)

    def text_pairs(to):
        near = pl.ds(pl.multiple_of((p.z * 8 + to) * HD, HD), HD)
        far = pl.ds(pl.multiple_of((p.zo * 8 + to) * HD, HD), HD)
        rows = pl.ds(row, ROWS)
        image_rows = pl.ds(TXT + row, ROWS)
        staged = pl.ds(stage_row, ROWS)
        return (
            (text.at[:, :, :, near], joint.at[:, :, rows], text_recv.at[0]),
            (text_cot.at[:, :, near], cots.at[:, rows], text_recv.at[1]),
            (image_cot.at[:, :, near], cots.at[:, image_rows], text_recv.at[2]),
            (text.at[:, :, :, far], tstage.at[:, :, staged], stage_recv.at[0]),
            (text_cot.at[:, :, far], cstage.at[0, :, staged], stage_recv.at[1]),
            (image_cot.at[:, :, far], cstage.at[1, :, staged], stage_recv.at[2]),
        )

    def text_copies(k):
        to = (q + k) % 8
        return [
            pltpu.make_async_remote_copy(
                src_ref=src,
                dst_ref=dst,
                send_sem=text_send.at[n, k],
                recv_sem=recv,
                device_id={"seq": p.z * 8 + to},
                device_id_type=MESH,
            )
            for n, (src, dst, recv) in enumerate(text_pairs(to))
        ]

    @pl.loop(1, 8)
    def _(k):
        for copy in text_copies(k):
            copy.start()

    for src, dst, recv in text_pairs(q):
        pltpu.make_async_copy(src, dst, recv).start()

    def text_second_hop(i):
        send(tstage.at[:, i], joint.at[:, i, plane], cross_recv.at[i, 0], **across)
        send(cstage.at[0, i], cots.at[i, plane], cross_recv.at[i, 1], **across)
        image_rows = pl.ds(pl.multiple_of(TXT + p.z * 256, 256), 256)
        send(cstage.at[1, i], cots.at[i, image_rows], cross_recv.at[i, 2], **across)

    def text_wait(i):
        arrived(joint.at[:, i, other_plane], cross_recv.at[i, 0])
        arrived(cots.at[i, other_plane], cross_recv.at[i, 1])
        image_rows = pl.ds(pl.multiple_of(TXT + p.zo * 256, 256), 256)
        arrived(cots.at[i, image_rows], cross_recv.at[i, 2])

    for copy in load_weight:
        copy.wait()
    weights = Gather4(
        send,
        lambda d: wall.at[d],
        lambda d, h: wall.at[d, pl.ds(h * 384, 384)],
        w_sem,
        p.d,
        p.dl,
        p.dr,
        p.do,
        to_d,
    )
    weights.start()

    for copy in load_mod:
        copy.wait()
    offset[...] = jnp.dot(
        activated[...], dn[:8].reshape(FREQ, D), preferred_element_type=F32
    )
    stretch[...] = 1.0 + jnp.dot(
        activated[...], dn[8:].reshape(FREQ, D), preferred_element_type=F32
    )
    load_base.wait()

    to_group[0].pass_on()
    weights.pass_left()
    weights.pass_right()
    to_group[0].sent()
    to_group[1].start()
    to_group[1].direct()

    gathers = [
        [
            Gather4(
                send,
                lambda y, i=i, z=z: normed.at[i, z, y, p.c],
                lambda y, h, i=i, z=z: normed.at[i, z, y, p.c, pl.ds(h * 16, 16)],
                ag_sem.at[i, pl.ds(which * 4, 4)],
                p.y,
                p.yl,
                p.yr,
                p.yo,
                to_y,
            )
            for which, z in enumerate((p.z, p.zo))
        ]
        for i in range(2)
    ]

    def share(i, z, y, sem):
        slot = normed.at[i, z, y, p.c]
        send(slot, slot, ag_sem.at[i, sem], **partner)

    def standardise(rows):
        values = rows.astype(F32)
        average = jnp.mean(values, axis=-1, keepdims=True)
        centred = values - average
        reciprocal = lax.rsqrt(jnp.mean(centred * centred, axis=-1, keepdims=True) + 1e-06)
        return centred * reciprocal, reciprocal

    def gather_first(i):
        for h in range(2):
            cols = pl.ds(h * HALF, HALF)
            residual = (
                partial[p.g, i, :, cols].astype(F32)
                + rg_left[i, h].astype(F32)
                + rg_right[i, h].astype(F32)
            )
            hidden[i, :, cols] = (base[i, :, cols].astype(F32) + residual).astype(BF)
        standard, _ = standardise(hidden[i])
        normed[i, p.z, p.y, p.c] = (
            standard * stretch[i : i + 1] + offset[i : i + 1]
        ).astype(BF)
        mine = normed.at[i, p.z, p.y, p.c]
        send(mine, mine, ag_sem.at[i, 8], **across)
        gathers[i][0].start()
        send(mine, mine, ag_sem.at[i, 9], **partner)

    def gather_second(i):
        arrived(normed.at[i, p.zo, p.y, p.c], ag_sem.at[i, 8])
        gathers[i][1].start()
        share(i, p.zo, p.y, 10)

    def gather_third(i, which):
        z = (p.z, p.zo)[which]
        gathers[i][which].pass_left()
        gathers[i][which].pass_right()
        share(i, z, p.yl, 11 + 3 * which)
        share(i, z, p.yr, 12 + 3 * which)

    def gather_fourth(i, which):
        z = (p.z, p.zo)[which]
        gathers[i][which].finish()
        share(i, z, p.yo, 13 + 3 * which)

    def gather_wait(i, which):
        z = (p.z, p.zo)[which]
        arrived(normed.at[i, z, p.y, p.co], ag_sem.at[i, 9 + which])
        for n, y in enumerate((p.yl, p.yr, p.yo)):
            arrived(normed.at[i, z, y, p.co], ag_sem.at[i, 11 + 3 * which + n])

    scaling = HD ** (-0.5)
    position = lax.broadcasted_iota(jnp.int32, (1, TXT + IMG), 1)

    def project(i, z):
        product = jnp.dot(
            normed[i, z].reshape(256, D), wall[...].reshape(D, 384), preferred_element_type=F32
        ).astype(BF)
        rows = pl.ds(pl.multiple_of(TXT + z * 256, 256), 256)
        for n in range(3):
            joint[n, i, rows] = product[:, n * HD : (n + 1) * HD]

    def attend(i, block):
        rows = pl.ds(block * BLOCK, BLOCK)
        bias = jnp.where((position >= TXT) | (position < lengths[i]), 0.0, -jnp.inf)
        query, cot = joint[0, i, rows], cots[i, rows]
        keys, values = joint[1, i], joint[2, i]
        scores = lax.dot_general(query, keys, NT, preferred_element_type=F32) + bias
        row_max = jnp.max(scores, axis=1, keepdims=True)
        terms = jnp.exp2((scores - row_max) * (scaling * math.log2(math.e)))
        prob = terms * (1.0 / jnp.sum(terms, axis=1, keepdims=True))
        low = prob.astype(BF)
        attended = jnp.dot(low, values, preferred_element_type=F32).astype(BF)
        attn[block // 2, i, pl.ds(block % 2 * BLOCK, BLOCK)] = attended
        dots = jnp.sum(cot.astype(F32) * attended.astype(F32), axis=1, keepdims=True)
        prob_grad = lax.dot_general(cot, values, NT, preferred_element_type=F32)
        score_grad = (prob * (prob_grad - dots)).astype(BF)
        if block >= 2:
            grads[pl.ds((block - 2) * BLOCK, BLOCK), :HD] = (
                jnp.dot(score_grad, keys, preferred_element_type=F32) * scaling
            ).astype(BF)
        key_part = lax.dot_general(score_grad[:, TXT:], query, TN, preferred_element_type=F32)
        value_part = lax.dot_general(low[:, TXT:], cot, TN, preferred_element_type=F32)
        if block == 0:
            key_acc[...] = key_part
            value_acc[...] = value_part
        elif block < 3:
            key_acc[...] += key_part
            value_acc[...] += value_part
        else:
            grads[:, HD : 2 * HD] = ((key_acc[...] + key_part) * scaling).astype(BF)
            grads[:, 2 * HD :] = (value_acc[...] + value_part).astype(BF)

    pair_sends = [Sends(send_sem.at[pl.ds(176 + 8 * i, 8)]) for i in range(2)]

    def back_project(i, n):
        if i == 1 and n == 0:
            pair_sends[0].drain()
        rows = pl.ds(n * 256, 256)
        for block in range(4):
            cols = pl.ds(block * 768, 768)
            product = lax.dot_general(
                grads[rows], wall[block], NT, preferred_element_type=F32
            ).astype(BF)
            dn[pl.ds(n * 8, 8), :, cols] = product.reshape(8, ROWS, 768)
        for y in range(4):
            pair_sends[i](
                dn.at[n * 8 + y * 2 + p.co], pair_in.at[i, n, y], pair_sem.at[i, n * 4 + y],
                **partner
            )

    def join(i, y):
        for z in range(2):
            arrived(pair_in.at[i, z, y], pair_sem.at[i, z * 4 + y])
            pair_sum[i, z, y] = (
                dn[z * 8 + y * 2 + p.c].astype(F32) + pair_in[i, z, y].astype(F32)
            ).astype(BF)

    half = lambda h: pl.ds(h * HALF, HALF)
    part = lambda r: pl.ds(r * 16, 16)
    chunks = [(i, r) for i in range(2) for r in range(2)]
    round_y = {
        (i, r): Scatter4(
            send,
            lambda y, h, i=i, r=r: pair_sum.at[i, :, y, part(r), half(h)],
            lambda h, i=i, r=r: ry_relay.at[i, h, :, part(r)],
            lambda h, i=i, r=r: ry_left.at[i, h, :, part(r)],
            lambda h, i=i, r=r: ry_right.at[i, h, :, part(r)],
            ry_sem.at[i * 2 + r],
            p.y,
            p.yl,
            p.yr,
            p.yo,
            to_y,
        )
        for i, r in chunks
    }
    rows_gather = {
        (i, r): Gather4(
            send,
            lambda g, i=i, r=r: rows_all.at[g, i, part(r)],
            lambda g, h, i=i, r=r: rows_all.at[g, i, part(r), half(h)],
            gg_sem.at[i * 2 + r],
            p.g,
            p.gl,
            p.gr,
            p.go,
            to_g,
        )
        for i, r in chunks
    }

    def back_first(i):
        join(i, p.yo)
        round_y[i, 0].start()
        join(i, p.yl)
        join(i, p.yr)
        round_y[i, 0].direct()
        join(i, p.y)

    def back_next(i):
        round_y[i, 0].pass_on()
        round_y[i, 1].start()

    def y_sum(i, r, z, h):
        return (
            pair_sum[i, z, p.y, part(r), half(h)].astype(F32)
            + ry_left[i, h, z, part(r)].astype(F32)
            + ry_right[i, h, z, part(r)].astype(F32)
        )

    def back_second(i, r):
        round_y[i, r].finish()
        for h in range(2):
            cross_out[i, part(r), half(h)] = y_sum(i, r, p.zo, h).astype(BF)
        send(
            cross_out.at[i, part(r)], cross_in.at[i, part(r)], cross_sem.at[i * 2 + r], **across
        )

    def back_third(i, r):
        mine = jnp.concatenate([y_sum(i, r, p.z, h) for h in range(2)], axis=1)
        standard, reciprocal = standardise(hidden[i, part(r)])
        arrived(cross_in.at[i, part(r)], cross_sem.at[i * 2 + r])
        scaled = (mine + cross_in[i, part(r)].astype(F32)) * stretch[i : i + 1]
        rows_all[p.g, i, part(r)] = (
            reciprocal
            * (
                scaled
                - jnp.mean(scaled, axis=-1, keepdims=True)
                - standard * jnp.mean(scaled * standard, axis=-1, keepdims=True)
            )
        ).astype(BF)
        rows_gather[i, r].start()

    def rows_pass(i, r):
        rows_gather[i, r].pass_left()
        rows_gather[i, r].pass_right()

    def attn_pairs(to):
        near = pl.ds(pl.multiple_of((p.z * 8 + to) * ROWS, ROWS), ROWS)
        far = pl.ds(pl.multiple_of((p.zo * 8 + to) * ROWS, ROWS), ROWS)
        cols = pl.ds(pl.multiple_of(p.s * HD, HD), HD)
        staged = pl.ds(pl.multiple_of(q * HD, HD), HD)
        return (
            (attn.at[:, :, near], attn_out.at[:, :, :, cols], attn_recv.at[0]),
            (attn.at[:, :, far], ostage.at[:, :, :, staged], attn_recv.at[1]),
        )

    def attn_copies(k):
        to = (q + k) % 8
        return [
            pltpu.make_async_remote_copy(
                src_ref=src,
                dst_ref=dst,
                send_sem=attn_send.at[n, k],
                recv_sem=recv,
                device_id={"seq": p.z * 8 + to},
                device_id_type=MESH,
            )
            for n, (src, dst, recv) in enumerate(attn_pairs(to))
        ]

    def attn_first_hop():
        @pl.loop(1, 8)
        def _(k):
            for copy in attn_copies(k):
                copy.start()

        for src, dst, recv in attn_pairs(q):
            pltpu.make_async_copy(src, dst, recv).start()

    half_cols = pl.ds(pl.multiple_of(p.z * 1024, 1024), 1024)
    other_cols = pl.ds(pl.multiple_of(p.zo * 1024, 1024), 1024)

    def attn_second_hop():
        arrived(ostage, attn_recv.at[1])
        send(ostage, attn_out.at[:, :, :, half_cols], attn_recv.at[2], **across)

    def control_part(i):
        control_grad[:, i] = (
            lax.dot_general(
                rows_all[:, i].reshape(128, D), zw[...], NT, preferred_element_type=F32
            )
            .astype(BF)
            .reshape(4, ROWS, 768)
        )

    to_group[0].finish()
    gather_first(0)
    to_group[1].pass_on()
    gather_third(0, 0)
    gather_second(0)
    to_group[1].finish()
    arrived(tstage, stage_recv.at[0])
    arrived(cstage.at[0], stage_recv.at[1])
    arrived(cstage.at[1], stage_recv.at[2])
    text_second_hop(0)
    gather_first(1)
    gather_fourth(0, 0)
    gather_third(0, 1)
    gather_wait(0, 0)
    weights.finish()
    project(0, p.z)
    gather_third(1, 0)
    gather_fourth(0, 1)
    gather_second(1)
    text_second_hop(1)
    gather_wait(0, 1)
    project(0, p.zo)
    gather_fourth(1, 0)
    arrived(joint.at[:, :, plane], text_recv.at[0])
    arrived(cots.at[:, plane], text_recv.at[1])
    arrived(
        cots.at[:, pl.ds(pl.multiple_of(TXT + p.z * 256, 256), 256)], text_recv.at[2]
    )
    text_wait(0)
    attend(0, 0)
    gather_third(1, 1)
    attend(0, 1)
    attend(0, 2)
    gather_fourth(1, 1)
    attend(0, 3)
    back_project(0, 0)
    back_project(0, 1)
    gather_wait(1, 0)
    project(1, p.z)
    back_first(0)
    gather_wait(1, 1)
    project(1, p.zo)
    text_wait(1)
    attend(1, 0)
    attend(1, 1)
    back_next(0)
    attend(1, 2)
    back_second(0, 0)
    round_y[0, 1].direct()
    attend(1, 3)
    round_y[0, 1].pass_on()
    back_third(0, 0)
    back_project(1, 0)
    back_second(0, 1)
    back_project(1, 1)
    back_third(0, 1)
    back_first(1)
    rows_pass(0, 0)
    back_next(1)
    rows_pass(0, 1)
    back_second(1, 0)
    round_y[1, 1].direct()
    round_y[1, 1].pass_on()
    back_third(1, 0)
    back_second(1, 1)
    attn_first_hop()
    back_third(1, 1)
    rows_pass(1, 0)
    rows_gather[0, 0].finish()
    rows_gather[0, 1].finish()
    control_part(0)
    rows_pass(1, 1)
    rows_gather[1, 0].finish()
    rows_gather[1, 1].finish()

    for z in range(2):
        for y in range(4):
            cols = pl.ds((z * 4 + y) * 384, 384)
            grad_cols = rows_all[:, :, :, cols].reshape(256, 384)
            product = lax.dot_general(grad_cols, ctl[...], TN, preferred_element_type=F32)
            zpart[z, y] = product.astype(BF).reshape(2, 192, 768)
            send(
                zpart.at[z, y, p.co], zpair_in.at[z, y], zpair_sem.at[z * 4 + y], **partner
            )
    attn_second_hop()

    cols_a, cols_b = pl.ds(0, 384), pl.ds(384, 384)
    quarter = lambda d: pl.ds(pl.multiple_of(d * 48, 16), 48)
    round_x = Scatter4(
        send,
        lambda d, h: zsum.at[h, :, quarter(d), cols_a],
        lambda h: zx_relay.at[h],
        lambda h: zx_left.at[h],
        lambda h: zx_right.at[h],
        zx_sem,
        p.d,
        p.dl,
        p.dr,
        p.do,
        to_d,
    )
    zero_y = Scatter4(
        send,
        lambda y, h: zsum.at[h, y, :, cols_b],
        lambda h: zy_relay.at[h],
        lambda h: zy_left.at[h],
        lambda h: zy_right.at[h],
        zy_sem,
        p.y,
        p.yl,
        p.yr,
        p.yo,
        to_y,
    )
    for z in range(2):
        for y in range(4):
            arrived(zpair_in.at[z, y], zpair_sem.at[z * 4 + y])
            zsum[z, y] = (
                zpart[z, y, p.c].astype(F32) + zpair_in[z, y].astype(F32)
            ).astype(BF)
        round_x.start(z)
        zero_y.start(z)
    round_x.direct()
    zero_y.direct()
    control_part(1)
    round_x.pass_on()
    zero_y.pass_on()
    round_x.finish()
    for z in range(2):
        za_out[z] = (
            zsum[z, :, quarter(p.d), cols_a].astype(F32)
            + zx_left[z].astype(F32)
            + zx_right[z].astype(F32)
        ).astype(BF)
    others_a = [(dz, dy) for dz in range(2) for dy in range(4) if dz or dy]
    for n, (dz, dy) in enumerate(others_a):
        z, y = (p.z + dz) % 2, (p.y + dy) % 4
        send(za_out.at[z, y], za_in.at[n], za_sem.at[n], seq=p.seq(z, y, p.c))
    zero_y.finish()
    for z in range(2):
        zb_out[z] = (
            (
                zsum[z, p.y, :, cols_b].astype(F32)
                + zy_left[z].astype(F32)
                + zy_right[z].astype(F32)
            )
            .astype(BF)
            .reshape(4, 48, 384)
        )
    for n, (dz, dd) in enumerate(others_a):
        z, d = (p.z + dz) % 2, (p.d + dd) % 4
        send(zb_out.at[z, d], zb_in.at[n], zb_sem.at[n], seq=p.seq(z, p.y, p.c), dp=d)
    total = za_out[p.z, p.y].astype(F32)
    for n in range(7):
        arrived(za_in.at[n], za_sem.at[n])
        total = total + za_in[n].astype(F32)
    zown[:, cols_a] = total.astype(BF)
    total = zb_out[p.z, p.d].astype(F32)
    for n in range(7):
        arrived(zb_in.at[n], zb_sem.at[n])
        total = total + zb_in[n].astype(F32)
    zown[:, cols_b] = total.astype(BF)
    for k in range(1, 4):
        send(zown, zall.at[p.d], zg_sem.at[k - 1], dp=(p.d + k) % 4)
    zall[p.d] = zown[...]
    for k in range(1, 4):
        arrived(zall.at[(p.d + 4 - k) % 4], zg_sem.at[k - 1])
    zero_out[...] = zall[...].reshape(192, 768).astype(F32) * (16384 ** (-0.5))

    arrived(attn_out.at[:, :, :, half_cols], attn_recv.at[0])
    arrived(attn_out.at[:, :, :, other_cols], attn_recv.at[2])
    send.drain()
    pair_sends[1].drain()

    @pl.loop(1, 8)
    def _(k):
        for copy in text_copies(k):
            copy.wait_send()
        for copy in attn_copies(k):
            copy.wait_send()


def whole_block(*operands):
    dma = pltpu.SemaphoreType.DMA
    bf = lambda *shape: pltpu.VMEM(shape, BF)
    return pl.pallas_call(
        block_kernel,
        out_shape=(
            jax.ShapeDtypeStruct((2, 2, ROWS, HEADS * HD), BF),
            jax.ShapeDtypeStruct((4, 2, ROWS, 768), BF),
            jax.ShapeDtypeStruct((192, 768), F32),
        ),
        in_specs=[pl.BlockSpec(memory_space=pltpu.SMEM), VMEM] + [ANY] * 8,
        out_specs=(ANY, VMEM, VMEM),
        scratch_shapes=[
            bf(256, 768),
            bf(768, D),
            bf(2, ROWS, D),
            bf(4, 768, 384),
            pltpu.VMEM((2, D), F32),
            pltpu.VMEM((2, D), F32),
            bf(4, 2, ROWS, D),
            bf(2, 2, ROWS, HALF),
            bf(2, 2, ROWS, HALF),
            bf(2, 2, ROWS, HALF),
            bf(2, ROWS, D),
            bf(2, 2, 4, 2, ROWS, D),
            bf(3, 2, TXT + IMG, HD),
            bf(2, TXT + IMG, HD),
            bf(3, 2, 256, HD),
            bf(2, 2, 256, HD),
            bf(2, 2, 512, HD),
            bf(2, 2, ROWS, 1024),
            bf(IMG, 384),
            pltpu.VMEM((IMG, HD), F32),
            pltpu.VMEM((IMG, HD), F32),
            bf(16, ROWS, D),
            bf(2, 2, 4, ROWS, D),
            bf(2, 2, 4, ROWS, D),
            bf(2, 2, 2, ROWS, HALF),
            bf(2, 2, 2, ROWS, HALF),
            bf(2, 2, 2, ROWS, HALF),
            bf(2, ROWS, D),
            bf(2, ROWS, D),
            bf(4, 2, ROWS, D),
            bf(2, 4, 2, 192, 768),
            bf(2, 4, 192, 768),
            bf(2, 4, 192, 768),
            bf(2, 4, 48, 384),
            bf(2, 4, 48, 384),
            bf(2, 4, 48, 384),
            bf(2, 192, 384),
            bf(2, 192, 384),
            bf(2, 192, 384),
            bf(2, 4, 48, 384),
            bf(2, 4, 48, 384),
            bf(7, 48, 384),
            bf(7, 48, 384),
            bf(48, 768),
            bf(4, 48, 768),
            dma((28,)),
            dma((192,)),
            dma((4,)),
            dma((2, 6)),
            dma((2, 17)),
            dma((6, 8)),
            dma((3,)),
            dma((3,)),
            dma((2, 3)),
            dma((2, 8)),
            dma((4, 6)),
            dma((4,)),
            dma((4, 4)),
            dma((2, 8)),
            dma((3,)),
            dma((8,)),
            dma((6,)),
            dma((6,)),
            dma((7,)),
            dma((7,)),
            dma((3,)),
        ],
        compiler_params=pltpu.CompilerParams(
            collective_id=1, has_side_effects=True, vmem_limit_bytes=VMEM_LIMIT
        ),
        name="whole_block",
    )(*operands)


def hand_over_kernel(attn, control, zero, image_out, text_out, control_out, zero_out, sems):
    copies = [
        pltpu.make_async_copy(src, dst, sems.at[n])
        for n, (src, dst) in enumerate(
            (
                (attn.at[1], image_out),
                (attn.at[0], text_out),
                (control, control_out),
                (zero, zero_out),
            )
        )
    ]
    for copy in copies:
        copy.start()
    for copy in copies:
        copy.wait()


def hand_over(attn, control, zero):
    return pl.pallas_call(
        hand_over_kernel,
        out_shape=(
            jax.ShapeDtypeStruct(attn.shape[1:], BF),
            jax.ShapeDtypeStruct(attn.shape[1:], BF),
            jax.ShapeDtypeStruct(control.shape, BF),
            jax.ShapeDtypeStruct(zero.shape, F32),
        ),
        in_specs=[HBM] * 3,
        out_specs=(HBM,) * 4,
        scratch_shapes=[pltpu.SemaphoreType.DMA((4,))],
        name="hand_over",
    )(attn, control, zero)


def timestep_activation(timesteps):
    half_freq = FREQ // 2
    frequency = jnp.exp(-math.log(10000.0) * jnp.arange(half_freq, dtype=F32) / half_freq)
    angles = timesteps.astype(F32)[..., None] * frequency
    embedding = jnp.concatenate([jnp.cos(angles), jnp.sin(angles)], axis=-1)
    return jax.nn.silu(embedding).astype(BF)


def body(
    image_hidden,
    control_hidden,
    text_qkv,
    text_lengths,
    timesteps,
    mod_weight,
    qkv_weight,
    zero_weight,
    image_cotangent,
    text_cotangent,
):
    activated = timestep_activation(timesteps.reshape(2))
    attn_out, control_grad, zero_t = whole_block(
        text_lengths.reshape(2),
        activated,
        mod_weight,
        control_hidden.reshape(256, 768),
        zero_weight,
        image_hidden.reshape(2, ROWS, D),
        jnp.transpose(qkv_weight, (1, 0, 2)),
        text_qkv.reshape(3, 2, ROWS, HEADS * HD),
        text_cotangent.reshape(2, ROWS, HEADS * HD),
        image_cotangent.reshape(2, ROWS, HEADS * HD),
    )
    image_attn, text_attn, control_grad, zero_t = hand_over(attn_out, control_grad, zero_t)
    return (
        image_attn.reshape(2, 1, ROWS, HEADS * HD),
        text_attn.reshape(2, 1, ROWS, HEADS * HD),
        control_grad.reshape(8, 1, ROWS, 768),
        jnp.transpose(zero_t),
    )


def solution(mesh):
    placed = (
        P("grp", "dp", "seq", None),
        P(None, "dp", "seq", "grp"),
        P(None, "grp", "dp", "seq", None),
        P("grp", "dp"),
        P("grp", "dp"),
        P(),
        P("dp", None, "seq"),
        P("grp", None),
        P("grp", "dp", "seq", None),
        P("grp", "dp", "seq", None),
    )
    return jax.shard_map(
        body,
        mesh=mesh,
        in_specs=placed,
        out_specs=(
            P("grp", "dp", "seq", None),
            P("grp", "dp", "seq", None),
            P(None, "dp", "seq", "grp"),
            P("grp", "seq"),
        ),
        check_vma=False,
    )
```

```python
import math

import jax
import jax.numpy as jnp
from jax import lax
from jax.experimental import pallas as pl
from jax.experimental.pallas import tpu as pltpu
from jax.sharding import PartitionSpec as P

D = 3072
HEADS = 16
HD = 128
IMG = 512
TXT = 512
FREQ = 256
ROWS = 32
HALF = D // 2
MESH = pl.DeviceIdType.MESH
BF = jnp.bfloat16
F32 = jnp.float32
VMEM_LIMIT = 60 * 1024 * 1024
ANY = pl.BlockSpec(memory_space=pl.ANY)
VMEM = pl.BlockSpec(memory_space=pltpu.VMEM)


class Sends:
    def __init__(self, sems):
        self.sems = sems
        self.copies = []
        self.started = 0

    def __call__(self, src, dst, recv, **to):
        copy = pltpu.make_async_remote_copy(
            src_ref=src,
            dst_ref=dst,
            send_sem=self.sems.at[self.started],
            recv_sem=recv,
            device_id=to,
            device_id_type=MESH,
        )
        copy.start()
        self.started += 1
        self.copies.append(copy)

    def drain(self):
        for copy in self.copies:
            copy.wait_send()


def arrived(dst, recv):
    pltpu.make_async_copy(dst, dst, recv).wait()


def greet(groups):
    barrier = pltpu.get_barrier_semaphore()
    for to in groups:
        pl.semaphore_signal(barrier, inc=1, device_id=to, device_id_type=MESH)
    return lambda: pl.semaphore_wait(barrier, len(groups))


class Place:
    def __init__(self):
        self.s = lax.axis_index("seq")
        self.g = lax.axis_index("grp")
        self.d = lax.axis_index("dp")
        self.z = self.s // 8
        self.y = (self.s // 2) % 4
        self.c = self.s % 2
        self.zo = 1 - self.z
        self.co = 1 - self.c
        self.yl = (self.y + 3) % 4
        self.yr = (self.y + 1) % 4
        self.yo = (self.y + 2) % 4
        self.gl = (self.g + 3) % 4
        self.gr = (self.g + 1) % 4
        self.go = (self.g + 2) % 4
        self.dl = (self.d + 3) % 4
        self.dr = (self.d + 1) % 4
        self.do = (self.d + 2) % 4

    def seq(self, z, y, c):
        return z * 8 + y * 2 + c


def add_into(dst, *others):
    total = dst[...].astype(F32)
    for other in others:
        total = total + other[...].astype(F32)
    dst[...] = total.astype(dst.dtype)


class Scatter4:
    def __init__(self, send, src, relay, from_left, from_right, sems, me, left, right, far, to):
        self.send, self.src, self.relay = send, src, relay
        self.from_left, self.from_right, self.sems = from_left, from_right, sems
        self.me, self.left, self.right, self.far, self.to = me, left, right, far, to

    def start(self, *halves):
        for h in halves or (0, 1):
            to = (self.left, self.right)[h]
            self.send(self.src(self.far, h), self.relay(h), self.sems.at[h], **self.to(to))

    def direct(self):
        self.send(
            self.src(self.left, 1), self.from_right(1), self.sems.at[2], **self.to(self.left)
        )
        self.send(
            self.src(self.right, 0), self.from_left(0), self.sems.at[3], **self.to(self.right)
        )

    def pass_on(self):
        arrived(self.relay(0), self.sems.at[0])
        add_into(self.src(self.left, 0), self.relay(0))
        self.send(
            self.src(self.left, 0), self.from_right(0), self.sems.at[4], **self.to(self.left)
        )
        arrived(self.relay(1), self.sems.at[1])
        add_into(self.src(self.right, 1), self.relay(1))
        self.send(
            self.src(self.right, 1), self.from_left(1), self.sems.at[5], **self.to(self.right)
        )
        self.passed = self.send.copies[-2:]

    def sent(self):
        for copy in self.passed:
            copy.wait_send()
        waited = [id(copy) for copy in self.passed]
        self.send.copies = [copy for copy in self.send.copies if id(copy) not in waited]

    def finish(self):
        arrived(self.from_right(1), self.sems.at[2])
        arrived(self.from_left(0), self.sems.at[3])
        arrived(self.from_right(0), self.sems.at[4])
        arrived(self.from_left(1), self.sems.at[5])


class Gather4:
    def __init__(self, send, slot, half, sems, me, left, right, far, to):
        self.send, self.slot, self.half, self.sems = send, slot, half, sems
        self.me, self.left, self.right, self.far, self.to = me, left, right, far, to

    def start(self, own=None):
        own = self.slot(self.me) if own is None else own
        self.send(own, self.slot(self.me), self.sems.at[0], **self.to(self.right))
        self.send(own, self.slot(self.me), self.sems.at[1], **self.to(self.left))

    def pass_left(self):
        arrived(self.slot(self.left), self.sems.at[0])
        part = self.half(self.left, 0)
        self.send(part, part, self.sems.at[2], **self.to(self.right))

    def pass_right(self):
        arrived(self.slot(self.right), self.sems.at[1])
        part = self.half(self.right, 1)
        self.send(part, part, self.sems.at[3], **self.to(self.left))

    def finish(self):
        arrived(self.half(self.far, 0), self.sems.at[2])
        arrived(self.half(self.far, 1), self.sems.at[3])


NT = (((1,), (1,)), ((), ()))
TN = (((0,), (0,)), ((), ()))
BLOCK = 256


def by_owner(columns, c):
    runs = columns.shape[1] // 384
    return jnp.concatenate(
        [columns[:, n * 384 + c * 192 : n * 384 + c * 192 + 192] for n in range(runs)], axis=1
    )


def block_kernel(
    lengths,
    activated,
    mod_weight,
    control,
    zero_weight,
    image_hidden,
    weight,
    text,
    text_cot,
    image_cot,
    attn_out,
    control_grad,
    zero_out,
    ctl,
    ctl_in,
    zw,
    zw_owner,
    base,
    wall,
    offset,
    stretch,
    partial,
    rg_relay,
    rg_left,
    rg_right,
    hidden,
    normed,
    qkv_out,
    joint,
    cots,
    tstage,
    cstage,
    attn,
    ostage,
    grads,
    both_grads,
    key_acc,
    value_acc,
    pair_sum,
    ry_relay,
    ry_left,
    ry_right,
    cross_out,
    cross_in,
    rows_all,
    rows_in,
    zacc,
    zsum,
    zx_relay,
    zx_left,
    zx_right,
    zy_relay,
    zy_left,
    zy_right,
    za_out,
    zb_out,
    za_in,
    zb_in,
    zown,
    zall,
    load_sem,
    send_sem,
    w_sem,
    share_sem,
    rg_sem,
    ag_sem,
    text_send,
    text_recv,
    stage_recv,
    cross_recv,
    qkv_sem,
    grads_sem,
    ry_sem,
    cross_sem,
    gg_sem,
    rows_sem,
    attn_send,
    attn_recv,
    zx_sem,
    zy_sem,
    za_sem,
    zb_sem,
    zg_sem,
):
    p = Place()
    send = Sends(send_sem)
    q = p.y * 2 + p.c
    partner = {"seq": p.seq(p.z, p.y, p.co)}
    across = {"seq": p.seq(p.zo, p.y, p.c)}
    to_y = lambda y: {"seq": p.seq(p.z, y, p.c)}
    to_g = lambda g: {"grp": g}
    to_d = lambda d: {"dp": d}

    all_here = greet(
        [{"seq": (p.s + k) % 16} for k in range(1, 16)]
        + [{"grp": p.gl}, {"grp": p.gr}]
        + [{"dp": (p.d + k) % 4} for k in range(1, 4)]
        + [{"dp": (p.d + k) % 4, "seq": p.seq(p.zo, p.y, p.c)} for k in range(1, 4)]
    )

    loads = []

    def load(src, dst):
        copy = pltpu.make_async_copy(src, dst, load_sem.at[len(loads)])
        copy.start()
        loads.append(copy)
        return copy

    load_control = load(control, ctl)
    load_zero = [
        load(zero_weight.at[:, pl.ds(n * 512, 512)], zw.at[:, pl.ds(n * 512, 512)])
        for n in range(6)
    ]
    load_weight = [
        load(weight.at[n], wall.at[p.d, :, pl.ds(n * HD, HD)]) for n in range(3)
    ]
    load_base = load(image_hidden, base)
    load_mod = [
        load(
            mod_weight.at[pl.ds(n % 8 * ROWS, ROWS), pl.ds(n // 8 * D, D)],
            pair_sum.at[n // 8, n // 4 % 2, n % 4],
        )
        for n in range(16)
    ]

    load_control.wait()

    def residual_part(h):
        for block in range(3 * h, 3 * h + 3):
            cols = pl.ds(block * 512, 512)
            load_zero[block].wait()
            product = jnp.dot(
                ctl[...].reshape(256, 768), zw[:, cols], preferred_element_type=F32
            )
            partial[:, :, :, cols] = product.astype(BF).reshape(4, 2, ROWS, 512)

    to_group = [
        Scatter4(
            send,
            lambda g, h, i=i: partial.at[g, i, :, pl.ds(h * HALF, HALF)],
            lambda h, i=i: rg_relay.at[i, h],
            lambda h, i=i: rg_left.at[i, h],
            lambda h, i=i: rg_right.at[i, h],
            rg_sem.at[i],
            p.g,
            p.gl,
            p.gr,
            p.go,
            to_g,
        )
        for i in range(2)
    ]
    residual_part(0)
    residual_part(1)
    all_here()
    to_group[0].start()
    to_group[0].direct()

    plane = pl.ds(p.z * 4, 4)
    other_plane = pl.ds(p.zo * 4, 4)
    zy = p.z * 4 + p.y

    def text_pairs(to):
        near = pl.ds(pl.multiple_of((p.z * 8 + to) * HD, HD), HD)
        far = pl.ds(pl.multiple_of((p.zo * 8 + to) * HD, HD), HD)
        return (
            (text.at[:, :, :, near], joint.at[:, :, 0, zy, p.c], text_recv.at[0]),
            (text_cot.at[:, :, near], cots.at[:, 0, zy, p.c], text_recv.at[1]),
            (image_cot.at[:, :, near], cots.at[:, 1, zy, p.c], text_recv.at[2]),
            (text.at[:, :, :, far], tstage.at[:, :, p.y, p.c], stage_recv.at[0]),
            (text_cot.at[:, :, far], cstage.at[0, :, p.y, p.c], stage_recv.at[1]),
            (image_cot.at[:, :, far], cstage.at[1, :, p.y, p.c], stage_recv.at[2]),
        )

    def text_copies(k):
        to = (q + k) % 8
        return [
            pltpu.make_async_remote_copy(
                src_ref=src,
                dst_ref=dst,
                send_sem=text_send.at[n, k],
                recv_sem=recv,
                device_id={"seq": p.z * 8 + to},
                device_id_type=MESH,
            )
            for n, (src, dst, recv) in enumerate(text_pairs(to))
        ]

    @pl.loop(1, 8)
    def _(k):
        for copy in text_copies(k):
            copy.start()

    for src, dst, recv in text_pairs(q):
        pltpu.make_async_copy(src, dst, recv).start()

    def text_second_hop(i):
        send(tstage.at[:, i], joint.at[:, i, 0, plane], cross_recv.at[i, 0], **across)
        send(cstage.at[0, i], cots.at[i, 0, plane], cross_recv.at[i, 1], **across)
        send(cstage.at[1, i], cots.at[i, 1, plane], cross_recv.at[i, 2], **across)

    def text_wait(i):
        arrived(joint.at[:, i, 0, other_plane], cross_recv.at[i, 0])
        arrived(cots.at[i, 0, other_plane], cross_recv.at[i, 1])
        arrived(cots.at[i, 1, other_plane], cross_recv.at[i, 2])

    for copy in load_weight:
        copy.wait()
    mine_cols, pair_cols = pl.ds(0, 384), pl.ds(384, 384)
    weights = Gather4(
        send,
        lambda d: wall.at[d, :, mine_cols],
        lambda d, h: wall.at[d, pl.ds(h * 384, 384), mine_cols],
        w_sem,
        p.d,
        p.dl,
        p.dr,
        p.do,
        to_d,
    )
    weights.start()

    def share_weight(d, sem):
        send(wall.at[d, :, mine_cols], wall.at[d, :, pair_cols], share_sem.at[sem], **partner)

    share_weight(p.d, 0)
    send(ctl, ctl_in, share_sem.at[4], **partner)

    for copy in load_mod:
        copy.wait()
    offset[...] = jnp.dot(
        activated[...], pair_sum[0].reshape(FREQ, D), preferred_element_type=F32
    )
    stretch[...] = 1.0 + jnp.dot(
        activated[...], pair_sum[1].reshape(FREQ, D), preferred_element_type=F32
    )
    load_base.wait()

    for block in range(4):
        columns = zw[:, pl.ds(block * 768, 768)].astype(F32)
        for c in range(2):
            zw_owner[c, :, pl.ds(block * 384, 384)] = by_owner(columns, c).astype(BF)

    to_group[0].pass_on()
    weights.pass_left()
    weights.pass_right()
    share_weight(p.dl, 1)
    share_weight(p.dr, 2)
    to_group[0].sent()
    to_group[1].start()
    to_group[1].direct()

    gathers = [
        [
            Gather4(
                send,
                lambda y, i=i, z=z: normed.at[i, z, y],
                lambda y, h, i=i, z=z: normed.at[i, z, y, pl.ds(h * 16, 16)],
                ag_sem.at[i, pl.ds(which * 4, 4)],
                p.y,
                p.yl,
                p.yr,
                p.yo,
                to_y,
            )
            for which, z in enumerate((p.z, p.zo))
        ]
        for i in range(2)
    ]

    def standardise(rows):
        values = rows.astype(F32)
        average = jnp.mean(values, axis=-1, keepdims=True)
        centred = values - average
        reciprocal = lax.rsqrt(jnp.mean(centred * centred, axis=-1, keepdims=True) + 1e-06)
        return centred * reciprocal, reciprocal

    def gather_first(i):
        for h in range(2):
            cols = pl.ds(h * HALF, HALF)
            residual = (
                partial[p.g, i, :, cols].astype(F32)
                + rg_left[i, h].astype(F32)
                + rg_right[i, h].astype(F32)
            )
            hidden[i, :, cols] = (base[i, :, cols].astype(F32) + residual).astype(BF)
        standard, _ = standardise(hidden[i])
        normed[i, p.z, p.y] = (standard * stretch[i : i + 1] + offset[i : i + 1]).astype(BF)
        mine = normed.at[i, p.z, p.y]
        send(mine, mine, ag_sem.at[i, 8], **across)
        gathers[i][0].start()

    def gather_second(i):
        arrived(normed.at[i, p.zo, p.y], ag_sem.at[i, 8])
        gathers[i][1].start()

    def gather_third(i, which):
        gathers[i][which].pass_left()
        gathers[i][which].pass_right()

    def gather_fourth(i, which):
        gathers[i][which].finish()

    scaling = HD ** (-0.5)
    position = lax.broadcasted_iota(jnp.int32, (1, TXT + IMG), 1)

    def project(i):
        product = jnp.dot(
            normed[i].reshape(256, D), wall[...].reshape(D, 768), preferred_element_type=F32
        ).astype(BF)
        for n in range(3):
            qkv_out[i, n] = product[:, 384 + n * HD : 384 + (n + 1) * HD].reshape(8, ROWS, HD)
        send(qkv_out.at[i], joint.at[:, i, 1, :, p.c], qkv_sem.at[i], **partner)
        for n in range(3):
            joint[n, i, 1, :, p.c] = product[:, n * HD : (n + 1) * HD].reshape(8, ROWS, HD)

    def project_wait(i):
        arrived(joint.at[:, i, 1, :, p.co], qkv_sem.at[i])

    def attend(i, block):
        slots = pl.ds(block % 2 * 4, 4)
        bias = jnp.where((position >= TXT) | (position < lengths[i]), 0.0, -jnp.inf)
        query = joint[0, i, block // 2, slots].reshape(BLOCK, HD)
        cot = cots[i, block // 2, slots].reshape(BLOCK, HD)
        keys = joint[1, i].reshape(TXT + IMG, HD)
        values = joint[2, i].reshape(TXT + IMG, HD)
        scores = lax.dot_general(query, keys, NT, preferred_element_type=F32) + bias
        row_max = jnp.max(scores, axis=1, keepdims=True)
        terms = jnp.exp2((scores - row_max) * (scaling * math.log2(math.e)))
        prob = terms * (1.0 / jnp.sum(terms, axis=1, keepdims=True))
        low = prob.astype(BF)
        attended = jnp.dot(low, values, preferred_element_type=F32).astype(BF)
        attn[block // 2, i, pl.ds(block % 2 * BLOCK, BLOCK)] = attended
        dots = jnp.sum(cot.astype(F32) * attended.astype(F32), axis=1, keepdims=True)
        prob_grad = lax.dot_general(cot, values, NT, preferred_element_type=F32)
        score_grad = (prob * (prob_grad - dots)).astype(BF)
        if block >= 2:
            query_grad = jnp.dot(score_grad, keys, preferred_element_type=F32) * scaling
            grads[i, slots, :, :, :HD] = query_grad.astype(BF).reshape(4, 2, ROWS, HD)
        key_part = lax.dot_general(score_grad[:, TXT:], query, TN, preferred_element_type=F32)
        value_part = lax.dot_general(low[:, TXT:], cot, TN, preferred_element_type=F32)
        if block == 0:
            key_acc[...] = key_part
            value_acc[...] = value_part
        elif block < 3:
            key_acc[...] += key_part
            value_acc[...] += value_part
        else:
            key_grad = ((key_acc[...] + key_part) * scaling).astype(BF)
            value_grad = (value_acc[...] + value_part).astype(BF)
            grads[i, :, :, :, HD : 2 * HD] = key_grad.reshape(8, 2, ROWS, HD)
            grads[i, :, :, :, 2 * HD :] = value_grad.reshape(8, 2, ROWS, HD)
            send(
                grads.at[i, :, p.co], both_grads.at[i, :, :, pair_cols], grads_sem.at[i],
                **partner
            )
            both_grads[i, :, :, :384] = grads[i, :, p.c]

    def back_project(i):
        arrived(both_grads.at[i, :, :, pair_cols], grads_sem.at[i])
        for block in range(4):
            cols = pl.ds(block * 768, 768)
            product = lax.dot_general(
                both_grads[i].reshape(256, 768), wall[block], NT, preferred_element_type=F32
            ).astype(BF)
            pair_sum[i, :, :, :, cols] = product.reshape(2, 4, ROWS, 768)
            if block % 2:
                round_y[i, 0].start(block // 2)
        round_y[i, 0].direct()

    half = lambda h: pl.ds(h * HALF, HALF)
    part = lambda r: pl.ds(r * 16, 16)
    chunks = [(i, r) for i in range(2) for r in range(2)]
    round_y = {
        (i, r): Scatter4(
            send,
            lambda y, h, i=i, r=r: pair_sum.at[i, :, y, part(r), half(h)],
            lambda h, i=i, r=r: ry_relay.at[i, h, :, part(r)],
            lambda h, i=i, r=r: ry_left.at[i, h, :, part(r)],
            lambda h, i=i, r=r: ry_right.at[i, h, :, part(r)],
            ry_sem.at[i * 2 + r],
            p.y,
            p.yl,
            p.yr,
            p.yo,
            to_y,
        )
        for i, r in chunks
    }
    rows_gather = {
        (i, r): Gather4(
            send,
            lambda g, i=i, r=r: rows_all.at[:, g, i, part(r)],
            lambda g, h, i=i, r=r: rows_all.at[h, g, i, part(r)],
            gg_sem.at[i * 2 + r],
            p.g,
            p.gl,
            p.gr,
            p.go,
            to_g,
        )
        for i, r in chunks
    }

    def back_next(i):
        round_y[i, 0].pass_on()
        round_y[i, 1].start()

    def y_sum(i, r, z, h):
        return (
            pair_sum[i, z, p.y, part(r), half(h)].astype(F32)
            + ry_left[i, h, z, part(r)].astype(F32)
            + ry_right[i, h, z, part(r)].astype(F32)
        )

    def back_second(i, r):
        round_y[i, r].finish()
        for h in range(2):
            cross_out[i, part(r), half(h)] = y_sum(i, r, p.zo, h).astype(BF)
        send(
            cross_out.at[i, part(r)], cross_in.at[i, part(r)], cross_sem.at[i * 2 + r], **across
        )

    def back_third(i, r):
        mine = jnp.concatenate([y_sum(i, r, p.z, h) for h in range(2)], axis=1)
        standard, reciprocal = standardise(hidden[i, part(r)])
        arrived(cross_in.at[i, part(r)], cross_sem.at[i * 2 + r])
        scaled = (mine + cross_in[i, part(r)].astype(F32)) * stretch[i : i + 1]
        residual_grad = reciprocal * (
            scaled
            - jnp.mean(scaled, axis=-1, keepdims=True)
            - standard * jnp.mean(scaled * standard, axis=-1, keepdims=True)
        )
        for c in range(2):
            rows_all[c, p.g, i, part(r)] = by_owner(residual_grad, c).astype(BF)
        rows_gather[i, r].start()

    def rows_pass(i, r):
        rows_gather[i, r].pass_left()
        rows_gather[i, r].pass_right()

    def rows_finish(i, r):
        rows_gather[i, r].finish()
        send(
            rows_all.at[p.co, :, i, part(r)],
            rows_in.at[:, i, part(r)],
            rows_sem.at[i * 2 + r],
            **partner
        )

    def attn_pairs(to):
        near = pl.ds(pl.multiple_of((p.z * 8 + to) * ROWS, ROWS), ROWS)
        far = pl.ds(pl.multiple_of((p.zo * 8 + to) * ROWS, ROWS), ROWS)
        cols = pl.ds(pl.multiple_of(p.s * HD, HD), HD)
        staged = pl.ds(pl.multiple_of(q * HD, HD), HD)
        return (
            (attn.at[:, :, near], attn_out.at[:, :, :, cols], attn_recv.at[0]),
            (attn.at[:, :, far], ostage.at[:, :, :, staged], attn_recv.at[1]),
        )

    def attn_copies(k):
        to = (q + k) % 8
        return [
            pltpu.make_async_remote_copy(
                src_ref=src,
                dst_ref=dst,
                send_sem=attn_send.at[n, k],
                recv_sem=recv,
                device_id={"seq": p.z * 8 + to},
                device_id_type=MESH,
            )
            for n, (src, dst, recv) in enumerate(attn_pairs(to))
        ]

    def attn_first_hop():
        @pl.loop(1, 8)
        def _(k):
            for copy in attn_copies(k):
                copy.start()

        for src, dst, recv in attn_pairs(q):
            pltpu.make_async_copy(src, dst, recv).start()

    half_cols = pl.ds(pl.multiple_of(p.z * 1024, 1024), 1024)
    other_cols = pl.ds(pl.multiple_of(p.zo * 1024, 1024), 1024)

    def attn_second_hop():
        arrived(ostage, attn_recv.at[1])
        send(ostage, attn_out.at[:, :, :, half_cols], attn_recv.at[2], **across)

    def control_part(i):
        total = 0.0
        for c in range(2):
            total = total + lax.dot_general(
                rows_all[c, :, i].reshape(128, HALF),
                zw_owner[c],
                NT,
                preferred_element_type=F32,
            )
        control_grad[:, i] = total.astype(BF).reshape(4, ROWS, 768)

    def zero_part(i, block):
        cols = pl.ds(block * 384, 384)
        left = jnp.concatenate(
            [ref.reshape(128, 384) for ref in (rows_all[p.c, :, i, :, cols], rows_in[:, i, :, cols])]
        )
        right = jnp.concatenate([ctl[:, i].reshape(128, 768), ctl_in[:, i].reshape(128, 768)])
        product = lax.dot_general(left, right, TN, preferred_element_type=F32)
        if i == 0:
            zacc[cols] = product
        else:
            z, y = block // 2, block % 2 * 2
            zsum[z, pl.ds(y, 2)] = (zacc[cols] + product).astype(BF).reshape(2, 192, 768)

    to_group[0].finish()
    gather_first(0)
    to_group[1].pass_on()
    gather_third(0, 0)
    gather_second(0)
    to_group[1].finish()
    arrived(tstage, stage_recv.at[0])
    arrived(cstage.at[0], stage_recv.at[1])
    arrived(cstage.at[1], stage_recv.at[2])
    text_second_hop(0)
    gather_first(1)
    gather_fourth(0, 0)
    gather_third(0, 1)
    gather_third(1, 0)
    weights.finish()
    share_weight(p.do, 3)
    gather_fourth(0, 1)
    for n, d in enumerate((p.d, p.dl, p.dr, p.do)):
        arrived(wall.at[d, :, pair_cols], share_sem.at[n])
    project(0)
    gather_second(1)
    text_second_hop(1)
    gather_fourth(1, 0)
    arrived(joint.at[:, :, 0, plane], text_recv.at[0])
    arrived(cots.at[:, 0, plane], text_recv.at[1])
    arrived(cots.at[:, 1, plane], text_recv.at[2])
    text_wait(0)
    project_wait(0)
    attend(0, 0)
    gather_third(1, 1)
    attend(0, 1)
    attend(0, 2)
    gather_fourth(1, 1)
    attend(0, 3)
    project(1)
    back_project(0)
    text_wait(1)
    project_wait(1)
    attend(1, 0)
    attend(1, 1)
    back_next(0)
    attend(1, 2)
    back_second(0, 0)
    round_y[0, 1].direct()
    attend(1, 3)
    round_y[0, 1].pass_on()
    back_third(0, 0)
    back_second(0, 1)
    back_project(1)
    back_third(0, 1)
    rows_pass(0, 0)
    back_next(1)
    rows_pass(0, 1)
    back_second(1, 0)
    round_y[1, 1].direct()
    round_y[1, 1].pass_on()
    back_third(1, 0)
    rows_finish(0, 0)
    back_second(1, 1)
    attn_first_hop()
    back_third(1, 1)
    rows_pass(1, 0)
    rows_finish(0, 1)
    arrived(ctl_in, share_sem.at[4])
    control_part(0)
    rows_pass(1, 1)
    for r in range(2):
        arrived(rows_in.at[:, 0, part(r)], rows_sem.at[r])
    for block in range(4):
        zero_part(0, block)
    rows_finish(1, 0)
    rows_finish(1, 1)
    for r in range(2):
        arrived(rows_in.at[:, 1, part(r)], rows_sem.at[2 + r])

    cols_a, cols_b = pl.ds(0, 384), pl.ds(384, 384)
    quarter = lambda d: pl.ds(pl.multiple_of(d * 48, 16), 48)
    round_x = Scatter4(
        send,
        lambda d, h: zsum.at[h, :, quarter(d), cols_a],
        lambda h: zx_relay.at[h],
        lambda h: zx_left.at[h],
        lambda h: zx_right.at[h],
        zx_sem,
        p.d,
        p.dl,
        p.dr,
        p.do,
        to_d,
    )
    zero_y = Scatter4(
        send,
        lambda y, h: zsum.at[h, y, :, cols_b],
        lambda h: zy_relay.at[h],
        lambda h: zy_left.at[h],
        lambda h: zy_right.at[h],
        zy_sem,
        p.y,
        p.yl,
        p.yr,
        p.yo,
        to_y,
    )
    for z in range(2):
        zero_part(1, 2 * z)
        zero_part(1, 2 * z + 1)
        round_x.start(z)
        zero_y.start(z)
    round_x.direct()
    zero_y.direct()
    attn_second_hop()
    control_part(1)
    round_x.pass_on()
    zero_y.pass_on()
    round_x.finish()
    for z in range(2):
        za_out[z] = (
            zsum[z, :, quarter(p.d), cols_a].astype(F32)
            + zx_left[z].astype(F32)
            + zx_right[z].astype(F32)
        ).astype(BF)
    others_a = [(dz, dy) for dz in range(2) for dy in range(4) if dz or dy]
    for n, (dz, dy) in enumerate(others_a):
        z, y = (p.z + dz) % 2, (p.y + dy) % 4
        send(za_out.at[z, y], za_in.at[n], za_sem.at[n], seq=p.seq(z, y, p.c))
    zero_y.finish()
    for z in range(2):
        zb_out[z] = (
            (
                zsum[z, p.y, :, cols_b].astype(F32)
                + zy_left[z].astype(F32)
                + zy_right[z].astype(F32)
            )
            .astype(BF)
            .reshape(4, 48, 384)
        )
    for n, (dz, dd) in enumerate(others_a):
        z, d = (p.z + dz) % 2, (p.d + dd) % 4
        send(zb_out.at[z, d], zb_in.at[n], zb_sem.at[n], seq=p.seq(z, p.y, p.c), dp=d)
    total = za_out[p.z, p.y].astype(F32)
    for n in range(7):
        arrived(za_in.at[n], za_sem.at[n])
        total = total + za_in[n].astype(F32)
    zown[:, cols_a] = total.astype(BF)
    total = zb_out[p.z, p.d].astype(F32)
    for n in range(7):
        arrived(zb_in.at[n], zb_sem.at[n])
        total = total + zb_in[n].astype(F32)
    zown[:, cols_b] = total.astype(BF)
    for k in range(1, 4):
        send(zown, zall.at[p.d], zg_sem.at[k - 1], dp=(p.d + k) % 4)
    zall[p.d] = zown[...]
    for k in range(1, 4):
        arrived(zall.at[(p.d + 4 - k) % 4], zg_sem.at[k - 1])
    zero_out[...] = zall[...].reshape(192, 768).astype(F32) * (16384 ** (-0.5))

    arrived(attn_out.at[:, :, :, half_cols], attn_recv.at[0])
    arrived(attn_out.at[:, :, :, other_cols], attn_recv.at[2])
    send.drain()

    @pl.loop(1, 8)
    def _(k):
        for copy in text_copies(k):
            copy.wait_send()
        for copy in attn_copies(k):
            copy.wait_send()


def whole_block(*operands):
    dma = pltpu.SemaphoreType.DMA
    bf = lambda *shape: pltpu.VMEM(shape, BF)
    return pl.pallas_call(
        block_kernel,
        out_shape=(
            jax.ShapeDtypeStruct((2, 2, ROWS, HEADS * HD), BF),
            jax.ShapeDtypeStruct((4, 2, ROWS, 768), BF),
            jax.ShapeDtypeStruct((192, 768), F32),
        ),
        in_specs=[pl.BlockSpec(memory_space=pltpu.SMEM), VMEM] + [ANY] * 8,
        out_specs=(ANY, VMEM, VMEM),
        scratch_shapes=[
            bf(4, 2, ROWS, 768),
            bf(4, 2, ROWS, 768),
            bf(768, D),
            bf(2, 768, HALF),
            bf(2, ROWS, D),
            bf(4, 768, 768),
            pltpu.VMEM((2, D), F32),
            pltpu.VMEM((2, D), F32),
            bf(4, 2, ROWS, D),
            bf(2, 2, ROWS, HALF),
            bf(2, 2, ROWS, HALF),
            bf(2, 2, ROWS, HALF),
            bf(2, ROWS, D),
            bf(2, 2, 4, ROWS, D),
            bf(2, 3, 8, ROWS, HD),
            bf(3, 2, 2, 8, 2, ROWS, HD),
            bf(2, 2, 8, 2, ROWS, HD),
            bf(3, 2, 4, 2, ROWS, HD),
            bf(2, 2, 4, 2, ROWS, HD),
            bf(2, 2, 512, HD),
            bf(2, 2, ROWS, 1024),
            bf(2, 8, 2, ROWS, 384),
            bf(2, 8, ROWS, 768),
            pltpu.VMEM((IMG, HD), F32),
            pltpu.VMEM((IMG, HD), F32),
            bf(2, 2, 4, ROWS, D),
            bf(2, 2, 2, ROWS, HALF),
            bf(2, 2, 2, ROWS, HALF),
            bf(2, 2, 2, ROWS, HALF),
            bf(2, ROWS, D),
            bf(2, ROWS, D),
            bf(2, 4, 2, ROWS, HALF),
            bf(4, 2, ROWS, HALF),
            pltpu.VMEM((HALF, 768), F32),
            bf(2, 4, 192, 768),
            bf(2, 4, 48, 384),
            bf(2, 4, 48, 384),
            bf(2, 4, 48, 384),
            bf(2, 192, 384),
            bf(2, 192, 384),
            bf(2, 192, 384),
            bf(2, 4, 48, 384),
            bf(2, 4, 48, 384),
            bf(7, 48, 384),
            bf(7, 48, 384),
            bf(48, 768),
            bf(4, 48, 768),
            dma((28,)),
            dma((176,)),
            dma((4,)),
            dma((5,)),
            dma((2, 6)),
            dma((2, 9)),
            dma((6, 8)),
            dma((3,)),
            dma((3,)),
            dma((2, 3)),
            dma((2,)),
            dma((2,)),
            dma((4, 6)),
            dma((4,)),
            dma((4, 4)),
            dma((4,)),
            dma((2, 8)),
            dma((3,)),
            dma((6,)),
            dma((6,)),
            dma((7,)),
            dma((7,)),
            dma((3,)),
        ],
        compiler_params=pltpu.CompilerParams(
            collective_id=1, has_side_effects=True, vmem_limit_bytes=VMEM_LIMIT
        ),
        name="whole_block",
    )(*operands)


def hand_over_kernel(attn, control, zero, image_out, text_out, control_out, zero_out, sems):
    copies = [
        pltpu.make_async_copy(src, dst, sems.at[n])
        for n, (src, dst) in enumerate(
            (
                (attn.at[1], image_out),
                (attn.at[0], text_out),
                (control, control_out),
                (zero, zero_out),
            )
        )
    ]
    for copy in copies:
        copy.start()
    for copy in copies:
        copy.wait()


def hand_over(attn, control, zero):
    return pl.pallas_call(
        hand_over_kernel,
        out_shape=(
            jax.ShapeDtypeStruct(attn.shape[1:], BF),
            jax.ShapeDtypeStruct(attn.shape[1:], BF),
            jax.ShapeDtypeStruct(control.shape, BF),
            jax.ShapeDtypeStruct(zero.shape, F32),
        ),
        in_specs=[VMEM] * 3,
        out_specs=(ANY,) * 4,
        scratch_shapes=[pltpu.SemaphoreType.DMA((4,))],
        name="hand_over",
    )(attn, control, zero)


def timestep_activation(timesteps):
    half_freq = FREQ // 2
    frequency = jnp.exp(-math.log(10000.0) * jnp.arange(half_freq, dtype=F32) / half_freq)
    angles = timesteps.astype(F32)[..., None] * frequency
    embedding = jnp.concatenate([jnp.cos(angles), jnp.sin(angles)], axis=-1)
    return jax.nn.silu(embedding).astype(BF)


def body(
    image_hidden,
    control_hidden,
    text_qkv,
    text_lengths,
    timesteps,
    mod_weight,
    qkv_weight,
    zero_weight,
    image_cotangent,
    text_cotangent,
):
    activated = timestep_activation(timesteps.reshape(2))
    attn_out, control_grad, zero_t = whole_block(
        text_lengths.reshape(2),
        activated,
        mod_weight,
        control_hidden.reshape(4, 2, ROWS, 768),
        zero_weight,
        image_hidden.reshape(2, ROWS, D),
        jnp.transpose(qkv_weight, (1, 0, 2)),
        text_qkv.reshape(3, 2, ROWS, HEADS * HD),
        text_cotangent.reshape(2, ROWS, HEADS * HD),
        image_cotangent.reshape(2, ROWS, HEADS * HD),
    )
    image_attn, text_attn, control_grad, zero_t = hand_over(attn_out, control_grad, zero_t)
    return (
        image_attn.reshape(2, 1, ROWS, HEADS * HD),
        text_attn.reshape(2, 1, ROWS, HEADS * HD),
        control_grad.reshape(8, 1, ROWS, 768),
        jnp.transpose(zero_t),
    )


def solution(mesh):
    placed = (
        P("grp", "dp", "seq", None),
        P(None, "dp", "seq", "grp"),
        P(None, "grp", "dp", "seq", None),
        P("grp", "dp"),
        P("grp", "dp"),
        P(),
        P("dp", None, "seq"),
        P("grp", None),
        P("grp", "dp", "seq", None),
        P("grp", "dp", "seq", None),
    )
    return jax.shard_map(
        body,
        mesh=mesh,
        in_specs=placed,
        out_specs=(
            P("grp", "dp", "seq", None),
            P("grp", "dp", "seq", None),
            P(None, "dp", "seq", "grp"),
            P("grp", "seq"),
        ),
        check_vma=False,
    )
```

```python
import math

import jax
import jax.numpy as jnp
from jax import lax
from jax.experimental import pallas as pl
from jax.experimental.pallas import tpu as pltpu
from jax.sharding import PartitionSpec as P

D = 3072
HEADS = 16
HD = 128
IMG = 512
TXT = 512
FREQ = 256
ROWS = 32
HALF = D // 2
MESH = pl.DeviceIdType.MESH
BF = jnp.bfloat16
F32 = jnp.float32
VMEM_LIMIT = 60 * 1024 * 1024
ANY = pl.BlockSpec(memory_space=pl.ANY)
VMEM = pl.BlockSpec(memory_space=pltpu.VMEM)


class Sends:
    def __init__(self, sems):
        self.sems = sems
        self.copies = []
        self.started = 0

    def __call__(self, src, dst, recv, **to):
        copy = pltpu.make_async_remote_copy(
            src_ref=src,
            dst_ref=dst,
            send_sem=self.sems.at[self.started],
            recv_sem=recv,
            device_id=to,
            device_id_type=MESH,
        )
        copy.start()
        self.started += 1
        self.copies.append(copy)

    def drain(self):
        for copy in self.copies:
            copy.wait_send()


def arrived(dst, recv):
    pltpu.make_async_copy(dst, dst, recv).wait()


def greet(groups):
    barrier = pltpu.get_barrier_semaphore()
    for to in groups:
        pl.semaphore_signal(barrier, inc=1, device_id=to, device_id_type=MESH)
    return lambda: pl.semaphore_wait(barrier, len(groups))


class Place:
    def __init__(self):
        self.s = lax.axis_index("seq")
        self.g = lax.axis_index("grp")
        self.d = lax.axis_index("dp")
        self.z = self.s // 8
        self.y = (self.s // 2) % 4
        self.c = self.s % 2
        self.zo = 1 - self.z
        self.co = 1 - self.c
        self.yl = (self.y + 3) % 4
        self.yr = (self.y + 1) % 4
        self.yo = (self.y + 2) % 4
        self.gl = (self.g + 3) % 4
        self.gr = (self.g + 1) % 4
        self.go = (self.g + 2) % 4
        self.dl = (self.d + 3) % 4
        self.dr = (self.d + 1) % 4
        self.do = (self.d + 2) % 4

    def seq(self, z, y, c):
        return z * 8 + y * 2 + c


def add_into(dst, *others):
    total = dst[...].astype(F32)
    for other in others:
        total = total + other[...].astype(F32)
    dst[...] = total.astype(dst.dtype)


class Scatter4:
    def __init__(self, send, src, relay, from_left, from_right, sems, me, left, right, far, to):
        self.send, self.src, self.relay = send, src, relay
        self.from_left, self.from_right, self.sems = from_left, from_right, sems
        self.me, self.left, self.right, self.far, self.to = me, left, right, far, to

    def start(self, *halves):
        for h in halves or (0, 1):
            to = (self.left, self.right)[h]
            self.send(self.src(self.far, h), self.relay(h), self.sems.at[h], **self.to(to))

    def direct(self):
        self.send(
            self.src(self.left, 1), self.from_right(1), self.sems.at[2], **self.to(self.left)
        )
        self.send(
            self.src(self.right, 0), self.from_left(0), self.sems.at[3], **self.to(self.right)
        )

    def pass_on(self):
        arrived(self.relay(0), self.sems.at[0])
        add_into(self.src(self.left, 0), self.relay(0))
        self.send(
            self.src(self.left, 0), self.from_right(0), self.sems.at[4], **self.to(self.left)
        )
        arrived(self.relay(1), self.sems.at[1])
        add_into(self.src(self.right, 1), self.relay(1))
        self.send(
            self.src(self.right, 1), self.from_left(1), self.sems.at[5], **self.to(self.right)
        )
        self.passed = self.send.copies[-2:]

    def sent(self):
        for copy in self.passed:
            copy.wait_send()
        waited = [id(copy) for copy in self.passed]
        self.send.copies = [copy for copy in self.send.copies if id(copy) not in waited]

    def finish(self):
        arrived(self.from_right(1), self.sems.at[2])
        arrived(self.from_left(0), self.sems.at[3])
        arrived(self.from_right(0), self.sems.at[4])
        arrived(self.from_left(1), self.sems.at[5])


class Gather4:
    def __init__(self, send, slot, half, sems, me, left, right, far, to):
        self.send, self.slot, self.half, self.sems = send, slot, half, sems
        self.me, self.left, self.right, self.far, self.to = me, left, right, far, to

    def start(self, own=None):
        own = self.slot(self.me) if own is None else own
        self.send(own, self.slot(self.me), self.sems.at[0], **self.to(self.right))
        self.send(own, self.slot(self.me), self.sems.at[1], **self.to(self.left))

    def pass_left(self):
        arrived(self.slot(self.left), self.sems.at[0])
        part = self.half(self.left, 0)
        self.send(part, part, self.sems.at[2], **self.to(self.right))

    def pass_right(self):
        arrived(self.slot(self.right), self.sems.at[1])
        part = self.half(self.right, 1)
        self.send(part, part, self.sems.at[3], **self.to(self.left))

    def finish(self):
        arrived(self.half(self.far, 0), self.sems.at[2])
        arrived(self.half(self.far, 1), self.sems.at[3])


NT = (((1,), (1,)), ((), ()))
TN = (((0,), (0,)), ((), ()))
BLOCK = 256


def by_owner(columns, c):
    runs = columns.shape[1] // 384
    return jnp.concatenate(
        [columns[:, n * 384 + c * 192 : n * 384 + c * 192 + 192] for n in range(runs)], axis=1
    )


def block_kernel(
    lengths,
    activated,
    mod_weight,
    control,
    zero_weight,
    image_hidden,
    weight,
    text,
    text_cot,
    image_cot,
    attn_out,
    control_grad,
    zero_out,
    ctl,
    ctl_in,
    zw,
    zw_owner,
    base,
    wall,
    offset,
    stretch,
    partial,
    rg_relay,
    rg_left,
    rg_right,
    hidden,
    normed,
    qkv_out,
    joint,
    cots,
    tstage,
    cstage,
    attn,
    ostage,
    grads,
    both_grads,
    key_acc,
    value_acc,
    pair_sum,
    ry_relay,
    ry_left,
    ry_right,
    cross_out,
    cross_in,
    rows_all,
    rows_in,
    zacc,
    zsum,
    zx_relay,
    zx_left,
    zx_right,
    zy_relay,
    zy_left,
    zy_right,
    za_out,
    zb_out,
    za_in,
    zb_in,
    zown,
    zall,
    text_mine,
    cots_mine,
    load_sem,
    send_sem,
    w_sem,
    share_sem,
    rg_sem,
    ag_sem,
    text_send,
    text_recv,
    stage_recv,
    cross_recv,
    qkv_sem,
    grads_sem,
    ry_sem,
    cross_sem,
    gg_sem,
    rows_sem,
    attn_send,
    attn_recv,
    zx_sem,
    zy_sem,
    za_sem,
    zb_sem,
    zg_sem,
):
    p = Place()
    send = Sends(send_sem)
    q = p.y * 2 + p.c
    partner = {"seq": p.seq(p.z, p.y, p.co)}
    across = {"seq": p.seq(p.zo, p.y, p.c)}
    to_y = lambda y: {"seq": p.seq(p.z, y, p.c)}
    to_g = lambda g: {"grp": g}
    to_d = lambda d: {"dp": d}

    all_here = greet(
        [{"seq": (p.s + k) % 16} for k in range(1, 16)]
        + [{"grp": p.gl}, {"grp": p.gr}]
        + [{"dp": (p.d + k) % 4} for k in range(1, 4)]
        + [{"dp": (p.d + k) % 4, "seq": p.seq(p.zo, p.y, p.c)} for k in range(1, 4)]
    )

    loads = []

    def load(src, dst):
        copy = pltpu.make_async_copy(src, dst, load_sem.at[len(loads)])
        copy.start()
        loads.append(copy)
        return copy

    load_control = load(control, ctl)
    load_zero = [
        load(zero_weight.at[:, pl.ds(n * 512, 512)], zw.at[:, pl.ds(n * 512, 512)])
        for n in range(6)
    ]
    load_weight = [
        load(weight.at[n], wall.at[p.d, :, pl.ds(n * HD, HD)]) for n in range(3)
    ]
    load_text = [
        load(text, text_mine),
        load(text_cot, cots_mine.at[0]),
        load(image_cot, cots_mine.at[1]),
    ]
    load_base = load(image_hidden, base)
    load_mod = [
        load(
            mod_weight.at[pl.ds(n % 8 * ROWS, ROWS), pl.ds(n // 8 * D, D)],
            pair_sum.at[n // 8, n // 4 % 2, n % 4],
        )
        for n in range(16)
    ]

    load_control.wait()

    def residual_part(h):
        for block in range(3 * h, 3 * h + 3):
            cols = pl.ds(block * 512, 512)
            load_zero[block].wait()
            product = jnp.dot(
                ctl[...].reshape(256, 768), zw[:, cols], preferred_element_type=F32
            )
            partial[:, :, :, cols] = product.astype(BF).reshape(4, 2, ROWS, 512)

    to_group = [
        Scatter4(
            send,
            lambda g, h, i=i: partial.at[g, i, :, pl.ds(h * HALF, HALF)],
            lambda h, i=i: rg_relay.at[i, h],
            lambda h, i=i: rg_left.at[i, h],
            lambda h, i=i: rg_right.at[i, h],
            rg_sem.at[i],
            p.g,
            p.gl,
            p.gr,
            p.go,
            to_g,
        )
        for i in range(2)
    ]
    residual_part(0)
    residual_part(1)
    all_here()
    to_group[0].start()
    to_group[0].direct()

    plane = pl.ds(p.z * 4, 4)
    other_plane = pl.ds(p.zo * 4, 4)
    zy = p.z * 4 + p.y

    def text_pairs(to):
        near = pl.ds(pl.multiple_of((p.z * 8 + to) * HD, HD), HD)
        far = pl.ds(pl.multiple_of((p.zo * 8 + to) * HD, HD), HD)
        return (
            (text_mine.at[:, :, :, far], tstage.at[:, :, p.y, p.c], stage_recv.at[0]),
            (cots_mine.at[:, :, :, far], cstage.at[:, :, p.y, p.c], stage_recv.at[1]),
            (text_mine.at[:, :, :, near], joint.at[:, :, 0, zy, p.c], text_recv.at[0]),
            (cots_mine.at[:, :, :, near], cots.at[:, :, zy, p.c], text_recv.at[1]),
        )

    def text_copies(k):
        to = (q + k) % 8
        return [
            pltpu.make_async_remote_copy(
                src_ref=src,
                dst_ref=dst,
                send_sem=text_send.at[n, k],
                recv_sem=recv,
                device_id={"seq": p.z * 8 + to},
                device_id_type=MESH,
            )
            for n, (src, dst, recv) in enumerate(text_pairs(to))
        ]

    for copy in load_text:
        copy.wait()

    @pl.loop(1, 8)
    def _(k):
        for copy in text_copies(k):
            copy.start()

    for src, dst, recv in text_pairs(q):
        pltpu.make_async_copy(src, dst, recv).start()

    def text_second_hop(i):
        send(tstage.at[:, i], joint.at[:, i, 0, plane], cross_recv.at[i, 0], **across)
        send(cstage.at[:, i], cots.at[:, i, plane], cross_recv.at[i, 1], **across)

    def text_wait(i):
        arrived(joint.at[:, i, 0, other_plane], cross_recv.at[i, 0])
        arrived(cots.at[:, i, other_plane], cross_recv.at[i, 1])

    for copy in load_weight:
        copy.wait()
    mine_cols, pair_cols = pl.ds(0, 384), pl.ds(384, 384)
    weights = Gather4(
        send,
        lambda d: wall.at[d, :, mine_cols],
        lambda d, h: wall.at[d, pl.ds(h * 384, 384), mine_cols],
        w_sem,
        p.d,
        p.dl,
        p.dr,
        p.do,
        to_d,
    )
    weights.start()

    def share_weight(d, sem):
        send(wall.at[d, :, mine_cols], wall.at[d, :, pair_cols], share_sem.at[sem], **partner)

    share_weight(p.d, 0)
    send(ctl, ctl_in, share_sem.at[4], **partner)

    for copy in load_mod:
        copy.wait()
    offset[...] = jnp.dot(
        activated[...], pair_sum[0].reshape(FREQ, D), preferred_element_type=F32
    )
    stretch[...] = 1.0 + jnp.dot(
        activated[...], pair_sum[1].reshape(FREQ, D), preferred_element_type=F32
    )
    load_base.wait()

    for block in range(4):
        columns = zw[:, pl.ds(block * 768, 768)].astype(F32)
        for c in range(2):
            zw_owner[c, :, pl.ds(block * 384, 384)] = by_owner(columns, c).astype(BF)

    to_group[0].pass_on()
    weights.pass_left()
    weights.pass_right()
    share_weight(p.dl, 1)
    share_weight(p.dr, 2)
    to_group[0].sent()
    to_group[1].start()
    to_group[1].direct()

    gathers = [
        [
            Gather4(
                send,
                lambda y, i=i, z=z: normed.at[i, z, y],
                lambda y, h, i=i, z=z: normed.at[i, z, y, pl.ds(h * 16, 16)],
                ag_sem.at[i, pl.ds(which * 4, 4)],
                p.y,
                p.yl,
                p.yr,
                p.yo,
                to_y,
            )
            for which, z in enumerate((p.z, p.zo))
        ]
        for i in range(2)
    ]

    def standardise(rows):
        values = rows.astype(F32)
        average = jnp.mean(values, axis=-1, keepdims=True)
        centred = values - average
        reciprocal = lax.rsqrt(jnp.mean(centred * centred, axis=-1, keepdims=True) + 1e-06)
        return centred * reciprocal, reciprocal

    def gather_first(i):
        for h in range(2):
            cols = pl.ds(h * HALF, HALF)
            residual = (
                partial[p.g, i, :, cols].astype(F32)
                + rg_left[i, h].astype(F32)
                + rg_right[i, h].astype(F32)
            )
            hidden[i, :, cols] = (base[i, :, cols].astype(F32) + residual).astype(BF)
        standard, _ = standardise(hidden[i])
        normed[i, p.z, p.y] = (standard * stretch[i : i + 1] + offset[i : i + 1]).astype(BF)
        mine = normed.at[i, p.z, p.y]
        send(mine, mine, ag_sem.at[i, 8], **across)
        gathers[i][0].start()

    def gather_second(i):
        arrived(normed.at[i, p.zo, p.y], ag_sem.at[i, 8])
        gathers[i][1].start()

    def gather_third(i, which):
        gathers[i][which].pass_left()
        gathers[i][which].pass_right()

    def gather_fourth(i, which):
        gathers[i][which].finish()

    scaling = HD ** (-0.5)
    position = lax.broadcasted_iota(jnp.int32, (1, TXT + IMG), 1)

    def project(i):
        product = jnp.dot(
            normed[i].reshape(256, D), wall[...].reshape(D, 768), preferred_element_type=F32
        ).astype(BF)
        for n in range(3):
            qkv_out[i, n] = product[:, 384 + n * HD : 384 + (n + 1) * HD].reshape(8, ROWS, HD)
        send(qkv_out.at[i], joint.at[:, i, 1, :, p.c], qkv_sem.at[i], **partner)
        for n in range(3):
            joint[n, i, 1, :, p.c] = product[:, n * HD : (n + 1) * HD].reshape(8, ROWS, HD)

    def project_wait(i):
        arrived(joint.at[:, i, 1, :, p.co], qkv_sem.at[i])

    def attend(i, block):
        slots = pl.ds(block % 2 * 4, 4)
        bias = jnp.where((position >= TXT) | (position < lengths[i]), 0.0, -jnp.inf)
        query = joint[0, i, block // 2, slots].reshape(BLOCK, HD)
        cot = cots[block // 2, i, slots].reshape(BLOCK, HD)
        keys = joint[1, i].reshape(TXT + IMG, HD)
        values = joint[2, i].reshape(TXT + IMG, HD)
        scores = lax.dot_general(query, keys, NT, preferred_element_type=F32) + bias
        row_max = jnp.max(scores, axis=1, keepdims=True)
        terms = jnp.exp2((scores - row_max) * (scaling * math.log2(math.e)))
        prob = terms * (1.0 / jnp.sum(terms, axis=1, keepdims=True))
        low = prob.astype(BF)
        attended = jnp.dot(low, values, preferred_element_type=F32).astype(BF)
        attn[block // 2, i, pl.ds(block % 2 * BLOCK, BLOCK)] = attended
        dots = jnp.sum(cot.astype(F32) * attended.astype(F32), axis=1, keepdims=True)
        prob_grad = lax.dot_general(cot, values, NT, preferred_element_type=F32)
        score_grad = (prob * (prob_grad - dots)).astype(BF)
        if block >= 2:
            query_grad = jnp.dot(score_grad, keys, preferred_element_type=F32) * scaling
            grads[i, slots, :, :, :HD] = query_grad.astype(BF).reshape(4, 2, ROWS, HD)
        key_part = lax.dot_general(score_grad[:, TXT:], query, TN, preferred_element_type=F32)
        value_part = lax.dot_general(low[:, TXT:], cot, TN, preferred_element_type=F32)
        if block == 0:
            key_acc[...] = key_part
            value_acc[...] = value_part
        elif block < 3:
            key_acc[...] += key_part
            value_acc[...] += value_part
        else:
            key_grad = ((key_acc[...] + key_part) * scaling).astype(BF)
            value_grad = (value_acc[...] + value_part).astype(BF)
            grads[i, :, :, :, HD : 2 * HD] = key_grad.reshape(8, 2, ROWS, HD)
            grads[i, :, :, :, 2 * HD :] = value_grad.reshape(8, 2, ROWS, HD)
            send(
                grads.at[i, :, p.co], both_grads.at[i, :, :, pair_cols], grads_sem.at[i],
                **partner
            )
            both_grads[i, :, :, :384] = grads[i, :, p.c]

    def back_project(i):
        arrived(both_grads.at[i, :, :, pair_cols], grads_sem.at[i])
        for block in range(4):
            cols = pl.ds(block * 768, 768)
            product = lax.dot_general(
                both_grads[i].reshape(256, 768), wall[block], NT, preferred_element_type=F32
            ).astype(BF)
            pair_sum[i, :, :, :, cols] = product.reshape(2, 4, ROWS, 768)
            if block % 2:
                round_y[i, 0].start(block // 2)
        round_y[i, 0].direct()

    half = lambda h: pl.ds(h * HALF, HALF)
    part = lambda r: pl.ds(r * 16, 16)
    chunks = [(i, r) for i in range(2) for r in range(2)]
    round_y = {
        (i, r): Scatter4(
            send,
            lambda y, h, i=i, r=r: pair_sum.at[i, :, y, part(r), half(h)],
            lambda h, i=i, r=r: ry_relay.at[i, h, :, part(r)],
            lambda h, i=i, r=r: ry_left.at[i, h, :, part(r)],
            lambda h, i=i, r=r: ry_right.at[i, h, :, part(r)],
            ry_sem.at[i * 2 + r],
            p.y,
            p.yl,
            p.yr,
            p.yo,
            to_y,
        )
        for i, r in chunks
    }
    rows_gather = {
        (i, r): Gather4(
            send,
            lambda g, i=i, r=r: rows_all.at[:, g, i, part(r)],
            lambda g, h, i=i, r=r: rows_all.at[h, g, i, part(r)],
            gg_sem.at[i * 2 + r],
            p.g,
            p.gl,
            p.gr,
            p.go,
            to_g,
        )
        for i, r in chunks
    }

    def back_next(i):
        round_y[i, 0].pass_on()
        round_y[i, 1].start()

    def y_sum(i, r, z, h):
        return (
            pair_sum[i, z, p.y, part(r), half(h)].astype(F32)
            + ry_left[i, h, z, part(r)].astype(F32)
            + ry_right[i, h, z, part(r)].astype(F32)
        )

    def back_second(i, r):
        round_y[i, r].finish()
        for h in range(2):
            cross_out[i, part(r), half(h)] = y_sum(i, r, p.zo, h).astype(BF)
        send(
            cross_out.at[i, part(r)], cross_in.at[i, part(r)], cross_sem.at[i * 2 + r], **across
        )

    def back_third(i, r):
        mine = jnp.concatenate([y_sum(i, r, p.z, h) for h in range(2)], axis=1)
        standard, reciprocal = standardise(hidden[i, part(r)])
        arrived(cross_in.at[i, part(r)], cross_sem.at[i * 2 + r])
        scaled = (mine + cross_in[i, part(r)].astype(F32)) * stretch[i : i + 1]
        residual_grad = reciprocal * (
            scaled
            - jnp.mean(scaled, axis=-1, keepdims=True)
            - standard * jnp.mean(scaled * standard, axis=-1, keepdims=True)
        )
        for c in range(2):
            rows_all[c, p.g, i, part(r)] = by_owner(residual_grad, c).astype(BF)
        rows_gather[i, r].start()

    def rows_pass(i, r):
        rows_gather[i, r].pass_left()
        rows_gather[i, r].pass_right()

    def rows_finish(i, r):
        rows_gather[i, r].finish()
        send(
            rows_all.at[p.co, :, i, part(r)],
            rows_in.at[:, i, part(r)],
            rows_sem.at[i * 2 + r],
            **partner
        )

    def attn_pairs(to):
        near = pl.ds(pl.multiple_of((p.z * 8 + to) * ROWS, ROWS), ROWS)
        far = pl.ds(pl.multiple_of((p.zo * 8 + to) * ROWS, ROWS), ROWS)
        cols = pl.ds(pl.multiple_of(p.s * HD, HD), HD)
        staged = pl.ds(pl.multiple_of(q * HD, HD), HD)
        return (
            (attn.at[:, :, near], attn_out.at[:, :, :, cols], attn_recv.at[0]),
            (attn.at[:, :, far], ostage.at[:, :, :, staged], attn_recv.at[1]),
        )

    def attn_copies(k):
        to = (q + k) % 8
        return [
            pltpu.make_async_remote_copy(
                src_ref=src,
                dst_ref=dst,
                send_sem=attn_send.at[n, k],
                recv_sem=recv,
                device_id={"seq": p.z * 8 + to},
                device_id_type=MESH,
            )
            for n, (src, dst, recv) in enumerate(attn_pairs(to))
        ]

    def attn_first_hop():
        @pl.loop(1, 8)
        def _(k):
            for copy in attn_copies(k):
                copy.start()

        for src, dst, recv in attn_pairs(q):
            pltpu.make_async_copy(src, dst, recv).start()

    half_cols = pl.ds(pl.multiple_of(p.z * 1024, 1024), 1024)
    other_cols = pl.ds(pl.multiple_of(p.zo * 1024, 1024), 1024)

    def attn_second_hop():
        arrived(ostage, attn_recv.at[1])
        send(ostage, attn_out.at[:, :, :, half_cols], attn_recv.at[2], **across)

    def control_part(i):
        total = 0.0
        for c in range(2):
            total = total + lax.dot_general(
                rows_all[c, :, i].reshape(128, HALF),
                zw_owner[c],
                NT,
                preferred_element_type=F32,
            )
        control_grad[:, i] = total.astype(BF).reshape(4, ROWS, 768)

    def zero_part(i, block):
        cols = pl.ds(block * 384, 384)
        left = jnp.concatenate(
            [ref.reshape(128, 384) for ref in (rows_all[p.c, :, i, :, cols], rows_in[:, i, :, cols])]
        )
        right = jnp.concatenate([ctl[:, i].reshape(128, 768), ctl_in[:, i].reshape(128, 768)])
        product = lax.dot_general(left, right, TN, preferred_element_type=F32)
        if i == 0:
            zacc[cols] = product
        else:
            z, y = block // 2, block % 2 * 2
            zsum[z, pl.ds(y, 2)] = (zacc[cols] + product).astype(BF).reshape(2, 192, 768)

    to_group[0].finish()
    gather_first(0)
    to_group[1].pass_on()
    gather_third(0, 0)
    gather_second(0)
    gather_fourth(0, 0)
    gather_third(0, 1)
    arrived(tstage, stage_recv.at[0])
    arrived(cstage, stage_recv.at[1])
    text_second_hop(0)
    to_group[1].finish()
    gather_first(1)
    weights.finish()
    share_weight(p.do, 3)
    gather_fourth(0, 1)
    for n, d in enumerate((p.d, p.dl, p.dr, p.do)):
        arrived(wall.at[d, :, pair_cols], share_sem.at[n])
    project(0)
    gather_third(1, 0)
    gather_second(1)
    text_second_hop(1)
    arrived(joint.at[:, :, 0, plane], text_recv.at[0])
    arrived(cots.at[:, :, plane], text_recv.at[1])
    text_wait(0)
    project_wait(0)
    attend(0, 0)
    gather_fourth(1, 0)
    attend(0, 1)
    gather_third(1, 1)
    attend(0, 2)
    attend(0, 3)
    gather_fourth(1, 1)
    project(1)
    back_project(0)
    text_wait(1)
    project_wait(1)
    attend(1, 0)
    attend(1, 1)
    back_next(0)
    attend(1, 2)
    back_second(0, 0)
    round_y[0, 1].direct()
    attend(1, 3)
    round_y[0, 1].pass_on()
    back_third(0, 0)
    back_project(1)
    back_second(0, 1)
    rows_pass(0, 0)
    back_third(0, 1)
    back_next(1)
    rows_pass(0, 1)
    back_second(1, 0)
    round_y[1, 1].direct()
    round_y[1, 1].pass_on()
    back_third(1, 0)
    rows_finish(0, 0)
    back_second(1, 1)
    attn_first_hop()
    back_third(1, 1)
    rows_pass(1, 0)
    rows_finish(0, 1)
    arrived(ctl_in, share_sem.at[4])
    control_part(0)
    rows_pass(1, 1)
    for r in range(2):
        arrived(rows_in.at[:, 0, part(r)], rows_sem.at[r])
    for block in range(4):
        zero_part(0, block)
    rows_finish(1, 0)
    rows_finish(1, 1)
    for r in range(2):
        arrived(rows_in.at[:, 1, part(r)], rows_sem.at[2 + r])

    cols_a, cols_b = pl.ds(0, 384), pl.ds(384, 384)
    quarter = lambda d: pl.ds(pl.multiple_of(d * 48, 16), 48)
    round_x = Scatter4(
        send,
        lambda d, h: zsum.at[h, :, quarter(d), cols_a],
        lambda h: zx_relay.at[h],
        lambda h: zx_left.at[h],
        lambda h: zx_right.at[h],
        zx_sem,
        p.d,
        p.dl,
        p.dr,
        p.do,
        to_d,
    )
    zero_y = Scatter4(
        send,
        lambda y, h: zsum.at[h, y, :, cols_b],
        lambda h: zy_relay.at[h],
        lambda h: zy_left.at[h],
        lambda h: zy_right.at[h],
        zy_sem,
        p.y,
        p.yl,
        p.yr,
        p.yo,
        to_y,
    )
    for z in range(2):
        zero_part(1, 2 * z)
        zero_part(1, 2 * z + 1)
        round_x.start(z)
        zero_y.start(z)
    round_x.direct()
    zero_y.direct()
    attn_second_hop()
    control_part(1)
    round_x.pass_on()
    zero_y.pass_on()
    round_x.finish()
    for z in range(2):
        za_out[z] = (
            zsum[z, :, quarter(p.d), cols_a].astype(F32)
            + zx_left[z].astype(F32)
            + zx_right[z].astype(F32)
        ).astype(BF)
    others_a = [(dz, dy) for dz in range(2) for dy in range(4) if dz or dy]
    for n, (dz, dy) in enumerate(others_a):
        z, y = (p.z + dz) % 2, (p.y + dy) % 4
        send(za_out.at[z, y], za_in.at[n], za_sem.at[n], seq=p.seq(z, y, p.c))
    zero_y.finish()
    for z in range(2):
        zb_out[z] = (
            (
                zsum[z, p.y, :, cols_b].astype(F32)
                + zy_left[z].astype(F32)
                + zy_right[z].astype(F32)
            )
            .astype(BF)
            .reshape(4, 48, 384)
        )
    for n, (dz, dd) in enumerate(others_a):
        z, d = (p.z + dz) % 2, (p.d + dd) % 4
        send(zb_out.at[z, d], zb_in.at[n], zb_sem.at[n], seq=p.seq(z, p.y, p.c), dp=d)
    total = za_out[p.z, p.y].astype(F32)
    for n in range(7):
        arrived(za_in.at[n], za_sem.at[n])
        total = total + za_in[n].astype(F32)
    zown[:, cols_a] = total.astype(BF)
    total = zb_out[p.z, p.d].astype(F32)
    for n in range(7):
        arrived(zb_in.at[n], zb_sem.at[n])
        total = total + zb_in[n].astype(F32)
    zown[:, cols_b] = total.astype(BF)
    for k in range(1, 4):
        send(zown, zall.at[p.d], zg_sem.at[k - 1], dp=(p.d + k) % 4)
    zall[p.d] = zown[...]
    for k in range(1, 4):
        arrived(zall.at[(p.d + 4 - k) % 4], zg_sem.at[k - 1])
    zero_out[...] = zall[...].reshape(192, 768).astype(F32) * (16384 ** (-0.5))

    arrived(attn_out.at[:, :, :, half_cols], attn_recv.at[0])
    arrived(attn_out.at[:, :, :, other_cols], attn_recv.at[2])
    send.drain()

    @pl.loop(1, 8)
    def _(k):
        for copy in text_copies(k):
            copy.wait_send()
        for copy in attn_copies(k):
            copy.wait_send()


def whole_block(*operands):
    dma = pltpu.SemaphoreType.DMA
    bf = lambda *shape: pltpu.VMEM(shape, BF)
    return pl.pallas_call(
        block_kernel,
        out_shape=(
            jax.ShapeDtypeStruct((2, 2, ROWS, HEADS * HD), BF),
            jax.ShapeDtypeStruct((4, 2, ROWS, 768), BF),
            jax.ShapeDtypeStruct((192, 768), F32),
        ),
        in_specs=[pl.BlockSpec(memory_space=pltpu.SMEM), VMEM] + [ANY] * 8,
        out_specs=(VMEM, VMEM, VMEM),
        scratch_shapes=[
            bf(4, 2, ROWS, 768),
            bf(4, 2, ROWS, 768),
            bf(768, D),
            bf(2, 768, HALF),
            bf(2, ROWS, D),
            bf(4, 768, 768),
            pltpu.VMEM((2, D), F32),
            pltpu.VMEM((2, D), F32),
            bf(4, 2, ROWS, D),
            bf(2, 2, ROWS, HALF),
            bf(2, 2, ROWS, HALF),
            bf(2, 2, ROWS, HALF),
            bf(2, ROWS, D),
            bf(2, 2, 4, ROWS, D),
            bf(2, 3, 8, ROWS, HD),
            bf(3, 2, 2, 8, 2, ROWS, HD),
            bf(2, 2, 8, 2, ROWS, HD),
            bf(3, 2, 4, 2, ROWS, HD),
            bf(2, 2, 4, 2, ROWS, HD),
            bf(2, 2, 512, HD),
            bf(2, 2, ROWS, 1024),
            bf(2, 8, 2, ROWS, 384),
            bf(2, 8, ROWS, 768),
            pltpu.VMEM((IMG, HD), F32),
            pltpu.VMEM((IMG, HD), F32),
            bf(2, 2, 4, ROWS, D),
            bf(2, 2, 2, ROWS, HALF),
            bf(2, 2, 2, ROWS, HALF),
            bf(2, 2, 2, ROWS, HALF),
            bf(2, ROWS, D),
            bf(2, ROWS, D),
            bf(2, 4, 2, ROWS, HALF),
            bf(4, 2, ROWS, HALF),
            pltpu.VMEM((HALF, 768), F32),
            bf(2, 4, 192, 768),
            bf(2, 4, 48, 384),
            bf(2, 4, 48, 384),
            bf(2, 4, 48, 384),
            bf(2, 192, 384),
            bf(2, 192, 384),
            bf(2, 192, 384),
            bf(2, 4, 48, 384),
            bf(2, 4, 48, 384),
            bf(7, 48, 384),
            bf(7, 48, 384),
            bf(48, 768),
            bf(4, 48, 768),
            bf(3, 2, ROWS, HEADS * HD),
            bf(2, 2, ROWS, HEADS * HD),
            dma((32,)),
            dma((176,)),
            dma((4,)),
            dma((5,)),
            dma((2, 6)),
            dma((2, 9)),
            dma((4, 8)),
            dma((2,)),
            dma((2,)),
            dma((2, 2)),
            dma((2,)),
            dma((2,)),
            dma((4, 6)),
            dma((4,)),
            dma((4, 4)),
            dma((4,)),
            dma((2, 8)),
            dma((3,)),
            dma((6,)),
            dma((6,)),
            dma((7,)),
            dma((7,)),
            dma((3,)),
        ],
        compiler_params=pltpu.CompilerParams(
            collective_id=1, has_side_effects=True, vmem_limit_bytes=VMEM_LIMIT
        ),
        name="whole_block",
    )(*operands)


def hand_over_kernel(attn, control, zero, image_out, text_out, control_out, zero_out, sems):
    copies = [
        pltpu.make_async_copy(src, dst, sems.at[n])
        for n, (src, dst) in enumerate(
            (
                (attn.at[1], image_out),
                (attn.at[0], text_out),
                (control, control_out),
                (zero, zero_out),
            )
        )
    ]
    for copy in copies:
        copy.start()
    for copy in copies:
        copy.wait()


def hand_over(attn, control, zero):
    return pl.pallas_call(
        hand_over_kernel,
        out_shape=(
            jax.ShapeDtypeStruct(attn.shape[1:], BF),
            jax.ShapeDtypeStruct(attn.shape[1:], BF),
            jax.ShapeDtypeStruct(control.shape, BF),
            jax.ShapeDtypeStruct(zero.shape, F32),
        ),
        in_specs=[VMEM] * 3,
        out_specs=(ANY,) * 4,
        scratch_shapes=[pltpu.SemaphoreType.DMA((4,))],
        name="hand_over",
    )(attn, control, zero)


def timestep_activation(timesteps):
    half_freq = FREQ // 2
    frequency = jnp.exp(-math.log(10000.0) * jnp.arange(half_freq, dtype=F32) / half_freq)
    angles = timesteps.astype(F32)[..., None] * frequency
    embedding = jnp.concatenate([jnp.cos(angles), jnp.sin(angles)], axis=-1)
    return jax.nn.silu(embedding).astype(BF)


def body(
    image_hidden,
    control_hidden,
    text_qkv,
    text_lengths,
    timesteps,
    mod_weight,
    qkv_weight,
    zero_weight,
    image_cotangent,
    text_cotangent,
):
    activated = timestep_activation(timesteps.reshape(2))
    attn_out, control_grad, zero_t = whole_block(
        text_lengths.reshape(2),
        activated,
        mod_weight,
        control_hidden.reshape(4, 2, ROWS, 768),
        zero_weight,
        image_hidden.reshape(2, ROWS, D),
        jnp.transpose(qkv_weight, (1, 0, 2)),
        text_qkv.reshape(3, 2, ROWS, HEADS * HD),
        text_cotangent.reshape(2, ROWS, HEADS * HD),
        image_cotangent.reshape(2, ROWS, HEADS * HD),
    )
    image_attn, text_attn, control_grad, zero_t = hand_over(attn_out, control_grad, zero_t)
    return (
        image_attn.reshape(2, 1, ROWS, HEADS * HD),
        text_attn.reshape(2, 1, ROWS, HEADS * HD),
        control_grad.reshape(8, 1, ROWS, 768),
        jnp.transpose(zero_t),
    )


def solution(mesh):
    placed = (
        P("grp", "dp", "seq", None),
        P(None, "dp", "seq", "grp"),
        P(None, "grp", "dp", "seq", None),
        P("grp", "dp"),
        P("grp", "dp"),
        P(),
        P("dp", None, "seq"),
        P("grp", None),
        P("grp", "dp", "seq", None),
        P("grp", "dp", "seq", None),
    )
    return jax.shard_map(
        body,
        mesh=mesh,
        in_specs=placed,
        out_specs=(
            P("grp", "dp", "seq", None),
            P("grp", "dp", "seq", None),
            P(None, "dp", "seq", "grp"),
            P("grp", "seq"),
        ),
        check_vma=False,
    )
```

```python
import math

import jax
import jax.numpy as jnp
from jax import lax
from jax.experimental import pallas as pl
from jax.experimental.pallas import tpu as pltpu
from jax.sharding import PartitionSpec as P

D = 3072
HEADS = 16
HD = 128
IMG = 512
TXT = 512
FREQ = 256
ROWS = 32
HALF = D // 2
MESH = pl.DeviceIdType.MESH
BF = jnp.bfloat16
F32 = jnp.float32
VMEM_LIMIT = 60 * 1024 * 1024
ANY = pl.BlockSpec(memory_space=pl.ANY)
VMEM = pl.BlockSpec(memory_space=pltpu.VMEM)


class Sends:
    def __init__(self, sems):
        self.sems = sems
        self.copies = []
        self.started = 0

    def __call__(self, src, dst, recv, **to):
        copy = pltpu.make_async_remote_copy(
            src_ref=src,
            dst_ref=dst,
            send_sem=self.sems.at[self.started],
            recv_sem=recv,
            device_id=to,
            device_id_type=MESH,
        )
        copy.start()
        self.started += 1
        self.copies.append(copy)
        return copy

    def sent(self, copies):
        for copy in copies:
            copy.wait_send()
        waited = [id(copy) for copy in copies]
        self.copies = [copy for copy in self.copies if id(copy) not in waited]

    def drain(self):
        self.sent(list(self.copies))


def arrived(dst, recv):
    pltpu.make_async_copy(dst, dst, recv).wait()


def greet(groups):
    barrier = pltpu.get_barrier_semaphore()
    for to in groups:
        pl.semaphore_signal(barrier, inc=1, device_id=to, device_id_type=MESH)
    return lambda: pl.semaphore_wait(barrier, len(groups))


class Place:
    def __init__(self):
        self.s = lax.axis_index("seq")
        self.g = lax.axis_index("grp")
        self.d = lax.axis_index("dp")
        self.z = self.s // 8
        self.y = (self.s // 2) % 4
        self.c = self.s % 2
        self.zo = 1 - self.z
        self.co = 1 - self.c
        self.yl = (self.y + 3) % 4
        self.yr = (self.y + 1) % 4
        self.yo = (self.y + 2) % 4
        self.gl = (self.g + 3) % 4
        self.gr = (self.g + 1) % 4
        self.go = (self.g + 2) % 4
        self.dl = (self.d + 3) % 4
        self.dr = (self.d + 1) % 4
        self.do = (self.d + 2) % 4

    def seq(self, z, y, c):
        return z * 8 + y * 2 + c


def add_into(dst, *others):
    total = dst[...].astype(F32)
    for other in others:
        total = total + other[...].astype(F32)
    dst[...] = total.astype(dst.dtype)


class Scatter4:
    def __init__(self, send, src, relay, from_left, from_right, sems, me, left, right, far, to):
        self.send, self.src, self.relay = send, src, relay
        self.from_left, self.from_right, self.sems = from_left, from_right, sems
        self.me, self.left, self.right, self.far, self.to = me, left, right, far, to
        self.passed = []

    def start(self, h):
        to = (self.left, self.right)[h]
        self.send(self.src(self.far, h), self.relay(h), self.sems.at[h], **self.to(to))

    def direct(self, h):
        if h:
            dst, to = self.from_right(1), self.left
        else:
            dst, to = self.from_left(0), self.right
        self.send(self.src(to, h), dst, self.sems.at[3 - h], **self.to(to))

    def pass_on(self, h):
        arrived(self.relay(h), self.sems.at[h])
        if h:
            dst, to = self.from_left(1), self.right
        else:
            dst, to = self.from_right(0), self.left
        add_into(self.src(to, h), self.relay(h))
        self.passed.append(self.send(self.src(to, h), dst, self.sems.at[4 + h], **self.to(to)))

    def finish(self):
        arrived(self.from_right(1), self.sems.at[2])
        arrived(self.from_left(0), self.sems.at[3])
        arrived(self.from_right(0), self.sems.at[4])
        arrived(self.from_left(1), self.sems.at[5])


class Gather4:
    def __init__(self, send, slot, half, sems, me, left, right, far, to):
        self.send, self.slot, self.half, self.sems = send, slot, half, sems
        self.me, self.left, self.right, self.far, self.to = me, left, right, far, to

    def start(self, own=None):
        own = self.slot(self.me) if own is None else own
        self.begun = [
            self.send(own, self.slot(self.me), self.sems.at[0], **self.to(self.right)),
            self.send(own, self.slot(self.me), self.sems.at[1], **self.to(self.left)),
        ]

    def pass_left(self):
        arrived(self.slot(self.left), self.sems.at[0])
        part = self.half(self.left, 0)
        self.send(part, part, self.sems.at[2], **self.to(self.right))

    def pass_right(self):
        arrived(self.slot(self.right), self.sems.at[1])
        part = self.half(self.right, 1)
        self.send(part, part, self.sems.at[3], **self.to(self.left))

    def finish(self):
        arrived(self.half(self.far, 0), self.sems.at[2])
        arrived(self.half(self.far, 1), self.sems.at[3])


ORDER = (
    "res0", "res1", "Rs00", "T10", "Ws", "mod", "zwo", "Rp000", "Rp100", "Rs01", "LN00", "GL000",
    "GR000", "Rp001", "Rp101", "WL", "WR_", "Gz00", "Rs10", "LN01", "T20", "T11", "GR001",
    "GL001", "Wf", "Rp010", "Rp110", "Gz01", "Rs11", "LN10", "GL010", "GR010", "GR011", "GL011",
    "GL100", "GR100", "Rp011", "Rp111", "proj0", "Gz10", "LN11", "att00", "att01", "GL101",
    "Gz11", "att02", "att03", "T21", "GL110", "GR101", "GR110", "GR111", "bpa0", "GL111", "bpb0",
    "Bs00", "Bd00", "proj1", "Bp100", "Bp000", "att10", "Bs01", "att11", "att12", "Bd01", "att13",
    "BX00", "Bp101", "Bp001", "bpa1", "bpb1", "Bs10", "Bd10", "BL00", "BX01", "Bp110", "Bp010",
    "Bs11", "Bd11", "AL00", "AR00", "BL01", "Af00", "Bp111", "BX10", "Bp011", "AL01", "AR01",
    "BX11", "O1", "BL10", "Af01", "ctl0", "BL11", "AS10", "zp0", "AS11", "AL10", "AR10", "Af10",
    "AL11", "AR11", "zp1a", "Af11", "ctl1", "zp1b", "Zp0y", "Zp0x", "O2", "Zp1x", "Zp1y", "ZA",
    "ZB", "ZS", "zgL_", "zgR_",
)
NT = (((1,), (1,)), ((), ()))
TN = (((0,), (0,)), ((), ()))
BLOCK = 256


def by_owner(columns, c):
    runs = columns.shape[1] // 384
    return jnp.concatenate(
        [columns[:, n * 384 + c * 192 : n * 384 + c * 192 + 192] for n in range(runs)], axis=1
    )


def block_kernel(
    lengths,
    activated,
    mod_weight,
    control,
    zero_weight,
    image_hidden,
    weight,
    text,
    text_cot,
    image_cot,
    attn_out,
    control_grad,
    zero_out,
    ctl,
    ctl_in,
    zw,
    zw_owner,
    base,
    wall,
    offset,
    stretch,
    partial,
    rg_relay,
    rg_left,
    rg_right,
    hidden,
    normed,
    qkv_out,
    joint,
    cots,
    tstage,
    cstage,
    attn,
    ostage,
    grads,
    both_grads,
    key_acc,
    value_acc,
    pair_sum,
    ry_relay,
    ry_left,
    ry_right,
    cross_out,
    cross_in,
    rows_all,
    rows_in,
    zacc,
    zsum,
    zx_relay,
    zx_left,
    zx_right,
    zy_relay,
    zy_left,
    zy_right,
    za_out,
    zb_out,
    za_in,
    zb_in,
    zall,
    text_mine,
    cots_mine,
    load_sem,
    send_sem,
    w_sem,
    share_sem,
    rg_sem,
    ag_sem,
    text_send,
    text_recv,
    stage_recv,
    cross_recv,
    qkv_sem,
    grads_sem,
    ry_sem,
    cross_sem,
    gg_sem,
    rows_sem,
    attn_send,
    attn_recv,
    zx_sem,
    zy_sem,
    za_sem,
    zb_sem,
    zg_sem,
):
    p = Place()
    send = Sends(send_sem)
    q = p.y * 2 + p.c
    partner = {"seq": p.seq(p.z, p.y, p.co)}
    across = {"seq": p.seq(p.zo, p.y, p.c)}
    to_y = lambda y: {"seq": p.seq(p.z, y, p.c)}
    to_g = lambda g: {"grp": g}
    to_d = lambda d: {"dp": d}

    all_here = greet(
        [{"seq": (p.s + k) % 16} for k in range(1, 16)]
        + [{"grp": p.gl}, {"grp": p.gr}]
        + [{"dp": (p.d + k) % 4} for k in range(1, 4)]
        + [{"dp": (p.d + k) % 4, "seq": p.seq(p.zo, p.y, p.c)} for k in range(1, 4)]
    )

    loads = []

    def load(src, dst):
        copy = pltpu.make_async_copy(src, dst, load_sem.at[len(loads)])
        copy.start()
        loads.append(copy)
        return copy

    load_control = load(control, ctl)
    load_zero = [
        load(zero_weight.at[:, pl.ds(n * 512, 512)], zw.at[:, pl.ds(n * 512, 512)])
        for n in range(6)
    ]
    load_weight = [
        load(weight.at[n], wall.at[p.d, :, pl.ds(n * HD, HD)]) for n in range(3)
    ]
    load_text = [
        load(text, text_mine),
        load(text_cot, cots_mine.at[0]),
        load(image_cot, cots_mine.at[1]),
    ]
    load_base = load(image_hidden, base)
    load_mod = [
        load(
            mod_weight.at[pl.ds(n % 8 * ROWS, ROWS), pl.ds(n // 8 * D, D)],
            pair_sum.at[n // 8, n // 4 % 2, n % 4],
        )
        for n in range(16)
    ]

    half = lambda h: pl.ds(h * HALF, HALF)
    part = lambda r: pl.ds(r * 16, 16)
    chunks = [(i, r) for i in range(2) for r in range(2)]
    steps = {}

    def step(name, *args):
        def add(f):
            steps[name] = lambda: f(*args)
            return f

        return add

    def residual_part(h):
        if h == 0:
            load_control.wait()
        for block in range(3 * h, 3 * h + 3):
            cols = pl.ds(block * 512, 512)
            load_zero[block].wait()
            product = jnp.dot(
                ctl[...].reshape(256, 768), zw[:, cols], preferred_element_type=F32
            )
            partial[:, :, :, cols] = product.astype(BF).reshape(4, 2, ROWS, 512)
        if h == 1:
            all_here()

    step("res0", 0)(residual_part)
    step("res1", 1)(residual_part)

    to_group = {
        (i, r): Scatter4(
            send,
            lambda g, h, i=i, r=r: partial.at[g, i, part(r), half(h)],
            lambda h, i=i, r=r: rg_relay.at[i, h, part(r)],
            lambda h, i=i, r=r: rg_left.at[i, h, part(r)],
            lambda h, i=i, r=r: rg_right.at[i, h, part(r)],
            rg_sem.at[i * 2 + r],
            p.g,
            p.gl,
            p.gr,
            p.go,
            to_g,
        )
        for i, r in chunks
    }

    def group_start(n):
        if n:
            send.sent(to_group[chunks[n - 1]].passed)
        scatter = to_group[chunks[n]]
        for h in range(2):
            scatter.start(h)
        scatter.direct(1)
        scatter.direct(0)

    for n, (i, r) in enumerate(chunks):
        step(f"Rs{i}{r}", n)(group_start)
        for h in range(2):
            step(f"Rp{h}{i}{r}", h)(to_group[i, r].pass_on)

    plane = pl.ds(p.z * 4, 4)
    other_plane = pl.ds(p.zo * 4, 4)
    zy = p.z * 4 + p.y

    def text_pairs(i, to):
        near = pl.ds(pl.multiple_of((p.z * 8 + to) * HD, HD), HD)
        far = pl.ds(pl.multiple_of((p.zo * 8 + to) * HD, HD), HD)
        return (
            (text_mine.at[:, i, :, far], tstage.at[:, i, p.y, p.c], stage_recv.at[0, i]),
            (cots_mine.at[:, i, :, far], cstage.at[:, i, p.y, p.c], stage_recv.at[1, i]),
            (text_mine.at[:, i, :, near], joint.at[:, i, 0, zy, p.c], text_recv.at[0, i]),
            (cots_mine.at[:, i, :, near], cots.at[:, i, zy, p.c], text_recv.at[1, i]),
        )

    def text_copies(i, k):
        to = (q + k) % 8
        return [
            pltpu.make_async_remote_copy(
                src_ref=src,
                dst_ref=dst,
                send_sem=text_send.at[n, i, k],
                recv_sem=recv,
                device_id={"seq": p.z * 8 + to},
                device_id_type=MESH,
            )
            for n, (src, dst, recv) in enumerate(text_pairs(i, to))
        ]

    def text_first_hop(i):
        if i == 0:
            for copy in load_text:
                copy.wait()

        @pl.loop(1, 8)
        def _(k):
            for copy in text_copies(i, k):
                copy.start()

        for src, dst, recv in text_pairs(i, q):
            pltpu.make_async_copy(src, dst, recv).start()

    def text_second_hop(i):
        arrived(tstage.at[:, i], stage_recv.at[0, i])
        arrived(cstage.at[:, i], stage_recv.at[1, i])
        send(tstage.at[:, i], joint.at[:, i, 0, plane], cross_recv.at[i, 0], **across)
        send(cstage.at[:, i], cots.at[:, i, plane], cross_recv.at[i, 1], **across)

    def text_wait(i):
        arrived(joint.at[:, i, 0, plane], text_recv.at[0, i])
        arrived(cots.at[:, i, plane], text_recv.at[1, i])
        arrived(joint.at[:, i, 0, other_plane], cross_recv.at[i, 0])
        arrived(cots.at[:, i, other_plane], cross_recv.at[i, 1])

    for i in range(2):
        step(f"T1{i}", i)(text_first_hop)
        step(f"T2{i}", i)(text_second_hop)

    mine_cols, pair_cols = pl.ds(0, 384), pl.ds(384, 384)
    weights = Gather4(
        send,
        lambda d: wall.at[d, :, mine_cols],
        lambda d, h: wall.at[d, pl.ds(h * 384, 384), mine_cols],
        w_sem,
        p.d,
        p.dl,
        p.dr,
        p.do,
        to_d,
    )

    def share_weight(d, sem):
        send(wall.at[d, :, mine_cols], wall.at[d, :, pair_cols], share_sem.at[sem], **partner)

    @step("Ws")
    def _():
        for copy in load_weight:
            copy.wait()
        weights.start()
        share_weight(p.d, 0)
        send(ctl, ctl_in, share_sem.at[4], **partner)

    @step("WL")
    def _():
        weights.pass_left()
        share_weight(p.dl, 1)

    @step("WR_")
    def _():
        weights.pass_right()
        share_weight(p.dr, 2)

    @step("Wf")
    def _():
        weights.finish()
        share_weight(p.do, 3)

    @step("mod")
    def _():
        for copy in load_mod:
            copy.wait()
        offset[...] = jnp.dot(
            activated[...], pair_sum[0].reshape(FREQ, D), preferred_element_type=F32
        )
        stretch[...] = 1.0 + jnp.dot(
            activated[...], pair_sum[1].reshape(FREQ, D), preferred_element_type=F32
        )
        load_base.wait()

    @step("zwo")
    def _():
        for block in range(4):
            columns = zw[:, pl.ds(block * 768, 768)].astype(F32)
            for c in range(2):
                zw_owner[c, :, pl.ds(block * 384, 384)] = by_owner(columns, c).astype(BF)

    gathers = {
        (i, r, which): Gather4(
            send,
            lambda y, i=i, r=r, z=z: normed.at[i, z, y, part(r)],
            lambda y, h, i=i, r=r, z=z: normed.at[i, z, y, part(r), half(h)],
            ag_sem.at[i * 2 + r, pl.ds(which * 4, 4)],
            p.y,
            p.yl,
            p.yr,
            p.yo,
            to_y,
        )
        for i, r in chunks
        for which, z in enumerate((p.z, p.zo))
    }

    def standardise(rows):
        values = rows.astype(F32)
        average = jnp.mean(values, axis=-1, keepdims=True)
        centred = values - average
        reciprocal = lax.rsqrt(jnp.mean(centred * centred, axis=-1, keepdims=True) + 1e-06)
        return centred * reciprocal, reciprocal

    def gather_first(i, r):
        to_group[i, r].finish()
        rows = part(r)
        for h in range(2):
            residual = (
                partial[p.g, i, rows, half(h)].astype(F32)
                + rg_left[i, h, rows].astype(F32)
                + rg_right[i, h, rows].astype(F32)
            )
            hidden[i, rows, half(h)] = (base[i, rows, half(h)].astype(F32) + residual).astype(BF)
        standard, _ = standardise(hidden[i, rows])
        normed[i, p.z, p.y, rows] = (
            standard * stretch[i : i + 1] + offset[i : i + 1]
        ).astype(BF)
        mine = normed.at[i, p.z, p.y, rows]
        send(mine, mine, ag_sem.at[i * 2 + r, 8], **across)
        gathers[i, r, 0].start()

    def gather_second(i, r):
        arrived(normed.at[i, p.zo, p.y, part(r)], ag_sem.at[i * 2 + r, 8])
        gathers[i, r, 1].start()

    for i, r in chunks:
        step(f"LN{i}{r}", i, r)(gather_first)
        step(f"Gz{i}{r}", i, r)(gather_second)
        for which in range(2):
            step(f"GL{i}{r}{which}")(gathers[i, r, which].pass_left)
            step(f"GR{i}{r}{which}")(gathers[i, r, which].pass_right)

    scaling = HD ** (-0.5)
    position = lax.broadcasted_iota(jnp.int32, (1, TXT + IMG), 1)

    def project(i):
        for r in range(2):
            for which in range(2):
                gathers[i, r, which].finish()
        if i == 0:
            for n, d in enumerate((p.d, p.dl, p.dr, p.do)):
                arrived(wall.at[d, :, pair_cols], share_sem.at[n])
        product = jnp.dot(
            normed[i].reshape(256, D), wall[...].reshape(D, 768), preferred_element_type=F32
        ).astype(BF)
        for n in range(3):
            qkv_out[i, n] = product[:, 384 + n * HD : 384 + (n + 1) * HD].reshape(8, ROWS, HD)
        send(qkv_out.at[i], joint.at[:, i, 1, :, p.c], qkv_sem.at[i], **partner)
        for n in range(3):
            joint[n, i, 1, :, p.c] = product[:, n * HD : (n + 1) * HD].reshape(8, ROWS, HD)

    def attend(i, block):
        if block == 0:
            text_wait(i)
            arrived(joint.at[:, i, 1, :, p.co], qkv_sem.at[i])
        slots = pl.ds(block % 2 * 4, 4)
        bias = jnp.where((position >= TXT) | (position < lengths[i]), 0.0, -jnp.inf)
        query = joint[0, i, block // 2, slots].reshape(BLOCK, HD)
        cot = cots[block // 2, i, slots].reshape(BLOCK, HD)
        keys = joint[1, i].reshape(TXT + IMG, HD)
        values = joint[2, i].reshape(TXT + IMG, HD)
        scores = lax.dot_general(query, keys, NT, preferred_element_type=F32) + bias
        row_max = jnp.max(scores, axis=1, keepdims=True)
        terms = jnp.exp2((scores - row_max) * (scaling * math.log2(math.e)))
        prob = terms * (1.0 / jnp.sum(terms, axis=1, keepdims=True))
        low = prob.astype(BF)
        attended = jnp.dot(low, values, preferred_element_type=F32).astype(BF)
        attn[block // 2, i, pl.ds(block % 2 * BLOCK, BLOCK)] = attended
        dots = jnp.sum(cot.astype(F32) * attended.astype(F32), axis=1, keepdims=True)
        prob_grad = lax.dot_general(cot, values, NT, preferred_element_type=F32)
        score_grad = (prob * (prob_grad - dots)).astype(BF)
        if block >= 2:
            query_grad = jnp.dot(score_grad, keys, preferred_element_type=F32) * scaling
            grads[i, slots, :, :, :HD] = query_grad.astype(BF).reshape(4, 2, ROWS, HD)
        key_part = lax.dot_general(score_grad[:, TXT:], query, TN, preferred_element_type=F32)
        value_part = lax.dot_general(low[:, TXT:], cot, TN, preferred_element_type=F32)
        if block == 0:
            key_acc[...] = key_part
            value_acc[...] = value_part
        elif block < 3:
            key_acc[...] += key_part
            value_acc[...] += value_part
        else:
            key_grad = ((key_acc[...] + key_part) * scaling).astype(BF)
            value_grad = (value_acc[...] + value_part).astype(BF)
            grads[i, :, :, :, HD : 2 * HD] = key_grad.reshape(8, 2, ROWS, HD)
            grads[i, :, :, :, 2 * HD :] = value_grad.reshape(8, 2, ROWS, HD)
            send(
                grads.at[i, :, p.co], both_grads.at[i, :, :, pair_cols], grads_sem.at[i],
                **partner
            )
            both_grads[i, :, :, :384] = grads[i, :, p.c]

    for i in range(2):
        step(f"proj{i}", i)(project)
        for block in range(4):
            step(f"att{i}{block}", i, block)(attend)

    def back_project(i, h):
        if h == 0:
            arrived(both_grads.at[i, :, :, pair_cols], grads_sem.at[i])
        for block in range(2 * h, 2 * h + 2):
            cols = pl.ds(block * 768, 768)
            product = lax.dot_general(
                both_grads[i].reshape(256, 768), wall[block], NT, preferred_element_type=F32
            ).astype(BF)
            pair_sum[i, :, :, :, cols] = product.reshape(2, 4, ROWS, 768)

    round_y = {
        (i, r): Scatter4(
            send,
            lambda y, h, i=i, r=r: pair_sum.at[i, :, y, part(r), half(h)],
            lambda h, i=i, r=r: ry_relay.at[i, h, :, part(r)],
            lambda h, i=i, r=r: ry_left.at[i, h, :, part(r)],
            lambda h, i=i, r=r: ry_right.at[i, h, :, part(r)],
            ry_sem.at[i * 2 + r],
            p.y,
            p.yl,
            p.yr,
            p.yo,
            to_y,
        )
        for i, r in chunks
    }

    def scatter_start(i, r):
        round_y[i, r].start(0)
        round_y[i, r].start(1)

    def scatter_direct(i, r):
        round_y[i, r].direct(1)
        round_y[i, r].direct(0)

    def y_sum(i, r, z, h):
        return (
            pair_sum[i, z, p.y, part(r), half(h)].astype(F32)
            + ry_left[i, h, z, part(r)].astype(F32)
            + ry_right[i, h, z, part(r)].astype(F32)
        )

    def scatter_cross(i, r):
        round_y[i, r].finish()
        for h in range(2):
            cross_out[i, part(r), half(h)] = y_sum(i, r, p.zo, h).astype(BF)
        send(
            cross_out.at[i, part(r)], cross_in.at[i, part(r)], cross_sem.at[i * 2 + r], **across
        )

    def norm_back(i, r):
        mine = jnp.concatenate([y_sum(i, r, p.z, h) for h in range(2)], axis=1)
        standard, reciprocal = standardise(hidden[i, part(r)])
        arrived(cross_in.at[i, part(r)], cross_sem.at[i * 2 + r])
        scaled = (mine + cross_in[i, part(r)].astype(F32)) * stretch[i : i + 1]
        residual_grad = reciprocal * (
            scaled
            - jnp.mean(scaled, axis=-1, keepdims=True)
            - standard * jnp.mean(scaled * standard, axis=-1, keepdims=True)
        )
        for c in range(2):
            rows_all[c, p.g, i, part(r)] = by_owner(residual_grad, c).astype(BF)
        if i == 0:
            rows_gather[0, r].start()

    def rows_at(c, g, i, n):
        if i:
            return rows_all.at[c, g, 1, :, pl.ds(n * 768, 768)]
        return rows_all.at[c, g, 0, part(n)]

    def rows_in_at(i, n):
        if i:
            return rows_in.at[:, 1, :, pl.ds(n * 768, 768)]
        return rows_in.at[:, 0, part(n)]

    every = slice(None)
    rows_gather = {
        (i, n): Gather4(
            send,
            lambda g, i=i, n=n: rows_at(every, g, i, n),
            lambda g, h, i=i, n=n: rows_at(h, g, i, n),
            gg_sem.at[i * 2 + n],
            p.g,
            p.gl,
            p.gr,
            p.go,
            to_g,
        )
        for i, n in chunks
    }

    def rows_start(n):
        if n:
            send.sent(rows_gather[1, 0].begun)
        rows_gather[1, n].start()

    def rows_finish(i, n):
        rows_gather[i, n].finish()
        send(rows_at(p.co, every, i, n), rows_in_at(i, n), rows_sem.at[i * 2 + n], **partner)

    for i in range(2):
        step(f"bpa{i}", i, 0)(back_project)
        step(f"bpb{i}", i, 1)(back_project)
        step(f"AS1{i}", i)(rows_start)
    for i, r in chunks:
        step(f"Bs{i}{r}", i, r)(scatter_start)
        step(f"Bd{i}{r}", i, r)(scatter_direct)
        for h in range(2):
            step(f"Bp{h}{i}{r}", h)(round_y[i, r].pass_on)
        step(f"BX{i}{r}", i, r)(scatter_cross)
        step(f"BL{i}{r}", i, r)(norm_back)
        step(f"AL{i}{r}")(rows_gather[i, r].pass_left)
        step(f"AR{i}{r}")(rows_gather[i, r].pass_right)
        step(f"Af{i}{r}", i, r)(rows_finish)

    def attn_pairs(to):
        near = pl.ds(pl.multiple_of((p.z * 8 + to) * ROWS, ROWS), ROWS)
        far = pl.ds(pl.multiple_of((p.zo * 8 + to) * ROWS, ROWS), ROWS)
        cols = pl.ds(pl.multiple_of(p.s * HD, HD), HD)
        staged = pl.ds(pl.multiple_of(q * HD, HD), HD)
        return (
            (attn.at[:, :, near], attn_out.at[:, :, :, cols], attn_recv.at[0]),
            (attn.at[:, :, far], ostage.at[:, :, :, staged], attn_recv.at[1]),
        )

    def attn_copies(k):
        to = (q + k) % 8
        return [
            pltpu.make_async_remote_copy(
                src_ref=src,
                dst_ref=dst,
                send_sem=attn_send.at[n, k],
                recv_sem=recv,
                device_id={"seq": p.z * 8 + to},
                device_id_type=MESH,
            )
            for n, (src, dst, recv) in enumerate(attn_pairs(to))
        ]

    @step("O1")
    def _():
        @pl.loop(1, 8)
        def _(k):
            for copy in attn_copies(k):
                copy.start()

        for src, dst, recv in attn_pairs(q):
            pltpu.make_async_copy(src, dst, recv).start()

    half_cols = pl.ds(pl.multiple_of(p.z * 1024, 1024), 1024)
    other_cols = pl.ds(pl.multiple_of(p.zo * 1024, 1024), 1024)

    @step("O2")
    def _():
        arrived(ostage, attn_recv.at[1])
        send(ostage, attn_out.at[:, :, :, half_cols], attn_recv.at[2], **across)

    def control_part(i):
        total = 0.0
        for c in range(2):
            total = total + lax.dot_general(
                rows_all[c, :, i].reshape(128, HALF),
                zw_owner[c],
                NT,
                preferred_element_type=F32,
            )
        control_grad[:, i] = total.astype(BF).reshape(4, ROWS, 768)

    def zero_part(i, block):
        cols = pl.ds(block * 384, 384)
        left = jnp.concatenate(
            [ref.reshape(128, 384) for ref in (rows_all[p.c, :, i, :, cols], rows_in[:, i, :, cols])]
        )
        right = jnp.concatenate([ctl[:, i].reshape(128, 768), ctl_in[:, i].reshape(128, 768)])
        product = lax.dot_general(left, right, TN, preferred_element_type=F32)
        if i == 0:
            zacc[cols] = product
        else:
            z, y = block // 2, block % 2 * 2
            zsum[z, pl.ds(y, 2)] = (zacc[cols] + product).astype(BF).reshape(2, 192, 768)

    step("ctl0", 0)(control_part)
    step("ctl1", 1)(control_part)

    @step("zp0")
    def _():
        arrived(ctl_in, share_sem.at[4])
        for n in range(2):
            arrived(rows_in_at(0, n), rows_sem.at[n])
        for block in range(4):
            zero_part(0, block)

    cols_a, cols_b = pl.ds(0, 384), pl.ds(384, 384)
    quarter = lambda d: pl.ds(pl.multiple_of(d * 48, 16), 48)
    round_x = Scatter4(
        send,
        lambda d, h: zsum.at[h, :, quarter(d), cols_a],
        lambda h: zx_relay.at[h],
        lambda h: zx_left.at[h],
        lambda h: zx_right.at[h],
        zx_sem,
        p.d,
        p.dl,
        p.dr,
        p.do,
        to_d,
    )
    zero_y = Scatter4(
        send,
        lambda y, h: zsum.at[h, y, :, cols_b],
        lambda h: zy_relay.at[h],
        lambda h: zy_left.at[h],
        lambda h: zy_right.at[h],
        zy_sem,
        p.y,
        p.yl,
        p.yr,
        p.yo,
        to_y,
    )
    def zero_send(z):
        arrived(rows_in_at(1, z), rows_sem.at[2 + z])
        zero_part(1, 2 * z)
        zero_part(1, 2 * z + 1)
        round_x.start(z)
        zero_y.start(z)
        round_x.direct(z)
        zero_y.direct(z)

    step("zp1a", 0)(zero_send)
    step("zp1b", 1)(zero_send)
    for h in range(2):
        step(f"Zp{h}x", h)(round_x.pass_on)
        step(f"Zp{h}y", h)(zero_y.pass_on)
    others = [(dz, dy) for dz in range(2) for dy in range(4) if dz or dy]

    @step("ZA")
    def _():
        round_x.finish()
        for z in range(2):
            za_out[z] = (
                zsum[z, :, quarter(p.d), cols_a].astype(F32)
                + zx_left[z].astype(F32)
                + zx_right[z].astype(F32)
            ).astype(BF)
        for n, (dz, dy) in enumerate(others):
            z, y = (p.z + dz) % 2, (p.y + dy) % 4
            send(za_out.at[z, y], za_in.at[n], za_sem.at[n], seq=p.seq(z, y, p.c))

    @step("ZB")
    def _():
        zero_y.finish()
        for z in range(2):
            zb_out[z] = (
                (
                    zsum[z, p.y, :, cols_b].astype(F32)
                    + zy_left[z].astype(F32)
                    + zy_right[z].astype(F32)
                )
                .astype(BF)
                .reshape(4, 48, 384)
            )
        for n, (dz, dd) in enumerate(others):
            z, d = (p.z + dz) % 2, (p.d + dd) % 4
            send(zb_out.at[z, d], zb_in.at[n], zb_sem.at[n], seq=p.seq(z, p.y, p.c), dp=d)

    zero_gather = Gather4(
        send,
        lambda d: zall.at[d],
        lambda d, h: zall.at[d, :, pl.ds(h * 384, 384)],
        zg_sem,
        p.d,
        p.dl,
        p.dr,
        p.do,
        to_d,
    )

    @step("ZS")
    def _():
        total = za_out[p.z, p.y].astype(F32)
        for n in range(7):
            arrived(za_in.at[n], za_sem.at[n])
            total = total + za_in[n].astype(F32)
        zall[p.d, :, cols_a] = total.astype(BF)
        total = zb_out[p.z, p.d].astype(F32)
        for n in range(7):
            arrived(zb_in.at[n], zb_sem.at[n])
            total = total + zb_in[n].astype(F32)
        zall[p.d, :, cols_b] = total.astype(BF)
        zero_gather.start()

    step("zgL_")(zero_gather.pass_left)
    step("zgR_")(zero_gather.pass_right)

    for name in ORDER:
        steps.pop(name)()
    assert not steps

    zero_gather.finish()
    zero_out[...] = zall[...].reshape(192, 768).astype(F32) * (16384 ** (-0.5))

    arrived(attn_out.at[:, :, :, half_cols], attn_recv.at[0])
    arrived(attn_out.at[:, :, :, other_cols], attn_recv.at[2])
    send.drain()

    @pl.loop(1, 8)
    def _(k):
        for i in range(2):
            for copy in text_copies(i, k):
                copy.wait_send()
        for copy in attn_copies(k):
            copy.wait_send()


def whole_block(*operands):
    dma = pltpu.SemaphoreType.DMA
    bf = lambda *shape: pltpu.VMEM(shape, BF)
    return pl.pallas_call(
        block_kernel,
        out_shape=(
            jax.ShapeDtypeStruct((2, 2, ROWS, HEADS * HD), BF),
            jax.ShapeDtypeStruct((4, 2, ROWS, 768), BF),
            jax.ShapeDtypeStruct((192, 768), F32),
        ),
        in_specs=[pl.BlockSpec(memory_space=pltpu.SMEM), VMEM] + [ANY] * 8,
        out_specs=(VMEM, VMEM, VMEM),
        scratch_shapes=[
            bf(4, 2, ROWS, 768),
            bf(4, 2, ROWS, 768),
            bf(768, D),
            bf(2, 768, HALF),
            bf(2, ROWS, D),
            bf(4, 768, 768),
            pltpu.VMEM((2, D), F32),
            pltpu.VMEM((2, D), F32),
            bf(4, 2, ROWS, D),
            bf(2, 2, ROWS, HALF),
            bf(2, 2, ROWS, HALF),
            bf(2, 2, ROWS, HALF),
            bf(2, ROWS, D),
            bf(2, 2, 4, ROWS, D),
            bf(2, 3, 8, ROWS, HD),
            bf(3, 2, 2, 8, 2, ROWS, HD),
            bf(2, 2, 8, 2, ROWS, HD),
            bf(3, 2, 4, 2, ROWS, HD),
            bf(2, 2, 4, 2, ROWS, HD),
            bf(2, 2, 512, HD),
            bf(2, 2, ROWS, 1024),
            bf(2, 8, 2, ROWS, 384),
            bf(2, 8, ROWS, 768),
            pltpu.VMEM((IMG, HD), F32),
            pltpu.VMEM((IMG, HD), F32),
            bf(2, 2, 4, ROWS, D),
            bf(2, 2, 2, ROWS, HALF),
            bf(2, 2, 2, ROWS, HALF),
            bf(2, 2, 2, ROWS, HALF),
            bf(2, ROWS, D),
            bf(2, ROWS, D),
            bf(2, 4, 2, ROWS, HALF),
            bf(4, 2, ROWS, HALF),
            pltpu.VMEM((HALF, 768), F32),
            bf(2, 4, 192, 768),
            bf(2, 4, 48, 384),
            bf(2, 4, 48, 384),
            bf(2, 4, 48, 384),
            bf(2, 192, 384),
            bf(2, 192, 384),
            bf(2, 192, 384),
            bf(2, 4, 48, 384),
            bf(2, 4, 48, 384),
            bf(7, 48, 384),
            bf(7, 48, 384),
            bf(4, 48, 768),
            bf(3, 2, ROWS, HEADS * HD),
            bf(2, 2, ROWS, HEADS * HD),
            dma((32,)),
            dma((224,)),
            dma((4,)),
            dma((5,)),
            dma((4, 6)),
            dma((4, 9)),
            dma((4, 2, 8)),
            dma((2, 2)),
            dma((2, 2)),
            dma((2, 2)),
            dma((2,)),
            dma((2,)),
            dma((4, 6)),
            dma((4,)),
            dma((4, 4)),
            dma((4,)),
            dma((2, 8)),
            dma((3,)),
            dma((6,)),
            dma((6,)),
            dma((7,)),
            dma((7,)),
            dma((4,)),
        ],
        compiler_params=pltpu.CompilerParams(
            collective_id=1, has_side_effects=True, vmem_limit_bytes=VMEM_LIMIT
        ),
        name="whole_block",
    )(*operands)


def hand_over_kernel(attn, control, zero, image_out, text_out, control_out, zero_out, sems):
    copies = [
        pltpu.make_async_copy(src, dst, sems.at[n])
        for n, (src, dst) in enumerate(
            (
                (attn.at[1], image_out),
                (attn.at[0], text_out),
                (control, control_out),
                (zero, zero_out),
            )
        )
    ]
    for copy in copies:
        copy.start()
    for copy in copies:
        copy.wait()


def hand_over(attn, control, zero):
    return pl.pallas_call(
        hand_over_kernel,
        out_shape=(
            jax.ShapeDtypeStruct(attn.shape[1:], BF),
            jax.ShapeDtypeStruct(attn.shape[1:], BF),
            jax.ShapeDtypeStruct(control.shape, BF),
            jax.ShapeDtypeStruct(zero.shape, F32),
        ),
        in_specs=[VMEM] * 3,
        out_specs=(ANY,) * 4,
        scratch_shapes=[pltpu.SemaphoreType.DMA((4,))],
        name="hand_over",
    )(attn, control, zero)


def timestep_activation(timesteps):
    half_freq = FREQ // 2
    frequency = jnp.exp(-math.log(10000.0) * jnp.arange(half_freq, dtype=F32) / half_freq)
    angles = timesteps.astype(F32)[..., None] * frequency
    embedding = jnp.concatenate([jnp.cos(angles), jnp.sin(angles)], axis=-1)
    return jax.nn.silu(embedding).astype(BF)


def body(
    image_hidden,
    control_hidden,
    text_qkv,
    text_lengths,
    timesteps,
    mod_weight,
    qkv_weight,
    zero_weight,
    image_cotangent,
    text_cotangent,
):
    activated = timestep_activation(timesteps.reshape(2))
    attn_out, control_grad, zero_t = whole_block(
        text_lengths.reshape(2),
        activated,
        mod_weight,
        control_hidden.reshape(4, 2, ROWS, 768),
        zero_weight,
        image_hidden.reshape(2, ROWS, D),
        jnp.transpose(qkv_weight, (1, 0, 2)),
        text_qkv.reshape(3, 2, ROWS, HEADS * HD),
        text_cotangent.reshape(2, ROWS, HEADS * HD),
        image_cotangent.reshape(2, ROWS, HEADS * HD),
    )
    image_attn, text_attn, control_grad, zero_t = hand_over(attn_out, control_grad, zero_t)
    return (
        image_attn.reshape(2, 1, ROWS, HEADS * HD),
        text_attn.reshape(2, 1, ROWS, HEADS * HD),
        control_grad.reshape(8, 1, ROWS, 768),
        jnp.transpose(zero_t),
    )


def solution(mesh):
    placed = (
        P("grp", "dp", "seq", None),
        P(None, "dp", "seq", "grp"),
        P(None, "grp", "dp", "seq", None),
        P("grp", "dp"),
        P("grp", "dp"),
        P(),
        P("dp", None, "seq"),
        P("grp", None),
        P("grp", "dp", "seq", None),
        P("grp", "dp", "seq", None),
    )
    return jax.shard_map(
        body,
        mesh=mesh,
        in_specs=placed,
        out_specs=(
            P("grp", "dp", "seq", None),
            P("grp", "dp", "seq", None),
            P(None, "dp", "seq", "grp"),
            P("grp", "seq"),
        ),
        check_vma=False,
    )
```

```python
import math

import jax
import jax.numpy as jnp
from jax import lax
from jax.experimental import pallas as pl
from jax.experimental.pallas import tpu as pltpu
from jax.sharding import PartitionSpec as P

D = 3072
HEADS = 16
HD = 128
IMG = 512
TXT = 512
FREQ = 256
ROWS = 32
HALF = D // 2
MESH = pl.DeviceIdType.MESH
BF = jnp.bfloat16
F32 = jnp.float32
VMEM_LIMIT = 60 * 1024 * 1024
ANY = pl.BlockSpec(memory_space=pl.ANY)
VMEM = pl.BlockSpec(memory_space=pltpu.VMEM)


class Sends:
    def __init__(self, sems):
        self.sems = sems
        self.copies = []
        self.started = 0

    def __call__(self, src, dst, recv, **to):
        copy = pltpu.make_async_remote_copy(
            src_ref=src,
            dst_ref=dst,
            send_sem=self.sems.at[self.started],
            recv_sem=recv,
            device_id=to,
            device_id_type=MESH,
        )
        copy.start()
        self.started += 1
        self.copies.append(copy)
        return copy

    def sent(self, copies):
        for copy in copies:
            copy.wait_send()
        waited = [id(copy) for copy in copies]
        self.copies = [copy for copy in self.copies if id(copy) not in waited]

    def drain(self):
        self.sent(list(self.copies))


def arrived(dst, recv):
    pltpu.make_async_copy(dst, dst, recv).wait()


def greet(groups):
    barrier = pltpu.get_barrier_semaphore()
    for to in groups:
        pl.semaphore_signal(barrier, inc=1, device_id=to, device_id_type=MESH)
    return lambda: pl.semaphore_wait(barrier, len(groups))


class Place:
    def __init__(self):
        self.s = lax.axis_index("seq")
        self.g = lax.axis_index("grp")
        self.d = lax.axis_index("dp")
        self.z = self.s // 8
        self.y = (self.s // 2) % 4
        self.c = self.s % 2
        self.zo = 1 - self.z
        self.co = 1 - self.c
        self.yl = (self.y + 3) % 4
        self.yr = (self.y + 1) % 4
        self.yo = (self.y + 2) % 4
        self.gl = (self.g + 3) % 4
        self.gr = (self.g + 1) % 4
        self.go = (self.g + 2) % 4
        self.dl = (self.d + 3) % 4
        self.dr = (self.d + 1) % 4
        self.do = (self.d + 2) % 4

    def seq(self, z, y, c):
        return z * 8 + y * 2 + c


def add_into(dst, *others):
    total = dst[...].astype(F32)
    for other in others:
        total = total + other[...].astype(F32)
    dst[...] = total.astype(dst.dtype)


class Scatter4:
    def __init__(self, send, src, relay, from_left, from_right, sems, me, left, right, far, to):
        self.send, self.src, self.relay = send, src, relay
        self.from_left, self.from_right, self.sems = from_left, from_right, sems
        self.me, self.left, self.right, self.far, self.to = me, left, right, far, to
        self.passed = []

    def start(self, h):
        to = (self.left, self.right)[h]
        self.send(self.src(self.far, h), self.relay(h), self.sems.at[h], **self.to(to))

    def direct(self, h):
        if h:
            dst, to = self.from_right(1), self.left
        else:
            dst, to = self.from_left(0), self.right
        self.send(self.src(to, h), dst, self.sems.at[3 - h], **self.to(to))

    def pass_on(self, h):
        arrived(self.relay(h), self.sems.at[h])
        if h:
            dst, to = self.from_left(1), self.right
        else:
            dst, to = self.from_right(0), self.left
        add_into(self.src(to, h), self.relay(h))
        self.passed.append(self.send(self.src(to, h), dst, self.sems.at[4 + h], **self.to(to)))

    def finish(self):
        arrived(self.from_right(1), self.sems.at[2])
        arrived(self.from_left(0), self.sems.at[3])
        arrived(self.from_right(0), self.sems.at[4])
        arrived(self.from_left(1), self.sems.at[5])


class Gather4:
    def __init__(self, send, slot, half, sems, me, left, right, far, to):
        self.send, self.slot, self.half, self.sems = send, slot, half, sems
        self.me, self.left, self.right, self.far, self.to = me, left, right, far, to

    def start(self, own=None):
        own = self.slot(self.me) if own is None else own
        self.begun = [
            self.send(own, self.slot(self.me), self.sems.at[0], **self.to(self.right)),
            self.send(own, self.slot(self.me), self.sems.at[1], **self.to(self.left)),
        ]

    def pass_left(self):
        arrived(self.slot(self.left), self.sems.at[0])
        part = self.half(self.left, 0)
        self.send(part, part, self.sems.at[2], **self.to(self.right))

    def pass_right(self):
        arrived(self.slot(self.right), self.sems.at[1])
        part = self.half(self.right, 1)
        self.send(part, part, self.sems.at[3], **self.to(self.left))

    def finish(self):
        arrived(self.half(self.far, 0), self.sems.at[2])
        arrived(self.half(self.far, 1), self.sems.at[3])


ORDER = (
    "res0", "res1", "Rs00", "T10", "Ws", "Rp000", "Rp100", "Rs01", "mod", "LN00", "Rp101",
    "Rp001", "T11", "WL", "Rs10", "GR000", "WR_", "LN01", "zwo", "T20", "Gz00", "GL000", "Rp110",
    "Rp010", "GR001", "Gz01", "Rs11", "Wf", "LN10", "GL010", "GL001", "GR011", "GR100", "GR010",
    "GL011", "Rp111", "Rp011", "GL100", "proj0", "Gz10", "LN11", "att00", "att01", "Gz11",
    "att02", "att03", "GR101", "GL101", "T21", "GR111", "GL111", "GL110", "GR110", "bpa0", "bpb0",
    "Bs00", "proj1", "Bd00", "Bp100", "Bp000", "att10", "att11", "att12", "Bs01", "att13", "BX00",
    "Bd01", "bpa1", "Bp001", "Bp101", "BL00", "bpb1", "Bs10", "BX01", "Bd10", "Bp010", "Bp110",
    "Bs11", "AR00", "AL00", "BL01", "Bd11", "Bp011", "BX10", "Bp111", "AL01", "AR01", "BX11",
    "Af00", "Af01", "BL10", "BL11", "AS10", "O1", "AS11", "AL10", "AR10", "zp0", "Af10", "AL11",
    "AR11", "zp1a", "Af11", "zp1b", "Zp0y", "Zp0x", "Zp1x", "ctl1", "Zp1y", "ctl0", "ZA", "ZB",
    "ZS", "zgL_", "zgR_", "O2",
)
NT = (((1,), (1,)), ((), ()))
TN = (((0,), (0,)), ((), ()))
BLOCK = 256


def by_owner(columns, c):
    runs = columns.shape[1] // 384
    return jnp.concatenate(
        [columns[:, n * 384 + c * 192 : n * 384 + c * 192 + 192] for n in range(runs)], axis=1
    )


def block_kernel(
    lengths,
    timesteps,
    mod_weight,
    control,
    zero_weight,
    image_hidden,
    weight,
    text,
    text_cot,
    image_cot,
    attn_out,
    control_grad,
    zero_out,
    ctl,
    ctl_in,
    zw,
    zw_owner,
    base,
    wall,
    offset,
    stretch,
    partial,
    rg_relay,
    rg_left,
    rg_right,
    hidden,
    normed,
    qkv_out,
    joint,
    cots,
    tstage,
    cstage,
    attn,
    ostage,
    grads,
    both_grads,
    key_acc,
    value_acc,
    pair_sum,
    ry_relay,
    ry_left,
    ry_right,
    cross_out,
    cross_in,
    rows_all,
    rows_in,
    zacc,
    zsum,
    zx_relay,
    zx_left,
    zx_right,
    zy_relay,
    zy_left,
    zy_right,
    za_out,
    zb_out,
    za_in,
    zb_in,
    zall,
    text_mine,
    cots_mine,
    load_sem,
    send_sem,
    w_sem,
    share_sem,
    rg_sem,
    ag_sem,
    text_send,
    text_recv,
    stage_recv,
    cross_recv,
    qkv_sem,
    grads_sem,
    ry_sem,
    cross_sem,
    gg_sem,
    rows_sem,
    attn_send,
    attn_recv,
    zx_sem,
    zy_sem,
    za_sem,
    zb_sem,
    zg_sem,
):
    p = Place()
    send = Sends(send_sem)
    q = p.y * 2 + p.c
    partner = {"seq": p.seq(p.z, p.y, p.co)}
    across = {"seq": p.seq(p.zo, p.y, p.c)}
    to_y = lambda y: {"seq": p.seq(p.z, y, p.c)}
    to_g = lambda g: {"grp": g}
    to_d = lambda d: {"dp": d}

    all_here = greet(
        [{"seq": (p.s + k) % 16} for k in range(1, 16)]
        + [{"grp": p.gl}, {"grp": p.gr}]
        + [{"dp": (p.d + k) % 4} for k in range(1, 4)]
        + [{"dp": (p.d + k) % 4, "seq": p.seq(p.zo, p.y, p.c)} for k in range(1, 4)]
    )

    loads = []

    def load(src, dst):
        copy = pltpu.make_async_copy(src, dst, load_sem.at[len(loads)])
        copy.start()
        loads.append(copy)
        return copy

    load_control = load(control, ctl)
    load_zero = [
        load(zero_weight.at[:, pl.ds(n * 512, 512)], zw.at[:, pl.ds(n * 512, 512)])
        for n in range(6)
    ]
    load_weight = [
        load(weight.at[n], wall.at[p.d, :, pl.ds(n * HD, HD)]) for n in range(3)
    ]
    load_text = [
        load(text, text_mine),
        load(text_cot, cots_mine.at[0]),
        load(image_cot, cots_mine.at[1]),
    ]
    load_base = load(image_hidden, base)
    load_mod = [
        load(
            mod_weight.at[pl.ds(n % 8 * ROWS, ROWS), pl.ds(n // 8 * D, D)],
            pair_sum.at[n // 8, n // 4 % 2, n % 4],
        )
        for n in range(16)
    ]

    half = lambda h: pl.ds(h * HALF, HALF)
    part = lambda r: pl.ds(r * 16, 16)
    chunks = [(i, r) for i in range(2) for r in range(2)]
    steps = {}

    def step(name, *args):
        def add(f):
            steps[name] = lambda: f(*args)
            return f

        return add

    def residual_part(h):
        if h == 0:
            load_control.wait()
        for block in range(3 * h, 3 * h + 3):
            cols = pl.ds(block * 512, 512)
            load_zero[block].wait()
            product = jnp.dot(
                ctl[...].reshape(256, 768), zw[:, cols], preferred_element_type=F32
            )
            partial[:, :, :, cols] = product.astype(BF).reshape(4, 2, ROWS, 512)
        if h == 0:
            all_here()
            to_group[0, 0].start(0)
            to_group[0, 0].direct(0)

    step("res0", 0)(residual_part)
    step("res1", 1)(residual_part)

    to_group = {
        (i, r): Scatter4(
            send,
            lambda g, h, i=i, r=r: partial.at[g, i, part(r), half(h)],
            lambda h, i=i, r=r: rg_relay.at[i, h, part(r)],
            lambda h, i=i, r=r: rg_left.at[i, h, part(r)],
            lambda h, i=i, r=r: rg_right.at[i, h, part(r)],
            rg_sem.at[i * 2 + r],
            p.g,
            p.gl,
            p.gr,
            p.go,
            to_g,
        )
        for i, r in chunks
    }

    def group_start(n):
        if n:
            send.sent(to_group[chunks[n - 1]].passed)
        scatter = to_group[chunks[n]]
        for h in range(0 if n else 1, 2):
            scatter.start(h)
        scatter.direct(1)
        if n:
            scatter.direct(0)

    for n, (i, r) in enumerate(chunks):
        step(f"Rs{i}{r}", n)(group_start)
        for h in range(2):
            step(f"Rp{h}{i}{r}", h)(to_group[i, r].pass_on)

    plane = pl.ds(p.z * 4, 4)
    other_plane = pl.ds(p.zo * 4, 4)
    zy = p.z * 4 + p.y

    def text_pairs(i, to):
        near = pl.ds(pl.multiple_of((p.z * 8 + to) * HD, HD), HD)
        far = pl.ds(pl.multiple_of((p.zo * 8 + to) * HD, HD), HD)
        return (
            (text_mine.at[:, i, :, far], tstage.at[:, i, p.y, p.c], stage_recv.at[0, i]),
            (cots_mine.at[:, i, :, far], cstage.at[:, i, p.y, p.c], stage_recv.at[1, i]),
            (text_mine.at[:, i, :, near], joint.at[:, i, 0, zy, p.c], text_recv.at[0, i]),
            (cots_mine.at[:, i, :, near], cots.at[:, i, zy, p.c], text_recv.at[1, i]),
        )

    def text_copies(i, k):
        to = (q + k) % 8
        return [
            pltpu.make_async_remote_copy(
                src_ref=src,
                dst_ref=dst,
                send_sem=text_send.at[n, i, k],
                recv_sem=recv,
                device_id={"seq": p.z * 8 + to},
                device_id_type=MESH,
            )
            for n, (src, dst, recv) in enumerate(text_pairs(i, to))
        ]

    def text_first_hop(i):
        if i == 0:
            for copy in load_text:
                copy.wait()

        @pl.loop(1, 8)
        def _(k):
            for copy in text_copies(i, k):
                copy.start()

        for src, dst, recv in text_pairs(i, q):
            pltpu.make_async_copy(src, dst, recv).start()

    def text_second_hop(i):
        arrived(tstage.at[:, i], stage_recv.at[0, i])
        arrived(cstage.at[:, i], stage_recv.at[1, i])
        send(tstage.at[:, i], joint.at[:, i, 0, plane], cross_recv.at[i, 0], **across)
        send(cstage.at[:, i], cots.at[:, i, plane], cross_recv.at[i, 1], **across)

    def text_wait(i):
        arrived(joint.at[:, i, 0, plane], text_recv.at[0, i])
        arrived(cots.at[:, i, plane], text_recv.at[1, i])
        arrived(joint.at[:, i, 0, other_plane], cross_recv.at[i, 0])
        arrived(cots.at[:, i, other_plane], cross_recv.at[i, 1])

    for i in range(2):
        step(f"T1{i}", i)(text_first_hop)
        step(f"T2{i}", i)(text_second_hop)

    mine_cols, pair_cols = pl.ds(0, 384), pl.ds(384, 384)
    weights = Gather4(
        send,
        lambda d: wall.at[d, :, mine_cols],
        lambda d, h: wall.at[d, pl.ds(h * 384, 384), mine_cols],
        w_sem,
        p.d,
        p.dl,
        p.dr,
        p.do,
        to_d,
    )

    def share_weight(d, sem):
        send(wall.at[d, :, mine_cols], wall.at[d, :, pair_cols], share_sem.at[sem], **partner)

    @step("Ws")
    def _():
        for copy in load_weight:
            copy.wait()
        weights.start()
        share_weight(p.d, 0)
        send(ctl, ctl_in, share_sem.at[4], **partner)

    @step("WL")
    def _():
        weights.pass_left()
        share_weight(p.dl, 1)

    @step("WR_")
    def _():
        weights.pass_right()
        share_weight(p.dr, 2)

    @step("Wf")
    def _():
        weights.finish()
        share_weight(p.do, 3)

    @step("mod")
    def _():
        for copy in load_mod:
            copy.wait()
        lane = lax.broadcasted_iota(jnp.int32, (1, FREQ // 2), 1).astype(F32)
        frequency = jnp.exp(lane * (-math.log(10000.0) / (FREQ // 2)))
        angles = jnp.concatenate([timesteps[i].astype(F32) * frequency for i in range(2)])
        embedding = jnp.concatenate([jnp.cos(angles), jnp.sin(angles)], axis=1)
        activated = (embedding / (1.0 + jnp.exp(-embedding))).astype(BF)
        offset[...] = jnp.dot(
            activated, pair_sum[0].reshape(FREQ, D), preferred_element_type=F32
        )
        stretch[...] = 1.0 + jnp.dot(
            activated, pair_sum[1].reshape(FREQ, D), preferred_element_type=F32
        )
        load_base.wait()

    @step("zwo")
    def _():
        for block in range(4):
            columns = zw[:, pl.ds(block * 768, 768)].astype(F32)
            for c in range(2):
                zw_owner[c, :, pl.ds(block * 384, 384)] = by_owner(columns, c).astype(BF)

    gathers = {
        (i, r, which): Gather4(
            send,
            lambda y, i=i, r=r, z=z: normed.at[i, z, y, part(r)],
            lambda y, h, i=i, r=r, z=z: normed.at[i, z, y, part(r), half(h)],
            ag_sem.at[i * 2 + r, pl.ds(which * 4, 4)],
            p.y,
            p.yl,
            p.yr,
            p.yo,
            to_y,
        )
        for i, r in chunks
        for which, z in enumerate((p.z, p.zo))
    }

    def standardise(rows):
        values = rows.astype(F32)
        average = jnp.mean(values, axis=-1, keepdims=True)
        centred = values - average
        reciprocal = lax.rsqrt(jnp.mean(centred * centred, axis=-1, keepdims=True) + 1e-06)
        return centred * reciprocal, reciprocal

    def gather_first(i, r):
        to_group[i, r].finish()
        rows = part(r)
        for h in range(2):
            residual = (
                partial[p.g, i, rows, half(h)].astype(F32)
                + rg_left[i, h, rows].astype(F32)
                + rg_right[i, h, rows].astype(F32)
            )
            hidden[i, rows, half(h)] = (base[i, rows, half(h)].astype(F32) + residual).astype(BF)
        standard, _ = standardise(hidden[i, rows])
        normed[i, p.z, p.y, rows] = (
            standard * stretch[i : i + 1] + offset[i : i + 1]
        ).astype(BF)
        mine = normed.at[i, p.z, p.y, rows]
        send(mine, mine, ag_sem.at[i * 2 + r, 8], **across)
        gathers[i, r, 0].start()

    def gather_second(i, r):
        arrived(normed.at[i, p.zo, p.y, part(r)], ag_sem.at[i * 2 + r, 8])
        gathers[i, r, 1].start()

    for i, r in chunks:
        step(f"LN{i}{r}", i, r)(gather_first)
        step(f"Gz{i}{r}", i, r)(gather_second)
        for which in range(2):
            step(f"GL{i}{r}{which}")(gathers[i, r, which].pass_left)
            step(f"GR{i}{r}{which}")(gathers[i, r, which].pass_right)

    scaling = HD ** (-0.5)

    def project(i):
        for r in range(2):
            for which in range(2):
                gathers[i, r, which].finish()
        if i == 0:
            for n, d in enumerate((p.d, p.dl, p.dr, p.do)):
                arrived(wall.at[d, :, pair_cols], share_sem.at[n])
        product = jnp.dot(
            normed[i].reshape(256, D), wall[...].reshape(D, 768), preferred_element_type=F32
        ).astype(BF)
        for n in range(3):
            qkv_out[i, n] = product[:, 384 + n * HD : 384 + (n + 1) * HD].reshape(8, ROWS, HD)
        send(qkv_out.at[i], joint.at[:, i, 1, :, p.c], qkv_sem.at[i], **partner)
        for n in range(3):
            joint[n, i, 1, :, p.c] = product[:, n * HD : (n + 1) * HD].reshape(8, ROWS, HD)

    def attend(i, block):
        if block == 0:
            text_wait(i)
            arrived(joint.at[:, i, 1, :, p.co], qkv_sem.at[i])
        slots = pl.ds(block % 2 * 4, 4)
        query = joint[0, i, block // 2, slots].reshape(BLOCK, HD)
        cot = cots[block // 2, i, slots].reshape(BLOCK, HD)
        keys = joint[1, i].reshape(TXT + IMG, HD)
        values = joint[2, i].reshape(TXT + IMG, HD)
        scores = lax.dot_general(keys, query, NT, preferred_element_type=F32)
        text_live = lax.broadcasted_iota(jnp.int32, (TXT, 1), 0) < lengths[i]
        text_scores = jnp.where(text_live, scores[:TXT], -jnp.inf)
        image_scores = scores[TXT:]
        col_max = jnp.maximum(
            jnp.max(text_scores, axis=0, keepdims=True),
            jnp.max(image_scores, axis=0, keepdims=True),
        )
        rate = scaling * math.log2(math.e)
        text_terms = jnp.exp2((text_scores - col_max) * rate)
        image_terms = jnp.exp2((image_scores - col_max) * rate)
        share = 1.0 / (
            jnp.sum(text_terms, axis=0, keepdims=True) + jnp.sum(image_terms, axis=0, keepdims=True)
        )
        text_prob, image_prob = text_terms * share, image_terms * share
        image_low = image_prob.astype(BF)
        attended = lax.dot_general(
            values[:TXT], text_prob.astype(BF), TN, preferred_element_type=F32
        ) + lax.dot_general(values[TXT:], image_low, TN, preferred_element_type=F32)
        low_attended = attended.astype(BF).astype(F32)
        attn[block // 2, i, pl.ds(block % 2 * BLOCK, BLOCK)] = low_attended.T.astype(BF)
        dots = jnp.sum(cot.astype(F32).T * low_attended, axis=0, keepdims=True)
        prob_grad = lax.dot_general(values, cot, NT, preferred_element_type=F32)
        image_grad = (image_prob * (prob_grad[TXT:] - dots)).astype(BF)
        if block >= 2:
            text_grad = (text_prob * (prob_grad[:TXT] - dots)).astype(BF)
            query_grad = lax.dot_general(
                keys[:TXT], text_grad, TN, preferred_element_type=F32
            ) + lax.dot_general(keys[TXT:], image_grad, TN, preferred_element_type=F32)
            query_grad = (query_grad * scaling).T.astype(BF)
            grads[i, slots, :, :, :HD] = query_grad.reshape(4, 2, ROWS, HD)
        key_part = jnp.dot(image_grad, query, preferred_element_type=F32)
        value_part = jnp.dot(image_low, cot, preferred_element_type=F32)
        if block == 0:
            key_acc[...] = key_part
            value_acc[...] = value_part
        elif block < 3:
            key_acc[...] += key_part
            value_acc[...] += value_part
        else:
            key_grad = ((key_acc[...] + key_part) * scaling).astype(BF)
            value_grad = (value_acc[...] + value_part).astype(BF)
            grads[i, :, :, :, HD : 2 * HD] = key_grad.reshape(8, 2, ROWS, HD)
            grads[i, :, :, :, 2 * HD :] = value_grad.reshape(8, 2, ROWS, HD)
            send(
                grads.at[i, :, p.co], both_grads.at[i, :, :, pair_cols], grads_sem.at[i],
                **partner
            )
            both_grads[i, :, :, :384] = grads[i, :, p.c]

    for i in range(2):
        step(f"proj{i}", i)(project)
        for block in range(4):
            step(f"att{i}{block}", i, block)(attend)

    def back_project(i, h):
        if h == 0:
            arrived(both_grads.at[i, :, :, pair_cols], grads_sem.at[i])
        for block in range(2 * h, 2 * h + 2):
            cols = pl.ds(block * 768, 768)
            product = lax.dot_general(
                both_grads[i].reshape(256, 768), wall[block], NT, preferred_element_type=F32
            ).astype(BF)
            pair_sum[i, :, :, :, cols] = product.reshape(2, 4, ROWS, 768)

    round_y = {
        (i, r): Scatter4(
            send,
            lambda y, h, i=i, r=r: pair_sum.at[i, :, y, part(r), half(h)],
            lambda h, i=i, r=r: ry_relay.at[i, h, :, part(r)],
            lambda h, i=i, r=r: ry_left.at[i, h, :, part(r)],
            lambda h, i=i, r=r: ry_right.at[i, h, :, part(r)],
            ry_sem.at[i * 2 + r],
            p.y,
            p.yl,
            p.yr,
            p.yo,
            to_y,
        )
        for i, r in chunks
    }

    def scatter_start(i, r):
        round_y[i, r].start(0)
        round_y[i, r].start(1)

    def scatter_direct(i, r):
        round_y[i, r].direct(1)
        round_y[i, r].direct(0)

    def y_sum(i, r, z, h):
        return (
            pair_sum[i, z, p.y, part(r), half(h)].astype(F32)
            + ry_left[i, h, z, part(r)].astype(F32)
            + ry_right[i, h, z, part(r)].astype(F32)
        )

    def scatter_cross(i, r):
        round_y[i, r].finish()
        for h in range(2):
            cross_out[i, part(r), half(h)] = y_sum(i, r, p.zo, h).astype(BF)
        send(
            cross_out.at[i, part(r)], cross_in.at[i, part(r)], cross_sem.at[i * 2 + r], **across
        )

    def norm_back(i, r):
        mine = jnp.concatenate([y_sum(i, r, p.z, h) for h in range(2)], axis=1)
        standard, reciprocal = standardise(hidden[i, part(r)])
        arrived(cross_in.at[i, part(r)], cross_sem.at[i * 2 + r])
        scaled = (mine + cross_in[i, part(r)].astype(F32)) * stretch[i : i + 1]
        residual_grad = reciprocal * (
            scaled
            - jnp.mean(scaled, axis=-1, keepdims=True)
            - standard * jnp.mean(scaled * standard, axis=-1, keepdims=True)
        )
        for c in range(2):
            rows_all[c, p.g, i, part(r)] = by_owner(residual_grad, c).astype(BF)
        if i == 0:
            rows_gather[0, r].start()

    def rows_at(c, g, i, n):
        if i:
            return rows_all.at[c, g, 1, :, pl.ds(n * 768, 768)]
        return rows_all.at[c, g, 0, part(n)]

    def rows_in_at(i, n):
        if i:
            return rows_in.at[:, 1, :, pl.ds(n * 768, 768)]
        return rows_in.at[:, 0, part(n)]

    every = slice(None)
    rows_gather = {
        (i, n): Gather4(
            send,
            lambda g, i=i, n=n: rows_at(every, g, i, n),
            lambda g, h, i=i, n=n: rows_at(h, g, i, n),
            gg_sem.at[i * 2 + n],
            p.g,
            p.gl,
            p.gr,
            p.go,
            to_g,
        )
        for i, n in chunks
    }

    def rows_start(n):
        if n:
            send.sent(rows_gather[1, 0].begun)
        rows_gather[1, n].start()

    def rows_finish(i, n):
        rows_gather[i, n].finish()
        send(rows_at(p.co, every, i, n), rows_in_at(i, n), rows_sem.at[i * 2 + n], **partner)

    for i in range(2):
        step(f"bpa{i}", i, 0)(back_project)
        step(f"bpb{i}", i, 1)(back_project)
        step(f"AS1{i}", i)(rows_start)
    for i, r in chunks:
        step(f"Bs{i}{r}", i, r)(scatter_start)
        step(f"Bd{i}{r}", i, r)(scatter_direct)
        for h in range(2):
            step(f"Bp{h}{i}{r}", h)(round_y[i, r].pass_on)
        step(f"BX{i}{r}", i, r)(scatter_cross)
        step(f"BL{i}{r}", i, r)(norm_back)
        step(f"AL{i}{r}")(rows_gather[i, r].pass_left)
        step(f"AR{i}{r}")(rows_gather[i, r].pass_right)
        step(f"Af{i}{r}", i, r)(rows_finish)

    def attn_pairs(to):
        near = pl.ds(pl.multiple_of((p.z * 8 + to) * ROWS, ROWS), ROWS)
        far = pl.ds(pl.multiple_of((p.zo * 8 + to) * ROWS, ROWS), ROWS)
        cols = pl.ds(pl.multiple_of(p.s * HD, HD), HD)
        staged = pl.ds(pl.multiple_of(q * HD, HD), HD)
        return (
            (attn.at[:, :, near], attn_out.at[:, :, :, cols], attn_recv.at[0]),
            (attn.at[:, :, far], ostage.at[:, :, :, staged], attn_recv.at[1]),
        )

    def attn_copies(k):
        to = (q + k) % 8
        return [
            pltpu.make_async_remote_copy(
                src_ref=src,
                dst_ref=dst,
                send_sem=attn_send.at[n, k],
                recv_sem=recv,
                device_id={"seq": p.z * 8 + to},
                device_id_type=MESH,
            )
            for n, (src, dst, recv) in enumerate(attn_pairs(to))
        ]

    @step("O1")
    def _():
        @pl.loop(1, 8)
        def _(k):
            for copy in attn_copies(k):
                copy.start()

        for src, dst, recv in attn_pairs(q):
            pltpu.make_async_copy(src, dst, recv).start()

    half_cols = pl.ds(pl.multiple_of(p.z * 1024, 1024), 1024)
    other_cols = pl.ds(pl.multiple_of(p.zo * 1024, 1024), 1024)

    @step("O2")
    def _():
        arrived(ostage, attn_recv.at[1])
        send(ostage, attn_out.at[:, :, :, half_cols], attn_recv.at[2], **across)

    def control_part(i):
        total = 0.0
        for c in range(2):
            total = total + lax.dot_general(
                rows_all[c, :, i].reshape(128, HALF),
                zw_owner[c],
                NT,
                preferred_element_type=F32,
            )
        control_grad[:, i] = total.astype(BF).reshape(4, ROWS, 768)

    def zero_part(i, block):
        cols = pl.ds(block * 384, 384)
        left = jnp.concatenate(
            [ref.reshape(128, 384) for ref in (rows_all[p.c, :, i, :, cols], rows_in[:, i, :, cols])]
        )
        right = jnp.concatenate([ctl[:, i].reshape(128, 768), ctl_in[:, i].reshape(128, 768)])
        product = lax.dot_general(left, right, TN, preferred_element_type=F32)
        if i == 0:
            zacc[cols] = product
        else:
            z, y = block // 2, block % 2 * 2
            zsum[z, pl.ds(y, 2)] = (zacc[cols] + product).astype(BF).reshape(2, 192, 768)

    step("ctl0", 0)(control_part)
    step("ctl1", 1)(control_part)

    @step("zp0")
    def _():
        arrived(ctl_in, share_sem.at[4])
        for n in range(2):
            arrived(rows_in_at(0, n), rows_sem.at[n])
        for block in range(4):
            zero_part(0, block)

    cols_a, cols_b = pl.ds(0, 384), pl.ds(384, 384)
    quarter = lambda d: pl.ds(pl.multiple_of(d * 48, 16), 48)
    round_x = Scatter4(
        send,
        lambda d, h: zsum.at[h, :, quarter(d), cols_a],
        lambda h: zx_relay.at[h],
        lambda h: zx_left.at[h],
        lambda h: zx_right.at[h],
        zx_sem,
        p.d,
        p.dl,
        p.dr,
        p.do,
        to_d,
    )
    zero_y = Scatter4(
        send,
        lambda y, h: zsum.at[h, y, :, cols_b],
        lambda h: zy_relay.at[h],
        lambda h: zy_left.at[h],
        lambda h: zy_right.at[h],
        zy_sem,
        p.y,
        p.yl,
        p.yr,
        p.yo,
        to_y,
    )
    def zero_send(z):
        arrived(rows_in_at(1, z), rows_sem.at[2 + z])
        zero_part(1, 2 * z)
        zero_part(1, 2 * z + 1)
        round_x.start(z)
        zero_y.start(z)
        round_x.direct(z)
        zero_y.direct(z)

    step("zp1a", 0)(zero_send)
    step("zp1b", 1)(zero_send)
    for h in range(2):
        step(f"Zp{h}x", h)(round_x.pass_on)
        step(f"Zp{h}y", h)(zero_y.pass_on)
    others = [(dz, dy) for dz in range(2) for dy in range(4) if dz or dy]

    @step("ZA")
    def _():
        round_x.finish()
        for z in range(2):
            za_out[z] = (
                zsum[z, :, quarter(p.d), cols_a].astype(F32)
                + zx_left[z].astype(F32)
                + zx_right[z].astype(F32)
            ).astype(BF)
        for n, (dz, dy) in enumerate(others):
            z, y = (p.z + dz) % 2, (p.y + dy) % 4
            send(za_out.at[z, y], za_in.at[n], za_sem.at[n], seq=p.seq(z, y, p.c))

    @step("ZB")
    def _():
        zero_y.finish()
        for z in range(2):
            zb_out[z] = (
                (
                    zsum[z, p.y, :, cols_b].astype(F32)
                    + zy_left[z].astype(F32)
                    + zy_right[z].astype(F32)
                )
                .astype(BF)
                .reshape(4, 48, 384)
            )
        for n, (dz, dd) in enumerate(others):
            z, d = (p.z + dz) % 2, (p.d + dd) % 4
            send(zb_out.at[z, d], zb_in.at[n], zb_sem.at[n], seq=p.seq(z, p.y, p.c), dp=d)

    zero_gather = Gather4(
        send,
        lambda d: zall.at[d],
        lambda d, h: zall.at[d, :, pl.ds(h * 384, 384)],
        zg_sem,
        p.d,
        p.dl,
        p.dr,
        p.do,
        to_d,
    )

    @step("ZS")
    def _():
        total = za_out[p.z, p.y].astype(F32)
        for n in range(7):
            arrived(za_in.at[n], za_sem.at[n])
            total = total + za_in[n].astype(F32)
        zall[p.d, :, cols_a] = total.astype(BF)
        total = zb_out[p.z, p.d].astype(F32)
        for n in range(7):
            arrived(zb_in.at[n], zb_sem.at[n])
            total = total + zb_in[n].astype(F32)
        zall[p.d, :, cols_b] = total.astype(BF)
        zero_gather.start()

    step("zgL_")(zero_gather.pass_left)
    step("zgR_")(zero_gather.pass_right)

    for name in ORDER:
        steps.pop(name)()
    assert not steps

    zero_gather.finish()
    zero_out[...] = zall[...].reshape(192, 768).astype(F32) * (16384 ** (-0.5))

    arrived(attn_out.at[:, :, :, half_cols], attn_recv.at[0])
    arrived(attn_out.at[:, :, :, other_cols], attn_recv.at[2])
    send.drain()

    @pl.loop(1, 8)
    def _(k):
        for i in range(2):
            for copy in text_copies(i, k):
                copy.wait_send()
        for copy in attn_copies(k):
            copy.wait_send()


def whole_block(*operands):
    dma = pltpu.SemaphoreType.DMA
    bf = lambda *shape: pltpu.VMEM(shape, BF)
    return pl.pallas_call(
        block_kernel,
        out_shape=(
            jax.ShapeDtypeStruct((2, 2, ROWS, HEADS * HD), BF),
            jax.ShapeDtypeStruct((4, 2, ROWS, 768), BF),
            jax.ShapeDtypeStruct((192, 768), F32),
        ),
        in_specs=[pl.BlockSpec(memory_space=pltpu.SMEM)] * 2 + [ANY] * 8,
        out_specs=(VMEM, VMEM, VMEM),
        scratch_shapes=[
            bf(4, 2, ROWS, 768),
            bf(4, 2, ROWS, 768),
            bf(768, D),
            bf(2, 768, HALF),
            bf(2, ROWS, D),
            bf(4, 768, 768),
            pltpu.VMEM((2, D), F32),
            pltpu.VMEM((2, D), F32),
            bf(4, 2, ROWS, D),
            bf(2, 2, ROWS, HALF),
            bf(2, 2, ROWS, HALF),
            bf(2, 2, ROWS, HALF),
            bf(2, ROWS, D),
            bf(2, 2, 4, ROWS, D),
            bf(2, 3, 8, ROWS, HD),
            bf(3, 2, 2, 8, 2, ROWS, HD),
            bf(2, 2, 8, 2, ROWS, HD),
            bf(3, 2, 4, 2, ROWS, HD),
            bf(2, 2, 4, 2, ROWS, HD),
            bf(2, 2, 512, HD),
            bf(2, 2, ROWS, 1024),
            bf(2, 8, 2, ROWS, 384),
            bf(2, 8, ROWS, 768),
            pltpu.VMEM((IMG, HD), F32),
            pltpu.VMEM((IMG, HD), F32),
            bf(2, 2, 4, ROWS, D),
            bf(2, 2, 2, ROWS, HALF),
            bf(2, 2, 2, ROWS, HALF),
            bf(2, 2, 2, ROWS, HALF),
            bf(2, ROWS, D),
            bf(2, ROWS, D),
            bf(2, 4, 2, ROWS, HALF),
            bf(4, 2, ROWS, HALF),
            pltpu.VMEM((HALF, 768), F32),
            bf(2, 4, 192, 768),
            bf(2, 4, 48, 384),
            bf(2, 4, 48, 384),
            bf(2, 4, 48, 384),
            bf(2, 192, 384),
            bf(2, 192, 384),
            bf(2, 192, 384),
            bf(2, 4, 48, 384),
            bf(2, 4, 48, 384),
            bf(7, 48, 384),
            bf(7, 48, 384),
            bf(4, 48, 768),
            bf(3, 2, ROWS, HEADS * HD),
            bf(2, 2, ROWS, HEADS * HD),
            dma((32,)),
            dma((224,)),
            dma((4,)),
            dma((5,)),
            dma((4, 6)),
            dma((4, 9)),
            dma((4, 2, 8)),
            dma((2, 2)),
            dma((2, 2)),
            dma((2, 2)),
            dma((2,)),
            dma((2,)),
            dma((4, 6)),
            dma((4,)),
            dma((4, 4)),
            dma((4,)),
            dma((2, 8)),
            dma((3,)),
            dma((6,)),
            dma((6,)),
            dma((7,)),
            dma((7,)),
            dma((4,)),
        ],
        compiler_params=pltpu.CompilerParams(
            collective_id=1, has_side_effects=True, vmem_limit_bytes=VMEM_LIMIT
        ),
        name="whole_block",
    )(*operands)


def hand_over_kernel(attn, control, zero, image_out, text_out, control_out, zero_out, sems):
    copies = [
        pltpu.make_async_copy(src, dst, sems.at[n])
        for n, (src, dst) in enumerate(
            (
                (attn.at[1], image_out),
                (attn.at[0], text_out),
                (control, control_out),
                (zero, zero_out),
            )
        )
    ]
    for copy in copies:
        copy.start()
    for copy in copies:
        copy.wait()


def hand_over(attn, control, zero):
    return pl.pallas_call(
        hand_over_kernel,
        out_shape=(
            jax.ShapeDtypeStruct(attn.shape[1:], BF),
            jax.ShapeDtypeStruct(attn.shape[1:], BF),
            jax.ShapeDtypeStruct(control.shape, BF),
            jax.ShapeDtypeStruct(zero.shape, F32),
        ),
        in_specs=[VMEM] * 3,
        out_specs=(ANY,) * 4,
        scratch_shapes=[pltpu.SemaphoreType.DMA((4,))],
        name="hand_over",
    )(attn, control, zero)


def body(
    image_hidden,
    control_hidden,
    text_qkv,
    text_lengths,
    timesteps,
    mod_weight,
    qkv_weight,
    zero_weight,
    image_cotangent,
    text_cotangent,
):
    attn_out, control_grad, zero_t = whole_block(
        text_lengths.reshape(2),
        timesteps.reshape(2),
        mod_weight,
        control_hidden.reshape(4, 2, ROWS, 768),
        zero_weight,
        image_hidden.reshape(2, ROWS, D),
        jnp.transpose(qkv_weight, (1, 0, 2)),
        text_qkv.reshape(3, 2, ROWS, HEADS * HD),
        text_cotangent.reshape(2, ROWS, HEADS * HD),
        image_cotangent.reshape(2, ROWS, HEADS * HD),
    )
    image_attn, text_attn, control_grad, zero_t = hand_over(attn_out, control_grad, zero_t)
    return (
        image_attn.reshape(2, 1, ROWS, HEADS * HD),
        text_attn.reshape(2, 1, ROWS, HEADS * HD),
        control_grad.reshape(8, 1, ROWS, 768),
        jnp.transpose(zero_t),
    )


def solution(mesh):
    placed = (
        P("grp", "dp", "seq", None),
        P(None, "dp", "seq", "grp"),
        P(None, "grp", "dp", "seq", None),
        P("grp", "dp"),
        P("grp", "dp"),
        P(),
        P("dp", None, "seq"),
        P("grp", None),
        P("grp", "dp", "seq", None),
        P("grp", "dp", "seq", None),
    )
    return jax.shard_map(
        body,
        mesh=mesh,
        in_specs=placed,
        out_specs=(
            P("grp", "dp", "seq", None),
            P("grp", "dp", "seq", None),
            P(None, "dp", "seq", "grp"),
            P("grp", "seq"),
        ),
        check_vma=False,
    )
```

```python
import math

import jax
import jax.numpy as jnp
from jax import lax
from jax.experimental import pallas as pl
from jax.experimental.pallas import tpu as pltpu
from jax.sharding import PartitionSpec as P

D = 3072
HEADS = 16
HD = 128
IMG = 512
TXT = 512
FREQ = 256
ROWS = 32
HALF = D // 2
MESH = pl.DeviceIdType.MESH
BF = jnp.bfloat16
F32 = jnp.float32
VMEM_LIMIT = 60 * 1024 * 1024
ANY = pl.BlockSpec(memory_space=pl.ANY)
VMEM = pl.BlockSpec(memory_space=pltpu.VMEM)


class Sends:
    def __init__(self, sems):
        self.sems = sems
        self.copies = []
        self.started = 0

    def __call__(self, src, dst, recv, **to):
        copy = pltpu.make_async_remote_copy(
            src_ref=src,
            dst_ref=dst,
            send_sem=self.sems.at[self.started],
            recv_sem=recv,
            device_id=to,
            device_id_type=MESH,
        )
        copy.start()
        self.started += 1
        self.copies.append(copy)
        return copy

    def sent(self, copies):
        for copy in copies:
            copy.wait_send()
        waited = [id(copy) for copy in copies]
        self.copies = [copy for copy in self.copies if id(copy) not in waited]

    def drain(self):
        self.sent(list(self.copies))


def arrived(dst, recv):
    pltpu.make_async_copy(dst, dst, recv).wait()


def greet(groups):
    barrier = pltpu.get_barrier_semaphore()
    for to in groups:
        pl.semaphore_signal(barrier, inc=1, device_id=to, device_id_type=MESH)
    return lambda: pl.semaphore_wait(barrier, len(groups))


class Place:
    def __init__(self):
        self.s = lax.axis_index("seq")
        self.g = lax.axis_index("grp")
        self.d = lax.axis_index("dp")
        self.z = self.s // 8
        self.y = (self.s // 2) % 4
        self.c = self.s % 2
        self.zo = 1 - self.z
        self.co = 1 - self.c
        self.yl = (self.y + 3) % 4
        self.yr = (self.y + 1) % 4
        self.yo = (self.y + 2) % 4
        self.gl = (self.g + 3) % 4
        self.gr = (self.g + 1) % 4
        self.go = (self.g + 2) % 4
        self.dl = (self.d + 3) % 4
        self.dr = (self.d + 1) % 4
        self.do = (self.d + 2) % 4

    def seq(self, z, y, c):
        return z * 8 + y * 2 + c


def add_into(dst, *others):
    total = dst[...].astype(F32)
    for other in others:
        total = total + other[...].astype(F32)
    dst[...] = total.astype(dst.dtype)


class Scatter4:
    def __init__(self, send, src, relay, from_left, from_right, sems, me, left, right, far, to):
        self.send, self.src, self.relay = send, src, relay
        self.from_left, self.from_right, self.sems = from_left, from_right, sems
        self.me, self.left, self.right, self.far, self.to = me, left, right, far, to
        self.passed = []

    def start(self, h):
        to = (self.left, self.right)[h]
        self.send(self.src(self.far, h), self.relay(h), self.sems.at[h], **self.to(to))

    def direct(self, h):
        if h:
            dst, to = self.from_right(1), self.left
        else:
            dst, to = self.from_left(0), self.right
        self.send(self.src(to, h), dst, self.sems.at[3 - h], **self.to(to))

    def pass_on(self, h):
        arrived(self.relay(h), self.sems.at[h])
        if h:
            dst, to = self.from_left(1), self.right
        else:
            dst, to = self.from_right(0), self.left
        add_into(self.src(to, h), self.relay(h))
        self.passed.append(self.send(self.src(to, h), dst, self.sems.at[4 + h], **self.to(to)))

    def finish(self):
        arrived(self.from_right(1), self.sems.at[2])
        arrived(self.from_left(0), self.sems.at[3])
        arrived(self.from_right(0), self.sems.at[4])
        arrived(self.from_left(1), self.sems.at[5])


class Gather4:
    def __init__(self, send, slot, half, sems, me, left, right, far, to):
        self.send, self.slot, self.half, self.sems = send, slot, half, sems
        self.me, self.left, self.right, self.far, self.to = me, left, right, far, to

    def start(self, own=None):
        own = self.slot(self.me) if own is None else own
        self.begun = [
            self.send(own, self.slot(self.me), self.sems.at[0], **self.to(self.right)),
            self.send(own, self.slot(self.me), self.sems.at[1], **self.to(self.left)),
        ]

    def pass_left(self):
        arrived(self.slot(self.left), self.sems.at[0])
        part = self.half(self.left, 0)
        self.send(part, part, self.sems.at[2], **self.to(self.right))

    def pass_right(self):
        arrived(self.slot(self.right), self.sems.at[1])
        part = self.half(self.right, 1)
        self.send(part, part, self.sems.at[3], **self.to(self.left))

    def finish(self):
        arrived(self.half(self.far, 0), self.sems.at[2])
        arrived(self.half(self.far, 1), self.sems.at[3])


ORDER = (
    "res0", "res1", "Rs00", "T10", "Ws", "mod", "Rp000", "Rp100", "Rs01", "LN00", "GL000",
    "GR000", "Rp001", "Rp101", "WL", "WR_", "Gz00", "Rs10", "LN01", "T20", "T11", "GR001",
    "GL001", "Wf", "Rp010", "Rp110", "Gz01", "Rs11", "LN10", "GL010", "GR010", "GR011", "GL011",
    "GL100", "GR100", "Rp011", "Rp111", "proj0", "Gz10", "LN11", "att00", "att01", "GL101",
    "Gz11", "att02", "att03", "T21", "GL110", "GR101", "GR110", "GR111", "bpa0", "GL111", "bpb0",
    "Bs00", "Bd00", "proj1", "Bp100", "Bp000", "att10", "Bs01", "att11", "att12", "Bd01", "att13",
    "BX00", "Bp101", "Bp001", "bpa1", "bpb1", "Bs10", "Bd10", "BL00", "BX01", "Bp110", "Bp010",
    "Bs11", "Bd11", "AL00", "AR00", "BL01", "zwo", "Af00", "Bp111", "BX10", "Bp011", "AL01",
    "AR01", "BX11", "O1", "BL10", "Af01", "ctl0", "BL11", "AS10", "zp0", "AS11", "AL10", "AR10",
    "Af10", "AL11", "AR11", "zp1a", "Af11", "ctl1", "zp1b", "Zp0y", "Zp0x", "O2", "Zp1x", "Zp1y",
    "ZA", "ZB", "ZS", "zgL_", "zgR_",
)
NT = (((1,), (1,)), ((), ()))
TN = (((0,), (0,)), ((), ()))
BLOCK = 256


def by_owner(columns, c):
    runs = columns.shape[1] // 384
    return jnp.concatenate(
        [columns[:, n * 384 + c * 192 : n * 384 + c * 192 + 192] for n in range(runs)], axis=1
    )


def block_kernel(
    lengths,
    timesteps,
    mod_weight,
    control,
    zero_weight,
    image_hidden,
    weight,
    text,
    text_cot,
    image_cot,
    attn_out,
    control_grad,
    zero_out,
    ctl,
    ctl_in,
    zw,
    zw_owner,
    base,
    wall,
    offset,
    stretch,
    partial,
    rg_relay,
    rg_left,
    rg_right,
    hidden,
    normed,
    qkv_out,
    joint,
    cots,
    tstage,
    cstage,
    attn,
    ostage,
    grads,
    both_grads,
    key_acc,
    value_acc,
    pair_sum,
    ry_relay,
    ry_left,
    ry_right,
    cross_out,
    cross_in,
    rows_all,
    rows_in,
    zacc,
    zsum,
    zx_relay,
    zx_left,
    zx_right,
    zy_relay,
    zy_left,
    zy_right,
    za_out,
    zb_out,
    za_in,
    zb_in,
    zall,
    text_mine,
    cots_mine,
    load_sem,
    send_sem,
    w_sem,
    share_sem,
    rg_sem,
    ag_sem,
    text_send,
    text_recv,
    stage_recv,
    cross_recv,
    qkv_sem,
    grads_sem,
    ry_sem,
    cross_sem,
    gg_sem,
    rows_sem,
    attn_send,
    attn_recv,
    zx_sem,
    zy_sem,
    za_sem,
    zb_sem,
    zg_sem,
):
    p = Place()
    send = Sends(send_sem)
    q = p.y * 2 + p.c
    partner = {"seq": p.seq(p.z, p.y, p.co)}
    across = {"seq": p.seq(p.zo, p.y, p.c)}
    to_y = lambda y: {"seq": p.seq(p.z, y, p.c)}
    to_g = lambda g: {"grp": g}
    to_d = lambda d: {"dp": d}

    all_here = greet(
        [{"seq": (p.s + k) % 16} for k in range(1, 16)]
        + [{"grp": p.gl}, {"grp": p.gr}]
        + [{"dp": (p.d + k) % 4} for k in range(1, 4)]
        + [{"dp": (p.d + k) % 4, "seq": p.seq(p.zo, p.y, p.c)} for k in range(1, 4)]
    )

    loads = []

    def load(src, dst):
        copy = pltpu.make_async_copy(src, dst, load_sem.at[len(loads)])
        copy.start()
        loads.append(copy)
        return copy

    load_control = load(control, ctl)
    load_zero = [
        load(zero_weight.at[:, pl.ds(n * 512, 512)], zw.at[:, pl.ds(n * 512, 512)])
        for n in range(6)
    ]
    load_weight = [
        load(weight.at[n], wall.at[p.d, :, pl.ds(n * HD, HD)]) for n in range(3)
    ]
    load_text = [
        load(text, text_mine),
        load(text_cot, cots_mine.at[0]),
        load(image_cot, cots_mine.at[1]),
    ]
    load_base = load(image_hidden, base)
    load_mod = [
        load(
            mod_weight.at[pl.ds(n % 8 * ROWS, ROWS), pl.ds(n // 8 * D, D)],
            pair_sum.at[n // 8, n // 4 % 2, n % 4],
        )
        for n in range(16)
    ]

    half = lambda h: pl.ds(h * HALF, HALF)
    part = lambda r: pl.ds(r * 16, 16)
    chunks = [(i, r) for i in range(2) for r in range(2)]
    steps = {}

    def step(name, *args):
        def add(f):
            steps[name] = lambda: f(*args)
            return f

        return add

    def residual_part(h):
        if h == 0:
            load_control.wait()
        for block in range(3 * h, 3 * h + 3):
            cols = pl.ds(block * 512, 512)
            load_zero[block].wait()
            product = jnp.dot(
                ctl[...].reshape(256, 768), zw[:, cols], preferred_element_type=F32
            )
            partial[:, :, :, cols] = product.astype(BF).reshape(4, 2, ROWS, 512)
        if h == 0:
            all_here()
            to_group[0, 0].start(0)
            to_group[0, 0].direct(0)

    step("res0", 0)(residual_part)
    step("res1", 1)(residual_part)

    to_group = {
        (i, r): Scatter4(
            send,
            lambda g, h, i=i, r=r: partial.at[g, i, part(r), half(h)],
            lambda h, i=i, r=r: rg_relay.at[i, h, part(r)],
            lambda h, i=i, r=r: rg_left.at[i, h, part(r)],
            lambda h, i=i, r=r: rg_right.at[i, h, part(r)],
            rg_sem.at[i * 2 + r],
            p.g,
            p.gl,
            p.gr,
            p.go,
            to_g,
        )
        for i, r in chunks
    }

    def group_start(n):
        if n:
            send.sent(to_group[chunks[n - 1]].passed)
        scatter = to_group[chunks[n]]
        for h in range(0 if n else 1, 2):
            scatter.start(h)
        scatter.direct(1)
        if n:
            scatter.direct(0)

    for n, (i, r) in enumerate(chunks):
        step(f"Rs{i}{r}", n)(group_start)
        for h in range(2):
            step(f"Rp{h}{i}{r}", h)(to_group[i, r].pass_on)

    plane = pl.ds(p.z * 4, 4)
    other_plane = pl.ds(p.zo * 4, 4)
    zy = p.z * 4 + p.y

    def text_pairs(i, to):
        near = pl.ds(pl.multiple_of((p.z * 8 + to) * HD, HD), HD)
        far = pl.ds(pl.multiple_of((p.zo * 8 + to) * HD, HD), HD)
        return (
            (text_mine.at[:, i, :, far], tstage.at[:, i, p.y, p.c], stage_recv.at[0, i]),
            (cots_mine.at[:, i, :, far], cstage.at[:, i, p.y, p.c], stage_recv.at[1, i]),
            (text_mine.at[:, i, :, near], joint.at[:, i, 0, zy, p.c], text_recv.at[0, i]),
            (cots_mine.at[:, i, :, near], cots.at[:, i, zy, p.c], text_recv.at[1, i]),
        )

    def text_copies(i, k):
        to = (q + k) % 8
        return [
            pltpu.make_async_remote_copy(
                src_ref=src,
                dst_ref=dst,
                send_sem=text_send.at[n, i, k],
                recv_sem=recv,
                device_id={"seq": p.z * 8 + to},
                device_id_type=MESH,
            )
            for n, (src, dst, recv) in enumerate(text_pairs(i, to))
        ]

    def text_first_hop(i):
        if i == 0:
            for copy in load_text:
                copy.wait()

        @pl.loop(1, 8)
        def _(k):
            for copy in text_copies(i, k):
                copy.start()

        for src, dst, recv in text_pairs(i, q):
            pltpu.make_async_copy(src, dst, recv).start()

    def text_second_hop(i):
        arrived(tstage.at[:, i], stage_recv.at[0, i])
        arrived(cstage.at[:, i], stage_recv.at[1, i])
        send(tstage.at[:, i], joint.at[:, i, 0, plane], cross_recv.at[i, 0], **across)
        send(cstage.at[:, i], cots.at[:, i, plane], cross_recv.at[i, 1], **across)

    def text_wait(i):
        arrived(joint.at[:, i, 0, plane], text_recv.at[0, i])
        arrived(cots.at[:, i, plane], text_recv.at[1, i])
        arrived(joint.at[:, i, 0, other_plane], cross_recv.at[i, 0])
        arrived(cots.at[:, i, other_plane], cross_recv.at[i, 1])

    for i in range(2):
        step(f"T1{i}", i)(text_first_hop)
        step(f"T2{i}", i)(text_second_hop)

    mine_cols, pair_cols = pl.ds(0, 384), pl.ds(384, 384)
    weights = Gather4(
        send,
        lambda d: wall.at[d, :, mine_cols],
        lambda d, h: wall.at[d, pl.ds(h * 384, 384), mine_cols],
        w_sem,
        p.d,
        p.dl,
        p.dr,
        p.do,
        to_d,
    )

    def share_weight(d, sem):
        send(wall.at[d, :, mine_cols], wall.at[d, :, pair_cols], share_sem.at[sem], **partner)

    @step("Ws")
    def _():
        for copy in load_weight:
            copy.wait()
        weights.start()
        share_weight(p.d, 0)
        send(ctl, ctl_in, share_sem.at[4], **partner)

    @step("WL")
    def _():
        weights.pass_left()
        share_weight(p.dl, 1)

    @step("WR_")
    def _():
        weights.pass_right()
        share_weight(p.dr, 2)

    @step("Wf")
    def _():
        weights.finish()
        share_weight(p.do, 3)

    @step("mod")
    def _():
        for copy in load_mod:
            copy.wait()
        lane = lax.broadcasted_iota(jnp.int32, (1, FREQ // 2), 1).astype(F32)
        frequency = jnp.exp(lane * (-math.log(10000.0) / (FREQ // 2)))
        angles = jnp.concatenate([timesteps[i].astype(F32) * frequency for i in range(2)])
        embedding = jnp.concatenate([jnp.cos(angles), jnp.sin(angles)], axis=1)
        activated = (embedding / (1.0 + jnp.exp(-embedding))).astype(BF)
        offset[...] = jnp.dot(
            activated, pair_sum[0].reshape(FREQ, D), preferred_element_type=F32
        )
        stretch[...] = 1.0 + jnp.dot(
            activated, pair_sum[1].reshape(FREQ, D), preferred_element_type=F32
        )
        load_base.wait()

    @step("zwo")
    def _():
        for block in range(4):
            columns = zw[:, pl.ds(block * 768, 768)].astype(F32)
            for c in range(2):
                zw_owner[c, :, pl.ds(block * 384, 384)] = by_owner(columns, c).astype(BF)

    gathers = {
        (i, r, which): Gather4(
            send,
            lambda y, i=i, r=r, z=z: normed.at[i, z, y, part(r)],
            lambda y, h, i=i, r=r, z=z: normed.at[i, z, y, part(r), half(h)],
            ag_sem.at[i * 2 + r, pl.ds(which * 4, 4)],
            p.y,
            p.yl,
            p.yr,
            p.yo,
            to_y,
        )
        for i, r in chunks
        for which, z in enumerate((p.z, p.zo))
    }

    def standardise(rows):
        values = rows.astype(F32)
        average = jnp.mean(values, axis=-1, keepdims=True)
        centred = values - average
        reciprocal = lax.rsqrt(jnp.mean(centred * centred, axis=-1, keepdims=True) + 1e-06)
        return centred * reciprocal, reciprocal

    def gather_first(i, r):
        to_group[i, r].finish()
        rows = part(r)
        for h in range(2):
            residual = (
                partial[p.g, i, rows, half(h)].astype(F32)
                + rg_left[i, h, rows].astype(F32)
                + rg_right[i, h, rows].astype(F32)
            )
            hidden[i, rows, half(h)] = (base[i, rows, half(h)].astype(F32) + residual).astype(BF)
        standard, _ = standardise(hidden[i, rows])
        normed[i, p.z, p.y, rows] = (
            standard * stretch[i : i + 1] + offset[i : i + 1]
        ).astype(BF)
        mine = normed.at[i, p.z, p.y, rows]
        send(mine, mine, ag_sem.at[i * 2 + r, 8], **across)
        gathers[i, r, 0].start()

    def gather_second(i, r):
        arrived(normed.at[i, p.zo, p.y, part(r)], ag_sem.at[i * 2 + r, 8])
        gathers[i, r, 1].start()

    for i, r in chunks:
        step(f"LN{i}{r}", i, r)(gather_first)
        step(f"Gz{i}{r}", i, r)(gather_second)
        for which in range(2):
            step(f"GL{i}{r}{which}")(gathers[i, r, which].pass_left)
            step(f"GR{i}{r}{which}")(gathers[i, r, which].pass_right)

    scaling = HD ** (-0.5)
    position = lax.broadcasted_iota(jnp.int32, (1, TXT + IMG), 1)

    def project(i):
        for r in range(2):
            for which in range(2):
                gathers[i, r, which].finish()
        if i == 0:
            for n, d in enumerate((p.d, p.dl, p.dr, p.do)):
                arrived(wall.at[d, :, pair_cols], share_sem.at[n])
        product = jnp.dot(
            normed[i].reshape(256, D), wall[...].reshape(D, 768), preferred_element_type=F32
        ).astype(BF)
        for n in range(3):
            qkv_out[i, n] = product[:, 384 + n * HD : 384 + (n + 1) * HD].reshape(8, ROWS, HD)
        send(qkv_out.at[i], joint.at[:, i, 1, :, p.c], qkv_sem.at[i], **partner)
        for n in range(3):
            joint[n, i, 1, :, p.c] = product[:, n * HD : (n + 1) * HD].reshape(8, ROWS, HD)

    def attend(i, block):
        if block == 0:
            text_wait(i)
            arrived(joint.at[:, i, 1, :, p.co], qkv_sem.at[i])
        slots = pl.ds(block % 2 * 4, 4)
        bias = jnp.where((position >= TXT) | (position < lengths[i]), 0.0, -jnp.inf)
        query = joint[0, i, block // 2, slots].reshape(BLOCK, HD)
        cot = cots[block // 2, i, slots].reshape(BLOCK, HD)
        keys = joint[1, i].reshape(TXT + IMG, HD)
        values = joint[2, i].reshape(TXT + IMG, HD)
        scores = lax.dot_general(query, keys, NT, preferred_element_type=F32) + bias
        row_max = jnp.max(scores, axis=1, keepdims=True)
        terms = jnp.exp2((scores - row_max) * (scaling * math.log2(math.e)))
        prob = terms * (1.0 / jnp.sum(terms, axis=1, keepdims=True))
        low = prob.astype(BF)
        attended = jnp.dot(low, values, preferred_element_type=F32).astype(BF)
        attn[block // 2, i, pl.ds(block % 2 * BLOCK, BLOCK)] = attended
        dots = jnp.sum(cot.astype(F32) * attended.astype(F32), axis=1, keepdims=True)
        prob_grad = lax.dot_general(cot, values, NT, preferred_element_type=F32)
        score_grad = (prob * (prob_grad - dots)).astype(BF)
        if block >= 2:
            query_grad = jnp.dot(score_grad, keys, preferred_element_type=F32) * scaling
            grads[i, slots, :, :, :HD] = query_grad.astype(BF).reshape(4, 2, ROWS, HD)
        key_part = lax.dot_general(score_grad[:, TXT:], query, TN, preferred_element_type=F32)
        value_part = lax.dot_general(low[:, TXT:], cot, TN, preferred_element_type=F32)
        if block == 0:
            key_acc[...] = key_part
            value_acc[...] = value_part
        elif block < 3:
            key_acc[...] += key_part
            value_acc[...] += value_part
        else:
            key_grad = ((key_acc[...] + key_part) * scaling).astype(BF)
            value_grad = (value_acc[...] + value_part).astype(BF)
            grads[i, :, :, :, HD : 2 * HD] = key_grad.reshape(8, 2, ROWS, HD)
            grads[i, :, :, :, 2 * HD :] = value_grad.reshape(8, 2, ROWS, HD)
            send(
                grads.at[i, :, p.co], both_grads.at[i, :, :, pair_cols], grads_sem.at[i],
                **partner
            )
            both_grads[i, :, :, :384] = grads[i, :, p.c]

    for i in range(2):
        step(f"proj{i}", i)(project)
        for block in range(4):
            step(f"att{i}{block}", i, block)(attend)

    def back_project(i, h):
        if h == 0:
            arrived(both_grads.at[i, :, :, pair_cols], grads_sem.at[i])
        for block in range(2 * h, 2 * h + 2):
            cols = pl.ds(block * 768, 768)
            product = lax.dot_general(
                both_grads[i].reshape(256, 768), wall[block], NT, preferred_element_type=F32
            ).astype(BF)
            pair_sum[i, :, :, :, cols] = product.reshape(2, 4, ROWS, 768)

    round_y = {
        (i, r): Scatter4(
            send,
            lambda y, h, i=i, r=r: pair_sum.at[i, :, y, part(r), half(h)],
            lambda h, i=i, r=r: ry_relay.at[i, h, :, part(r)],
            lambda h, i=i, r=r: ry_left.at[i, h, :, part(r)],
            lambda h, i=i, r=r: ry_right.at[i, h, :, part(r)],
            ry_sem.at[i * 2 + r],
            p.y,
            p.yl,
            p.yr,
            p.yo,
            to_y,
        )
        for i, r in chunks
    }

    def scatter_start(i, r):
        round_y[i, r].start(0)
        round_y[i, r].start(1)

    def scatter_direct(i, r):
        round_y[i, r].direct(1)
        round_y[i, r].direct(0)

    def y_sum(i, r, z, h):
        return (
            pair_sum[i, z, p.y, part(r), half(h)].astype(F32)
            + ry_left[i, h, z, part(r)].astype(F32)
            + ry_right[i, h, z, part(r)].astype(F32)
        )

    def scatter_cross(i, r):
        round_y[i, r].finish()
        for h in range(2):
            cross_out[i, part(r), half(h)] = y_sum(i, r, p.zo, h).astype(BF)
        send(
            cross_out.at[i, part(r)], cross_in.at[i, part(r)], cross_sem.at[i * 2 + r], **across
        )

    def norm_back(i, r):
        mine = jnp.concatenate([y_sum(i, r, p.z, h) for h in range(2)], axis=1)
        standard, reciprocal = standardise(hidden[i, part(r)])
        arrived(cross_in.at[i, part(r)], cross_sem.at[i * 2 + r])
        scaled = (mine + cross_in[i, part(r)].astype(F32)) * stretch[i : i + 1]
        residual_grad = reciprocal * (
            scaled
            - jnp.mean(scaled, axis=-1, keepdims=True)
            - standard * jnp.mean(scaled * standard, axis=-1, keepdims=True)
        )
        for c in range(2):
            rows_all[c, p.g, i, part(r)] = by_owner(residual_grad, c).astype(BF)
        if i == 0:
            rows_gather[0, r].start()

    def rows_at(c, g, i, n):
        if i:
            return rows_all.at[c, g, 1, :, pl.ds(n * 768, 768)]
        return rows_all.at[c, g, 0, part(n)]

    def rows_in_at(i, n):
        if i:
            return rows_in.at[:, 1, :, pl.ds(n * 768, 768)]
        return rows_in.at[:, 0, part(n)]

    every = slice(None)
    rows_gather = {
        (i, n): Gather4(
            send,
            lambda g, i=i, n=n: rows_at(every, g, i, n),
            lambda g, h, i=i, n=n: rows_at(h, g, i, n),
            gg_sem.at[i * 2 + n],
            p.g,
            p.gl,
            p.gr,
            p.go,
            to_g,
        )
        for i, n in chunks
    }

    def rows_start(n):
        if n:
            send.sent(rows_gather[1, 0].begun)
        rows_gather[1, n].start()

    def rows_finish(i, n):
        rows_gather[i, n].finish()
        send(rows_at(p.co, every, i, n), rows_in_at(i, n), rows_sem.at[i * 2 + n], **partner)

    for i in range(2):
        step(f"bpa{i}", i, 0)(back_project)
        step(f"bpb{i}", i, 1)(back_project)
        step(f"AS1{i}", i)(rows_start)
    for i, r in chunks:
        step(f"Bs{i}{r}", i, r)(scatter_start)
        step(f"Bd{i}{r}", i, r)(scatter_direct)
        for h in range(2):
            step(f"Bp{h}{i}{r}", h)(round_y[i, r].pass_on)
        step(f"BX{i}{r}", i, r)(scatter_cross)
        step(f"BL{i}{r}", i, r)(norm_back)
        step(f"AL{i}{r}")(rows_gather[i, r].pass_left)
        step(f"AR{i}{r}")(rows_gather[i, r].pass_right)
        step(f"Af{i}{r}", i, r)(rows_finish)

    def attn_pairs(to):
        near = pl.ds(pl.multiple_of((p.z * 8 + to) * ROWS, ROWS), ROWS)
        far = pl.ds(pl.multiple_of((p.zo * 8 + to) * ROWS, ROWS), ROWS)
        cols = pl.ds(pl.multiple_of(p.s * HD, HD), HD)
        staged = pl.ds(pl.multiple_of(q * HD, HD), HD)
        return (
            (attn.at[:, :, near], attn_out.at[:, :, :, cols], attn_recv.at[0]),
            (attn.at[:, :, far], ostage.at[:, :, :, staged], attn_recv.at[1]),
        )

    def attn_copies(k):
        to = (q + k) % 8
        return [
            pltpu.make_async_remote_copy(
                src_ref=src,
                dst_ref=dst,
                send_sem=attn_send.at[n, k],
                recv_sem=recv,
                device_id={"seq": p.z * 8 + to},
                device_id_type=MESH,
            )
            for n, (src, dst, recv) in enumerate(attn_pairs(to))
        ]

    @step("O1")
    def _():
        @pl.loop(1, 8)
        def _(k):
            for copy in attn_copies(k):
                copy.start()

        for src, dst, recv in attn_pairs(q):
            pltpu.make_async_copy(src, dst, recv).start()

    half_cols = pl.ds(pl.multiple_of(p.z * 1024, 1024), 1024)
    other_cols = pl.ds(pl.multiple_of(p.zo * 1024, 1024), 1024)

    @step("O2")
    def _():
        arrived(ostage, attn_recv.at[1])
        send(ostage, attn_out.at[:, :, :, half_cols], attn_recv.at[2], **across)

    def control_part(i):
        total = 0.0
        for c in range(2):
            total = total + lax.dot_general(
                rows_all[c, :, i].reshape(128, HALF),
                zw_owner[c],
                NT,
                preferred_element_type=F32,
            )
        control_grad[:, i] = total.astype(BF).reshape(4, ROWS, 768)

    def zero_part(i, block):
        cols = pl.ds(block * 384, 384)
        left = jnp.concatenate(
            [ref.reshape(128, 384) for ref in (rows_all[p.c, :, i, :, cols], rows_in[:, i, :, cols])]
        )
        right = jnp.concatenate([ctl[:, i].reshape(128, 768), ctl_in[:, i].reshape(128, 768)])
        product = lax.dot_general(left, right, TN, preferred_element_type=F32)
        if i == 0:
            zacc[cols] = product
        else:
            z, y = block // 2, block % 2 * 2
            zsum[z, pl.ds(y, 2)] = (zacc[cols] + product).astype(BF).reshape(2, 192, 768)

    step("ctl0", 0)(control_part)
    step("ctl1", 1)(control_part)

    @step("zp0")
    def _():
        arrived(ctl_in, share_sem.at[4])
        for n in range(2):
            arrived(rows_in_at(0, n), rows_sem.at[n])
        for block in range(4):
            zero_part(0, block)

    cols_a, cols_b = pl.ds(0, 384), pl.ds(384, 384)
    quarter = lambda d: pl.ds(pl.multiple_of(d * 48, 16), 48)
    round_x = Scatter4(
        send,
        lambda d, h: zsum.at[h, :, quarter(d), cols_a],
        lambda h: zx_relay.at[h],
        lambda h: zx_left.at[h],
        lambda h: zx_right.at[h],
        zx_sem,
        p.d,
        p.dl,
        p.dr,
        p.do,
        to_d,
    )
    zero_y = Scatter4(
        send,
        lambda y, h: zsum.at[h, y, :, cols_b],
        lambda h: zy_relay.at[h],
        lambda h: zy_left.at[h],
        lambda h: zy_right.at[h],
        zy_sem,
        p.y,
        p.yl,
        p.yr,
        p.yo,
        to_y,
    )
    def zero_send(z):
        arrived(rows_in_at(1, z), rows_sem.at[2 + z])
        zero_part(1, 2 * z)
        zero_part(1, 2 * z + 1)
        round_x.start(z)
        zero_y.start(z)
        round_x.direct(z)
        zero_y.direct(z)

    step("zp1a", 0)(zero_send)
    step("zp1b", 1)(zero_send)
    for h in range(2):
        step(f"Zp{h}x", h)(round_x.pass_on)
        step(f"Zp{h}y", h)(zero_y.pass_on)
    others = [(dz, dy) for dz in range(2) for dy in range(4) if dz or dy]

    @step("ZA")
    def _():
        round_x.finish()
        for z in range(2):
            za_out[z] = (
                zsum[z, :, quarter(p.d), cols_a].astype(F32)
                + zx_left[z].astype(F32)
                + zx_right[z].astype(F32)
            ).astype(BF)
        for n, (dz, dy) in enumerate(others):
            z, y = (p.z + dz) % 2, (p.y + dy) % 4
            send(za_out.at[z, y], za_in.at[n], za_sem.at[n], seq=p.seq(z, y, p.c))

    @step("ZB")
    def _():
        zero_y.finish()
        for z in range(2):
            zb_out[z] = (
                (
                    zsum[z, p.y, :, cols_b].astype(F32)
                    + zy_left[z].astype(F32)
                    + zy_right[z].astype(F32)
                )
                .astype(BF)
                .reshape(4, 48, 384)
            )
        for n, (dz, dd) in enumerate(others):
            z, d = (p.z + dz) % 2, (p.d + dd) % 4
            send(zb_out.at[z, d], zb_in.at[n], zb_sem.at[n], seq=p.seq(z, p.y, p.c), dp=d)

    zero_gather = Gather4(
        send,
        lambda d: zall.at[d],
        lambda d, h: zall.at[d, :, pl.ds(h * 384, 384)],
        zg_sem,
        p.d,
        p.dl,
        p.dr,
        p.do,
        to_d,
    )

    @step("ZS")
    def _():
        total = za_out[p.z, p.y].astype(F32)
        for n in range(7):
            arrived(za_in.at[n], za_sem.at[n])
            total = total + za_in[n].astype(F32)
        zall[p.d, :, cols_a] = total.astype(BF)
        total = zb_out[p.z, p.d].astype(F32)
        for n in range(7):
            arrived(zb_in.at[n], zb_sem.at[n])
            total = total + zb_in[n].astype(F32)
        zall[p.d, :, cols_b] = total.astype(BF)
        zero_gather.start()

    step("zgL_")(zero_gather.pass_left)
    step("zgR_")(zero_gather.pass_right)

    for name in ORDER:
        steps.pop(name)()
    assert not steps

    zero_gather.finish()
    zero_out[...] = zall[...].reshape(192, 768).astype(F32) * (16384 ** (-0.5))

    arrived(attn_out.at[:, :, :, half_cols], attn_recv.at[0])
    arrived(attn_out.at[:, :, :, other_cols], attn_recv.at[2])
    send.drain()

    @pl.loop(1, 8)
    def _(k):
        for i in range(2):
            for copy in text_copies(i, k):
                copy.wait_send()
        for copy in attn_copies(k):
            copy.wait_send()


def whole_block(*operands):
    dma = pltpu.SemaphoreType.DMA
    bf = lambda *shape: pltpu.VMEM(shape, BF)
    return pl.pallas_call(
        block_kernel,
        out_shape=(
            jax.ShapeDtypeStruct((2, 2, ROWS, HEADS * HD), BF),
            jax.ShapeDtypeStruct((4, 2, ROWS, 768), BF),
            jax.ShapeDtypeStruct((192, 768), F32),
        ),
        in_specs=[pl.BlockSpec(memory_space=pltpu.SMEM)] * 2 + [ANY] * 8,
        out_specs=(VMEM, VMEM, VMEM),
        scratch_shapes=[
            bf(4, 2, ROWS, 768),
            bf(4, 2, ROWS, 768),
            bf(768, D),
            bf(2, 768, HALF),
            bf(2, ROWS, D),
            bf(4, 768, 768),
            pltpu.VMEM((2, D), F32),
            pltpu.VMEM((2, D), F32),
            bf(4, 2, ROWS, D),
            bf(2, 2, ROWS, HALF),
            bf(2, 2, ROWS, HALF),
            bf(2, 2, ROWS, HALF),
            bf(2, ROWS, D),
            bf(2, 2, 4, ROWS, D),
            bf(2, 3, 8, ROWS, HD),
            bf(3, 2, 2, 8, 2, ROWS, HD),
            bf(2, 2, 8, 2, ROWS, HD),
            bf(3, 2, 4, 2, ROWS, HD),
            bf(2, 2, 4, 2, ROWS, HD),
            bf(2, 2, 512, HD),
            bf(2, 2, ROWS, 1024),
            bf(2, 8, 2, ROWS, 384),
            bf(2, 8, ROWS, 768),
            pltpu.VMEM((IMG, HD), F32),
            pltpu.VMEM((IMG, HD), F32),
            bf(2, 2, 4, ROWS, D),
            bf(2, 2, 2, ROWS, HALF),
            bf(2, 2, 2, ROWS, HALF),
            bf(2, 2, 2, ROWS, HALF),
            bf(2, ROWS, D),
            bf(2, ROWS, D),
            bf(2, 4, 2, ROWS, HALF),
            bf(4, 2, ROWS, HALF),
            pltpu.VMEM((HALF, 768), F32),
            bf(2, 4, 192, 768),
            bf(2, 4, 48, 384),
            bf(2, 4, 48, 384),
            bf(2, 4, 48, 384),
            bf(2, 192, 384),
            bf(2, 192, 384),
            bf(2, 192, 384),
            bf(2, 4, 48, 384),
            bf(2, 4, 48, 384),
            bf(7, 48, 384),
            bf(7, 48, 384),
            bf(4, 48, 768),
            bf(3, 2, ROWS, HEADS * HD),
            bf(2, 2, ROWS, HEADS * HD),
            dma((32,)),
            dma((224,)),
            dma((4,)),
            dma((5,)),
            dma((4, 6)),
            dma((4, 9)),
            dma((4, 2, 8)),
            dma((2, 2)),
            dma((2, 2)),
            dma((2, 2)),
            dma((2,)),
            dma((2,)),
            dma((4, 6)),
            dma((4,)),
            dma((4, 4)),
            dma((4,)),
            dma((2, 8)),
            dma((3,)),
            dma((6,)),
            dma((6,)),
            dma((7,)),
            dma((7,)),
            dma((4,)),
        ],
        compiler_params=pltpu.CompilerParams(
            collective_id=1, has_side_effects=True, vmem_limit_bytes=VMEM_LIMIT
        ),
        name="whole_block",
    )(*operands)


def hand_over_kernel(attn, control, zero, image_out, text_out, control_out, zero_out, sems):
    copies = [
        pltpu.make_async_copy(src, dst, sems.at[n])
        for n, (src, dst) in enumerate(
            (
                (attn.at[1], image_out),
                (attn.at[0], text_out),
                (control, control_out),
                (zero, zero_out),
            )
        )
    ]
    for copy in copies:
        copy.start()
    for copy in copies:
        copy.wait()


def hand_over(attn, control, zero):
    return pl.pallas_call(
        hand_over_kernel,
        out_shape=(
            jax.ShapeDtypeStruct(attn.shape[1:], BF),
            jax.ShapeDtypeStruct(attn.shape[1:], BF),
            jax.ShapeDtypeStruct(control.shape, BF),
            jax.ShapeDtypeStruct(zero.shape, F32),
        ),
        in_specs=[VMEM] * 3,
        out_specs=(ANY,) * 4,
        scratch_shapes=[pltpu.SemaphoreType.DMA((4,))],
        name="hand_over",
    )(attn, control, zero)


def body(
    image_hidden,
    control_hidden,
    text_qkv,
    text_lengths,
    timesteps,
    mod_weight,
    qkv_weight,
    zero_weight,
    image_cotangent,
    text_cotangent,
):
    attn_out, control_grad, zero_t = whole_block(
        text_lengths.reshape(2),
        timesteps.reshape(2),
        mod_weight,
        control_hidden.reshape(4, 2, ROWS, 768),
        zero_weight,
        image_hidden.reshape(2, ROWS, D),
        jnp.transpose(qkv_weight, (1, 0, 2)),
        text_qkv.reshape(3, 2, ROWS, HEADS * HD),
        text_cotangent.reshape(2, ROWS, HEADS * HD),
        image_cotangent.reshape(2, ROWS, HEADS * HD),
    )
    image_attn, text_attn, control_grad, zero_t = hand_over(attn_out, control_grad, zero_t)
    return (
        image_attn.reshape(2, 1, ROWS, HEADS * HD),
        text_attn.reshape(2, 1, ROWS, HEADS * HD),
        control_grad.reshape(8, 1, ROWS, 768),
        jnp.transpose(zero_t),
    )


def solution(mesh):
    placed = (
        P("grp", "dp", "seq", None),
        P(None, "dp", "seq", "grp"),
        P(None, "grp", "dp", "seq", None),
        P("grp", "dp"),
        P("grp", "dp"),
        P(),
        P("dp", None, "seq"),
        P("grp", None),
        P("grp", "dp", "seq", None),
        P("grp", "dp", "seq", None),
    )
    return jax.shard_map(
        body,
        mesh=mesh,
        in_specs=placed,
        out_specs=(
            P("grp", "dp", "seq", None),
            P("grp", "dp", "seq", None),
            P(None, "dp", "seq", "grp"),
            P("grp", "seq"),
        ),
        check_vma=False,
    )
```

```python
import math

import jax
import jax.numpy as jnp
from jax import lax
from jax.experimental import pallas as pl
from jax.experimental.pallas import tpu as pltpu
from jax.sharding import PartitionSpec as P

D = 3072
HEADS = 16
HD = 128
IMG = 512
TXT = 512
FREQ = 256
ROWS = 32
HALF = D // 2
MESH = pl.DeviceIdType.MESH
BF = jnp.bfloat16
F32 = jnp.float32
VMEM_LIMIT = 60 * 1024 * 1024
ANY = pl.BlockSpec(memory_space=pl.ANY)
VMEM = pl.BlockSpec(memory_space=pltpu.VMEM)


class Sends:
    def __init__(self, sems):
        self.sems = sems
        self.copies = []
        self.started = 0

    def __call__(self, src, dst, recv, **to):
        copy = pltpu.make_async_remote_copy(
            src_ref=src,
            dst_ref=dst,
            send_sem=self.sems.at[self.started],
            recv_sem=recv,
            device_id=to,
            device_id_type=MESH,
        )
        copy.start()
        self.started += 1
        self.copies.append(copy)
        return copy

    def sent(self, copies):
        for copy in copies:
            copy.wait_send()
        waited = [id(copy) for copy in copies]
        self.copies = [copy for copy in self.copies if id(copy) not in waited]

    def drain(self):
        self.sent(list(self.copies))


def arrived(dst, recv):
    pltpu.make_async_copy(dst, dst, recv).wait()


def greet(groups):
    barrier = pltpu.get_barrier_semaphore()
    for to in groups:
        pl.semaphore_signal(barrier, inc=1, device_id=to, device_id_type=MESH)
    return lambda: pl.semaphore_wait(barrier, len(groups))


class Place:
    def __init__(self):
        self.s = lax.axis_index("seq")
        self.g = lax.axis_index("grp")
        self.d = lax.axis_index("dp")
        self.z = self.s // 8
        self.y = (self.s // 2) % 4
        self.c = self.s % 2
        self.zo = 1 - self.z
        self.co = 1 - self.c
        self.yl = (self.y + 3) % 4
        self.yr = (self.y + 1) % 4
        self.yo = (self.y + 2) % 4
        self.gl = (self.g + 3) % 4
        self.gr = (self.g + 1) % 4
        self.go = (self.g + 2) % 4
        self.dl = (self.d + 3) % 4
        self.dr = (self.d + 1) % 4
        self.do = (self.d + 2) % 4

    def seq(self, z, y, c):
        return z * 8 + y * 2 + c


def add_into(dst, *others):
    total = dst[...].astype(F32)
    for other in others:
        total = total + other[...].astype(F32)
    dst[...] = total.astype(dst.dtype)


class Scatter4:
    def __init__(self, send, src, relay, from_left, from_right, sems, me, left, right, far, to):
        self.send, self.src, self.relay = send, src, relay
        self.from_left, self.from_right, self.sems = from_left, from_right, sems
        self.me, self.left, self.right, self.far, self.to = me, left, right, far, to
        self.passed = []

    def start(self, h):
        to = (self.left, self.right)[h]
        self.send(self.src(self.far, h), self.relay(h), self.sems.at[h], **self.to(to))

    def direct(self, h):
        if h:
            dst, to = self.from_right(1), self.left
        else:
            dst, to = self.from_left(0), self.right
        self.send(self.src(to, h), dst, self.sems.at[3 - h], **self.to(to))

    def pass_on(self, h):
        arrived(self.relay(h), self.sems.at[h])
        if h:
            dst, to = self.from_left(1), self.right
        else:
            dst, to = self.from_right(0), self.left
        add_into(self.src(to, h), self.relay(h))
        self.passed.append(self.send(self.src(to, h), dst, self.sems.at[4 + h], **self.to(to)))

    def finish(self):
        arrived(self.from_right(1), self.sems.at[2])
        arrived(self.from_left(0), self.sems.at[3])
        arrived(self.from_right(0), self.sems.at[4])
        arrived(self.from_left(1), self.sems.at[5])


class Gather4:
    def __init__(self, send, slot, half, sems, me, left, right, far, to):
        self.send, self.slot, self.half, self.sems = send, slot, half, sems
        self.me, self.left, self.right, self.far, self.to = me, left, right, far, to

    def start(self, own=None):
        own = self.slot(self.me) if own is None else own
        self.begun = [
            self.send(own, self.slot(self.me), self.sems.at[0], **self.to(self.right)),
            self.send(own, self.slot(self.me), self.sems.at[1], **self.to(self.left)),
        ]

    def pass_left(self):
        arrived(self.slot(self.left), self.sems.at[0])
        part = self.half(self.left, 0)
        self.send(part, part, self.sems.at[2], **self.to(self.right))

    def pass_right(self):
        arrived(self.slot(self.right), self.sems.at[1])
        part = self.half(self.right, 1)
        self.send(part, part, self.sems.at[3], **self.to(self.left))

    def finish(self):
        arrived(self.half(self.far, 0), self.sems.at[2])
        arrived(self.half(self.far, 1), self.sems.at[3])


ORDER = (
    "res0", "res1", "Rs00", "T10", "Ws", "Rp000", "Rp100", "Rs01", "mod", "LN00", "Rp101",
    "Rp001", "T11", "WL", "Rs10", "GR000", "WR_", "LN01", "T20", "Gz00", "GL000", "Rp110",
    "Rp010", "GR001", "Gz01", "Rs11", "Wf", "LN10", "GL010", "GL001", "GR011", "GR100", "GR010",
    "GL011", "Rp111", "Rp011", "GL100", "proj0", "Gz10", "LN11", "att00", "att01", "Gz11",
    "att02", "att03", "GR101", "GL101", "T21", "GR111", "GL111", "GL110", "GR110", "bpa0", "bpb0",
    "Bs00", "proj1", "Bd00", "Bp100", "Bp000", "att10", "att11", "att12", "Bs01", "att13", "BX00",
    "Bd01", "bpa1", "Bp001", "Bp101", "BL00", "bpb1", "Bs10", "BX01", "Bd10", "Bp010", "Bp110",
    "Bs11", "AR00", "AL00", "BL01", "zwo", "Bd11", "Bp011", "BX10", "Bp111", "AL01", "AR01",
    "BX11", "Af00", "Af01", "BL10", "BL11", "AS10", "O1", "AS11", "AL10", "AR10", "zp0", "Af10",
    "AL11", "AR11", "zp1a", "Af11", "zp1b", "Zp0y", "Zp0x", "Zp1x", "ctl1", "Zp1y", "ctl0", "ZA",
    "ZB", "ZS", "zgL_", "zgR_", "O2",
)
NT = (((1,), (1,)), ((), ()))
TN = (((0,), (0,)), ((), ()))
BLOCK = 256


def by_owner(columns, c):
    runs = columns.shape[1] // 384
    return jnp.concatenate(
        [columns[:, n * 384 + c * 192 : n * 384 + c * 192 + 192] for n in range(runs)], axis=1
    )


def block_kernel(
    lengths,
    timesteps,
    mod_weight,
    control,
    zero_weight,
    image_hidden,
    weight,
    text,
    text_cot,
    image_cot,
    attn_out,
    control_grad,
    zero_out,
    ctl,
    ctl_in,
    zw,
    zw_owner,
    base,
    wall,
    offset,
    stretch,
    partial,
    rg_relay,
    rg_left,
    rg_right,
    hidden,
    normed,
    qkv_out,
    joint,
    cots,
    tstage,
    cstage,
    attn,
    ostage,
    grads,
    both_grads,
    key_acc,
    value_acc,
    pair_sum,
    ry_relay,
    ry_left,
    ry_right,
    cross_out,
    cross_in,
    rows_all,
    rows_in,
    zacc,
    zsum,
    zx_relay,
    zx_left,
    zx_right,
    zy_relay,
    zy_left,
    zy_right,
    za_out,
    zb_out,
    za_in,
    zb_in,
    zall,
    text_mine,
    cots_mine,
    load_sem,
    send_sem,
    w_sem,
    share_sem,
    rg_sem,
    ag_sem,
    text_send,
    text_recv,
    stage_recv,
    cross_recv,
    qkv_sem,
    grads_sem,
    ry_sem,
    cross_sem,
    gg_sem,
    rows_sem,
    attn_send,
    attn_recv,
    zx_sem,
    zy_sem,
    za_sem,
    zb_sem,
    zg_sem,
):
    p = Place()
    send = Sends(send_sem)
    q = p.y * 2 + p.c
    partner = {"seq": p.seq(p.z, p.y, p.co)}
    across = {"seq": p.seq(p.zo, p.y, p.c)}
    to_y = lambda y: {"seq": p.seq(p.z, y, p.c)}
    to_g = lambda g: {"grp": g}
    to_d = lambda d: {"dp": d}

    all_here = greet(
        [{"seq": (p.s + k) % 16} for k in range(1, 16)]
        + [{"grp": p.gl}, {"grp": p.gr}]
        + [{"dp": (p.d + k) % 4} for k in range(1, 4)]
        + [{"dp": (p.d + k) % 4, "seq": p.seq(p.zo, p.y, p.c)} for k in range(1, 4)]
    )

    loads = []

    def load(src, dst):
        copy = pltpu.make_async_copy(src, dst, load_sem.at[len(loads)])
        copy.start()
        loads.append(copy)
        return copy

    load_control = load(control, ctl)
    load_zero = [
        load(zero_weight.at[:, pl.ds(n * 512, 512)], zw.at[:, pl.ds(n * 512, 512)])
        for n in range(6)
    ]
    load_weight = [
        load(weight.at[n], wall.at[p.d, :, pl.ds(n * HD, HD)]) for n in range(3)
    ]
    load_text = [
        load(text, text_mine),
        load(text_cot, cots_mine.at[0]),
        load(image_cot, cots_mine.at[1]),
    ]
    load_base = load(image_hidden, base)
    load_mod = [
        load(
            mod_weight.at[pl.ds(n % 8 * ROWS, ROWS), pl.ds(n // 8 * D, D)],
            pair_sum.at[n // 8, n // 4 % 2, n % 4],
        )
        for n in range(16)
    ]

    half = lambda h: pl.ds(h * HALF, HALF)
    part = lambda r: pl.ds(r * 16, 16)
    chunks = [(i, r) for i in range(2) for r in range(2)]
    steps = {}

    def step(name, *args):
        def add(f):
            steps[name] = lambda: f(*args)
            return f

        return add

    def residual_part(h):
        if h == 0:
            load_control.wait()
        for block in range(3 * h, 3 * h + 3):
            cols = pl.ds(block * 512, 512)
            load_zero[block].wait()
            product = jnp.dot(
                ctl[...].reshape(256, 768), zw[:, cols], preferred_element_type=F32
            )
            partial[:, :, :, cols] = product.astype(BF).reshape(4, 2, ROWS, 512)
        if h == 0:
            all_here()
            to_group[0, 0].start(0)
            to_group[0, 0].direct(0)

    step("res0", 0)(residual_part)
    step("res1", 1)(residual_part)

    to_group = {
        (i, r): Scatter4(
            send,
            lambda g, h, i=i, r=r: partial.at[g, i, part(r), half(h)],
            lambda h, i=i, r=r: rg_relay.at[i, h, part(r)],
            lambda h, i=i, r=r: rg_left.at[i, h, part(r)],
            lambda h, i=i, r=r: rg_right.at[i, h, part(r)],
            rg_sem.at[i * 2 + r],
            p.g,
            p.gl,
            p.gr,
            p.go,
            to_g,
        )
        for i, r in chunks
    }

    def group_start(n):
        if n:
            send.sent(to_group[chunks[n - 1]].passed)
        scatter = to_group[chunks[n]]
        for h in range(0 if n else 1, 2):
            scatter.start(h)
        scatter.direct(1)
        if n:
            scatter.direct(0)

    for n, (i, r) in enumerate(chunks):
        step(f"Rs{i}{r}", n)(group_start)
        for h in range(2):
            step(f"Rp{h}{i}{r}", h)(to_group[i, r].pass_on)

    plane = pl.ds(p.z * 4, 4)
    other_plane = pl.ds(p.zo * 4, 4)
    zy = p.z * 4 + p.y

    def text_pairs(i, to):
        near = pl.ds(pl.multiple_of((p.z * 8 + to) * HD, HD), HD)
        far = pl.ds(pl.multiple_of((p.zo * 8 + to) * HD, HD), HD)
        return (
            (text_mine.at[:, i, :, far], tstage.at[:, i, p.y, p.c], stage_recv.at[0, i]),
            (cots_mine.at[:, i, :, far], cstage.at[:, i, p.y, p.c], stage_recv.at[1, i]),
            (text_mine.at[:, i, :, near], joint.at[:, i, 0, zy, p.c], text_recv.at[0, i]),
            (cots_mine.at[:, i, :, near], cots.at[:, i, zy, p.c], text_recv.at[1, i]),
        )

    def text_copies(i, k):
        to = (q + k) % 8
        return [
            pltpu.make_async_remote_copy(
                src_ref=src,
                dst_ref=dst,
                send_sem=text_send.at[n, i, k],
                recv_sem=recv,
                device_id={"seq": p.z * 8 + to},
                device_id_type=MESH,
            )
            for n, (src, dst, recv) in enumerate(text_pairs(i, to))
        ]

    def text_first_hop(i):
        if i == 0:
            for copy in load_text:
                copy.wait()

        @pl.loop(1, 8)
        def _(k):
            for copy in text_copies(i, k):
                copy.start()

        for src, dst, recv in text_pairs(i, q):
            pltpu.make_async_copy(src, dst, recv).start()

    def text_second_hop(i):
        arrived(tstage.at[:, i], stage_recv.at[0, i])
        arrived(cstage.at[:, i], stage_recv.at[1, i])
        send(tstage.at[:, i], joint.at[:, i, 0, plane], cross_recv.at[i, 0], **across)
        send(cstage.at[:, i], cots.at[:, i, plane], cross_recv.at[i, 1], **across)

    def text_wait(i):
        arrived(joint.at[:, i, 0, plane], text_recv.at[0, i])
        arrived(cots.at[:, i, plane], text_recv.at[1, i])
        arrived(joint.at[:, i, 0, other_plane], cross_recv.at[i, 0])
        arrived(cots.at[:, i, other_plane], cross_recv.at[i, 1])

    for i in range(2):
        step(f"T1{i}", i)(text_first_hop)
        step(f"T2{i}", i)(text_second_hop)

    mine_cols, pair_cols = pl.ds(0, 384), pl.ds(384, 384)
    weights = Gather4(
        send,
        lambda d: wall.at[d, :, mine_cols],
        lambda d, h: wall.at[d, pl.ds(h * 384, 384), mine_cols],
        w_sem,
        p.d,
        p.dl,
        p.dr,
        p.do,
        to_d,
    )

    def share_weight(d, sem):
        send(wall.at[d, :, mine_cols], wall.at[d, :, pair_cols], share_sem.at[sem], **partner)

    @step("Ws")
    def _():
        for copy in load_weight:
            copy.wait()
        weights.start()
        share_weight(p.d, 0)
        send(ctl, ctl_in, share_sem.at[4], **partner)

    @step("WL")
    def _():
        weights.pass_left()
        share_weight(p.dl, 1)

    @step("WR_")
    def _():
        weights.pass_right()
        share_weight(p.dr, 2)

    @step("Wf")
    def _():
        weights.finish()
        share_weight(p.do, 3)

    @step("mod")
    def _():
        for copy in load_mod:
            copy.wait()
        lane = lax.broadcasted_iota(jnp.int32, (1, FREQ // 2), 1).astype(F32)
        frequency = jnp.exp(lane * (-math.log(10000.0) / (FREQ // 2)))
        angles = jnp.concatenate([timesteps[i].astype(F32) * frequency for i in range(2)])
        embedding = jnp.concatenate([jnp.cos(angles), jnp.sin(angles)], axis=1)
        activated = (embedding / (1.0 + jnp.exp(-embedding))).astype(BF)
        offset[...] = jnp.dot(
            activated, pair_sum[0].reshape(FREQ, D), preferred_element_type=F32
        )
        stretch[...] = 1.0 + jnp.dot(
            activated, pair_sum[1].reshape(FREQ, D), preferred_element_type=F32
        )
        load_base.wait()

    @step("zwo")
    def _():
        for block in range(4):
            columns = zw[:, pl.ds(block * 768, 768)].astype(F32)
            for c in range(2):
                zw_owner[c, :, pl.ds(block * 384, 384)] = by_owner(columns, c).astype(BF)

    gathers = {
        (i, r, which): Gather4(
            send,
            lambda y, i=i, r=r, z=z: normed.at[i, z, y, part(r)],
            lambda y, h, i=i, r=r, z=z: normed.at[i, z, y, part(r), half(h)],
            ag_sem.at[i * 2 + r, pl.ds(which * 4, 4)],
            p.y,
            p.yl,
            p.yr,
            p.yo,
            to_y,
        )
        for i, r in chunks
        for which, z in enumerate((p.z, p.zo))
    }

    def standardise(rows):
        values = rows.astype(F32)
        average = jnp.mean(values, axis=-1, keepdims=True)
        centred = values - average
        reciprocal = lax.rsqrt(jnp.mean(centred * centred, axis=-1, keepdims=True) + 1e-06)
        return centred * reciprocal, reciprocal

    def gather_first(i, r):
        to_group[i, r].finish()
        rows = part(r)
        for h in range(2):
            residual = (
                partial[p.g, i, rows, half(h)].astype(F32)
                + rg_left[i, h, rows].astype(F32)
                + rg_right[i, h, rows].astype(F32)
            )
            hidden[i, rows, half(h)] = (base[i, rows, half(h)].astype(F32) + residual).astype(BF)
        standard, _ = standardise(hidden[i, rows])
        normed[i, p.z, p.y, rows] = (
            standard * stretch[i : i + 1] + offset[i : i + 1]
        ).astype(BF)
        mine = normed.at[i, p.z, p.y, rows]
        send(mine, mine, ag_sem.at[i * 2 + r, 8], **across)
        gathers[i, r, 0].start()

    def gather_second(i, r):
        arrived(normed.at[i, p.zo, p.y, part(r)], ag_sem.at[i * 2 + r, 8])
        gathers[i, r, 1].start()

    for i, r in chunks:
        step(f"LN{i}{r}", i, r)(gather_first)
        step(f"Gz{i}{r}", i, r)(gather_second)
        for which in range(2):
            step(f"GL{i}{r}{which}")(gathers[i, r, which].pass_left)
            step(f"GR{i}{r}{which}")(gathers[i, r, which].pass_right)

    scaling = HD ** (-0.5)
    position = lax.broadcasted_iota(jnp.int32, (1, TXT + IMG), 1)

    def project(i):
        for r in range(2):
            for which in range(2):
                gathers[i, r, which].finish()
        if i == 0:
            for n, d in enumerate((p.d, p.dl, p.dr, p.do)):
                arrived(wall.at[d, :, pair_cols], share_sem.at[n])
        product = jnp.dot(
            normed[i].reshape(256, D), wall[...].reshape(D, 768), preferred_element_type=F32
        ).astype(BF)
        for n in range(3):
            qkv_out[i, n] = product[:, 384 + n * HD : 384 + (n + 1) * HD].reshape(8, ROWS, HD)
        send(qkv_out.at[i], joint.at[:, i, 1, :, p.c], qkv_sem.at[i], **partner)
        for n in range(3):
            joint[n, i, 1, :, p.c] = product[:, n * HD : (n + 1) * HD].reshape(8, ROWS, HD)

    def attend(i, block):
        if block == 0:
            text_wait(i)
            arrived(joint.at[:, i, 1, :, p.co], qkv_sem.at[i])
        slots = pl.ds(block % 2 * 4, 4)
        bias = jnp.where((position >= TXT) | (position < lengths[i]), 0.0, -jnp.inf)
        query = joint[0, i, block // 2, slots].reshape(BLOCK, HD)
        cot = cots[block // 2, i, slots].reshape(BLOCK, HD)
        keys = joint[1, i].reshape(TXT + IMG, HD)
        values = joint[2, i].reshape(TXT + IMG, HD)
        scores = lax.dot_general(query, keys, NT, preferred_element_type=F32) + bias
        row_max = jnp.max(scores, axis=1, keepdims=True)
        terms = jnp.exp2((scores - row_max) * (scaling * math.log2(math.e)))
        prob = terms * (1.0 / jnp.sum(terms, axis=1, keepdims=True))
        low = prob.astype(BF)
        attended = jnp.dot(low, values, preferred_element_type=F32).astype(BF)
        attn[block // 2, i, pl.ds(block % 2 * BLOCK, BLOCK)] = attended
        dots = jnp.sum(cot.astype(F32) * attended.astype(F32), axis=1, keepdims=True)
        prob_grad = lax.dot_general(cot, values, NT, preferred_element_type=F32)
        score_grad = (prob * (prob_grad - dots)).astype(BF)
        if block >= 2:
            query_grad = jnp.dot(score_grad, keys, preferred_element_type=F32) * scaling
            grads[i, slots, :, :, :HD] = query_grad.astype(BF).reshape(4, 2, ROWS, HD)
        key_part = lax.dot_general(score_grad[:, TXT:], query, TN, preferred_element_type=F32)
        value_part = lax.dot_general(low[:, TXT:], cot, TN, preferred_element_type=F32)
        if block == 0:
            key_acc[...] = key_part
            value_acc[...] = value_part
        elif block < 3:
            key_acc[...] += key_part
            value_acc[...] += value_part
        else:
            key_grad = ((key_acc[...] + key_part) * scaling).astype(BF)
            value_grad = (value_acc[...] + value_part).astype(BF)
            grads[i, :, :, :, HD : 2 * HD] = key_grad.reshape(8, 2, ROWS, HD)
            grads[i, :, :, :, 2 * HD :] = value_grad.reshape(8, 2, ROWS, HD)
            send(
                grads.at[i, :, p.co], both_grads.at[i, :, :, pair_cols], grads_sem.at[i],
                **partner
            )
            both_grads[i, :, :, :384] = grads[i, :, p.c]

    for i in range(2):
        step(f"proj{i}", i)(project)
        for block in range(4):
            step(f"att{i}{block}", i, block)(attend)

    def back_project(i, h):
        if h == 0:
            arrived(both_grads.at[i, :, :, pair_cols], grads_sem.at[i])
        for block in range(2 * h, 2 * h + 2):
            cols = pl.ds(block * 768, 768)
            product = lax.dot_general(
                both_grads[i].reshape(256, 768), wall[block], NT, preferred_element_type=F32
            ).astype(BF)
            pair_sum[i, :, :, :, cols] = product.reshape(2, 4, ROWS, 768)

    round_y = {
        (i, r): Scatter4(
            send,
            lambda y, h, i=i, r=r: pair_sum.at[i, :, y, part(r), half(h)],
            lambda h, i=i, r=r: ry_relay.at[i, h, :, part(r)],
            lambda h, i=i, r=r: ry_left.at[i, h, :, part(r)],
            lambda h, i=i, r=r: ry_right.at[i, h, :, part(r)],
            ry_sem.at[i * 2 + r],
            p.y,
            p.yl,
            p.yr,
            p.yo,
            to_y,
        )
        for i, r in chunks
    }

    def scatter_start(i, r):
        round_y[i, r].start(0)
        round_y[i, r].start(1)

    def scatter_direct(i, r):
        round_y[i, r].direct(1)
        round_y[i, r].direct(0)

    def y_sum(i, r, z, h):
        return (
            pair_sum[i, z, p.y, part(r), half(h)].astype(F32)
            + ry_left[i, h, z, part(r)].astype(F32)
            + ry_right[i, h, z, part(r)].astype(F32)
        )

    def scatter_cross(i, r):
        round_y[i, r].finish()
        for h in range(2):
            cross_out[i, part(r), half(h)] = y_sum(i, r, p.zo, h).astype(BF)
        send(
            cross_out.at[i, part(r)], cross_in.at[i, part(r)], cross_sem.at[i * 2 + r], **across
        )

    def norm_back(i, r):
        mine = jnp.concatenate([y_sum(i, r, p.z, h) for h in range(2)], axis=1)
        standard, reciprocal = standardise(hidden[i, part(r)])
        arrived(cross_in.at[i, part(r)], cross_sem.at[i * 2 + r])
        scaled = (mine + cross_in[i, part(r)].astype(F32)) * stretch[i : i + 1]
        residual_grad = reciprocal * (
            scaled
            - jnp.mean(scaled, axis=-1, keepdims=True)
            - standard * jnp.mean(scaled * standard, axis=-1, keepdims=True)
        )
        for c in range(2):
            rows_all[c, p.g, i, part(r)] = by_owner(residual_grad, c).astype(BF)
        if i == 0:
            rows_gather[0, r].start()

    def rows_at(c, g, i, n):
        if i:
            return rows_all.at[c, g, 1, :, pl.ds(n * 768, 768)]
        return rows_all.at[c, g, 0, part(n)]

    def rows_in_at(i, n):
        if i:
            return rows_in.at[:, 1, :, pl.ds(n * 768, 768)]
        return rows_in.at[:, 0, part(n)]

    every = slice(None)
    rows_gather = {
        (i, n): Gather4(
            send,
            lambda g, i=i, n=n: rows_at(every, g, i, n),
            lambda g, h, i=i, n=n: rows_at(h, g, i, n),
            gg_sem.at[i * 2 + n],
            p.g,
            p.gl,
            p.gr,
            p.go,
            to_g,
        )
        for i, n in chunks
    }

    def rows_start(n):
        if n:
            send.sent(rows_gather[1, 0].begun)
        rows_gather[1, n].start()

    def rows_finish(i, n):
        rows_gather[i, n].finish()
        send(rows_at(p.co, every, i, n), rows_in_at(i, n), rows_sem.at[i * 2 + n], **partner)

    for i in range(2):
        step(f"bpa{i}", i, 0)(back_project)
        step(f"bpb{i}", i, 1)(back_project)
        step(f"AS1{i}", i)(rows_start)
    for i, r in chunks:
        step(f"Bs{i}{r}", i, r)(scatter_start)
        step(f"Bd{i}{r}", i, r)(scatter_direct)
        for h in range(2):
            step(f"Bp{h}{i}{r}", h)(round_y[i, r].pass_on)
        step(f"BX{i}{r}", i, r)(scatter_cross)
        step(f"BL{i}{r}", i, r)(norm_back)
        step(f"AL{i}{r}")(rows_gather[i, r].pass_left)
        step(f"AR{i}{r}")(rows_gather[i, r].pass_right)
        step(f"Af{i}{r}", i, r)(rows_finish)

    def attn_pairs(to):
        near = pl.ds(pl.multiple_of((p.z * 8 + to) * ROWS, ROWS), ROWS)
        far = pl.ds(pl.multiple_of((p.zo * 8 + to) * ROWS, ROWS), ROWS)
        cols = pl.ds(pl.multiple_of(p.s * HD, HD), HD)
        staged = pl.ds(pl.multiple_of(q * HD, HD), HD)
        return (
            (attn.at[:, :, near], attn_out.at[:, :, :, cols], attn_recv.at[0]),
            (attn.at[:, :, far], ostage.at[:, :, :, staged], attn_recv.at[1]),
        )

    def attn_copies(k):
        to = (q + k) % 8
        return [
            pltpu.make_async_remote_copy(
                src_ref=src,
                dst_ref=dst,
                send_sem=attn_send.at[n, k],
                recv_sem=recv,
                device_id={"seq": p.z * 8 + to},
                device_id_type=MESH,
            )
            for n, (src, dst, recv) in enumerate(attn_pairs(to))
        ]

    @step("O1")
    def _():
        @pl.loop(1, 8)
        def _(k):
            for copy in attn_copies(k):
                copy.start()

        for src, dst, recv in attn_pairs(q):
            pltpu.make_async_copy(src, dst, recv).start()

    half_cols = pl.ds(pl.multiple_of(p.z * 1024, 1024), 1024)
    other_cols = pl.ds(pl.multiple_of(p.zo * 1024, 1024), 1024)

    @step("O2")
    def _():
        arrived(ostage, attn_recv.at[1])
        send(ostage, attn_out.at[:, :, :, half_cols], attn_recv.at[2], **across)

    def control_part(i):
        total = 0.0
        for c in range(2):
            total = total + lax.dot_general(
                rows_all[c, :, i].reshape(128, HALF),
                zw_owner[c],
                NT,
                preferred_element_type=F32,
            )
        control_grad[:, i] = total.astype(BF).reshape(4, ROWS, 768)

    def zero_part(i, block):
        cols = pl.ds(block * 384, 384)
        left = jnp.concatenate(
            [ref.reshape(128, 384) for ref in (rows_all[p.c, :, i, :, cols], rows_in[:, i, :, cols])]
        )
        right = jnp.concatenate([ctl[:, i].reshape(128, 768), ctl_in[:, i].reshape(128, 768)])
        product = lax.dot_general(left, right, TN, preferred_element_type=F32)
        if i == 0:
            zacc[cols] = product
        else:
            z, y = block // 2, block % 2 * 2
            zsum[z, pl.ds(y, 2)] = (zacc[cols] + product).astype(BF).reshape(2, 192, 768)

    step("ctl0", 0)(control_part)
    step("ctl1", 1)(control_part)

    @step("zp0")
    def _():
        arrived(ctl_in, share_sem.at[4])
        for n in range(2):
            arrived(rows_in_at(0, n), rows_sem.at[n])
        for block in range(4):
            zero_part(0, block)

    cols_a, cols_b = pl.ds(0, 384), pl.ds(384, 384)
    quarter = lambda d: pl.ds(pl.multiple_of(d * 48, 16), 48)
    round_x = Scatter4(
        send,
        lambda d, h: zsum.at[h, :, quarter(d), cols_a],
        lambda h: zx_relay.at[h],
        lambda h: zx_left.at[h],
        lambda h: zx_right.at[h],
        zx_sem,
        p.d,
        p.dl,
        p.dr,
        p.do,
        to_d,
    )
    zero_y = Scatter4(
        send,
        lambda y, h: zsum.at[h, y, :, cols_b],
        lambda h: zy_relay.at[h],
        lambda h: zy_left.at[h],
        lambda h: zy_right.at[h],
        zy_sem,
        p.y,
        p.yl,
        p.yr,
        p.yo,
        to_y,
    )
    def zero_send(z):
        arrived(rows_in_at(1, z), rows_sem.at[2 + z])
        zero_part(1, 2 * z)
        zero_part(1, 2 * z + 1)
        round_x.start(z)
        zero_y.start(z)
        round_x.direct(z)
        zero_y.direct(z)

    step("zp1a", 0)(zero_send)
    step("zp1b", 1)(zero_send)
    for h in range(2):
        step(f"Zp{h}x", h)(round_x.pass_on)
        step(f"Zp{h}y", h)(zero_y.pass_on)
    others = [(dz, dy) for dz in range(2) for dy in range(4) if dz or dy]

    @step("ZA")
    def _():
        round_x.finish()
        for z in range(2):
            za_out[z] = (
                zsum[z, :, quarter(p.d), cols_a].astype(F32)
                + zx_left[z].astype(F32)
                + zx_right[z].astype(F32)
            ).astype(BF)
        for n, (dz, dy) in enumerate(others):
            z, y = (p.z + dz) % 2, (p.y + dy) % 4
            send(za_out.at[z, y], za_in.at[n], za_sem.at[n], seq=p.seq(z, y, p.c))

    @step("ZB")
    def _():
        zero_y.finish()
        for z in range(2):
            zb_out[z] = (
                (
                    zsum[z, p.y, :, cols_b].astype(F32)
                    + zy_left[z].astype(F32)
                    + zy_right[z].astype(F32)
                )
                .astype(BF)
                .reshape(4, 48, 384)
            )
        for n, (dz, dd) in enumerate(others):
            z, d = (p.z + dz) % 2, (p.d + dd) % 4
            send(zb_out.at[z, d], zb_in.at[n], zb_sem.at[n], seq=p.seq(z, p.y, p.c), dp=d)

    zero_gather = Gather4(
        send,
        lambda d: zall.at[d],
        lambda d, h: zall.at[d, :, pl.ds(h * 384, 384)],
        zg_sem,
        p.d,
        p.dl,
        p.dr,
        p.do,
        to_d,
    )

    @step("ZS")
    def _():
        total = za_out[p.z, p.y].astype(F32)
        for n in range(7):
            arrived(za_in.at[n], za_sem.at[n])
            total = total + za_in[n].astype(F32)
        zall[p.d, :, cols_a] = total.astype(BF)
        total = zb_out[p.z, p.d].astype(F32)
        for n in range(7):
            arrived(zb_in.at[n], zb_sem.at[n])
            total = total + zb_in[n].astype(F32)
        zall[p.d, :, cols_b] = total.astype(BF)
        zero_gather.start()

    step("zgL_")(zero_gather.pass_left)
    step("zgR_")(zero_gather.pass_right)

    for name in ORDER:
        steps.pop(name)()
    assert not steps

    zero_gather.finish()
    zero_out[...] = zall[...].reshape(192, 768).astype(F32) * (16384 ** (-0.5))

    arrived(attn_out.at[:, :, :, half_cols], attn_recv.at[0])
    arrived(attn_out.at[:, :, :, other_cols], attn_recv.at[2])
    send.drain()

    @pl.loop(1, 8)
    def _(k):
        for i in range(2):
            for copy in text_copies(i, k):
                copy.wait_send()
        for copy in attn_copies(k):
            copy.wait_send()


def whole_block(*operands):
    dma = pltpu.SemaphoreType.DMA
    bf = lambda *shape: pltpu.VMEM(shape, BF)
    return pl.pallas_call(
        block_kernel,
        out_shape=(
            jax.ShapeDtypeStruct((2, 2, ROWS, HEADS * HD), BF),
            jax.ShapeDtypeStruct((4, 2, ROWS, 768), BF),
            jax.ShapeDtypeStruct((192, 768), F32),
        ),
        in_specs=[pl.BlockSpec(memory_space=pltpu.SMEM)] * 2 + [ANY] * 8,
        out_specs=(VMEM, VMEM, VMEM),
        scratch_shapes=[
            bf(4, 2, ROWS, 768),
            bf(4, 2, ROWS, 768),
            bf(768, D),
            bf(2, 768, HALF),
            bf(2, ROWS, D),
            bf(4, 768, 768),
            pltpu.VMEM((2, D), F32),
            pltpu.VMEM((2, D), F32),
            bf(4, 2, ROWS, D),
            bf(2, 2, ROWS, HALF),
            bf(2, 2, ROWS, HALF),
            bf(2, 2, ROWS, HALF),
            bf(2, ROWS, D),
            bf(2, 2, 4, ROWS, D),
            bf(2, 3, 8, ROWS, HD),
            bf(3, 2, 2, 8, 2, ROWS, HD),
            bf(2, 2, 8, 2, ROWS, HD),
            bf(3, 2, 4, 2, ROWS, HD),
            bf(2, 2, 4, 2, ROWS, HD),
            bf(2, 2, 512, HD),
            bf(2, 2, ROWS, 1024),
            bf(2, 8, 2, ROWS, 384),
            bf(2, 8, ROWS, 768),
            pltpu.VMEM((IMG, HD), F32),
            pltpu.VMEM((IMG, HD), F32),
            bf(2, 2, 4, ROWS, D),
            bf(2, 2, 2, ROWS, HALF),
            bf(2, 2, 2, ROWS, HALF),
            bf(2, 2, 2, ROWS, HALF),
            bf(2, ROWS, D),
            bf(2, ROWS, D),
            bf(2, 4, 2, ROWS, HALF),
            bf(4, 2, ROWS, HALF),
            pltpu.VMEM((HALF, 768), F32),
            bf(2, 4, 192, 768),
            bf(2, 4, 48, 384),
            bf(2, 4, 48, 384),
            bf(2, 4, 48, 384),
            bf(2, 192, 384),
            bf(2, 192, 384),
            bf(2, 192, 384),
            bf(2, 4, 48, 384),
            bf(2, 4, 48, 384),
            bf(7, 48, 384),
            bf(7, 48, 384),
            bf(4, 48, 768),
            bf(3, 2, ROWS, HEADS * HD),
            bf(2, 2, ROWS, HEADS * HD),
            dma((32,)),
            dma((224,)),
            dma((4,)),
            dma((5,)),
            dma((4, 6)),
            dma((4, 9)),
            dma((4, 2, 8)),
            dma((2, 2)),
            dma((2, 2)),
            dma((2, 2)),
            dma((2,)),
            dma((2,)),
            dma((4, 6)),
            dma((4,)),
            dma((4, 4)),
            dma((4,)),
            dma((2, 8)),
            dma((3,)),
            dma((6,)),
            dma((6,)),
            dma((7,)),
            dma((7,)),
            dma((4,)),
        ],
        compiler_params=pltpu.CompilerParams(
            collective_id=1, has_side_effects=True, vmem_limit_bytes=VMEM_LIMIT
        ),
        name="whole_block",
    )(*operands)


def hand_over_kernel(attn, control, zero, image_out, text_out, control_out, zero_out, sems):
    copies = [
        pltpu.make_async_copy(src, dst, sems.at[n])
        for n, (src, dst) in enumerate(
            (
                (attn.at[1], image_out),
                (attn.at[0], text_out),
                (control, control_out),
                (zero, zero_out),
            )
        )
    ]
    for copy in copies:
        copy.start()
    for copy in copies:
        copy.wait()


def hand_over(attn, control, zero):
    return pl.pallas_call(
        hand_over_kernel,
        out_shape=(
            jax.ShapeDtypeStruct(attn.shape[1:], BF),
            jax.ShapeDtypeStruct(attn.shape[1:], BF),
            jax.ShapeDtypeStruct(control.shape, BF),
            jax.ShapeDtypeStruct(zero.shape, F32),
        ),
        in_specs=[VMEM] * 3,
        out_specs=(ANY,) * 4,
        scratch_shapes=[pltpu.SemaphoreType.DMA((4,))],
        name="hand_over",
    )(attn, control, zero)


def body(
    image_hidden,
    control_hidden,
    text_qkv,
    text_lengths,
    timesteps,
    mod_weight,
    qkv_weight,
    zero_weight,
    image_cotangent,
    text_cotangent,
):
    attn_out, control_grad, zero_t = whole_block(
        text_lengths.reshape(2),
        timesteps.reshape(2),
        mod_weight,
        control_hidden.reshape(4, 2, ROWS, 768),
        zero_weight,
        image_hidden.reshape(2, ROWS, D),
        jnp.transpose(qkv_weight, (1, 0, 2)),
        text_qkv.reshape(3, 2, ROWS, HEADS * HD),
        text_cotangent.reshape(2, ROWS, HEADS * HD),
        image_cotangent.reshape(2, ROWS, HEADS * HD),
    )
    image_attn, text_attn, control_grad, zero_t = hand_over(attn_out, control_grad, zero_t)
    return (
        image_attn.reshape(2, 1, ROWS, HEADS * HD),
        text_attn.reshape(2, 1, ROWS, HEADS * HD),
        control_grad.reshape(8, 1, ROWS, 768),
        jnp.transpose(zero_t),
    )


def solution(mesh):
    placed = (
        P("grp", "dp", "seq", None),
        P(None, "dp", "seq", "grp"),
        P(None, "grp", "dp", "seq", None),
        P("grp", "dp"),
        P("grp", "dp"),
        P(),
        P("dp", None, "seq"),
        P("grp", None),
        P("grp", "dp", "seq", None),
        P("grp", "dp", "seq", None),
    )
    return jax.shard_map(
        body,
        mesh=mesh,
        in_specs=placed,
        out_specs=(
            P("grp", "dp", "seq", None),
            P("grp", "dp", "seq", None),
            P(None, "dp", "seq", "grp"),
            P("grp", "seq"),
        ),
        check_vma=False,
    )
```

```python
import math

import jax
import jax.numpy as jnp
from jax import lax
from jax.experimental import pallas as pl
from jax.experimental.pallas import tpu as pltpu
from jax.sharding import PartitionSpec as P

D = 3072
HEADS = 16
HD = 128
IMG = 512
TXT = 512
FREQ = 256
ROWS = 32
HALF = D // 2
MESH = pl.DeviceIdType.MESH
BF = jnp.bfloat16
F32 = jnp.float32
VMEM_LIMIT = 60 * 1024 * 1024
ANY = pl.BlockSpec(memory_space=pl.ANY)
VMEM = pl.BlockSpec(memory_space=pltpu.VMEM)


class Sends:
    def __init__(self, sems):
        self.sems = sems
        self.copies = []
        self.started = 0

    def __call__(self, src, dst, recv, **to):
        copy = pltpu.make_async_remote_copy(
            src_ref=src,
            dst_ref=dst,
            send_sem=self.sems.at[self.started],
            recv_sem=recv,
            device_id=to,
            device_id_type=MESH,
        )
        copy.start()
        self.started += 1
        self.copies.append(copy)
        return copy

    def sent(self, copies):
        for copy in copies:
            copy.wait_send()
        waited = [id(copy) for copy in copies]
        self.copies = [copy for copy in self.copies if id(copy) not in waited]

    def drain(self):
        self.sent(list(self.copies))


def arrived(dst, recv):
    pltpu.make_async_copy(dst, dst, recv).wait()


def greet(groups):
    barrier = pltpu.get_barrier_semaphore()
    for to in groups:
        pl.semaphore_signal(barrier, inc=1, device_id=to, device_id_type=MESH)
    return lambda: pl.semaphore_wait(barrier, len(groups))


class Place:
    def __init__(self):
        self.s = lax.axis_index("seq")
        self.g = lax.axis_index("grp")
        self.d = lax.axis_index("dp")
        self.z = self.s // 8
        self.y = (self.s // 2) % 4
        self.c = self.s % 2
        self.zo = 1 - self.z
        self.co = 1 - self.c
        self.yl = (self.y + 3) % 4
        self.yr = (self.y + 1) % 4
        self.yo = (self.y + 2) % 4
        self.gl = (self.g + 3) % 4
        self.gr = (self.g + 1) % 4
        self.go = (self.g + 2) % 4
        self.dl = (self.d + 3) % 4
        self.dr = (self.d + 1) % 4
        self.do = (self.d + 2) % 4

    def seq(self, z, y, c):
        return z * 8 + y * 2 + c


def add_into(dst, *others):
    total = dst[...].astype(F32)
    for other in others:
        total = total + other[...].astype(F32)
    dst[...] = total.astype(dst.dtype)


class Scatter4:
    def __init__(self, send, src, relay, from_left, from_right, sems, me, left, right, far, to):
        self.send, self.src, self.relay = send, src, relay
        self.from_left, self.from_right, self.sems = from_left, from_right, sems
        self.me, self.left, self.right, self.far, self.to = me, left, right, far, to
        self.passed = []

    def start(self, h):
        to = (self.left, self.right)[h]
        self.send(self.src(self.far, h), self.relay(h), self.sems.at[h], **self.to(to))

    def direct(self, h):
        if h:
            dst, to = self.from_right(1), self.left
        else:
            dst, to = self.from_left(0), self.right
        self.send(self.src(to, h), dst, self.sems.at[3 - h], **self.to(to))

    def pass_on(self, h):
        arrived(self.relay(h), self.sems.at[h])
        if h:
            dst, to = self.from_left(1), self.right
        else:
            dst, to = self.from_right(0), self.left
        add_into(self.src(to, h), self.relay(h))
        self.passed.append(self.send(self.src(to, h), dst, self.sems.at[4 + h], **self.to(to)))

    def finish(self):
        arrived(self.from_right(1), self.sems.at[2])
        arrived(self.from_left(0), self.sems.at[3])
        arrived(self.from_right(0), self.sems.at[4])
        arrived(self.from_left(1), self.sems.at[5])


class Gather4:
    def __init__(self, send, slot, half, sems, me, left, right, far, to):
        self.send, self.slot, self.half, self.sems = send, slot, half, sems
        self.me, self.left, self.right, self.far, self.to = me, left, right, far, to

    def start(self, own=None):
        own = self.slot(self.me) if own is None else own
        self.begun = [
            self.send(own, self.slot(self.me), self.sems.at[0], **self.to(self.right)),
            self.send(own, self.slot(self.me), self.sems.at[1], **self.to(self.left)),
        ]

    def pass_left(self):
        arrived(self.slot(self.left), self.sems.at[0])
        part = self.half(self.left, 0)
        self.send(part, part, self.sems.at[2], **self.to(self.right))

    def pass_right(self):
        arrived(self.slot(self.right), self.sems.at[1])
        part = self.half(self.right, 1)
        self.send(part, part, self.sems.at[3], **self.to(self.left))

    def finish(self):
        arrived(self.half(self.far, 0), self.sems.at[2])
        arrived(self.half(self.far, 1), self.sems.at[3])


ORDER = (
    "res0", "res1", "Rs00", "T11", "Rp100", "Rp000", "T10", "Rs01", "mod", "Ws", "LN00", "Rp001",
    "Rp101", "Rs10", "zwo", "LN01", "Rp110", "Rp010", "WR_", "Gz00", "GR000", "Gz01", "Rs11",
    "WL", "LN10", "T20", "GR010", "GL010", "GL001", "GL011", "GR011", "GR001", "Rp011", "Rp111",
    "Wf", "GL000", "Gz10", "GR100", "proj0", "GL100", "GL101", "LN11", "GR101", "att00", "att01",
    "Gz11", "att02", "GR110", "att03", "T21", "GL111", "GR111", "GL110", "bpa0", "bpb0", "Bs00",
    "proj1", "Bd00", "Bp100", "Bp000", "att10", "att11", "Bs01", "att12", "BX00", "att13", "Bd01",
    "Bp001", "Bp101", "BL00", "bpa1", "bpb1", "Bs10", "BX01", "Bd10", "Bp010", "Bp110", "AL00",
    "AR00", "Bs11", "BL01", "Af00", "Bd11", "BX10", "Bp011", "Bp111", "AR01", "AL01", "BX11",
    "Af01", "BL10", "BL11", "AS10", "zp0", "AS11", "AR10", "AL10", "ctl0", "O1", "Af10", "AL11",
    "AR11", "zp1a", "Af11", "zp1b", "O2", "Zp0y", "Zp1y", "Zp0x", "Zp1x", "ZB", "ZA", "ZS",
    "zgL_", "zgR_", "ctl1",
)
NT = (((1,), (1,)), ((), ()))
TN = (((0,), (0,)), ((), ()))
BLOCK = 256


def by_owner(columns, c):
    runs = columns.shape[1] // 384
    return jnp.concatenate(
        [columns[:, n * 384 + c * 192 : n * 384 + c * 192 + 192] for n in range(runs)], axis=1
    )


def block_kernel(
    lengths,
    timesteps,
    mod_weight,
    control,
    zero_weight,
    image_hidden,
    weight,
    text,
    text_cot,
    image_cot,
    attn_out,
    control_grad,
    zero_out,
    ctl,
    ctl_in,
    zw,
    zw_owner,
    base,
    wall,
    offset,
    stretch,
    partial,
    rg_relay,
    rg_left,
    rg_right,
    hidden,
    normed,
    qkv_out,
    joint,
    cots,
    tstage,
    cstage,
    attn,
    ostage,
    grads,
    both_grads,
    key_acc,
    value_acc,
    pair_sum,
    ry_relay,
    ry_left,
    ry_right,
    cross_out,
    cross_in,
    rows_all,
    rows_in,
    zacc,
    zsum,
    zx_relay,
    zx_left,
    zx_right,
    zy_relay,
    zy_left,
    zy_right,
    za_out,
    zb_out,
    za_in,
    zb_in,
    zall,
    text_mine,
    cots_mine,
    load_sem,
    send_sem,
    w_sem,
    share_sem,
    rg_sem,
    ag_sem,
    text_send,
    text_recv,
    stage_recv,
    cross_recv,
    qkv_sem,
    grads_sem,
    ry_sem,
    cross_sem,
    gg_sem,
    rows_sem,
    attn_send,
    attn_recv,
    zx_sem,
    zy_sem,
    za_sem,
    zb_sem,
    zg_sem,
):
    p = Place()
    send = Sends(send_sem)
    q = p.y * 2 + p.c
    partner = {"seq": p.seq(p.z, p.y, p.co)}
    across = {"seq": p.seq(p.zo, p.y, p.c)}
    to_y = lambda y: {"seq": p.seq(p.z, y, p.c)}
    to_g = lambda g: {"grp": g}
    to_d = lambda d: {"dp": d}

    all_here = greet(
        [{"seq": (p.s + k) % 16} for k in range(1, 16)]
        + [{"grp": p.gl}, {"grp": p.gr}]
        + [{"dp": (p.d + k) % 4} for k in range(1, 4)]
        + [{"dp": (p.d + k) % 4, "seq": p.seq(p.zo, p.y, p.c)} for k in range(1, 4)]
    )

    loads = []

    def load(src, dst):
        copy = pltpu.make_async_copy(src, dst, load_sem.at[len(loads)])
        copy.start()
        loads.append(copy)
        return copy

    load_control = load(control, ctl)
    load_zero = [
        load(zero_weight.at[:, pl.ds(n * 512, 512)], zw.at[:, pl.ds(n * 512, 512)])
        for n in range(6)
    ]
    load_weight = [
        load(weight.at[n], wall.at[p.d, :, pl.ds(n * HD, HD)]) for n in range(3)
    ]
    load_text = [
        load(text, text_mine),
        load(text_cot, cots_mine.at[0]),
        load(image_cot, cots_mine.at[1]),
    ]
    load_base = load(image_hidden, base)
    load_mod = [
        load(
            mod_weight.at[pl.ds(n % 8 * ROWS, ROWS), pl.ds(n // 8 * D, D)],
            pair_sum.at[n // 8, n // 4 % 2, n % 4],
        )
        for n in range(16)
    ]

    half = lambda h: pl.ds(h * HALF, HALF)
    part = lambda r: pl.ds(r * 16, 16)
    chunks = [(i, r) for i in range(2) for r in range(2)]
    steps = {}

    def step(name, *args):
        def add(f):
            steps[name] = lambda: f(*args)
            return f

        return add

    def residual_part(h):
        if h == 0:
            load_control.wait()
        for block in range(3 * h, 3 * h + 3):
            cols = pl.ds(block * 512, 512)
            load_zero[block].wait()
            product = jnp.dot(
                ctl[...].reshape(256, 768), zw[:, cols], preferred_element_type=F32
            )
            partial[:, :, :, cols] = product.astype(BF).reshape(4, 2, ROWS, 512)
        if h == 0:
            all_here()
            to_group[0, 0].start(0)
            to_group[0, 0].direct(0)

    step("res0", 0)(residual_part)
    step("res1", 1)(residual_part)

    to_group = {
        (i, r): Scatter4(
            send,
            lambda g, h, i=i, r=r: partial.at[g, i, part(r), half(h)],
            lambda h, i=i, r=r: rg_relay.at[i, h, part(r)],
            lambda h, i=i, r=r: rg_left.at[i, h, part(r)],
            lambda h, i=i, r=r: rg_right.at[i, h, part(r)],
            rg_sem.at[i * 2 + r],
            p.g,
            p.gl,
            p.gr,
            p.go,
            to_g,
        )
        for i, r in chunks
    }

    def group_start(n):
        if n:
            send.sent(to_group[chunks[n - 1]].passed)
        scatter = to_group[chunks[n]]
        for h in range(0 if n else 1, 2):
            scatter.start(h)
        scatter.direct(1)
        if n:
            scatter.direct(0)

    for n, (i, r) in enumerate(chunks):
        step(f"Rs{i}{r}", n)(group_start)
        for h in range(2):
            step(f"Rp{h}{i}{r}", h)(to_group[i, r].pass_on)

    plane = pl.ds(p.z * 4, 4)
    other_plane = pl.ds(p.zo * 4, 4)
    zy = p.z * 4 + p.y

    def text_pairs(i, to):
        near = pl.ds(pl.multiple_of((p.z * 8 + to) * HD, HD), HD)
        far = pl.ds(pl.multiple_of((p.zo * 8 + to) * HD, HD), HD)
        return (
            (text_mine.at[:, i, :, far], tstage.at[:, i, p.y, p.c], stage_recv.at[0, i]),
            (cots_mine.at[:, i, :, far], cstage.at[:, i, p.y, p.c], stage_recv.at[1, i]),
            (text_mine.at[:, i, :, near], joint.at[:, i, 0, zy, p.c], text_recv.at[0, i]),
            (cots_mine.at[:, i, :, near], cots.at[:, i, zy, p.c], text_recv.at[1, i]),
        )

    def text_copies(i, k):
        to = (q + k) % 8
        return [
            pltpu.make_async_remote_copy(
                src_ref=src,
                dst_ref=dst,
                send_sem=text_send.at[n, i, k],
                recv_sem=recv,
                device_id={"seq": p.z * 8 + to},
                device_id_type=MESH,
            )
            for n, (src, dst, recv) in enumerate(text_pairs(i, to))
        ]

    def text_first_hop(i):
        while load_text:
            load_text.pop().wait()

        @pl.loop(1, 8)
        def _(k):
            for copy in text_copies(i, k):
                copy.start()

        for src, dst, recv in text_pairs(i, q):
            pltpu.make_async_copy(src, dst, recv).start()

    def text_second_hop(i):
        arrived(tstage.at[:, i], stage_recv.at[0, i])
        arrived(cstage.at[:, i], stage_recv.at[1, i])
        send(tstage.at[:, i], joint.at[:, i, 0, plane], cross_recv.at[i, 0], **across)
        send(cstage.at[:, i], cots.at[:, i, plane], cross_recv.at[i, 1], **across)

    def text_wait(i):
        arrived(joint.at[:, i, 0, plane], text_recv.at[0, i])
        arrived(cots.at[:, i, plane], text_recv.at[1, i])
        arrived(joint.at[:, i, 0, other_plane], cross_recv.at[i, 0])
        arrived(cots.at[:, i, other_plane], cross_recv.at[i, 1])

    for i in range(2):
        step(f"T1{i}", i)(text_first_hop)
        step(f"T2{i}", i)(text_second_hop)

    mine_cols, pair_cols = pl.ds(0, 384), pl.ds(384, 384)
    weights = Gather4(
        send,
        lambda d: wall.at[d, :, mine_cols],
        lambda d, h: wall.at[d, pl.ds(h * 384, 384), mine_cols],
        w_sem,
        p.d,
        p.dl,
        p.dr,
        p.do,
        to_d,
    )

    def share_weight(d, sem):
        send(wall.at[d, :, mine_cols], wall.at[d, :, pair_cols], share_sem.at[sem], **partner)

    @step("Ws")
    def _():
        for copy in load_weight:
            copy.wait()
        weights.start()
        share_weight(p.d, 0)
        send(ctl, ctl_in, share_sem.at[4], **partner)

    @step("WL")
    def _():
        weights.pass_left()
        share_weight(p.dl, 1)

    @step("WR_")
    def _():
        weights.pass_right()
        share_weight(p.dr, 2)

    @step("Wf")
    def _():
        weights.finish()
        share_weight(p.do, 3)

    @step("mod")
    def _():
        for copy in load_mod:
            copy.wait()
        lane = lax.broadcasted_iota(jnp.int32, (1, FREQ // 2), 1).astype(F32)
        frequency = jnp.exp(lane * (-math.log(10000.0) / (FREQ // 2)))
        angles = jnp.concatenate([timesteps[i].astype(F32) * frequency for i in range(2)])
        embedding = jnp.concatenate([jnp.cos(angles), jnp.sin(angles)], axis=1)
        activated = (embedding / (1.0 + jnp.exp(-embedding))).astype(BF)
        offset[...] = jnp.dot(
            activated, pair_sum[0].reshape(FREQ, D), preferred_element_type=F32
        )
        stretch[...] = 1.0 + jnp.dot(
            activated, pair_sum[1].reshape(FREQ, D), preferred_element_type=F32
        )
        load_base.wait()

    @step("zwo")
    def _():
        for block in range(4):
            columns = zw[:, pl.ds(block * 768, 768)].astype(F32)
            for c in range(2):
                zw_owner[c, :, pl.ds(block * 384, 384)] = by_owner(columns, c).astype(BF)

    gathers = {
        (i, r, which): Gather4(
            send,
            lambda y, i=i, r=r, z=z: normed.at[i, z, y, part(r)],
            lambda y, h, i=i, r=r, z=z: normed.at[i, z, y, part(r), half(h)],
            ag_sem.at[i * 2 + r, pl.ds(which * 4, 4)],
            p.y,
            p.yl,
            p.yr,
            p.yo,
            to_y,
        )
        for i, r in chunks
        for which, z in enumerate((p.z, p.zo))
    }

    def standardise(rows):
        values = rows.astype(F32)
        average = jnp.mean(values, axis=-1, keepdims=True)
        centred = values - average
        reciprocal = lax.rsqrt(jnp.mean(centred * centred, axis=-1, keepdims=True) + 1e-06)
        return centred * reciprocal, reciprocal

    def gather_first(i, r):
        to_group[i, r].finish()
        rows = part(r)
        for h in range(2):
            residual = (
                partial[p.g, i, rows, half(h)].astype(F32)
                + rg_left[i, h, rows].astype(F32)
                + rg_right[i, h, rows].astype(F32)
            )
            hidden[i, rows, half(h)] = (base[i, rows, half(h)].astype(F32) + residual).astype(BF)
        standard, _ = standardise(hidden[i, rows])
        normed[i, p.z, p.y, rows] = (
            standard * stretch[i : i + 1] + offset[i : i + 1]
        ).astype(BF)
        mine = normed.at[i, p.z, p.y, rows]
        send(mine, mine, ag_sem.at[i * 2 + r, 8], **across)
        gathers[i, r, 0].start()

    def gather_second(i, r):
        arrived(normed.at[i, p.zo, p.y, part(r)], ag_sem.at[i * 2 + r, 8])
        gathers[i, r, 1].start()

    for i, r in chunks:
        step(f"LN{i}{r}", i, r)(gather_first)
        step(f"Gz{i}{r}", i, r)(gather_second)
        for which in range(2):
            step(f"GL{i}{r}{which}")(gathers[i, r, which].pass_left)
            step(f"GR{i}{r}{which}")(gathers[i, r, which].pass_right)

    scaling = HD ** (-0.5)

    def project(i):
        for r in range(2):
            for which in range(2):
                gathers[i, r, which].finish()
        if i == 0:
            for n, d in enumerate((p.d, p.dl, p.dr, p.do)):
                arrived(wall.at[d, :, pair_cols], share_sem.at[n])
        product = jnp.dot(
            normed[i].reshape(256, D), wall[...].reshape(D, 768), preferred_element_type=F32
        ).astype(BF)
        for n in range(3):
            qkv_out[i, n] = product[:, 384 + n * HD : 384 + (n + 1) * HD].reshape(8, ROWS, HD)
        send(qkv_out.at[i], joint.at[:, i, 1, :, p.c], qkv_sem.at[i], **partner)
        for n in range(3):
            joint[n, i, 1, :, p.c] = product[:, n * HD : (n + 1) * HD].reshape(8, ROWS, HD)

    def attend(i, block):
        if block == 0:
            text_wait(i)
            arrived(joint.at[:, i, 1, :, p.co], qkv_sem.at[i])
        slots = pl.ds(block % 2 * 4, 4)
        query = joint[0, i, block // 2, slots].reshape(BLOCK, HD)
        cot = cots[block // 2, i, slots].reshape(BLOCK, HD)
        keys = joint[1, i].reshape(TXT + IMG, HD)
        values = joint[2, i].reshape(TXT + IMG, HD)
        scores = lax.dot_general(keys, query, NT, preferred_element_type=F32)
        text_live = lax.broadcasted_iota(jnp.int32, (TXT, 1), 0) < lengths[i]
        text_scores = jnp.where(text_live, scores[:TXT], -jnp.inf)
        image_scores = scores[TXT:]
        col_max = jnp.maximum(
            jnp.max(text_scores, axis=0, keepdims=True),
            jnp.max(image_scores, axis=0, keepdims=True),
        )
        rate = scaling * math.log2(math.e)
        text_terms = jnp.exp2((text_scores - col_max) * rate)
        image_terms = jnp.exp2((image_scores - col_max) * rate)
        share = 1.0 / (
            jnp.sum(text_terms, axis=0, keepdims=True) + jnp.sum(image_terms, axis=0, keepdims=True)
        )
        text_prob, image_prob = text_terms * share, image_terms * share
        image_low = image_prob.astype(BF)
        attended = lax.dot_general(
            values[:TXT], text_prob.astype(BF), TN, preferred_element_type=F32
        ) + lax.dot_general(values[TXT:], image_low, TN, preferred_element_type=F32)
        low_attended = attended.astype(BF).astype(F32)
        attn[block // 2, i, pl.ds(block % 2 * BLOCK, BLOCK)] = low_attended.T.astype(BF)
        dots = jnp.sum(cot.astype(F32).T * low_attended, axis=0, keepdims=True)
        prob_grad = lax.dot_general(values, cot, NT, preferred_element_type=F32)
        image_grad = (image_prob * (prob_grad[TXT:] - dots)).astype(BF)
        if block >= 2:
            text_grad = (text_prob * (prob_grad[:TXT] - dots)).astype(BF)
            query_grad = lax.dot_general(
                keys[:TXT], text_grad, TN, preferred_element_type=F32
            ) + lax.dot_general(keys[TXT:], image_grad, TN, preferred_element_type=F32)
            query_grad = (query_grad * scaling).T.astype(BF)
            grads[i, slots, :, :, :HD] = query_grad.reshape(4, 2, ROWS, HD)
        key_part = jnp.dot(image_grad, query, preferred_element_type=F32)
        value_part = jnp.dot(image_low, cot, preferred_element_type=F32)
        if block == 0:
            key_acc[...] = key_part
            value_acc[...] = value_part
        elif block < 3:
            key_acc[...] += key_part
            value_acc[...] += value_part
        else:
            key_grad = ((key_acc[...] + key_part) * scaling).astype(BF)
            value_grad = (value_acc[...] + value_part).astype(BF)
            grads[i, :, :, :, HD : 2 * HD] = key_grad.reshape(8, 2, ROWS, HD)
            grads[i, :, :, :, 2 * HD :] = value_grad.reshape(8, 2, ROWS, HD)
            send(
                grads.at[i, :, p.co], both_grads.at[i, :, :, pair_cols], grads_sem.at[i],
                **partner
            )
            both_grads[i, :, :, :384] = grads[i, :, p.c]

    for i in range(2):
        step(f"proj{i}", i)(project)
        for block in range(4):
            step(f"att{i}{block}", i, block)(attend)

    def back_project(i, h):
        if h == 0:
            arrived(both_grads.at[i, :, :, pair_cols], grads_sem.at[i])
        for block in range(2 * h, 2 * h + 2):
            cols = pl.ds(block * 768, 768)
            product = lax.dot_general(
                both_grads[i].reshape(256, 768), wall[block], NT, preferred_element_type=F32
            ).astype(BF)
            pair_sum[i, :, :, :, cols] = product.reshape(2, 4, ROWS, 768)

    round_y = {
        (i, r): Scatter4(
            send,
            lambda y, h, i=i, r=r: pair_sum.at[i, :, y, part(r), half(h)],
            lambda h, i=i, r=r: ry_relay.at[i, h, :, part(r)],
            lambda h, i=i, r=r: ry_left.at[i, h, :, part(r)],
            lambda h, i=i, r=r: ry_right.at[i, h, :, part(r)],
            ry_sem.at[i * 2 + r],
            p.y,
            p.yl,
            p.yr,
            p.yo,
            to_y,
        )
        for i, r in chunks
    }

    def scatter_start(i, r):
        round_y[i, r].start(0)
        round_y[i, r].start(1)

    def scatter_direct(i, r):
        round_y[i, r].direct(1)
        round_y[i, r].direct(0)

    def y_sum(i, r, z, h):
        return (
            pair_sum[i, z, p.y, part(r), half(h)].astype(F32)
            + ry_left[i, h, z, part(r)].astype(F32)
            + ry_right[i, h, z, part(r)].astype(F32)
        )

    def scatter_cross(i, r):
        round_y[i, r].finish()
        for h in range(2):
            cross_out[i, part(r), half(h)] = y_sum(i, r, p.zo, h).astype(BF)
        send(
            cross_out.at[i, part(r)], cross_in.at[i, part(r)], cross_sem.at[i * 2 + r], **across
        )

    def norm_back(i, r):
        mine = jnp.concatenate([y_sum(i, r, p.z, h) for h in range(2)], axis=1)
        standard, reciprocal = standardise(hidden[i, part(r)])
        arrived(cross_in.at[i, part(r)], cross_sem.at[i * 2 + r])
        scaled = (mine + cross_in[i, part(r)].astype(F32)) * stretch[i : i + 1]
        residual_grad = reciprocal * (
            scaled
            - jnp.mean(scaled, axis=-1, keepdims=True)
            - standard * jnp.mean(scaled * standard, axis=-1, keepdims=True)
        )
        for c in range(2):
            rows_all[c, p.g, i, part(r)] = by_owner(residual_grad, c).astype(BF)
        if i == 0:
            rows_gather[0, r].start()

    def rows_at(c, g, i, n):
        if i:
            return rows_all.at[c, g, 1, :, pl.ds(n * 768, 768)]
        return rows_all.at[c, g, 0, part(n)]

    def rows_in_at(i, n):
        if i:
            return rows_in.at[:, 1, :, pl.ds(n * 768, 768)]
        return rows_in.at[:, 0, part(n)]

    every = slice(None)
    rows_gather = {
        (i, n): Gather4(
            send,
            lambda g, i=i, n=n: rows_at(every, g, i, n),
            lambda g, h, i=i, n=n: rows_at(h, g, i, n),
            gg_sem.at[i * 2 + n],
            p.g,
            p.gl,
            p.gr,
            p.go,
            to_g,
        )
        for i, n in chunks
    }

    def rows_start(n):
        if n:
            send.sent(rows_gather[1, 0].begun)
        rows_gather[1, n].start()

    def rows_finish(i, n):
        rows_gather[i, n].finish()
        send(rows_at(p.co, every, i, n), rows_in_at(i, n), rows_sem.at[i * 2 + n], **partner)

    for i in range(2):
        step(f"bpa{i}", i, 0)(back_project)
        step(f"bpb{i}", i, 1)(back_project)
        step(f"AS1{i}", i)(rows_start)
    for i, r in chunks:
        step(f"Bs{i}{r}", i, r)(scatter_start)
        step(f"Bd{i}{r}", i, r)(scatter_direct)
        for h in range(2):
            step(f"Bp{h}{i}{r}", h)(round_y[i, r].pass_on)
        step(f"BX{i}{r}", i, r)(scatter_cross)
        step(f"BL{i}{r}", i, r)(norm_back)
        step(f"AL{i}{r}")(rows_gather[i, r].pass_left)
        step(f"AR{i}{r}")(rows_gather[i, r].pass_right)
        step(f"Af{i}{r}", i, r)(rows_finish)

    def attn_pairs(to):
        near = pl.ds(pl.multiple_of((p.z * 8 + to) * ROWS, ROWS), ROWS)
        far = pl.ds(pl.multiple_of((p.zo * 8 + to) * ROWS, ROWS), ROWS)
        cols = pl.ds(pl.multiple_of(p.s * HD, HD), HD)
        staged = pl.ds(pl.multiple_of(q * HD, HD), HD)
        return (
            (attn.at[:, :, near], attn_out.at[:, :, :, cols], attn_recv.at[0]),
            (attn.at[:, :, far], ostage.at[:, :, :, staged], attn_recv.at[1]),
        )

    def attn_copies(k):
        to = (q + k) % 8
        return [
            pltpu.make_async_remote_copy(
                src_ref=src,
                dst_ref=dst,
                send_sem=attn_send.at[n, k],
                recv_sem=recv,
                device_id={"seq": p.z * 8 + to},
                device_id_type=MESH,
            )
            for n, (src, dst, recv) in enumerate(attn_pairs(to))
        ]

    @step("O1")
    def _():
        @pl.loop(1, 8)
        def _(k):
            for copy in attn_copies(k):
                copy.start()

        for src, dst, recv in attn_pairs(q):
            pltpu.make_async_copy(src, dst, recv).start()

    half_cols = pl.ds(pl.multiple_of(p.z * 1024, 1024), 1024)
    other_cols = pl.ds(pl.multiple_of(p.zo * 1024, 1024), 1024)

    @step("O2")
    def _():
        arrived(ostage, attn_recv.at[1])
        send(ostage, attn_out.at[:, :, :, half_cols], attn_recv.at[2], **across)

    def control_part(i):
        total = 0.0
        for c in range(2):
            total = total + lax.dot_general(
                rows_all[c, :, i].reshape(128, HALF),
                zw_owner[c],
                NT,
                preferred_element_type=F32,
            )
        control_grad[:, i] = total.astype(BF).reshape(4, ROWS, 768)

    def zero_part(i, block):
        cols = pl.ds(block * 384, 384)
        left = jnp.concatenate(
            [ref.reshape(128, 384) for ref in (rows_all[p.c, :, i, :, cols], rows_in[:, i, :, cols])]
        )
        right = jnp.concatenate([ctl[:, i].reshape(128, 768), ctl_in[:, i].reshape(128, 768)])
        product = lax.dot_general(left, right, TN, preferred_element_type=F32)
        if i == 0:
            zacc[cols] = product
        else:
            z, y = block // 2, block % 2 * 2
            zsum[z, pl.ds(y, 2)] = (zacc[cols] + product).astype(BF).reshape(2, 192, 768)

    step("ctl0", 0)(control_part)
    step("ctl1", 1)(control_part)

    @step("zp0")
    def _():
        arrived(ctl_in, share_sem.at[4])
        for n in range(2):
            arrived(rows_in_at(0, n), rows_sem.at[n])
        for block in range(4):
            zero_part(0, block)

    cols_a, cols_b = pl.ds(0, 384), pl.ds(384, 384)
    quarter = lambda d: pl.ds(pl.multiple_of(d * 48, 16), 48)
    round_x = Scatter4(
        send,
        lambda d, h: zsum.at[h, :, quarter(d), cols_a],
        lambda h: zx_relay.at[h],
        lambda h: zx_left.at[h],
        lambda h: zx_right.at[h],
        zx_sem,
        p.d,
        p.dl,
        p.dr,
        p.do,
        to_d,
    )
    zero_y = Scatter4(
        send,
        lambda y, h: zsum.at[h, y, :, cols_b],
        lambda h: zy_relay.at[h],
        lambda h: zy_left.at[h],
        lambda h: zy_right.at[h],
        zy_sem,
        p.y,
        p.yl,
        p.yr,
        p.yo,
        to_y,
    )
    def zero_send(z):
        arrived(rows_in_at(1, z), rows_sem.at[2 + z])
        zero_part(1, 2 * z)
        zero_part(1, 2 * z + 1)
        round_x.start(z)
        zero_y.start(z)
        round_x.direct(z)
        zero_y.direct(z)

    step("zp1a", 0)(zero_send)
    step("zp1b", 1)(zero_send)
    for h in range(2):
        step(f"Zp{h}x", h)(round_x.pass_on)
        step(f"Zp{h}y", h)(zero_y.pass_on)
    others = [(dz, dy) for dz in range(2) for dy in range(4) if dz or dy]

    @step("ZA")
    def _():
        round_x.finish()
        for z in range(2):
            za_out[z] = (
                zsum[z, :, quarter(p.d), cols_a].astype(F32)
                + zx_left[z].astype(F32)
                + zx_right[z].astype(F32)
            ).astype(BF)
        for n, (dz, dy) in enumerate(others):
            z, y = (p.z + dz) % 2, (p.y + dy) % 4
            send(za_out.at[z, y], za_in.at[n], za_sem.at[n], seq=p.seq(z, y, p.c))

    @step("ZB")
    def _():
        zero_y.finish()
        for z in range(2):
            zb_out[z] = (
                (
                    zsum[z, p.y, :, cols_b].astype(F32)
                    + zy_left[z].astype(F32)
                    + zy_right[z].astype(F32)
                )
                .astype(BF)
                .reshape(4, 48, 384)
            )
        for n, (dz, dd) in enumerate(others):
            z, d = (p.z + dz) % 2, (p.d + dd) % 4
            send(zb_out.at[z, d], zb_in.at[n], zb_sem.at[n], seq=p.seq(z, p.y, p.c), dp=d)

    zero_gather = Gather4(
        send,
        lambda d: zall.at[d],
        lambda d, h: zall.at[d, :, pl.ds(h * 384, 384)],
        zg_sem,
        p.d,
        p.dl,
        p.dr,
        p.do,
        to_d,
    )

    @step("ZS")
    def _():
        total = za_out[p.z, p.y].astype(F32)
        for n in range(7):
            arrived(za_in.at[n], za_sem.at[n])
            total = total + za_in[n].astype(F32)
        zall[p.d, :, cols_a] = total.astype(BF)
        total = zb_out[p.z, p.d].astype(F32)
        for n in range(7):
            arrived(zb_in.at[n], zb_sem.at[n])
            total = total + zb_in[n].astype(F32)
        zall[p.d, :, cols_b] = total.astype(BF)
        zero_gather.start()

    step("zgL_")(zero_gather.pass_left)
    step("zgR_")(zero_gather.pass_right)

    for name in ORDER:
        steps.pop(name)()
    assert not steps

    zero_gather.finish()
    zero_out[...] = zall[...].reshape(192, 768).astype(F32) * (16384 ** (-0.5))

    arrived(attn_out.at[:, :, :, half_cols], attn_recv.at[0])
    arrived(attn_out.at[:, :, :, other_cols], attn_recv.at[2])
    send.drain()

    @pl.loop(1, 8)
    def _(k):
        for i in range(2):
            for copy in text_copies(i, k):
                copy.wait_send()
        for copy in attn_copies(k):
            copy.wait_send()


def whole_block(*operands):
    dma = pltpu.SemaphoreType.DMA
    bf = lambda *shape: pltpu.VMEM(shape, BF)
    return pl.pallas_call(
        block_kernel,
        out_shape=(
            jax.ShapeDtypeStruct((2, 2, ROWS, HEADS * HD), BF),
            jax.ShapeDtypeStruct((4, 2, ROWS, 768), BF),
            jax.ShapeDtypeStruct((192, 768), F32),
        ),
        in_specs=[pl.BlockSpec(memory_space=pltpu.SMEM)] * 2 + [ANY] * 8,
        out_specs=(VMEM, VMEM, VMEM),
        scratch_shapes=[
            bf(4, 2, ROWS, 768),
            bf(4, 2, ROWS, 768),
            bf(768, D),
            bf(2, 768, HALF),
            bf(2, ROWS, D),
            bf(4, 768, 768),
            pltpu.VMEM((2, D), F32),
            pltpu.VMEM((2, D), F32),
            bf(4, 2, ROWS, D),
            bf(2, 2, ROWS, HALF),
            bf(2, 2, ROWS, HALF),
            bf(2, 2, ROWS, HALF),
            bf(2, ROWS, D),
            bf(2, 2, 4, ROWS, D),
            bf(2, 3, 8, ROWS, HD),
            bf(3, 2, 2, 8, 2, ROWS, HD),
            bf(2, 2, 8, 2, ROWS, HD),
            bf(3, 2, 4, 2, ROWS, HD),
            bf(2, 2, 4, 2, ROWS, HD),
            bf(2, 2, 512, HD),
            bf(2, 2, ROWS, 1024),
            bf(2, 8, 2, ROWS, 384),
            bf(2, 8, ROWS, 768),
            pltpu.VMEM((IMG, HD), F32),
            pltpu.VMEM((IMG, HD), F32),
            bf(2, 2, 4, ROWS, D),
            bf(2, 2, 2, ROWS, HALF),
            bf(2, 2, 2, ROWS, HALF),
            bf(2, 2, 2, ROWS, HALF),
            bf(2, ROWS, D),
            bf(2, ROWS, D),
            bf(2, 4, 2, ROWS, HALF),
            bf(4, 2, ROWS, HALF),
            pltpu.VMEM((HALF, 768), F32),
            bf(2, 4, 192, 768),
            bf(2, 4, 48, 384),
            bf(2, 4, 48, 384),
            bf(2, 4, 48, 384),
            bf(2, 192, 384),
            bf(2, 192, 384),
            bf(2, 192, 384),
            bf(2, 4, 48, 384),
            bf(2, 4, 48, 384),
            bf(7, 48, 384),
            bf(7, 48, 384),
            bf(4, 48, 768),
            bf(3, 2, ROWS, HEADS * HD),
            bf(2, 2, ROWS, HEADS * HD),
            dma((32,)),
            dma((224,)),
            dma((4,)),
            dma((5,)),
            dma((4, 6)),
            dma((4, 9)),
            dma((4, 2, 8)),
            dma((2, 2)),
            dma((2, 2)),
            dma((2, 2)),
            dma((2,)),
            dma((2,)),
            dma((4, 6)),
            dma((4,)),
            dma((4, 4)),
            dma((4,)),
            dma((2, 8)),
            dma((3,)),
            dma((6,)),
            dma((6,)),
            dma((7,)),
            dma((7,)),
            dma((4,)),
        ],
        compiler_params=pltpu.CompilerParams(
            collective_id=1, has_side_effects=True, vmem_limit_bytes=VMEM_LIMIT
        ),
        name="whole_block",
    )(*operands)


def hand_over_kernel(attn, control, zero, image_out, text_out, control_out, zero_out, sems):
    copies = [
        pltpu.make_async_copy(src, dst, sems.at[n])
        for n, (src, dst) in enumerate(
            (
                (attn.at[1], image_out),
                (attn.at[0], text_out),
                (control, control_out),
                (zero, zero_out),
            )
        )
    ]
    for copy in copies:
        copy.start()
    for copy in copies:
        copy.wait()


def hand_over(attn, control, zero):
    return pl.pallas_call(
        hand_over_kernel,
        out_shape=(
            jax.ShapeDtypeStruct(attn.shape[1:], BF),
            jax.ShapeDtypeStruct(attn.shape[1:], BF),
            jax.ShapeDtypeStruct(control.shape, BF),
            jax.ShapeDtypeStruct(zero.shape, F32),
        ),
        in_specs=[VMEM] * 3,
        out_specs=(ANY,) * 4,
        scratch_shapes=[pltpu.SemaphoreType.DMA((4,))],
        name="hand_over",
    )(attn, control, zero)


def body(
    image_hidden,
    control_hidden,
    text_qkv,
    text_lengths,
    timesteps,
    mod_weight,
    qkv_weight,
    zero_weight,
    image_cotangent,
    text_cotangent,
):
    attn_out, control_grad, zero_t = whole_block(
        text_lengths.reshape(2),
        timesteps.reshape(2),
        mod_weight,
        control_hidden.reshape(4, 2, ROWS, 768),
        zero_weight,
        image_hidden.reshape(2, ROWS, D),
        jnp.transpose(qkv_weight, (1, 0, 2)),
        text_qkv.reshape(3, 2, ROWS, HEADS * HD),
        text_cotangent.reshape(2, ROWS, HEADS * HD),
        image_cotangent.reshape(2, ROWS, HEADS * HD),
    )
    image_attn, text_attn, control_grad, zero_t = hand_over(attn_out, control_grad, zero_t)
    return (
        image_attn.reshape(2, 1, ROWS, HEADS * HD),
        text_attn.reshape(2, 1, ROWS, HEADS * HD),
        control_grad.reshape(8, 1, ROWS, 768),
        jnp.transpose(zero_t),
    )


def solution(mesh):
    placed = (
        P("grp", "dp", "seq", None),
        P(None, "dp", "seq", "grp"),
        P(None, "grp", "dp", "seq", None),
        P("grp", "dp"),
        P("grp", "dp"),
        P(),
        P("dp", None, "seq"),
        P("grp", None),
        P("grp", "dp", "seq", None),
        P("grp", "dp", "seq", None),
    )
    return jax.shard_map(
        body,
        mesh=mesh,
        in_specs=placed,
        out_specs=(
            P("grp", "dp", "seq", None),
            P("grp", "dp", "seq", None),
            P(None, "dp", "seq", "grp"),
            P("grp", "seq"),
        ),
        check_vma=False,
    )
```

```python
import math

import jax
import jax.numpy as jnp
from jax import lax
from jax.experimental import pallas as pl
from jax.experimental.pallas import tpu as pltpu
from jax.sharding import PartitionSpec as P

D = 3072
HEADS = 16
HD = 128
IMG = 512
TXT = 512
FREQ = 256
ROWS = 32
HALF = D // 2
MESH = pl.DeviceIdType.MESH
BF = jnp.bfloat16
F32 = jnp.float32
VMEM_LIMIT = 60 * 1024 * 1024
ANY = pl.BlockSpec(memory_space=pl.ANY)
VMEM = pl.BlockSpec(memory_space=pltpu.VMEM)


class Sends:
    def __init__(self, sems):
        self.sems = sems
        self.copies = []
        self.started = 0

    def __call__(self, src, dst, recv, **to):
        copy = pltpu.make_async_remote_copy(
            src_ref=src,
            dst_ref=dst,
            send_sem=self.sems.at[self.started],
            recv_sem=recv,
            device_id=to,
            device_id_type=MESH,
        )
        copy.start()
        self.started += 1
        self.copies.append(copy)
        return copy

    def sent(self, copies):
        for copy in copies:
            copy.wait_send()
        waited = [id(copy) for copy in copies]
        self.copies = [copy for copy in self.copies if id(copy) not in waited]

    def drain(self):
        self.sent(list(self.copies))


def arrived(dst, recv):
    pltpu.make_async_copy(dst, dst, recv).wait()


def greet(groups):
    barrier = pltpu.get_barrier_semaphore()
    for to in groups:
        pl.semaphore_signal(barrier, inc=1, device_id=to, device_id_type=MESH)
    return lambda: pl.semaphore_wait(barrier, len(groups))


class Place:
    def __init__(self):
        self.s = lax.axis_index("seq")
        self.g = lax.axis_index("grp")
        self.d = lax.axis_index("dp")
        self.z = self.s // 8
        self.y = (self.s // 2) % 4
        self.c = self.s % 2
        self.zo = 1 - self.z
        self.co = 1 - self.c
        self.yl = (self.y + 3) % 4
        self.yr = (self.y + 1) % 4
        self.yo = (self.y + 2) % 4
        self.gl = (self.g + 3) % 4
        self.gr = (self.g + 1) % 4
        self.go = (self.g + 2) % 4
        self.dl = (self.d + 3) % 4
        self.dr = (self.d + 1) % 4
        self.do = (self.d + 2) % 4

    def seq(self, z, y, c):
        return z * 8 + y * 2 + c


def add_into(dst, *others):
    total = dst[...].astype(F32)
    for other in others:
        total = total + other[...].astype(F32)
    dst[...] = total.astype(dst.dtype)


class Scatter4:
    def __init__(self, send, src, relay, from_left, from_right, sems, me, left, right, far, to):
        self.send, self.src, self.relay = send, src, relay
        self.from_left, self.from_right, self.sems = from_left, from_right, sems
        self.me, self.left, self.right, self.far, self.to = me, left, right, far, to
        self.passed = []

    def start(self, h):
        to = (self.left, self.right)[h]
        self.send(self.src(self.far, h), self.relay(h), self.sems.at[h], **self.to(to))

    def direct(self, h):
        if h:
            dst, to = self.from_right(1), self.left
        else:
            dst, to = self.from_left(0), self.right
        self.send(self.src(to, h), dst, self.sems.at[3 - h], **self.to(to))

    def pass_on(self, h):
        arrived(self.relay(h), self.sems.at[h])
        if h:
            dst, to = self.from_left(1), self.right
        else:
            dst, to = self.from_right(0), self.left
        add_into(self.src(to, h), self.relay(h))
        self.passed.append(self.send(self.src(to, h), dst, self.sems.at[4 + h], **self.to(to)))

    def finish(self):
        arrived(self.from_right(1), self.sems.at[2])
        arrived(self.from_left(0), self.sems.at[3])
        arrived(self.from_right(0), self.sems.at[4])
        arrived(self.from_left(1), self.sems.at[5])


class Gather4:
    def __init__(self, send, slot, half, sems, me, left, right, far, to):
        self.send, self.slot, self.half, self.sems = send, slot, half, sems
        self.me, self.left, self.right, self.far, self.to = me, left, right, far, to

    def start(self, own=None):
        own = self.slot(self.me) if own is None else own
        self.begun = [
            self.send(own, self.slot(self.me), self.sems.at[0], **self.to(self.right)),
            self.send(own, self.slot(self.me), self.sems.at[1], **self.to(self.left)),
        ]

    def pass_left(self):
        arrived(self.slot(self.left), self.sems.at[0])
        part = self.half(self.left, 0)
        self.send(part, part, self.sems.at[2], **self.to(self.right))

    def pass_right(self):
        arrived(self.slot(self.right), self.sems.at[1])
        part = self.half(self.right, 1)
        self.send(part, part, self.sems.at[3], **self.to(self.left))

    def finish(self):
        arrived(self.half(self.far, 0), self.sems.at[2])
        arrived(self.half(self.far, 1), self.sems.at[3])


ORDER = (
    "res0", "res1", "Rs00", "T11", "Rp100", "Rp000", "T10", "Rs01", "mod", "Ws", "LN00", "Rp001",
    "Rp101", "Rs10", "zwo", "LN01", "Rp110", "Rp010", "WR_", "Gz00", "GR000", "Gz01", "Rs11",
    "WL", "LN10", "T20", "GR010", "GL010", "GL001", "GL011", "GR011", "GR001", "Rp011", "Rp111",
    "Wf", "GL000", "Gz10", "GR100", "proj0", "GL100", "GL101", "LN11", "GR101", "att00", "att01",
    "Gz11", "att02", "GR110", "att03", "T21", "GL111", "GR111", "GL110", "bpa0", "bpb0", "Bs00",
    "proj1", "Bd00", "Bp100", "Bp000", "att10", "att11", "Bs01", "att12", "BX00", "att13", "Bd01",
    "Bp001", "Bp101", "BL00", "bpa1", "bpb1", "Bs10", "BX01", "Bd10", "Bp010", "Bp110", "AL00",
    "AR00", "Bs11", "BL01", "Af00", "Bd11", "BX10", "Bp011", "Bp111", "AR01", "AL01", "BX11",
    "Af01", "BL10", "BL11", "AS10", "zp0", "AS11", "AR10", "AL10", "ctl0", "O1", "Af10", "AL11",
    "AR11", "zp1a", "Af11", "zp1b", "O2", "Zp0y0", "Zp1y0", "Zp0x0", "Zp1x0", "Zp0y1", "Zp1y1",
    "Zp0x1", "Zp1x1", "ZB", "ZA", "ZS", "zgL_", "zgR_", "ctl1",
)
NT = (((1,), (1,)), ((), ()))
TN = (((0,), (0,)), ((), ()))
BLOCK = 256


def by_owner(columns, c):
    runs = columns.shape[1] // 384
    return jnp.concatenate(
        [columns[:, n * 384 + c * 192 : n * 384 + c * 192 + 192] for n in range(runs)], axis=1
    )


def block_kernel(
    lengths,
    timesteps,
    mod_weight,
    control,
    zero_weight,
    image_hidden,
    weight,
    text,
    text_cot,
    image_cot,
    attn_out,
    control_grad,
    zero_out,
    ctl,
    ctl_in,
    zw,
    zw_owner,
    base,
    wall,
    offset,
    stretch,
    partial,
    rg_relay,
    rg_left,
    rg_right,
    hidden,
    normed,
    qkv_out,
    joint,
    cots,
    tstage,
    cstage,
    attn,
    ostage,
    grads,
    both_grads,
    key_acc,
    value_acc,
    pair_sum,
    ry_relay,
    ry_left,
    ry_right,
    cross_out,
    cross_in,
    rows_all,
    rows_in,
    zacc,
    zsum,
    zx_relay,
    zx_left,
    zx_right,
    zy_relay,
    zy_left,
    zy_right,
    za_out,
    zb_out,
    za_in,
    zb_in,
    zall,
    text_mine,
    cots_mine,
    load_sem,
    send_sem,
    w_sem,
    share_sem,
    rg_sem,
    ag_sem,
    text_send,
    text_recv,
    stage_recv,
    cross_recv,
    qkv_sem,
    grads_sem,
    ry_sem,
    cross_sem,
    gg_sem,
    rows_sem,
    attn_send,
    attn_recv,
    zx_sem,
    zy_sem,
    za_sem,
    zb_sem,
    zg_sem,
):
    p = Place()
    send = Sends(send_sem)
    q = p.y * 2 + p.c
    partner = {"seq": p.seq(p.z, p.y, p.co)}
    across = {"seq": p.seq(p.zo, p.y, p.c)}
    to_y = lambda y: {"seq": p.seq(p.z, y, p.c)}
    to_g = lambda g: {"grp": g}
    to_d = lambda d: {"dp": d}

    all_here = greet(
        [{"seq": (p.s + k) % 16} for k in range(1, 16)]
        + [{"grp": p.gl}, {"grp": p.gr}]
        + [{"dp": (p.d + k) % 4} for k in range(1, 4)]
        + [{"dp": (p.d + k) % 4, "seq": p.seq(p.zo, p.y, p.c)} for k in range(1, 4)]
    )

    loads = []

    def load(src, dst):
        copy = pltpu.make_async_copy(src, dst, load_sem.at[len(loads)])
        copy.start()
        loads.append(copy)
        return copy

    load_control = load(control, ctl)
    load_zero = [
        load(zero_weight.at[:, pl.ds(n * 512, 512)], zw.at[:, pl.ds(n * 512, 512)])
        for n in range(6)
    ]
    load_weight = [
        load(weight.at[n], wall.at[p.d, :, pl.ds(n * HD, HD)]) for n in range(3)
    ]
    load_text = [
        load(text, text_mine),
        load(text_cot, cots_mine.at[0]),
        load(image_cot, cots_mine.at[1]),
    ]
    load_base = load(image_hidden, base)
    load_mod = [
        load(
            mod_weight.at[pl.ds(n % 8 * ROWS, ROWS), pl.ds(n // 8 * D, D)],
            pair_sum.at[n // 8, n // 4 % 2, n % 4],
        )
        for n in range(16)
    ]

    half = lambda h: pl.ds(h * HALF, HALF)
    part = lambda r: pl.ds(r * 16, 16)
    chunks = [(i, r) for i in range(2) for r in range(2)]
    steps = {}

    def step(name, *args):
        def add(f):
            steps[name] = lambda: f(*args)
            return f

        return add

    def residual_part(h):
        if h == 0:
            load_control.wait()
        for block in range(3 * h, 3 * h + 3):
            cols = pl.ds(block * 512, 512)
            load_zero[block].wait()
            product = jnp.dot(
                ctl[...].reshape(256, 768), zw[:, cols], preferred_element_type=F32
            )
            partial[:, :, :, cols] = product.astype(BF).reshape(4, 2, ROWS, 512)
        if h == 0:
            all_here()
            to_group[0, 0].start(0)
            to_group[0, 0].direct(0)

    step("res0", 0)(residual_part)
    step("res1", 1)(residual_part)

    to_group = {
        (i, r): Scatter4(
            send,
            lambda g, h, i=i, r=r: partial.at[g, i, part(r), half(h)],
            lambda h, i=i, r=r: rg_relay.at[i, h, part(r)],
            lambda h, i=i, r=r: rg_left.at[i, h, part(r)],
            lambda h, i=i, r=r: rg_right.at[i, h, part(r)],
            rg_sem.at[i * 2 + r],
            p.g,
            p.gl,
            p.gr,
            p.go,
            to_g,
        )
        for i, r in chunks
    }

    def group_start(n):
        if n:
            send.sent(to_group[chunks[n - 1]].passed)
        scatter = to_group[chunks[n]]
        for h in range(0 if n else 1, 2):
            scatter.start(h)
        scatter.direct(1)
        if n:
            scatter.direct(0)

    for n, (i, r) in enumerate(chunks):
        step(f"Rs{i}{r}", n)(group_start)
        for h in range(2):
            step(f"Rp{h}{i}{r}", h)(to_group[i, r].pass_on)

    plane = pl.ds(p.z * 4, 4)
    other_plane = pl.ds(p.zo * 4, 4)
    zy = p.z * 4 + p.y

    def text_pairs(i, to):
        near = pl.ds(pl.multiple_of((p.z * 8 + to) * HD, HD), HD)
        far = pl.ds(pl.multiple_of((p.zo * 8 + to) * HD, HD), HD)
        return (
            (text_mine.at[:, i, :, far], tstage.at[:, i, p.y, p.c], stage_recv.at[0, i]),
            (cots_mine.at[:, i, :, far], cstage.at[:, i, p.y, p.c], stage_recv.at[1, i]),
            (text_mine.at[:, i, :, near], joint.at[:, i, 0, zy, p.c], text_recv.at[0, i]),
            (cots_mine.at[:, i, :, near], cots.at[:, i, zy, p.c], text_recv.at[1, i]),
        )

    def text_copies(i, k):
        to = (q + k) % 8
        return [
            pltpu.make_async_remote_copy(
                src_ref=src,
                dst_ref=dst,
                send_sem=text_send.at[n, i, k],
                recv_sem=recv,
                device_id={"seq": p.z * 8 + to},
                device_id_type=MESH,
            )
            for n, (src, dst, recv) in enumerate(text_pairs(i, to))
        ]

    def text_first_hop(i):
        while load_text:
            load_text.pop().wait()

        @pl.loop(1, 8)
        def _(k):
            for copy in text_copies(i, k):
                copy.start()

        for src, dst, recv in text_pairs(i, q):
            pltpu.make_async_copy(src, dst, recv).start()

    def text_second_hop(i):
        arrived(tstage.at[:, i], stage_recv.at[0, i])
        arrived(cstage.at[:, i], stage_recv.at[1, i])
        send(tstage.at[:, i], joint.at[:, i, 0, plane], cross_recv.at[i, 0], **across)
        send(cstage.at[:, i], cots.at[:, i, plane], cross_recv.at[i, 1], **across)

    def text_wait(i):
        arrived(joint.at[:, i, 0, plane], text_recv.at[0, i])
        arrived(cots.at[:, i, plane], text_recv.at[1, i])
        arrived(joint.at[:, i, 0, other_plane], cross_recv.at[i, 0])
        arrived(cots.at[:, i, other_plane], cross_recv.at[i, 1])

    for i in range(2):
        step(f"T1{i}", i)(text_first_hop)
        step(f"T2{i}", i)(text_second_hop)

    mine_cols, pair_cols = pl.ds(0, 384), pl.ds(384, 384)
    weights = Gather4(
        send,
        lambda d: wall.at[d, :, mine_cols],
        lambda d, h: wall.at[d, pl.ds(h * 384, 384), mine_cols],
        w_sem,
        p.d,
        p.dl,
        p.dr,
        p.do,
        to_d,
    )

    def share_weight(d, sem):
        send(wall.at[d, :, mine_cols], wall.at[d, :, pair_cols], share_sem.at[sem], **partner)

    @step("Ws")
    def _():
        for copy in load_weight:
            copy.wait()
        weights.start()
        share_weight(p.d, 0)
        send(ctl, ctl_in, share_sem.at[4], **partner)

    @step("WL")
    def _():
        weights.pass_left()
        share_weight(p.dl, 1)

    @step("WR_")
    def _():
        weights.pass_right()
        share_weight(p.dr, 2)

    @step("Wf")
    def _():
        weights.finish()
        share_weight(p.do, 3)

    @step("mod")
    def _():
        for copy in load_mod:
            copy.wait()
        lane = lax.broadcasted_iota(jnp.int32, (1, FREQ // 2), 1).astype(F32)
        frequency = jnp.exp(lane * (-math.log(10000.0) / (FREQ // 2)))
        angles = jnp.concatenate([timesteps[i].astype(F32) * frequency for i in range(2)])
        embedding = jnp.concatenate([jnp.cos(angles), jnp.sin(angles)], axis=1)
        activated = (embedding / (1.0 + jnp.exp(-embedding))).astype(BF)
        offset[...] = jnp.dot(
            activated, pair_sum[0].reshape(FREQ, D), preferred_element_type=F32
        )
        stretch[...] = 1.0 + jnp.dot(
            activated, pair_sum[1].reshape(FREQ, D), preferred_element_type=F32
        )
        load_base.wait()

    @step("zwo")
    def _():
        for block in range(4):
            columns = zw[:, pl.ds(block * 768, 768)].astype(F32)
            for c in range(2):
                zw_owner[c, :, pl.ds(block * 384, 384)] = by_owner(columns, c).astype(BF)

    gathers = {
        (i, r, which): Gather4(
            send,
            lambda y, i=i, r=r, z=z: normed.at[i, z, y, part(r)],
            lambda y, h, i=i, r=r, z=z: normed.at[i, z, y, part(r), half(h)],
            ag_sem.at[i * 2 + r, pl.ds(which * 4, 4)],
            p.y,
            p.yl,
            p.yr,
            p.yo,
            to_y,
        )
        for i, r in chunks
        for which, z in enumerate((p.z, p.zo))
    }

    def standardise(rows):
        values = rows.astype(F32)
        average = jnp.mean(values, axis=-1, keepdims=True)
        centred = values - average
        reciprocal = lax.rsqrt(jnp.mean(centred * centred, axis=-1, keepdims=True) + 1e-06)
        return centred * reciprocal, reciprocal

    def gather_first(i, r):
        to_group[i, r].finish()
        rows = part(r)
        for h in range(2):
            residual = (
                partial[p.g, i, rows, half(h)].astype(F32)
                + rg_left[i, h, rows].astype(F32)
                + rg_right[i, h, rows].astype(F32)
            )
            hidden[i, rows, half(h)] = (base[i, rows, half(h)].astype(F32) + residual).astype(BF)
        standard, _ = standardise(hidden[i, rows])
        normed[i, p.z, p.y, rows] = (
            standard * stretch[i : i + 1] + offset[i : i + 1]
        ).astype(BF)
        mine = normed.at[i, p.z, p.y, rows]
        send(mine, mine, ag_sem.at[i * 2 + r, 8], **across)
        gathers[i, r, 0].start()

    def gather_second(i, r):
        arrived(normed.at[i, p.zo, p.y, part(r)], ag_sem.at[i * 2 + r, 8])
        gathers[i, r, 1].start()

    for i, r in chunks:
        step(f"LN{i}{r}", i, r)(gather_first)
        step(f"Gz{i}{r}", i, r)(gather_second)
        for which in range(2):
            step(f"GL{i}{r}{which}")(gathers[i, r, which].pass_left)
            step(f"GR{i}{r}{which}")(gathers[i, r, which].pass_right)

    scaling = HD ** (-0.5)

    def project(i):
        for r in range(2):
            for which in range(2):
                gathers[i, r, which].finish()
        if i == 0:
            for n, d in enumerate((p.d, p.dl, p.dr, p.do)):
                arrived(wall.at[d, :, pair_cols], share_sem.at[n])
        product = jnp.dot(
            normed[i].reshape(256, D), wall[...].reshape(D, 768), preferred_element_type=F32
        ).astype(BF)
        for n in range(3):
            qkv_out[i, n] = product[:, 384 + n * HD : 384 + (n + 1) * HD].reshape(8, ROWS, HD)
        send(qkv_out.at[i], joint.at[:, i, 1, :, p.c], qkv_sem.at[i], **partner)
        for n in range(3):
            joint[n, i, 1, :, p.c] = product[:, n * HD : (n + 1) * HD].reshape(8, ROWS, HD)

    def attend(i, block):
        if block == 0:
            text_wait(i)
            arrived(joint.at[:, i, 1, :, p.co], qkv_sem.at[i])
        slots = pl.ds(block % 2 * 4, 4)
        query = joint[0, i, block // 2, slots].reshape(BLOCK, HD)
        cot = cots[block // 2, i, slots].reshape(BLOCK, HD)
        keys = joint[1, i].reshape(TXT + IMG, HD)
        values = joint[2, i].reshape(TXT + IMG, HD)
        scores = lax.dot_general(keys, query, NT, preferred_element_type=F32)
        text_live = lax.broadcasted_iota(jnp.int32, (TXT, 1), 0) < lengths[i]
        text_scores = jnp.where(text_live, scores[:TXT], -jnp.inf)
        image_scores = scores[TXT:]
        col_max = jnp.maximum(
            jnp.max(text_scores, axis=0, keepdims=True),
            jnp.max(image_scores, axis=0, keepdims=True),
        )
        rate = scaling * math.log2(math.e)
        text_terms = jnp.exp2((text_scores - col_max) * rate)
        image_terms = jnp.exp2((image_scores - col_max) * rate)
        share = 1.0 / (
            jnp.sum(text_terms, axis=0, keepdims=True) + jnp.sum(image_terms, axis=0, keepdims=True)
        )
        text_prob, image_prob = text_terms * share, image_terms * share
        image_low = image_prob.astype(BF)
        attended = lax.dot_general(
            values[:TXT], text_prob.astype(BF), TN, preferred_element_type=F32
        ) + lax.dot_general(values[TXT:], image_low, TN, preferred_element_type=F32)
        low_attended = attended.astype(BF).astype(F32)
        attn[block // 2, i, pl.ds(block % 2 * BLOCK, BLOCK)] = low_attended.T.astype(BF)
        dots = jnp.sum(cot.astype(F32).T * low_attended, axis=0, keepdims=True)
        prob_grad = lax.dot_general(values, cot, NT, preferred_element_type=F32)
        image_grad = (image_prob * (prob_grad[TXT:] - dots)).astype(BF)
        if block >= 2:
            text_grad = (text_prob * (prob_grad[:TXT] - dots)).astype(BF)
            query_grad = lax.dot_general(
                keys[:TXT], text_grad, TN, preferred_element_type=F32
            ) + lax.dot_general(keys[TXT:], image_grad, TN, preferred_element_type=F32)
            query_grad = (query_grad * scaling).T.astype(BF)
            grads[i, slots, :, :, :HD] = query_grad.reshape(4, 2, ROWS, HD)
        key_part = jnp.dot(image_grad, query, preferred_element_type=F32)
        value_part = jnp.dot(image_low, cot, preferred_element_type=F32)
        if block == 0:
            key_acc[...] = key_part
            value_acc[...] = value_part
        elif block < 3:
            key_acc[...] += key_part
            value_acc[...] += value_part
        else:
            key_grad = ((key_acc[...] + key_part) * scaling).astype(BF)
            value_grad = (value_acc[...] + value_part).astype(BF)
            grads[i, :, :, :, HD : 2 * HD] = key_grad.reshape(8, 2, ROWS, HD)
            grads[i, :, :, :, 2 * HD :] = value_grad.reshape(8, 2, ROWS, HD)
            send(
                grads.at[i, :, p.co], both_grads.at[i, :, :, pair_cols], grads_sem.at[i],
                **partner
            )
            both_grads[i, :, :, :384] = grads[i, :, p.c]

    for i in range(2):
        step(f"proj{i}", i)(project)
        for block in range(4):
            step(f"att{i}{block}", i, block)(attend)

    def back_project(i, h):
        if h == 0:
            arrived(both_grads.at[i, :, :, pair_cols], grads_sem.at[i])
        for block in range(2 * h, 2 * h + 2):
            cols = pl.ds(block * 768, 768)
            product = lax.dot_general(
                both_grads[i].reshape(256, 768), wall[block], NT, preferred_element_type=F32
            ).astype(BF)
            pair_sum[i, :, :, :, cols] = product.reshape(2, 4, ROWS, 768)

    round_y = {
        (i, r): Scatter4(
            send,
            lambda y, h, i=i, r=r: pair_sum.at[i, :, y, part(r), half(h)],
            lambda h, i=i, r=r: ry_relay.at[i, h, :, part(r)],
            lambda h, i=i, r=r: ry_left.at[i, h, :, part(r)],
            lambda h, i=i, r=r: ry_right.at[i, h, :, part(r)],
            ry_sem.at[i * 2 + r],
            p.y,
            p.yl,
            p.yr,
            p.yo,
            to_y,
        )
        for i, r in chunks
    }

    def scatter_start(i, r):
        round_y[i, r].start(0)
        round_y[i, r].start(1)

    def scatter_direct(i, r):
        round_y[i, r].direct(1)
        round_y[i, r].direct(0)

    def y_sum(i, r, z, h):
        return (
            pair_sum[i, z, p.y, part(r), half(h)].astype(F32)
            + ry_left[i, h, z, part(r)].astype(F32)
            + ry_right[i, h, z, part(r)].astype(F32)
        )

    def scatter_cross(i, r):
        round_y[i, r].finish()
        for h in range(2):
            cross_out[i, part(r), half(h)] = y_sum(i, r, p.zo, h).astype(BF)
        send(
            cross_out.at[i, part(r)], cross_in.at[i, part(r)], cross_sem.at[i * 2 + r], **across
        )

    def norm_back(i, r):
        mine = jnp.concatenate([y_sum(i, r, p.z, h) for h in range(2)], axis=1)
        standard, reciprocal = standardise(hidden[i, part(r)])
        arrived(cross_in.at[i, part(r)], cross_sem.at[i * 2 + r])
        scaled = (mine + cross_in[i, part(r)].astype(F32)) * stretch[i : i + 1]
        residual_grad = reciprocal * (
            scaled
            - jnp.mean(scaled, axis=-1, keepdims=True)
            - standard * jnp.mean(scaled * standard, axis=-1, keepdims=True)
        )
        for c in range(2):
            rows_all[c, p.g, i, part(r)] = by_owner(residual_grad, c).astype(BF)
        if i == 0:
            rows_gather[0, r].start()

    def rows_at(c, g, i, n):
        if i:
            return rows_all.at[c, g, 1, :, pl.ds(n * 768, 768)]
        return rows_all.at[c, g, 0, part(n)]

    def rows_in_at(i, n):
        if i:
            return rows_in.at[:, 1, :, pl.ds(n * 768, 768)]
        return rows_in.at[:, 0, part(n)]

    every = slice(None)
    rows_gather = {
        (i, n): Gather4(
            send,
            lambda g, i=i, n=n: rows_at(every, g, i, n),
            lambda g, h, i=i, n=n: rows_at(h, g, i, n),
            gg_sem.at[i * 2 + n],
            p.g,
            p.gl,
            p.gr,
            p.go,
            to_g,
        )
        for i, n in chunks
    }

    def rows_start(n):
        if n:
            send.sent(rows_gather[1, 0].begun)
        rows_gather[1, n].start()

    def rows_finish(i, n):
        rows_gather[i, n].finish()
        send(rows_at(p.co, every, i, n), rows_in_at(i, n), rows_sem.at[i * 2 + n], **partner)

    for i in range(2):
        step(f"bpa{i}", i, 0)(back_project)
        step(f"bpb{i}", i, 1)(back_project)
        step(f"AS1{i}", i)(rows_start)
    for i, r in chunks:
        step(f"Bs{i}{r}", i, r)(scatter_start)
        step(f"Bd{i}{r}", i, r)(scatter_direct)
        for h in range(2):
            step(f"Bp{h}{i}{r}", h)(round_y[i, r].pass_on)
        step(f"BX{i}{r}", i, r)(scatter_cross)
        step(f"BL{i}{r}", i, r)(norm_back)
        step(f"AL{i}{r}")(rows_gather[i, r].pass_left)
        step(f"AR{i}{r}")(rows_gather[i, r].pass_right)
        step(f"Af{i}{r}", i, r)(rows_finish)

    def attn_pairs(to):
        near = pl.ds(pl.multiple_of((p.z * 8 + to) * ROWS, ROWS), ROWS)
        far = pl.ds(pl.multiple_of((p.zo * 8 + to) * ROWS, ROWS), ROWS)
        cols = pl.ds(pl.multiple_of(p.s * HD, HD), HD)
        staged = pl.ds(pl.multiple_of(q * HD, HD), HD)
        return (
            (attn.at[:, :, near], attn_out.at[:, :, :, cols], attn_recv.at[0]),
            (attn.at[:, :, far], ostage.at[:, :, :, staged], attn_recv.at[1]),
        )

    def attn_copies(k):
        to = (q + k) % 8
        return [
            pltpu.make_async_remote_copy(
                src_ref=src,
                dst_ref=dst,
                send_sem=attn_send.at[n, k],
                recv_sem=recv,
                device_id={"seq": p.z * 8 + to},
                device_id_type=MESH,
            )
            for n, (src, dst, recv) in enumerate(attn_pairs(to))
        ]

    @step("O1")
    def _():
        @pl.loop(1, 8)
        def _(k):
            for copy in attn_copies(k):
                copy.start()

        for src, dst, recv in attn_pairs(q):
            pltpu.make_async_copy(src, dst, recv).start()

    half_cols = pl.ds(pl.multiple_of(p.z * 1024, 1024), 1024)
    other_cols = pl.ds(pl.multiple_of(p.zo * 1024, 1024), 1024)

    @step("O2")
    def _():
        arrived(ostage, attn_recv.at[1])
        send(ostage, attn_out.at[:, :, :, half_cols], attn_recv.at[2], **across)

    def control_part(i):
        total = 0.0
        for c in range(2):
            total = total + lax.dot_general(
                rows_all[c, :, i].reshape(128, HALF),
                zw_owner[c],
                NT,
                preferred_element_type=F32,
            )
        control_grad[:, i] = total.astype(BF).reshape(4, ROWS, 768)

    def zero_part(i, block):
        cols = pl.ds(block * 384, 384)
        left = jnp.concatenate(
            [ref.reshape(128, 384) for ref in (rows_all[p.c, :, i, :, cols], rows_in[:, i, :, cols])]
        )
        right = jnp.concatenate([ctl[:, i].reshape(128, 768), ctl_in[:, i].reshape(128, 768)])
        product = lax.dot_general(left, right, TN, preferred_element_type=F32)
        if i == 0:
            zacc[cols] = product
        else:
            z, y = block // 2, block % 2 * 2
            zsum[z, pl.ds(y, 2)] = (zacc[cols] + product).astype(BF).reshape(2, 192, 768)

    step("ctl0", 0)(control_part)
    step("ctl1", 1)(control_part)

    @step("zp0")
    def _():
        arrived(ctl_in, share_sem.at[4])
        for n in range(2):
            arrived(rows_in_at(0, n), rows_sem.at[n])
        for block in range(4):
            zero_part(0, block)

    cols_a, cols_b = pl.ds(0, 384), pl.ds(384, 384)
    quarter = lambda d: pl.ds(pl.multiple_of(d * 48, 16), 48)
    round_x = [
        Scatter4(
            send,
            lambda d, h, z=z: zsum.at[z, pl.ds(2 * h, 2), quarter(d), cols_a],
            lambda h, z=z: zx_relay.at[z, pl.ds(2 * h, 2)],
            lambda h, z=z: zx_left.at[z, pl.ds(2 * h, 2)],
            lambda h, z=z: zx_right.at[z, pl.ds(2 * h, 2)],
            zx_sem.at[z],
            p.d,
            p.dl,
            p.dr,
            p.do,
            to_d,
        )
        for z in range(2)
    ]
    zero_y = [
        Scatter4(
            send,
            lambda y, h, z=z: zsum.at[z, y, pl.ds(96 * h, 96), cols_b],
            lambda h, z=z: zy_relay.at[z, pl.ds(96 * h, 96)],
            lambda h, z=z: zy_left.at[z, pl.ds(96 * h, 96)],
            lambda h, z=z: zy_right.at[z, pl.ds(96 * h, 96)],
            zy_sem.at[z],
            p.y,
            p.yl,
            p.yr,
            p.yo,
            to_y,
        )
        for z in range(2)
    ]

    def zero_send(z):
        arrived(rows_in_at(1, z), rows_sem.at[2 + z])
        zero_part(1, 2 * z)
        zero_part(1, 2 * z + 1)
        for h in range(2):
            round_x[z].start(h)
            zero_y[z].start(h)
        for h in range(2):
            round_x[z].direct(h)
            zero_y[z].direct(h)

    step("zp1a", 0)(zero_send)
    step("zp1b", 1)(zero_send)
    for z in range(2):
        for h in range(2):
            step(f"Zp{h}x{z}", h)(round_x[z].pass_on)
            step(f"Zp{h}y{z}", h)(zero_y[z].pass_on)
    others = [(dz, dy) for dz in range(2) for dy in range(4) if dz or dy]

    @step("ZA")
    def _():
        for z in range(2):
            round_x[z].finish()
        for z in range(2):
            za_out[z] = (
                zsum[z, :, quarter(p.d), cols_a].astype(F32)
                + zx_left[z].astype(F32)
                + zx_right[z].astype(F32)
            ).astype(BF)
        for n, (dz, dy) in enumerate(others):
            z, y = (p.z + dz) % 2, (p.y + dy) % 4
            send(za_out.at[z, y], za_in.at[n], za_sem.at[n], seq=p.seq(z, y, p.c))

    @step("ZB")
    def _():
        for z in range(2):
            zero_y[z].finish()
        for z in range(2):
            zb_out[z] = (
                (
                    zsum[z, p.y, :, cols_b].astype(F32)
                    + zy_left[z].astype(F32)
                    + zy_right[z].astype(F32)
                )
                .astype(BF)
                .reshape(4, 48, 384)
            )
        for n, (dz, dd) in enumerate(others):
            z, d = (p.z + dz) % 2, (p.d + dd) % 4
            send(zb_out.at[z, d], zb_in.at[n], zb_sem.at[n], seq=p.seq(z, p.y, p.c), dp=d)

    zero_gather = Gather4(
        send,
        lambda d: zall.at[d],
        lambda d, h: zall.at[d, :, pl.ds(h * 384, 384)],
        zg_sem,
        p.d,
        p.dl,
        p.dr,
        p.do,
        to_d,
    )

    @step("ZS")
    def _():
        total = za_out[p.z, p.y].astype(F32)
        for n in range(7):
            arrived(za_in.at[n], za_sem.at[n])
            total = total + za_in[n].astype(F32)
        zall[p.d, :, cols_a] = total.astype(BF)
        total = zb_out[p.z, p.d].astype(F32)
        for n in range(7):
            arrived(zb_in.at[n], zb_sem.at[n])
            total = total + zb_in[n].astype(F32)
        zall[p.d, :, cols_b] = total.astype(BF)
        zero_gather.start()

    step("zgL_")(zero_gather.pass_left)
    step("zgR_")(zero_gather.pass_right)

    for name in ORDER:
        steps.pop(name)()
    assert not steps

    zero_gather.finish()
    zero_out[...] = zall[...].reshape(192, 768).astype(F32) * (16384 ** (-0.5))

    arrived(attn_out.at[:, :, :, half_cols], attn_recv.at[0])
    arrived(attn_out.at[:, :, :, other_cols], attn_recv.at[2])
    send.drain()

    @pl.loop(1, 8)
    def _(k):
        for i in range(2):
            for copy in text_copies(i, k):
                copy.wait_send()
        for copy in attn_copies(k):
            copy.wait_send()


def whole_block(*operands):
    dma = pltpu.SemaphoreType.DMA
    bf = lambda *shape: pltpu.VMEM(shape, BF)
    return pl.pallas_call(
        block_kernel,
        out_shape=(
            jax.ShapeDtypeStruct((2, 2, ROWS, HEADS * HD), BF),
            jax.ShapeDtypeStruct((4, 2, ROWS, 768), BF),
            jax.ShapeDtypeStruct((192, 768), F32),
        ),
        in_specs=[pl.BlockSpec(memory_space=pltpu.SMEM)] * 2 + [ANY] * 8,
        out_specs=(VMEM, VMEM, VMEM),
        scratch_shapes=[
            bf(4, 2, ROWS, 768),
            bf(4, 2, ROWS, 768),
            bf(768, D),
            bf(2, 768, HALF),
            bf(2, ROWS, D),
            bf(4, 768, 768),
            pltpu.VMEM((2, D), F32),
            pltpu.VMEM((2, D), F32),
            bf(4, 2, ROWS, D),
            bf(2, 2, ROWS, HALF),
            bf(2, 2, ROWS, HALF),
            bf(2, 2, ROWS, HALF),
            bf(2, ROWS, D),
            bf(2, 2, 4, ROWS, D),
            bf(2, 3, 8, ROWS, HD),
            bf(3, 2, 2, 8, 2, ROWS, HD),
            bf(2, 2, 8, 2, ROWS, HD),
            bf(3, 2, 4, 2, ROWS, HD),
            bf(2, 2, 4, 2, ROWS, HD),
            bf(2, 2, 512, HD),
            bf(2, 2, ROWS, 1024),
            bf(2, 8, 2, ROWS, 384),
            bf(2, 8, ROWS, 768),
            pltpu.VMEM((IMG, HD), F32),
            pltpu.VMEM((IMG, HD), F32),
            bf(2, 2, 4, ROWS, D),
            bf(2, 2, 2, ROWS, HALF),
            bf(2, 2, 2, ROWS, HALF),
            bf(2, 2, 2, ROWS, HALF),
            bf(2, ROWS, D),
            bf(2, ROWS, D),
            bf(2, 4, 2, ROWS, HALF),
            bf(4, 2, ROWS, HALF),
            pltpu.VMEM((HALF, 768), F32),
            bf(2, 4, 192, 768),
            bf(2, 4, 48, 384),
            bf(2, 4, 48, 384),
            bf(2, 4, 48, 384),
            bf(2, 192, 384),
            bf(2, 192, 384),
            bf(2, 192, 384),
            bf(2, 4, 48, 384),
            bf(2, 4, 48, 384),
            bf(7, 48, 384),
            bf(7, 48, 384),
            bf(4, 48, 768),
            bf(3, 2, ROWS, HEADS * HD),
            bf(2, 2, ROWS, HEADS * HD),
            dma((32,)),
            dma((224,)),
            dma((4,)),
            dma((5,)),
            dma((4, 6)),
            dma((4, 9)),
            dma((4, 2, 8)),
            dma((2, 2)),
            dma((2, 2)),
            dma((2, 2)),
            dma((2,)),
            dma((2,)),
            dma((4, 6)),
            dma((4,)),
            dma((4, 4)),
            dma((4,)),
            dma((2, 8)),
            dma((3,)),
            dma((2, 6)),
            dma((2, 6)),
            dma((7,)),
            dma((7,)),
            dma((4,)),
        ],
        compiler_params=pltpu.CompilerParams(
            collective_id=1, has_side_effects=True, vmem_limit_bytes=VMEM_LIMIT
        ),
        name="whole_block",
    )(*operands)


def hand_over_kernel(attn, control, zero, image_out, text_out, control_out, zero_out, sems):
    copies = [
        pltpu.make_async_copy(src, dst, sems.at[n])
        for n, (src, dst) in enumerate(
            (
                (attn.at[1], image_out),
                (attn.at[0], text_out),
                (control, control_out),
                (zero, zero_out),
            )
        )
    ]
    for copy in copies:
        copy.start()
    for copy in copies:
        copy.wait()


def hand_over(attn, control, zero):
    return pl.pallas_call(
        hand_over_kernel,
        out_shape=(
            jax.ShapeDtypeStruct(attn.shape[1:], BF),
            jax.ShapeDtypeStruct(attn.shape[1:], BF),
            jax.ShapeDtypeStruct(control.shape, BF),
            jax.ShapeDtypeStruct(zero.shape, F32),
        ),
        in_specs=[VMEM] * 3,
        out_specs=(ANY,) * 4,
        scratch_shapes=[pltpu.SemaphoreType.DMA((4,))],
        name="hand_over",
    )(attn, control, zero)


def body(
    image_hidden,
    control_hidden,
    text_qkv,
    text_lengths,
    timesteps,
    mod_weight,
    qkv_weight,
    zero_weight,
    image_cotangent,
    text_cotangent,
):
    attn_out, control_grad, zero_t = whole_block(
        text_lengths.reshape(2),
        timesteps.reshape(2),
        mod_weight,
        control_hidden.reshape(4, 2, ROWS, 768),
        zero_weight,
        image_hidden.reshape(2, ROWS, D),
        jnp.transpose(qkv_weight, (1, 0, 2)),
        text_qkv.reshape(3, 2, ROWS, HEADS * HD),
        text_cotangent.reshape(2, ROWS, HEADS * HD),
        image_cotangent.reshape(2, ROWS, HEADS * HD),
    )
    image_attn, text_attn, control_grad, zero_t = hand_over(attn_out, control_grad, zero_t)
    return (
        image_attn.reshape(2, 1, ROWS, HEADS * HD),
        text_attn.reshape(2, 1, ROWS, HEADS * HD),
        control_grad.reshape(8, 1, ROWS, 768),
        jnp.transpose(zero_t),
    )


def solution(mesh):
    placed = (
        P("grp", "dp", "seq", None),
        P(None, "dp", "seq", "grp"),
        P(None, "grp", "dp", "seq", None),
        P("grp", "dp"),
        P("grp", "dp"),
        P(),
        P("dp", None, "seq"),
        P("grp", None),
        P("grp", "dp", "seq", None),
        P("grp", "dp", "seq", None),
    )
    return jax.shard_map(
        body,
        mesh=mesh,
        in_specs=placed,
        out_specs=(
            P("grp", "dp", "seq", None),
            P("grp", "dp", "seq", None),
            P(None, "dp", "seq", "grp"),
            P("grp", "seq"),
        ),
        check_vma=False,
    )
```
